32 devices in a mesh: dp: 8 (over z, y), mp: 4 (over x, core).
Axes of the slice: x: 2, y: 2, z: 4, core: 2. Of those that a mesh axis runs over, the one named last changes fastest.
Arguments:
- tokens: bfloat16 [32, 412, 768], P('dp'), may hold values from -6 to 6
- cotangent: bfloat16 [32, 512, 768], P('dp'), may hold values from -6 to 6
- segment_ids: int32 [32, 412], P('dp'), may hold values from 0 to 3, never falling along the last dimension, each value on 1 to 206 neighbouring positions
- prompt_ids: int32 [100], replicated, may hold values from 0 to 32127
- rel_buckets: int32 [1023], replicated, may hold values from 0 to 31
- table: bfloat16 [32128, 768], P('dp'), may hold values from -6 to 6
- prompt_delta: float32 [76800], P('dp'), may hold values from -6 to 6
- norm1_gain: float32 [768], replicated, may hold values from 0.25 to 1.75
- w_query: bfloat16 [768, 768], P(None, 'mp'), may hold values from -0.0546875 to 0.0546875
- w_key: bfloat16 [768, 768], P(None, 'mp'), may hold values from -0.21875 to 0.21875
- w_value: bfloat16 [768, 768], P(None, 'mp'), may hold values from -0.21875 to 0.21875
- w_output: bfloat16 [768, 768], P('mp'), may hold values from -0.3125 to 0.3125
- rel_bias: float32 [32, 12], P(None, 'mp'), may hold values from -4 to 4
- norm2_gain: float32 [768], replicated, may hold values from 0.25 to 1.75
- w_inner: bfloat16 [768, 3072], P(None, 'mp'), may hold values from -0.21875 to 0.21875
- w_outer: bfloat16 [3072, 768], P('mp'), may hold values from -0.109375 to 0.109375
Outputs:
- out: bfloat16 [32, 512, 768], P('dp')
- grad_tokens: bfloat16 [32, 412, 768], P('dp')
- grad_prompt: float32 [76800], P('dp')
- grad_norm1: float32 [768], P('dp')
- grad_query: float32 [768, 768], P('dp', 'mp')
- grad_key: float32 [768, 768], P('dp', 'mp')
- grad_value: float32 [768, 768], P('dp', 'mp')
- grad_output: float32 [768, 768], P('mp', 'dp')
- grad_rel: float32 [32, 12], P('dp', 'mp')
- grad_norm2: float32 [768], P('dp')
- grad_inner: float32 [768, 3072], P('dp', 'mp')
- grad_outer: float32 [3072, 768], P('mp', 'dp')
The draws below stay inside these ranges and needn't reach their ends.
Inputs may be any that keep to these rules, and one draw needn't show every extreme that they name: `segment_ids`: in each pack the ids never fall and every id from 0 to 3 holds 1 to 206 rows; some id holds exactly 206.
All inputs are finite; a program needn't handle non-finite values.
Results may differ from the reference program's by a relative error of at most 0.025.
Values may be sent and summed in bfloat16 or wider, within the bound.
No kernel may reach another device: no remote copies, remote signals or barrier semaphores. Data moves between devices by JAX's collectives and lax.ppermute only.
A program may use at most 128 MiB of HBM per device.

```python
import math
import jax
import jax.numpy as jnp
import numpy as np
from jax import lax

D = 768
H = 12
DH = 64
FF = 3072
VOCAB = 32128
NB = 32
PROMPT = 100
ROWS = 512
TEXT = 412
PACKS = 32
N_MP = 4


def set_ends(entries, rng, smallest, high):
    longest = entries.shape.index(max(entries.shape))
    spots = []
    for shift in (0, 1):
        where = [jax.random.randint(jax.random.fold_in(rng, axis), (), 0, length) for axis, length in enumerate(entries.shape)]
        where[longest] = (where[longest] + shift) % entries.shape[longest]
        spots.append(tuple(where))
    return entries.at[spots[0]].set(smallest).at[spots[1]].set(high)


def with_spikes(drawn, key, source, target, blocks, factor):
    owner, partner = [(jnp.arange(drawn.shape[dim]) // (drawn.shape[dim] // blocks)).reshape([-1 if axis == dim else 1 for axis in range(drawn.ndim)]) for dim in (source, target)]
    chosen = jax.random.permutation(key, blocks)[partner]
    strong = (owner == chosen) | (owner == (partner + blocks // 2) % blocks)
    return jnp.where(strong, factor * drawn, drawn)


def block_scale(rng, dims, pieces, low, high):
    level, own = 1.0, jax.random.fold_in(rng, 6)
    for dim, shards_of in pieces:
        draws = jnp.exp(jax.random.uniform(jax.random.fold_in(own, dim), (shards_of,), jnp.float32, low / len(pieces), high / len(pieces)))
        level = level * jnp.repeat(draws, dims[dim] // shards_of).reshape([-1 if axis == dim else 1 for axis in range(len(dims))])
    return level


def split_up(amount, total, most, slope):
    loads = [(1 << 20) // math.isqrt(rank ** slope) + 1 for rank in range(2, amount + 1)]
    spare, counts = total - most - (amount - 1), [1] * (amount - 1)
    while spare > 0:
        candidates = [i for i in range(amount - 1) if counts[i] < most]
        pool, left = sum([loads[i] for i in candidates]), spare
        for i in candidates:
            extra = min(most - counts[i], max(1, left * loads[i] // pool), spare)
            counts[i] = counts[i] + extra
            spare = spare - extra
    return np.array([most] + counts)


def ragged(rng, number_of, total, most, slope):
    if number_of == 2:
        one = jax.random.randint(rng, (), max(1, total - most), min(most, total - 1) + 1)
        return jnp.stack([one, total - one])
    tallies = jnp.asarray(split_up(number_of, total, most, slope), jnp.int32)
    pairs = (number_of - 1) // 2
    giver, sink = tallies[1:1 + 2 * pairs:2], tallies[2:2 + 2 * pairs:2]
    margin = jnp.minimum(giver - 1, most - sink)
    passed = jax.random.randint(jax.random.fold_in(rng, 1), (pairs,), 0, 1 << 20) % (margin + 1)
    tallies = tallies.at[1:1 + 2 * pairs:2].set(giver - passed).at[2:2 + 2 * pairs:2].set(sink + passed)
    return tallies[jax.random.permutation(jax.random.fold_in(rng, 2), number_of)]


def gaussian(stream_key, shape, scale, bound, cuts=(), held_as=jnp.bfloat16):
    array = scale * jax.random.normal(stream_key, shape, jnp.float32)
    if cuts:
        array = array * block_scale(stream_key, shape, cuts, -0.22, 0.18)
    return jnp.clip(array, -bound, bound).astype(held_as)


def gaussian_with(own_key, extent, deviation, most, split, heavy, held_as=jnp.bfloat16):
    entries = deviation * jax.random.normal(own_key, extent, jnp.float32)
    if split:
        entries = entries * block_scale(own_key, extent, split, -0.22, 0.18)
    return jnp.clip(with_spikes(entries, jax.random.fold_in(own_key, 3), *heavy), -most, most).astype(held_as)


def setup_inputs(seed: int = 0) -> dict:
    key_list = jax.random.split(jax.random.key(seed), 17)
    return {
        "tokens": gaussian_with(key_list[0], (PACKS, TEXT, D), 1.0, 6.0, ((0, 8),), (0, 2, 8, 2.0)),
        "cotangent": gaussian_with(key_list[1], (PACKS, ROWS, D), 1.0, 6.0, ((0, 8),), (0, 2, 8, 2.0)),
        "segment_ids": jax.vmap(lambda own: jnp.searchsorted(jnp.cumsum(ragged(own, 4, TEXT, TEXT // 2, 1)), jnp.arange(TEXT), side="right"))(jax.random.split(key_list[2], PACKS)).reshape((PACKS, TEXT)).astype(jnp.int32),
        "prompt_ids": set_ends(jax.random.randint(key_list[3], (PROMPT,), 0, VOCAB), jax.random.fold_in(key_list[3], 1), 0, VOCAB - 1).astype(jnp.int32),
        "rel_buckets": set_ends(jax.random.randint(key_list[4], (2 * ROWS - 1,), 0, NB), jax.random.fold_in(key_list[4], 1), 0, NB - 1).astype(jnp.int32),
        "table": gaussian(key_list[5], (VOCAB, D), 1.0, 6.0, ((0, 8),)),
        "prompt_delta": gaussian(key_list[6], (PROMPT * D,), 1.0, 6.0, ((0, 8),), jnp.float32),
        "norm1_gain": jnp.clip(1.0 + 0.15 * jax.random.normal(key_list[7], (D,), jnp.float32), 0.25, 1.75),
        "w_query": gaussian(key_list[8], (D, H * DH), (16 * D) ** -0.5, 0.0546875, ((1, 4),)),
        "w_key": gaussian(key_list[9], (D, H * DH), D ** -0.5, 0.21875, ((1, 4),)),
        "w_value": gaussian(key_list[10], (D, H * DH), D ** -0.5, 0.21875, ((1, 4),)),
        "w_output": gaussian(key_list[11], (H * DH, D), (H * DH // 2) ** -0.5, 0.3125, ((0, 4),)),
        "rel_bias": gaussian(key_list[12], (NB, H), 1.0, 4.0, ((1, 4),), jnp.float32),
        "norm2_gain": jnp.clip(1.0 + 0.15 * jax.random.normal(key_list[13], (D,), jnp.float32), 0.25, 1.75),
        "w_inner": gaussian(key_list[14], (D, FF), D ** -0.5, 0.21875, ((1, 4),)),
        "w_outer": gaussian(key_list[15], (FF, D), FF ** -0.5, 0.109375, ((0, 4),)),
    }


epsilon = 1e-06
blocked = -1000000000.0
highest = lax.Precision.HIGHEST

@jax.custom_vjp
def low(v):
    return lax.optimization_barrier(v.astype(jnp.bfloat16)).astype(jnp.float32)

@jax.custom_vjp
def low_back(v):
    return v

def low_keep(v):
    return (low(v), None)

def low_pass(kept, grad):
    return (grad,)

def back_keep(v):
    return (v, None)

def back_low(kept, grad):
    return (low(grad),)
low.defvjp(low_keep, low_pass)
low_back.defvjp(back_keep, back_low)

def matmul(left_side, right_side):
    return jnp.dot(left_side, right_side, precision=highest)

def rms_norm(values, scale_gain):
    return values * lax.rsqrt(lax.optimization_barrier(jnp.mean(values * values, axis=-1, keepdims=True)) + epsilon) * scale_gain

def gelu(values):
    return jax.nn.gelu(values, approximate=False)

def pack_layer(weights, head_rows, text_rows, allowed, bucket_grid):
    w_query, w_key, w_value, w_output, w_inner, w_outer, norm1_gain, norm2_gain, rel_bias = weights
    whole_rows = jnp.concatenate([head_rows, text_rows], axis=0)
    normed = low(rms_norm(whole_rows, norm1_gain))
    bias_grid = jnp.transpose(rel_bias[bucket_grid], (2, 0, 1))
    group_heads = H // N_MP
    group_width = group_heads * DH
    attention = jnp.zeros((ROWS, D), jnp.float32)
    for group_idx in range(N_MP):
        local_in = low_back(normed)
        columns = slice(group_idx * group_width, (group_idx + 1) * group_width)
        queries = low_back(low(matmul(local_in, w_query[:, columns]))).reshape(ROWS, group_heads, DH)
        keys_low = low_back(low(matmul(local_in, w_key[:, columns]))).reshape(ROWS, group_heads, DH)
        values_low = low_back(low(matmul(local_in, w_value[:, columns]))).reshape(ROWS, group_heads, DH)
        scores = jnp.einsum('ihd,jhd->hij', queries, keys_low, precision=highest)
        scores = scores + bias_grid[group_idx * group_heads:(group_idx + 1) * group_heads]
        scores = low_back(scores)
        scores = jnp.where(allowed[None], scores, blocked)
        row_top = lax.optimization_barrier(jnp.max(scores, axis=-1, keepdims=True))
        exp_scores = jnp.exp(scores - row_top)
        attn_probs = low(exp_scores / lax.optimization_barrier(jnp.sum(exp_scores, axis=-1, keepdims=True)))
        mixed_heads = jnp.einsum('hij,jhd->ihd', attn_probs, values_low, precision=highest).reshape(ROWS, group_width)
        mixed_heads = low_back(low(mixed_heads))
        attention = attention + low(matmul(mixed_heads, w_output[columns, :]))
    middle = whole_rows + low_back(attention)
    normed2 = low(rms_norm(middle, norm2_gain))
    hidden_width = FF // N_MP
    feed_sum = jnp.zeros((ROWS, D), jnp.float32)
    for group_idx in range(N_MP):
        local_in = low_back(normed2)
        columns = slice(group_idx * hidden_width, (group_idx + 1) * hidden_width)
        inner_val = low_back(matmul(local_in, w_inner[:, columns]))
        active = low(gelu(inner_val))
        feed_sum = feed_sum + low(matmul(active, w_outer[columns, :]))
    return middle + low_back(feed_sum)

def reference(tokens, cotangent, segment_ids, prompt_ids, rel_buckets, table, prompt_delta, norm1_gain, w_query, w_key, w_value, w_output, rel_bias, norm2_gain, w_inner, w_outer):
    prompt = low(table[prompt_ids].astype(jnp.float32) + prompt_delta.reshape(PROMPT, D))
    positions = jnp.arange(ROWS, dtype=jnp.int32)
    bucket_grid = rel_buckets[positions[None, :] - positions[:, None] + ROWS - 1]
    weights = (w_query.astype(jnp.float32), w_key.astype(jnp.float32), w_value.astype(jnp.float32), w_output.astype(jnp.float32), w_inner.astype(jnp.float32), w_outer.astype(jnp.float32), norm1_gain, norm2_gain, rel_bias)

    def one_pack(totals, micro_batch):
        text_rows, cot_pack, seg_ids = micro_batch
        seg_marks = jnp.concatenate([jnp.full((PROMPT,), -1, jnp.int32), seg_ids.astype(jnp.int32)])
        allowed = (positions[:, None] < PROMPT) | (positions[None, :] < PROMPT) | (seg_marks[:, None] == seg_marks[None, :])

        def layer_of(params, head_rows, body_rows):
            return pack_layer(params, head_rows, body_rows, allowed, bucket_grid)
        result, pullback = jax.vjp(layer_of, weights, prompt, text_rows.astype(jnp.float32))
        grad_weights, grad_head, grad_text = pullback(cot_pack.astype(jnp.float32))
        totals = jax.tree.map(lambda first, second: first + second, totals, (grad_weights, grad_head))
        return (totals, (result.astype(jnp.bfloat16), grad_text.astype(jnp.bfloat16)))
    initial = jax.tree.map(jnp.zeros_like, (weights, prompt))
    totals, (results, grad_tokens) = lax.scan(one_pack, initial, (tokens, cotangent, segment_ids))
    grad_weights, grad_head = totals
    g_query, g_key, g_value, g_output, g_inner, g_outer, g_norm1, g_norm2, g_rel = grad_weights
    return (results, grad_tokens, grad_head.reshape(-1), g_norm1, g_query, g_key, g_value, g_output, g_rel, g_norm2, g_inner, g_outer)
```

```python
import functools

import jax
import jax.numpy as jnp
from jax import lax
from jax.experimental import pallas as pl
from jax.experimental.pallas import tpu as pltpu
from jax.sharding import PartitionSpec as P

epsilon = 1e-06
blocked = -1000000000.0
highest = lax.Precision.HIGHEST
low = jnp.bfloat16
wide = jnp.float32
root_half = 0.7071067811865476
inv_root_tau = 0.3989422804014327
vmem_bytes = 48 * 1024 * 1024


def nn(left, right):
    return lax.dot_general(left, right, (((1,), (0,)), ((), ())), preferred_element_type=wide)


def nt(left, right):
    return lax.dot_general(left, right, (((1,), (1,)), ((), ())), preferred_element_type=wide)


def tn(left, right):
    return lax.dot_general(left, right, (((0,), (0,)), ((), ())), preferred_element_type=wide)


def params():
    return pltpu.CompilerParams(vmem_limit_bytes=vmem_bytes)


def swap(value, axis, bit):
    count = lax.axis_size(axis)
    return lax.ppermute(value, axis, [(i, i ^ bit) for i in range(count)])


def bits_of(count):
    return [1 << i for i in range(count.bit_length() - 1)]


def bias_kernel(line_ref, grid_ref):
    rows = grid_ref.shape[1]
    spread = jnp.broadcast_to(line_ref[0], (rows, 2 * rows))
    grid_ref[0] = pltpu.roll(spread, 0, 1, stride=1, stride_axis=0)[:, :rows]


def bias_grid_of(line):
    heads, _, double = line.shape
    rows = double // 2
    return pl.pallas_call(
        bias_kernel,
        grid=(heads,),
        in_specs=[pl.BlockSpec((1, 1, double), lambda h: (h, 0, 0))],
        out_specs=pl.BlockSpec((1, rows, rows), lambda h: (h, 0, 0)),
        out_shape=jax.ShapeDtypeStruct((heads, rows, rows), wide),
        compiler_params=params(),
        name="bias_grid",
    )(line)


def diag_kernel(grid_ref, line_ref):
    packs, _, rows, _ = grid_ref.shape
    zero = jnp.zeros((8, rows), wide)
    held = None
    for slab in range(rows // 8):
        part = grid_ref[0, 0, 8 * slab : 8 * slab + 8, :].astype(wide)
        for pack in range(1, packs):
            part = part + grid_ref[pack, 0, 8 * slab : 8 * slab + 8, :].astype(wide)
        part = jnp.concatenate([part, zero], axis=1)
        if slab:
            part = pltpu.roll(part, 2 * rows - 8 * slab, 1)
        held = part if held is None else held + part
    total = held[0:1]
    for row in range(1, 8):
        total = total + pltpu.roll(held[row : row + 1], 2 * rows - row, 1)
    line_ref[0] = total


def diagonal_sums(grid):
    packs, heads, rows, _ = grid.shape
    return pl.pallas_call(
        diag_kernel,
        grid=(heads,),
        in_specs=[pl.BlockSpec((packs, 1, rows, rows), lambda h: (0, h, 0, 0))],
        out_specs=pl.BlockSpec((1, 1, 2 * rows), lambda h: (h, 0, 0)),
        out_shape=jax.ShapeDtypeStruct((heads, 1, 2 * rows), wide),
        compiler_params=params(),
        name="diagonal_sums",
    )(grid)


def attention_kernel(
    prompt_len, heads, core_ref, joined_ref, bias_ref, seg_rows_ref, seg_cols_ref, w_out_ref,
    part_ref, probs_ref, mixed_ref,
):
    rows = joined_ref.shape[1]
    half = rows // 2
    width = w_out_ref.shape[0]
    size = width // heads
    mine = jnp.bitwise_xor(core_ref[0], 1 - pl.program_id(0))
    start = pl.multiple_of(mine * half, half)
    row_pos = start + lax.broadcasted_iota(jnp.int32, (half, rows), 0)
    col_pos = lax.broadcasted_iota(jnp.int32, (half, rows), 1)
    allowed = (
        (row_pos < prompt_len) | (col_pos < prompt_len) | (seg_rows_ref[0] == seg_cols_ref[0])
    )
    queries = joined_ref[0, pl.ds(start, half), :width]
    mixed = []
    for head in range(heads):
        keys = joined_ref[0, :, width + head * size : width + (head + 1) * size]
        values = joined_ref[0, :, 2 * width + head * size : 2 * width + (head + 1) * size]
        scores = nt(queries[:, head * size : (head + 1) * size], keys) + bias_ref[head]
        scores = jnp.where(allowed, scores, blocked)
        top = jnp.max(scores, axis=-1, keepdims=True)
        raised = jnp.exp(scores - top)
        total = jnp.sum(raised, axis=-1, keepdims=True)
        probs = (raised * (1.0 / total)).astype(low)
        probs_ref[0, head] = probs
        mixed.append(nn(probs, values).astype(low))
    mixed = jnp.concatenate(mixed, axis=1)
    mixed_ref[0] = mixed
    part_ref[0] = nn(mixed, w_out_ref[...]).astype(low)


def attention_forward(pack, prompt_len, core, joined, bias, seg_rows, seg_cols, w_out):
    _, rows, triple = joined.shape
    heads = bias.shape[0]
    width, model = w_out.shape
    half = rows // 2

    def row_block(t, core_ref):
        return jnp.bitwise_xor(core_ref[0], 1 - t)

    return pl.pallas_call(
        functools.partial(attention_kernel, prompt_len, heads),
        grid_spec=pltpu.PrefetchScalarGridSpec(
            num_scalar_prefetch=1,
            grid=(2,),
            in_specs=[
                pl.BlockSpec((1, rows, triple), lambda t, c: (pack, 0, 0)),
                pl.BlockSpec((heads, half, rows), lambda t, c: (0, row_block(t, c), 0)),
                pl.BlockSpec((1, half, 1), lambda t, c: (pack, row_block(t, c), 0)),
                pl.BlockSpec((1, 1, rows), lambda t, c: (pack, 0, 0)),
                pl.BlockSpec((width, model), lambda t, c: (0, 0)),
            ],
            out_specs=[
                pl.BlockSpec((1, half, model), lambda t, c: (t, 0, 0)),
                pl.BlockSpec((1, heads, half, rows), lambda t, c: (0, 0, row_block(t, c), 0)),
                pl.BlockSpec((1, half, width), lambda t, c: (0, row_block(t, c), 0)),
            ],
        ),
        out_shape=[
            jax.ShapeDtypeStruct((2, half, model), low),
            jax.ShapeDtypeStruct((1, heads, rows, rows), low),
            jax.ShapeDtypeStruct((1, rows, width), low),
        ],
        compiler_params=params(),
        name="attention_forward",
    )(core, joined, bias, seg_rows, seg_cols, w_out)


def feed_kernel(
    core_ref, own_ref, far_ref, cot_ref, w_in_ref, w_out_ref,
    feed_ref, back_ref, normed_ref, active_ref, hidden_ref,
):
    normed = jnp.where(pl.program_id(0) == 0, far_ref[...], own_ref[...])
    normed_ref[0] = normed
    inner = nn(normed, w_in_ref[...])
    share = 0.5 + 0.5 * lax.erf(inner * root_half)
    active = (inner * share).astype(low)
    active_ref[0] = active
    slope = share + inner * (jnp.exp(-0.5 * inner * inner) * inv_root_tau)
    hidden = (nt(cot_ref[0], w_out_ref[...]) * slope).astype(low)
    hidden_ref[0] = hidden
    back_ref[0] = nt(hidden, w_in_ref[...]).astype(low)
    feed_ref[0] = nn(active, w_out_ref[...]).astype(low)


def feed_forward(pack, core, own, far, cot, w_in, w_out):
    half, model = own.shape
    rows = 2 * half
    hidden = w_in.shape[1]

    def row_block(t, core_ref):
        return jnp.bitwise_xor(core_ref[0], 1 - t)

    return pl.pallas_call(
        feed_kernel,
        grid_spec=pltpu.PrefetchScalarGridSpec(
            num_scalar_prefetch=1,
            grid=(2,),
            in_specs=[
                pl.BlockSpec((half, model), lambda t, c: (0, 0)),
                pl.BlockSpec((half, model), lambda t, c: (0, 0)),
                pl.BlockSpec((1, half, model), lambda t, c: (pack, row_block(t, c), 0)),
                pl.BlockSpec((model, hidden), lambda t, c: (0, 0)),
                pl.BlockSpec((hidden, model), lambda t, c: (0, 0)),
            ],
            out_specs=[
                pl.BlockSpec((1, half, model), lambda t, c: (t, 0, 0)),
                pl.BlockSpec((1, half, model), lambda t, c: (t, 0, 0)),
                pl.BlockSpec((1, half, model), lambda t, c: (0, row_block(t, c), 0)),
                pl.BlockSpec((1, half, hidden), lambda t, c: (0, row_block(t, c), 0)),
                pl.BlockSpec((1, half, hidden), lambda t, c: (0, row_block(t, c), 0)),
            ],
        ),
        out_shape=[
            jax.ShapeDtypeStruct((2, half, model), low),
            jax.ShapeDtypeStruct((2, half, model), low),
            jax.ShapeDtypeStruct((1, rows, model), low),
            jax.ShapeDtypeStruct((1, rows, hidden), low),
            jax.ShapeDtypeStruct((1, rows, hidden), low),
        ],
        compiler_params=params(),
        name="feed_forward",
    )(core, own, far, cot, w_in, w_out)


def attention_back_kernel(
    heads, core_ref, own_ref, far_ref, w_out_ref, probs_ref, joined_ref, w_joined_ref,
    part_ref, grads_ref, scores_ref, whole_ref,
):
    rows = joined_ref.shape[1]
    half = rows // 2
    width = w_out_ref.shape[0]
    size = width // heads
    core = core_ref[0]
    own_start = pl.multiple_of(core * half, half)
    far_start = pl.multiple_of((1 - core) * half, half)
    whole_ref[0, pl.ds(own_start, half), :] = own_ref[...]
    whole_ref[0, pl.ds(far_start, half), :] = far_ref[...]
    grad_mixed = nt(whole_ref[0], w_out_ref[...]).astype(low)
    grad_queries, grad_keys, grad_values = [], [], []
    for head in range(heads):
        cols = slice(head * size, (head + 1) * size)
        queries = joined_ref[0, :, head * size : (head + 1) * size]
        keys = joined_ref[0, :, width + head * size : width + (head + 1) * size]
        values = joined_ref[0, :, 2 * width + head * size : 2 * width + (head + 1) * size]
        probs = probs_ref[0, head]
        upstream = grad_mixed[:, cols]
        grad_probs = nt(upstream, values)
        spread = probs.astype(wide)
        inner = jnp.sum(spread * grad_probs, axis=-1, keepdims=True)
        grad_scores = (spread * (grad_probs - inner)).astype(low)
        scores_ref[0, head] = grad_scores
        grad_values.append(tn(upstream, probs).T)
        grad_keys.append(tn(queries, grad_scores).T)
        grad_queries.append(nn(grad_scores, keys))
    grads = jnp.concatenate(grad_queries + grad_keys + grad_values, axis=1).astype(low)
    grads_ref[0] = grads
    part_ref[0] = nt(grads_ref[0, pl.ds(far_start, half), :], w_joined_ref[...]).astype(low)
    part_ref[1] = nt(grads_ref[0, pl.ds(own_start, half), :], w_joined_ref[...]).astype(low)


def attention_backward(pack, core, own, far, w_out, probs, joined, w_joined):
    _, rows, triple = joined.shape
    heads = probs.shape[1]
    width, model = w_out.shape
    half = rows // 2
    return pl.pallas_call(
        functools.partial(attention_back_kernel, heads),
        grid_spec=pltpu.PrefetchScalarGridSpec(
            num_scalar_prefetch=1,
            grid=(1,),
            in_specs=[
                pl.BlockSpec((half, model), lambda t, c: (0, 0)),
                pl.BlockSpec((half, model), lambda t, c: (0, 0)),
                pl.BlockSpec((width, model), lambda t, c: (0, 0)),
                pl.BlockSpec((1, heads, rows, rows), lambda t, c: (0, 0, 0, 0)),
                pl.BlockSpec((1, rows, triple), lambda t, c: (pack, 0, 0)),
                pl.BlockSpec((model, triple), lambda t, c: (0, 0)),
            ],
            out_specs=[
                pl.BlockSpec((2, half, model), lambda t, c: (0, 0, 0)),
                pl.BlockSpec((1, rows, triple), lambda t, c: (0, 0, 0)),
                pl.BlockSpec((1, heads, rows, rows), lambda t, c: (0, 0, 0, 0)),
                pl.BlockSpec((1, rows, model), lambda t, c: (0, 0, 0)),
            ],
        ),
        out_shape=[
            jax.ShapeDtypeStruct((2, half, model), low),
            jax.ShapeDtypeStruct((1, rows, triple), low),
            jax.ShapeDtypeStruct((1, heads, rows, rows), low),
            jax.ShapeDtypeStruct((1, rows, model), low),
        ],
        compiler_params=params(),
        name="attention_backward",
    )(core, own, far, w_out, probs, joined, w_joined)


def sum_over_groups(part):
    count = lax.axis_size("mp")
    total = part[1].astype(wide) + swap(part[0], "mp", 1).astype(wide)
    for bit in bits_of(count)[1:]:
        mine = total.astype(low)
        total = mine.astype(wide) + swap(mine, "mp", bit).astype(wide)
    return total


def scatter_rows(share):
    count = lax.axis_size("dp")
    where = lax.axis_index("dp")
    bits = bits_of(count)
    order = bits[:1] + bits[1:][::-1]
    model, width = share.shape
    left = list(reversed(bits))
    share = share.reshape([2] * len(bits) + [model // count, width])
    for bit in order:
        axis = left.index(bit)
        left.remove(bit)
        side = (where // bit) % 2
        send = lax.dynamic_index_in_dim(share, 1 - side, axis, keepdims=False)
        keep = lax.dynamic_index_in_dim(share, side, axis, keepdims=False)
        share = keep.astype(wide) + swap(send, "dp", bit).astype(wide)
        if left:
            share = share.astype(low)
    return share


def norm_back(upstream, gain, values):
    scale = lax.rsqrt(jnp.mean(values * values, axis=-1, keepdims=True) + epsilon)
    scaled = upstream * gain
    inner = jnp.mean(scaled * values, axis=-1, keepdims=True)
    grad = scale * scaled - values * (scale * scale * scale * inner)
    return grad, jnp.sum(upstream * values * scale, axis=0)


def rms_norm(values, gain):
    return values * lax.rsqrt(jnp.mean(values * values, axis=-1, keepdims=True) + epsilon) * gain


def find_prompt(prompt_ids, table, prompt_delta):
    prompt_len = prompt_ids.shape[0]
    table_rows, model = table.shape
    groups = lax.axis_size("mp")
    part = -(-prompt_len // (16 * groups)) * 16
    dp_index, mp_index = lax.axis_index("dp"), lax.axis_index("mp")
    padded = jnp.pad(prompt_ids, (0, part * groups - prompt_len), constant_values=-1)
    ids = lax.dynamic_slice_in_dim(padded, mp_index * part, part)
    local = dp_index * table_rows + jnp.arange(table_rows, dtype=jnp.int32)
    selector = (ids[:, None] == local[None, :]).astype(low)
    looked = jnp.dot(selector, table, preferred_element_type=wide)
    placed = lax.dynamic_update_slice_in_dim(
        jnp.zeros((part * groups * model,), wide), prompt_delta, dp_index * prompt_delta.shape[0], 0
    ).reshape(part * groups, model)
    total = looked + lax.dynamic_slice_in_dim(placed, mp_index * part, part, axis=0)
    for bit in bits_of(lax.axis_size("dp")):
        total = total + swap(total, "dp", bit)
    mine = total.astype(low)
    pieces = jnp.stack([mine] + [swap(mine, "mp", k) for k in range(1, groups)])
    order = jnp.bitwise_xor(mp_index, jnp.arange(groups))
    return jnp.take(pieces, order, axis=0).reshape(part * groups, model)[:prompt_len]


def body(
    tokens, cotangent, segment_ids, prompt_ids, rel_buckets, table, prompt_delta, norm1_gain,
    w_query, w_key, w_value, w_output, rel_bias, norm2_gain, w_inner, w_outer,
):
    prompt_len = prompt_ids.shape[0]
    packs, rows, model = cotangent.shape
    bucket_count, heads = rel_bias.shape
    width = w_query.shape[1]
    hidden = w_inner.shape[1]
    half = rows // 2
    groups = lax.axis_size("dp")
    core = lax.axis_index("mp") % 2
    core_ref = core.astype(jnp.int32).reshape(1)
    own_start = core * half

    bucket_hot = (
        rel_buckets[:, None] == jnp.arange(bucket_count, dtype=jnp.int32)[None, :]
    ).astype(wide)
    bucket_hot = jnp.pad(bucket_hot, ((0, 1), (0, 0)))
    turned = jnp.roll(bucket_hot, -(rows - 1), axis=0)
    bias_line = jnp.dot(turned, rel_bias, precision=highest).T
    bias = bias_grid_of(bias_line[:, None, :])

    prompt = find_prompt(prompt_ids, table, prompt_delta)
    joined_rows = jnp.concatenate(
        [jnp.broadcast_to(prompt[None], (packs, prompt_len, model)), tokens], axis=1
    )
    normed1 = rms_norm(joined_rows.astype(wide), norm1_gain).astype(low)
    w_joined = jnp.concatenate([w_query, w_key, w_value], axis=1)
    joined = jnp.dot(
        normed1.reshape(packs * rows, model), w_joined, preferred_element_type=wide
    ).astype(low).reshape(packs, rows, 3 * width)
    own_rows = lax.dynamic_slice_in_dim(joined_rows, own_start, half, axis=1)
    own_cot = lax.dynamic_slice_in_dim(cotangent, own_start, half, axis=1)
    marks = jnp.pad(segment_ids, ((0, 0), (prompt_len, 0)), constant_values=-1)
    seg_rows, seg_cols = marks[:, :, None], marks[:, None, :]

    def whole(own, far):
        first = jnp.where(core == 0, own, far)
        second = jnp.where(core == 0, far, own)
        return jnp.concatenate([first, second], axis=0)

    probs, mixed, middle, saved = [], [], [], []
    for pack in range(packs):
        part, prob, mix = attention_forward(
            pack, prompt_len, core_ref, joined, bias, seg_rows, seg_cols, w_output
        )
        probs.append(prob)
        mixed.append(mix)
        middle.append(own_rows[pack].astype(wide) + sum_over_groups(part))
    for pack in range(packs):
        normed2 = rms_norm(middle[pack], norm2_gain).astype(low)
        far = swap(normed2, "mp", 1)
        saved.append(feed_forward(pack, core_ref, normed2, far, cotangent, w_inner, w_outer))
    grads, scores, wholes, tokens_out, gain1, gain2, heads_out = [], [], [], [], 0.0, 0.0, 0.0
    for pack in range(packs):
        summed = sum_over_groups(saved[pack][1])
        grad_norm, gain_share = norm_back(summed, norm2_gain, middle[pack])
        gain2 = gain2 + gain_share
        grad_middle = own_cot[pack].astype(wide) + grad_norm
        grad_low = grad_middle.astype(low)
        far = swap(grad_low, "mp", 1)
        part, grad_joined, score, whole_low = attention_backward(
            pack, core_ref, grad_low, far, w_output, probs[pack], joined, w_joined
        )
        grads.append(grad_joined)
        scores.append(score)
        wholes.append(whole_low)
        summed = sum_over_groups(part)
        grad_norm, gain_share = norm_back(summed, norm1_gain, own_rows[pack].astype(wide))
        gain1 = gain1 + gain_share
        grad_rows = grad_middle + grad_norm
        heads_out = heads_out + grad_rows[:prompt_len]
        rows_low = grad_rows.astype(low)
        tokens_out.append(whole(rows_low, swap(rows_low, "mp", 1))[prompt_len:])
    results = []
    for pack in range(packs):
        result = (middle[pack] + sum_over_groups(saved[pack][0])).astype(low)
        results.append(whole(result, swap(result, "mp", 1)))

    def flat(blocks):
        return jnp.concatenate(blocks, axis=0).reshape(packs * rows, -1)

    normed2_all = flat([s[2] for s in saved])
    active_all = flat([s[3] for s in saved])
    hidden_all = flat([s[4] for s in saved])
    cot_all = cotangent.reshape(packs * rows, model)
    inner_grad = scatter_rows(tn(normed2_all, hidden_all).astype(low))
    outer_grad = scatter_rows(tn(cot_all, active_all).astype(low)).T
    output_grad = scatter_rows(tn(flat(wholes), flat(mixed)).astype(low)).T

    line = diagonal_sums(jnp.concatenate(scores, axis=0))[:, 0, :]
    rel_grad = jnp.einsum("ht,tb->bh", line, turned, precision=highest)
    block = model // groups
    rel_column = jnp.pad(
        rel_grad.reshape(groups, -1), ((0, 0), (0, block - bucket_count * heads // groups))
    ).reshape(model, 1)
    heads_out = jnp.where(core == 0, heads_out, 0.0)
    small = jnp.concatenate(
        [heads_out.reshape(model, prompt_len), gain1[:, None], gain2[:, None]], axis=1
    ).astype(low)
    small = small.astype(wide) + swap(small, "mp", 1).astype(wide)
    small = jnp.pad(
        jnp.concatenate([small, rel_column], axis=1), ((0, 0), (0, 128 - prompt_len - 3))
    ).astype(low)
    joined_grad = tn(normed1.reshape(packs * rows, model), flat(grads)).astype(low)
    tail = scatter_rows(jnp.concatenate([joined_grad, small], axis=1))
    query_grad = tail[:, :width]
    key_grad = tail[:, width : 2 * width]
    value_grad = tail[:, 2 * width : 3 * width]
    prompt_grad = tail[:, 3 * width : 3 * width + prompt_len].reshape(-1)
    gain1_grad = tail[:, 3 * width + prompt_len]
    gain2_grad = tail[:, 3 * width + prompt_len + 1]
    rel_out = tail[: bucket_count * heads // groups, 3 * width + prompt_len + 2].reshape(-1, heads)
    return (
        jnp.stack(results), jnp.stack(tokens_out), prompt_grad, gain1_grad, query_grad, key_grad,
        value_grad, output_grad, rel_out, gain2_grad, inner_grad, outer_grad,
    )


def solution(mesh):
    in_specs = (
        P("dp", None, None),
        P("dp", None, None),
        P("dp", None),
        P(),
        P(),
        P("dp", None),
        P("dp"),
        P(),
        P(None, "mp"),
        P(None, "mp"),
        P(None, "mp"),
        P("mp", None),
        P(None, "mp"),
        P(),
        P(None, "mp"),
        P("mp", None),
    )
    out_specs = (
        P("dp", None, None),
        P("dp", None, None),
        P("dp"),
        P("dp"),
        P("dp", "mp"),
        P("dp", "mp"),
        P("dp", "mp"),
        P("mp", "dp"),
        P("dp", "mp"),
        P("dp"),
        P("dp", "mp"),
        P("mp", "dp"),
    )
    return jax.shard_map(body, mesh=mesh, in_specs=in_specs, out_specs=out_specs, check_vma=False)
```

```python
import functools

import jax
import jax.numpy as jnp
from jax import lax
from jax.experimental import pallas as pl
from jax.experimental.pallas import tpu as pltpu
from jax.sharding import PartitionSpec as P

epsilon = 1e-06
blocked = -1000000000.0
highest = lax.Precision.HIGHEST
low = jnp.bfloat16
wide = jnp.float32
root_half = 0.7071067811865476
inv_root_tau = 0.3989422804014327
vmem_bytes = 32 * 1024 * 1024


def nn(left, right):
    return lax.dot_general(left, right, (((1,), (0,)), ((), ())), preferred_element_type=wide)


def nt(left, right):
    return lax.dot_general(left, right, (((1,), (1,)), ((), ())), preferred_element_type=wide)


def tn(left, right):
    return lax.dot_general(left, right, (((0,), (0,)), ((), ())), preferred_element_type=wide)


def params():
    return pltpu.CompilerParams(vmem_limit_bytes=vmem_bytes)


def swap(value, axis, bit):
    count = lax.axis_size(axis)
    return lax.ppermute(value, axis, [(i, i ^ bit) for i in range(count)])


def bits_of(count):
    return [1 << i for i in range(count.bit_length() - 1)]


def rms_norm(values, gain):
    return values * lax.rsqrt(jnp.mean(values * values, axis=-1, keepdims=True) + epsilon) * gain


def bias_kernel(line_ref, grid_ref):
    rows = grid_ref.shape[1]
    spread = jnp.broadcast_to(line_ref[0], (rows, 2 * rows))
    grid_ref[0] = pltpu.roll(spread, 0, 1, stride=1, stride_axis=0)[:, :rows]


def bias_grid_of(line):
    heads, _, double = line.shape
    rows = double // 2
    return pl.pallas_call(
        bias_kernel,
        grid=(heads,),
        in_specs=[pl.BlockSpec((1, 1, double), lambda h: (h, 0, 0))],
        out_specs=pl.BlockSpec((1, rows, rows), lambda h: (h, 0, 0)),
        out_shape=jax.ShapeDtypeStruct((heads, rows, rows), wide),
        compiler_params=params(),
        name="bias_grid",
    )(line)


def diag_kernel(grid_ref, line_ref):
    packs, _, rows, _ = grid_ref.shape
    zero = jnp.zeros((8, rows), wide)
    held = None
    for slab in range(rows // 8):
        part = grid_ref[0, 0, 8 * slab : 8 * slab + 8, :].astype(wide)
        for pack in range(1, packs):
            part = part + grid_ref[pack, 0, 8 * slab : 8 * slab + 8, :].astype(wide)
        part = jnp.concatenate([part, zero], axis=1)
        if slab:
            part = pltpu.roll(part, 2 * rows - 8 * slab, 1)
        held = part if held is None else held + part
    total = held[0:1]
    for row in range(1, 8):
        total = total + pltpu.roll(held[row : row + 1], 2 * rows - row, 1)
    line_ref[0] = total


def diagonal_sums(grid):
    packs, heads, rows, _ = grid.shape
    return pl.pallas_call(
        diag_kernel,
        grid=(heads,),
        in_specs=[pl.BlockSpec((packs, 1, rows, rows), lambda h: (0, h, 0, 0))],
        out_specs=pl.BlockSpec((1, 1, 2 * rows), lambda h: (h, 0, 0)),
        out_shape=jax.ShapeDtypeStruct((heads, 1, 2 * rows), wide),
        compiler_params=params(),
        name="diagonal_sums",
    )(grid)


def shifted_text_kernel(tokens_ref, gain_ref, w_query_ref, w_key_ref, w_value_ref,
                        rows_ref, normed_ref, joined_ref, wide_ref):
    rows = rows_ref.shape[1]
    prompt_len = rows - tokens_ref.shape[1]
    width = w_query_ref.shape[0]
    wide_ref[:prompt_len, :] = jnp.zeros((prompt_len, wide_ref.shape[1]), wide)
    wide_ref[prompt_len:, :] = tokens_ref[0].astype(wide)
    values = wide_ref[...]
    rows_ref[0] = values.astype(low)
    normed = rms_norm(values, gain_ref[...]).astype(low)
    normed_ref[0] = normed
    for place, weight_ref in enumerate((w_query_ref, w_key_ref, w_value_ref)):
        joined_ref[0, :, place * width : (place + 1) * width] = nt(normed, weight_ref[...]).astype(low)


def text_projections(rows, tokens, gain, w_query, w_key, w_value):
    packs, text, model = tokens.shape
    width = w_query.shape[0]
    fixed = lambda p: (0, 0)
    moving = lambda p: (p, 0, 0)
    return pl.pallas_call(
        shifted_text_kernel,
        grid=(packs,),
        in_specs=[
            pl.BlockSpec((1, text, model), moving),
            pl.BlockSpec((1, model), fixed),
            pl.BlockSpec((width, model), fixed),
            pl.BlockSpec((width, model), fixed),
            pl.BlockSpec((width, model), fixed),
        ],
        out_specs=[
            pl.BlockSpec((1, rows, model), moving),
            pl.BlockSpec((1, rows, model), moving),
            pl.BlockSpec((1, rows, 3 * width), moving),
        ],
        out_shape=[
            jax.ShapeDtypeStruct((packs, rows, model), low),
            jax.ShapeDtypeStruct((packs, rows, model), low),
            jax.ShapeDtypeStruct((packs, rows, 3 * width), low),
        ],
        scratch_shapes=[pltpu.VMEM((rows, model), wide)],
        compiler_params=params(),
        name="text_projections",
    )(tokens, gain, w_query, w_key, w_value)


def prompt_kernel(place_ref, pieces_ref, gain_ref, w_query_ref, w_key_ref, w_value_ref,
                  rows_in, normed_in, joined_in, rows_ref, normed_ref, joined_ref,
                  prompt_ref, low_ref, projected_ref):
    count, part, _ = pieces_ref.shape
    width = w_query_ref.shape[0]

    @pl.when(pl.program_id(0) == 0)
    def _():
        for k in range(count):
            start = pl.multiple_of(jnp.bitwise_xor(place_ref[0], k) * part, part)
            prompt_ref[pl.ds(start, part), :] = pieces_ref[k]
        normed = rms_norm(prompt_ref[...].astype(wide), gain_ref[...]).astype(low)
        low_ref[...] = normed
        for place, weight_ref in enumerate((w_query_ref, w_key_ref, w_value_ref)):
            projected_ref[:, place * width : (place + 1) * width] = nt(normed, weight_ref[...]).astype(low)

    rows_ref[0] = rows_in[0] + prompt_ref[...]
    normed_ref[0] = normed_in[0] + low_ref[...]
    joined_ref[0] = joined_in[0] + projected_ref[...]


def add_prompt(place, pieces, gain, w_query, w_key, w_value, rows, normed, joined):
    packs, _, model = rows.shape
    width = w_query.shape[0]
    count, part, _ = pieces.shape
    top = count * part
    fixed = lambda p, s: (0, 0)
    moving = lambda p, s: (p, 0, 0)
    blocks = [
        pl.BlockSpec((1, top, model), moving),
        pl.BlockSpec((1, top, model), moving),
        pl.BlockSpec((1, top, 3 * width), moving),
    ]
    return pl.pallas_call(
        prompt_kernel,
        grid_spec=pltpu.PrefetchScalarGridSpec(
            num_scalar_prefetch=1,
            grid=(packs,),
            in_specs=[
                pl.BlockSpec((count, part, model), lambda p, s: (0, 0, 0)),
                pl.BlockSpec((1, model), fixed),
                pl.BlockSpec((width, model), fixed),
                pl.BlockSpec((width, model), fixed),
                pl.BlockSpec((width, model), fixed),
            ]
            + blocks,
            out_specs=blocks,
            scratch_shapes=[
                pltpu.VMEM((top, model), low),
                pltpu.VMEM((top, model), low),
                pltpu.VMEM((top, 3 * width), low),
            ],
        ),
        out_shape=[
            jax.ShapeDtypeStruct(rows.shape, low),
            jax.ShapeDtypeStruct(normed.shape, low),
            jax.ShapeDtypeStruct(joined.shape, low),
        ],
        input_output_aliases={6: 0, 7: 1, 8: 2},
        compiler_params=params(),
        name="add_prompt",
    )(place, pieces, gain, w_query, w_key, w_value, rows, normed, joined)


def attention_step_kernel(
    prompt_len, heads, first, last, core_ref, joined_ref, bias_ref, seg_rows_ref, seg_cols_ref, w_out_ref, got_ref,
    *refs,
):
    if first == 0 and last == 1:
        send_ref, pair_ref, probs_ref, mixed_ref = refs[-4:]
    elif first == 0:
        send_ref, probs_ref, mixed_ref = refs[-3:]
    else:
        pair_ref, probs_ref, mixed_ref = refs[-3:]
    turn = pl.program_id(0) + first
    rows = joined_ref.shape[1]
    half = rows // 2
    width = w_out_ref.shape[0]
    size = width // heads
    mine = jnp.bitwise_xor(core_ref[0], 1 - turn)
    start = pl.multiple_of(mine * half, half)
    row_pos = start + lax.broadcasted_iota(jnp.int32, (half, rows), 0)
    col_pos = lax.broadcasted_iota(jnp.int32, (half, rows), 1)
    allowed = (
        (row_pos < prompt_len) | (col_pos < prompt_len) | (seg_rows_ref[0] == seg_cols_ref[0])
    )
    queries = joined_ref[0, pl.ds(start, half), :width]
    mixed = []
    for head in range(heads):
        keys = joined_ref[0, :, width + head * size : width + (head + 1) * size]
        values = joined_ref[0, :, 2 * width + head * size : 2 * width + (head + 1) * size]
        scores = nt(queries[:, head * size : (head + 1) * size], keys) + bias_ref[head]
        scores = jnp.where(allowed, scores, blocked)
        top = jnp.max(scores, axis=-1, keepdims=True)
        raised = jnp.exp(scores - top)
        total = jnp.sum(raised, axis=-1, keepdims=True)
        probs = (raised * (1.0 / total)).astype(low)
        probs_ref[0, head] = probs
        mixed.append(nn(probs, values).astype(low))
    mixed = jnp.concatenate(mixed, axis=1)
    mixed_ref[0] = mixed
    share = nn(mixed, w_out_ref[...])

    if first == 0:

        @pl.when(turn == 0)
        def _():
            send_ref[...] = share.astype(low)

    if last == 1:

        @pl.when(turn == 1)
        def _():
            pair_ref[...] = (share + got_ref[...].astype(wide)).astype(low)


def attention_step(step, packs, prompt_len, core, joined, bias, seg_rows, seg_cols, w_out, got, mixed_all):
    _, rows, triple = joined.shape
    heads = bias.shape[0]
    width, model = w_out.shape
    half = rows // 2
    first, last = (0 if step < packs else 1), (1 if step > 0 else 0)
    steps = last - first + 1
    if got is None:
        got = jnp.zeros((half, model), low)

    def pack(t):
        return step - (t + first)

    def block(t, core_ref):
        return jnp.bitwise_xor(core_ref[0], 1 - (t + first))

    out_specs = [pl.BlockSpec((half, model), lambda t, c: (0, 0))] * steps + [
        pl.BlockSpec((1, heads, half, rows), lambda t, c: (t, 0, 0, 0)),
        pl.BlockSpec((1, half, width), lambda t, c: (pack(t), block(t, c), 0)),
    ]
    out_shape = [jax.ShapeDtypeStruct((half, model), low)] * steps + [
        jax.ShapeDtypeStruct((steps, heads, half, rows), low),
        jax.ShapeDtypeStruct((packs, rows, width), low),
    ]
    in_specs = [
        pl.BlockSpec((1, rows, triple), lambda t, c: (pack(t), 0, 0)),
        pl.BlockSpec((heads, half, rows), lambda t, c: (0, block(t, c), 0)),
        pl.BlockSpec((1, half, 1), lambda t, c: (pack(t), block(t, c), 0)),
        pl.BlockSpec((1, 1, rows), lambda t, c: (pack(t), 0, 0)),
        pl.BlockSpec((width, model), lambda t, c: (0, 0)),
        pl.BlockSpec((half, model), lambda t, c: (0, 0)),
    ]
    args = [core, joined, bias, seg_rows, seg_cols, w_out, got]
    aliases = {}
    if mixed_all is not None:
        in_specs.append(pl.BlockSpec(memory_space=pl.ANY))
        args.append(mixed_all)
        aliases = {7: steps + 1}
    outs = pl.pallas_call(
        functools.partial(attention_step_kernel, prompt_len, heads, first, last),
        grid_spec=pltpu.PrefetchScalarGridSpec(
            num_scalar_prefetch=1, grid=(steps,), in_specs=in_specs, out_specs=out_specs
        ),
        out_shape=out_shape,
        input_output_aliases=aliases,
        compiler_params=params(),
        name="attention_step",
    )(*args)
    send = outs[0] if first == 0 else None
    pair = outs[steps - 1] if last == 1 else None
    return send, pair, outs[-2], outs[-1]


def feed_step_kernel(
    first, last, place_ref, rows_ref, cot_ref, gain_ref, sums_ref, far_sums_ref, own_pair_ref, own_far_ref,
    got_feed_ref, got_back_ref, w_in_any, w_out_any, in_a, in_b, out_a, out_b, *refs,
):
    steps = last - first + 1
    outs = refs[-(3 + (2 if first == 0 else 0) + (4 if last == 1 else 0)) - 4 :]
    outs, scratch = outs[:-4], outs[-4:]
    normed_ref, active_ref, hidden_ref = outs[:3]
    rest = outs[3:]
    if first == 0:
        send_feed_ref, send_back_ref = rest[:2]
        rest = rest[2:]
    if last == 1:
        result_ref, middle_ref, grad_ref, gain_grad_ref = rest
    w_in_ref, w_out_ref, sems, keep_ref = scratch
    turn = pl.program_id(0) + first
    side, part = place_ref[1], place_ref[2]
    half_rows = in_a.shape[0]

    @pl.when(pl.program_id(0) == 0)
    def _():
        near = pl.ds(pl.multiple_of(part * half_rows, half_rows), half_rows)
        away = pl.ds(pl.multiple_of((1 - part) * half_rows, half_rows), half_rows)
        copies = [
            pltpu.make_async_copy(w_in_any, w_in_ref.at[side], sems.at[0]),
            pltpu.make_async_copy(w_out_any, w_out_ref.at[side], sems.at[1]),
            pltpu.make_async_copy(in_a, w_in_ref.at[1 - side, near], sems.at[2]),
            pltpu.make_async_copy(in_b, w_in_ref.at[1 - side, away], sems.at[3]),
            pltpu.make_async_copy(out_a, w_out_ref.at[1 - side, near], sems.at[4]),
            pltpu.make_async_copy(out_b, w_out_ref.at[1 - side, away], sems.at[5]),
        ]
        for copy in copies:
            copy.start()
        for copy in copies:
            copy.wait()

    own = turn == 1
    pair = jnp.where(own, own_pair_ref[...], sums_ref[...])
    far = jnp.where(own, own_far_ref[...], far_sums_ref[...])
    middle = rows_ref[0].astype(wide) + (pair.astype(wide) + far.astype(wide))
    scale = lax.rsqrt(jnp.mean(middle * middle, axis=-1, keepdims=True) + epsilon)
    normed = (middle * scale * gain_ref[...]).astype(low)
    normed_ref[0] = normed
    cot = cot_ref[0]
    feed, back = None, None
    for quarter in range(2):
        inner = nn(normed, w_in_ref[quarter])
        share = 0.5 + 0.5 * lax.erf(inner * root_half)
        active = (inner * share).astype(low)
        slope = share + inner * (jnp.exp(-0.5 * inner * inner) * inv_root_tau)
        hidden = (nt(cot, w_out_ref[quarter]) * slope).astype(low)

        @pl.when(side == quarter)
        def _():
            active_ref[0] = active
            hidden_ref[0] = hidden

        feed_share = nn(active, w_out_ref[quarter])
        back_share = nt(hidden, w_in_ref[quarter])
        feed = feed_share if feed is None else feed + feed_share
        back = back_share if back is None else back + back_share

    if first == 0:

        @pl.when(turn == 0)
        def _():
            send_feed_ref[...] = feed.astype(low)
            send_back_ref[...] = back.astype(low)

    if last == 1:

        @pl.when(turn == 1)
        def _():
            result_ref[...] = (middle + (feed + got_feed_ref[...].astype(wide))).astype(low)
            upstream = back + got_back_ref[...].astype(wide)
            scaled = upstream * gain_ref[...]
            inner = jnp.mean(scaled * middle, axis=-1, keepdims=True)
            grad = cot.astype(wide) + scale * scaled - middle * (scale * scale * scale * inner)
            middle_ref[...] = grad
            grad_ref[...] = grad.astype(low)
            gain_grad_ref[...] = jnp.sum(upstream * middle * scale, axis=0, keepdims=True)


def feed_step(step, packs, place, rows, cot, gain, sums, far_sums, own_pair, own_far, got_feed, got_back,
              w_in, w_out, in_halves, out_halves, kept):
    _, row_count, model = rows.shape
    hidden = w_in.shape[1]
    half = row_count // 2
    first, last = (0 if step < packs else 1), (1 if step > 0 else 0)
    steps = last - first + 1
    empty = jnp.zeros((half, model), low)
    sums, far_sums, own_pair, own_far, got_feed, got_back = [
        empty if v is None else v for v in (sums, far_sums, own_pair, own_far, got_feed, got_back)
    ]

    def moving(t, c):
        return (step - (t + first), jnp.bitwise_xor(c[0], 1 - (t + first)), 0)

    fixed = lambda t, c: (0, 0)
    flat = pl.BlockSpec((half, model), fixed)
    anywhere = pl.BlockSpec(memory_space=pl.ANY)
    in_specs = [
        pl.BlockSpec((1, half, model), moving),
        pl.BlockSpec((1, half, model), moving),
        pl.BlockSpec((1, model), fixed),
    ] + [flat] * 6 + [anywhere] * 6
    args = [place, rows, cot, gain, sums, far_sums, own_pair, own_far, got_feed, got_back,
            w_in, w_out, *in_halves, *out_halves]
    aliases = {}
    if kept is not None:
        in_specs += [anywhere] * 3
        aliases = {len(args) + i: i for i in range(3)}
        args += list(kept)
    out_specs = [
        pl.BlockSpec((1, half, model), moving),
        pl.BlockSpec((1, half, hidden), moving),
        pl.BlockSpec((1, half, hidden), moving),
    ]
    out_shape = [
        jax.ShapeDtypeStruct((packs, row_count, model), low),
        jax.ShapeDtypeStruct((packs, row_count, hidden), low),
        jax.ShapeDtypeStruct((packs, row_count, hidden), low),
    ]
    if first == 0:
        out_specs += [flat] * 2
        out_shape += [jax.ShapeDtypeStruct((half, model), low)] * 2
    if last == 1:
        out_specs += [flat] * 3 + [pl.BlockSpec((1, model), fixed)]
        out_shape += [
            jax.ShapeDtypeStruct((half, model), low),
            jax.ShapeDtypeStruct((half, model), wide),
            jax.ShapeDtypeStruct((half, model), low),
            jax.ShapeDtypeStruct((1, model), wide),
        ]
    outs = pl.pallas_call(
        functools.partial(feed_step_kernel, first, last),
        grid_spec=pltpu.PrefetchScalarGridSpec(
            num_scalar_prefetch=1,
            grid=(steps,),
            in_specs=in_specs,
            out_specs=out_specs,
            scratch_shapes=[
                pltpu.VMEM((2, model, hidden), low),
                pltpu.VMEM((2, hidden, model), low),
                pltpu.SemaphoreType.DMA((6,)),
                pltpu.VMEM((8, 128), wide),
            ],
        ),
        out_shape=out_shape,
        input_output_aliases=aliases,
        compiler_params=params(),
        name="feed_step",
    )(*args)
    sent = outs[3:5] if first == 0 else (None, None)
    own = outs[-4:] if last == 1 else (None,) * 4
    return outs[:3], sent, own


def attention_back_kernel(
    heads, has_back, has_prev, core_ref, *refs,
):
    refs = list(refs)
    if has_back:
        own_ref, far_ref, w_out_ref, probs_own_ref, probs_far_ref, joined_ref = refs[:6]
        refs = refs[6:]
    w_joined_ref = refs.pop(0)
    if has_prev:
        prev_ref, got_ref = refs[:2]
        refs = refs[2:]
    outs = refs[-((5 if has_back else 0) + (1 if has_prev else 0)):]
    if has_prev:
        pair_ref = outs.pop(0)
        pair_ref[...] = (nn(prev_ref[...], w_joined_ref[...]) + got_ref[...].astype(wide)).astype(low)
    if not has_back:
        return
    send_ref, own_grads_ref, grads_ref, scores_ref, whole_ref = outs
    rows = joined_ref.shape[1]
    half = rows // 2
    width = w_out_ref.shape[0]
    size = width // heads
    core = core_ref[0]
    starts = [pl.multiple_of(core * half, half), pl.multiple_of((1 - core) * half, half)]
    ups, asks, asked = [], [], [[], []]
    for side, ref in enumerate((own_ref, far_ref)):
        whole_ref[0, pl.ds(starts[side], half), :] = ref[...]
        ups.append(nt(ref[...], w_out_ref[...]).astype(low))
        asks.append(joined_ref[0, pl.ds(starts[side], half), :width])
    grad_keys, grad_values = [], []
    for head in range(heads):
        cols = slice(head * size, (head + 1) * size)
        keys = joined_ref[0, :, width + head * size : width + (head + 1) * size]
        values = joined_ref[0, :, 2 * width + head * size : 2 * width + (head + 1) * size]
        grad_key, grad_value = None, None
        for side, probs_ref in enumerate((probs_own_ref, probs_far_ref)):
            probs = probs_ref[0, head]
            upstream = ups[side][:, cols]
            grad_probs = nt(upstream, values)
            spread = probs.astype(wide)
            inner = jnp.sum(spread * grad_probs, axis=-1, keepdims=True)
            grad_scores = (spread * (grad_probs - inner)).astype(low)
            scores_ref[0, head, pl.ds(starts[side], half), :] = grad_scores
            value_share = tn(upstream, probs)
            key_share = tn(asks[side][:, cols], grad_scores)
            grad_value = value_share if grad_value is None else grad_value + value_share
            grad_key = key_share if grad_key is None else grad_key + key_share
            asked[side].append(nn(grad_scores, keys))
        grad_values.append(grad_value.T)
        grad_keys.append(grad_key.T)
    rest = jnp.concatenate(grad_keys + grad_values, axis=1).astype(low)
    grads_ref[0, :, width:] = rest
    for side in range(2):
        grads_ref[0, pl.ds(starts[side], half), :width] = jnp.concatenate(asked[side], axis=1).astype(low)
    own_grads_ref[...] = grads_ref[0, pl.ds(starts[0], half), :]
    send_ref[...] = nn(grads_ref[0, pl.ds(starts[1], half), :], w_joined_ref[...]).astype(low)


def attention_back_step(step, packs, heads, core, own, far, w_out, probs_own, probs_far, joined, w_joined, prev, got, kept):
    _, rows, triple = joined.shape
    width, model = w_out.shape
    half = rows // 2
    has_back, has_prev = step < packs, step > 0
    fixed = lambda t, c: (0, 0)
    flat = pl.BlockSpec((half, model), fixed)
    anywhere = pl.BlockSpec(memory_space=pl.ANY)
    in_specs, args, out_specs, out_shape, aliases = [], [core], [], [], {}
    if has_back:
        (own_place, probs_own), (far_place, probs_far) = probs_own, probs_far
        in_specs += [
            flat,
            flat,
            pl.BlockSpec((width, model), fixed),
            pl.BlockSpec((1, heads, half, rows), lambda t, c: (own_place, 0, 0, 0)),
            pl.BlockSpec((1, heads, half, rows), lambda t, c: (far_place, 0, 0, 0)),
            pl.BlockSpec((1, rows, triple), lambda t, c: (step, 0, 0)),
        ]
        args += [own, far, w_out, probs_own, probs_far, joined]
    in_specs.append(pl.BlockSpec((triple, model), fixed))
    args.append(w_joined)
    if has_prev:
        in_specs += [pl.BlockSpec((half, triple), fixed), flat]
        args += [prev, got]
        out_specs.append(flat)
        out_shape.append(jax.ShapeDtypeStruct((half, model), low))
    if has_back:
        if kept is not None:
            in_specs += [anywhere] * 3
            aliases = {len(args) + i: len(out_shape) + 2 + i for i in range(3)}
            args += list(kept)
        out_specs += [
            flat,
            pl.BlockSpec((half, triple), fixed),
            pl.BlockSpec((1, rows, triple), lambda t, c: (step, 0, 0)),
            pl.BlockSpec((1, heads, rows, rows), lambda t, c: (step, 0, 0, 0)),
            pl.BlockSpec((1, rows, model), lambda t, c: (step, 0, 0)),
        ]
        out_shape += [
            jax.ShapeDtypeStruct((half, model), low),
            jax.ShapeDtypeStruct((half, triple), low),
            jax.ShapeDtypeStruct((packs, rows, triple), low),
            jax.ShapeDtypeStruct((packs, heads, rows, rows), low),
            jax.ShapeDtypeStruct((packs, rows, model), low),
        ]
    outs = list(
        pl.pallas_call(
            functools.partial(attention_back_kernel, heads, has_back, has_prev),
            grid_spec=pltpu.PrefetchScalarGridSpec(
                num_scalar_prefetch=1, grid=(1,), in_specs=in_specs, out_specs=out_specs
            ),
            out_shape=out_shape,
            input_output_aliases=aliases,
            compiler_params=params(),
            name="attention_back_step",
        )(*args)
    )
    pair = outs.pop(0) if has_prev else None
    send, own_grads, *kept = outs if has_back else (None, None)
    return pair, send, own_grads, kept


def finish_kernel(top, core_ref, rows_ref, pair_ref, far_ref, grad_ref, gain_ref, gain_in_ref, head_in_ref,
                  out_ref, gain_out_ref, head_out_ref):
    values = rows_ref[0].astype(wide)
    upstream = pair_ref[...].astype(wide) + far_ref[...].astype(wide)
    scale = lax.rsqrt(jnp.mean(values * values, axis=-1, keepdims=True) + epsilon)
    scaled = upstream * gain_ref[...]
    inner = jnp.mean(scaled * values, axis=-1, keepdims=True)
    grad = grad_ref[...] + scale * scaled - values * (scale * scale * scale * inner)
    out_ref[...] = grad.astype(low)
    gain_out_ref[...] = gain_in_ref[...] + jnp.sum(upstream * values * scale, axis=0, keepdims=True)
    head_out_ref[...] = head_in_ref[...] + jnp.where(core_ref[0] == 0, grad[:top], 0.0)


def finish(pack, top, core, rows, pair, far, grad, gain, gain_sum, head_sum):
    half, model = pair.shape
    fixed = lambda t, c: (0, 0)
    flat = pl.BlockSpec((half, model), fixed)
    line = pl.BlockSpec((1, model), fixed)
    head = pl.BlockSpec((top, model), fixed)
    return pl.pallas_call(
        functools.partial(finish_kernel, top),
        grid_spec=pltpu.PrefetchScalarGridSpec(
            num_scalar_prefetch=1,
            grid=(1,),
            in_specs=[
                pl.BlockSpec((1, half, model), lambda t, c: (pack, c[0], 0)),
                flat, flat, flat, line, line, head,
            ],
            out_specs=[flat, line, head],
        ),
        out_shape=[
            jax.ShapeDtypeStruct((half, model), low),
            jax.ShapeDtypeStruct((1, model), wide),
            jax.ShapeDtypeStruct((top, model), wide),
        ],
        compiler_params=params(),
        name="finish",
    )(core, rows, pair, far, grad, gain, gain_sum, head_sum)


def place_kernel(packs, core_ref, *refs):
    out_ref, sems = refs[-2:]
    half = out_ref.shape[1] // 2
    copies = []
    for pack in range(packs):
        for side in range(2):
            start = pl.multiple_of(jnp.bitwise_xor(core_ref[0], side) * half, half)
            copies.append(
                pltpu.make_async_copy(
                    refs[2 * pack + side], out_ref.at[pack, pl.ds(start, half)], sems.at[2 * pack + side]
                )
            )
    for copy in copies:
        copy.start()
    for copy in copies:
        copy.wait()


def place_halves(core, pairs):
    packs = len(pairs)
    half, model = pairs[0][0].shape
    anywhere = pl.BlockSpec(memory_space=pl.ANY)
    return pl.pallas_call(
        functools.partial(place_kernel, packs),
        in_specs=[pl.BlockSpec(memory_space=pltpu.SMEM)] + [anywhere] * (2 * packs),
        out_specs=anywhere,
        out_shape=jax.ShapeDtypeStruct((packs, 2 * half, model), low),
        scratch_shapes=[pltpu.SemaphoreType.DMA((2 * packs,))],
        compiler_params=params(),
        name="place_halves",
    )(core, *[v for pair in pairs for v in pair])


def scatter_rows(share):
    count = lax.axis_size("dp")
    where = lax.axis_index("dp")
    bits = bits_of(count)
    order = bits[:1] + bits[1:][::-1]
    model, width = share.shape
    left = list(reversed(bits))
    share = share.reshape([2] * len(bits) + [model // count, width])
    for bit in order:
        axis = left.index(bit)
        left.remove(bit)
        side = (where // bit) % 2
        send = lax.dynamic_index_in_dim(share, 1 - side, axis, keepdims=False)
        keep = lax.dynamic_index_in_dim(share, side, axis, keepdims=False)
        share = keep.astype(wide) + swap(send, "dp", bit).astype(wide)
        if left:
            share = share.astype(low)
    return share


def find_prompt(prompt_ids, table, prompt_delta):
    prompt_len = prompt_ids.shape[0]
    table_rows, model = table.shape
    groups = lax.axis_size("mp")
    part = -(-prompt_len // (16 * groups)) * 16
    dp_index, mp_index = lax.axis_index("dp"), lax.axis_index("mp")
    padded = jnp.pad(prompt_ids, (0, part * groups - prompt_len), constant_values=-1)
    ids = lax.dynamic_slice_in_dim(padded, mp_index * part, part)
    local = dp_index * table_rows + jnp.arange(table_rows, dtype=jnp.int32)
    selector = (ids[:, None] == local[None, :]).astype(low)
    looked = jnp.dot(selector, table, preferred_element_type=wide)
    placed = lax.dynamic_update_slice_in_dim(
        jnp.zeros((part * groups * model,), wide), prompt_delta, dp_index * prompt_delta.shape[0], 0
    ).reshape(part * groups, model)
    total = looked + lax.dynamic_slice_in_dim(placed, mp_index * part, part, axis=0)
    for bit in bits_of(lax.axis_size("dp")):
        total = total + swap(total, "dp", bit)
    pieces = total.astype(low)[None]
    for bit in bits_of(groups):
        pieces = jnp.concatenate([pieces, swap(pieces, "mp", bit)], axis=0)
    return pieces


def peer_halves(weight):
    part = lax.axis_index("dp") % 2
    halves = weight.reshape(2, weight.shape[0] // 2, weight.shape[1])
    mine = swap(lax.dynamic_index_in_dim(halves, part, 0, keepdims=False), "mp", 2)
    return mine, swap(mine, "dp", 1)


def body(
    tokens, cotangent, segment_ids, prompt_ids, rel_buckets, table, prompt_delta, norm1_gain,
    w_query, w_key, w_value, w_output, rel_bias, norm2_gain, w_inner, w_outer,
):
    prompt_len = prompt_ids.shape[0]
    packs, rows, model = cotangent.shape
    bucket_count, heads = rel_bias.shape
    width = w_query.shape[1]
    groups = lax.axis_size("dp")
    mp_index = lax.axis_index("mp").astype(jnp.int32)
    core = (mp_index % 2).reshape(1)
    side = (mp_index // 2) % 2
    part = (lax.axis_index("dp") % 2).astype(jnp.int32)
    place = jnp.stack([core[0], side, part])
    gain1, gain2 = norm1_gain[None, :], norm2_gain[None, :]
    w_q, w_k, w_v = w_query.T, w_key.T, w_value.T

    pieces = find_prompt(prompt_ids, table, prompt_delta)
    in_halves, out_halves = peer_halves(w_inner), peer_halves(w_outer)
    bucket_hot = (
        rel_buckets[:, None] == jnp.arange(bucket_count, dtype=jnp.int32)[None, :]
    ).astype(wide)
    bucket_hot = jnp.pad(bucket_hot, ((0, 1), (0, 0)))
    turned = jnp.roll(bucket_hot, -(rows - 1), axis=0)
    bias_line = jnp.dot(turned, rel_bias, precision=highest).T
    bias = bias_grid_of(bias_line[:, None, :])
    marks = jnp.pad(segment_ids, ((0, 0), (prompt_len, 0)), constant_values=-1)
    seg_rows, seg_cols = marks[:, :, None], marks[:, None, :]
    w_joined = jnp.concatenate([w_q, w_k, w_v], axis=0)
    whole_rows, normed1, joined = text_projections(rows, tokens, gain1, w_q, w_k, w_v)
    whole_rows, normed1, joined = add_prompt(
        mp_index.reshape(1), pieces, gain1, w_q, w_k, w_v, whole_rows, normed1, joined
    )

    pairs, fars, probs_far, probs_own, mixed, got = [], [], [], [], None, None
    for step in range(packs + 1):
        send, pair, probs, mixed = attention_step(
            step, packs, prompt_len, core, joined, bias, seg_rows, seg_cols, w_output, got, mixed
        )
        if send is not None:
            probs_far.append((0, probs))
            got = swap(send, "mp", 1)
        if pair is not None:
            probs_own.append((probs.shape[0] - 1, probs))
            total = pair
            for bit in bits_of(lax.axis_size("mp"))[1:]:
                far = swap(total, "mp", bit)
            pairs.append(pair)
            fars.append(far)
    pairs_far = [swap(v, "mp", 1) for v in pairs]
    fars_far = [swap(v, "mp", 1) for v in fars]

    kept, sent, own = None, (None, None), []
    results, grads_wide, grads_low, gain2_sum = [], [], [], 0.0
    none = [None]
    for step in range(packs + 1):
        kept, new_sent, done = feed_step(
            step, packs, place, whole_rows, cotangent, gain2,
            (pairs_far + none)[step], (fars_far + none)[step],
            (none + pairs)[step], (none + fars)[step], *sent,
            w_inner, w_outer, in_halves, out_halves, kept,
        )
        if step < packs:
            sent = [swap(v, "mp", 1) for v in new_sent]
        if step > 0:
            results.append(done[0])
            grads_wide.append(done[1])
            grads_low.append(done[2])
            gain2_sum = gain2_sum + done[3]

    back_kept, prev, got = None, None, None
    gain1_sum, head_sum = jnp.zeros((1, model), wide), jnp.zeros((128, model), wide)
    text_rows = []
    for step in range(packs + 1):
        live = step < packs
        pair, send, own_grads, back_new = attention_back_step(
            step, packs, heads, core,
            grads_low[step] if live else None, swap(grads_low[step], "mp", 1) if live else None,
            w_output, probs_own[step] if live else None, probs_far[step] if live else None,
            joined, w_joined, prev, got, back_kept,
        )
        if live:
            back_kept, prev, got = back_new, own_grads, swap(send, "mp", 1)
        if pair is not None:
            far = swap(pair, "mp", 2)
            rows_low, gain1_sum, head_sum = finish(
                step - 1, 128, core, whole_rows, pair, far, grads_wide[step - 1], gain1, gain1_sum, head_sum
            )
            text_rows.append((rows_low, swap(rows_low, "mp", 1)))

    out = place_halves(core, [(v, swap(v, "mp", 1)) for v in results])
    grad_tokens = place_halves(core, text_rows)[:, prompt_len:]

    def flat(value):
        return value.reshape(packs * rows, -1)

    normed2, active, hidden = kept
    grad_joined, scores, grad_rows = back_kept
    inner_grad = scatter_rows(tn(flat(normed2), flat(hidden)).astype(low))
    outer_grad = scatter_rows(tn(flat(cotangent), flat(active)).astype(low)).T
    output_grad = scatter_rows(tn(flat(grad_rows), flat(mixed)).astype(low)).T
    joined_out = scatter_rows(tn(flat(normed1), flat(grad_joined)).astype(low))
    line = diagonal_sums(scores)[:, 0, :]
    rel_grad = jnp.einsum("ht,tb->bh", line, turned, precision=highest)
    block = model // groups
    rel_column = jnp.pad(
        rel_grad.reshape(groups, -1), ((0, 0), (0, block - bucket_count * heads // groups))
    ).reshape(model, 1)
    small = jnp.concatenate(
        [head_sum[:prompt_len].reshape(model, prompt_len), gain1_sum.T, gain2_sum.T], axis=1
    ).astype(low)
    small = small.astype(wide) + swap(small, "mp", 1).astype(wide)
    small = scatter_rows(jnp.concatenate([small, rel_column], axis=1).astype(low))
    return (
        out, grad_tokens, small[:, :prompt_len].reshape(-1), small[:, prompt_len],
        joined_out[:, :width], joined_out[:, width : 2 * width], joined_out[:, 2 * width :],
        output_grad, small[: bucket_count * heads // groups, prompt_len + 2].reshape(-1, heads),
        small[:, prompt_len + 1], inner_grad, outer_grad,
    )


def solution(mesh):
    in_specs = (
        P("dp", None, None),
        P("dp", None, None),
        P("dp", None),
        P(),
        P(),
        P("dp", None),
        P("dp"),
        P(),
        P(None, "mp"),
        P(None, "mp"),
        P(None, "mp"),
        P("mp", None),
        P(None, "mp"),
        P(),
        P(None, "mp"),
        P("mp", None),
    )
    out_specs = (
        P("dp", None, None),
        P("dp", None, None),
        P("dp"),
        P("dp"),
        P("dp", "mp"),
        P("dp", "mp"),
        P("dp", "mp"),
        P("mp", "dp"),
        P("dp", "mp"),
        P("dp"),
        P("dp", "mp"),
        P("mp", "dp"),
    )
    return jax.shard_map(body, mesh=mesh, in_specs=in_specs, out_specs=out_specs, check_vma=False)
```

```python
import functools

import jax
import jax.numpy as jnp
from jax import lax
from jax.experimental import pallas as pl
from jax.experimental.pallas import tpu as pltpu
from jax.sharding import PartitionSpec as P

epsilon = 1e-06
blocked = -1000000000.0
highest = lax.Precision.HIGHEST
low = jnp.bfloat16
wide = jnp.float32
root_half = 0.7071067811865476
inv_root_tau = 0.3989422804014327
vmem_bytes = 32 * 1024 * 1024


def nn(left, right):
    return lax.dot_general(left, right, (((1,), (0,)), ((), ())), preferred_element_type=wide)


def nt(left, right):
    return lax.dot_general(left, right, (((1,), (1,)), ((), ())), preferred_element_type=wide)


def tn(left, right):
    return lax.dot_general(left, right, (((0,), (0,)), ((), ())), preferred_element_type=wide)


def params():
    return pltpu.CompilerParams(vmem_limit_bytes=vmem_bytes)


def in_hbm(shape, dtype):
    return pltpu.HBM(shape, dtype)


def kernel_call(kernel, micros, **rest):
    cost = pl.CostEstimate(flops=0, bytes_accessed=int(micros * 3.6e6), transcendentals=0)
    call = pl.pallas_call(kernel, cost_estimate=cost, compiler_params=params(), **rest)

    def run(*args):
        return call(
            *[
                pltpu.with_memory_space_constraint(v, pltpu.HBM) if v.size >= 400000 else v
                for v in args
            ]
        )

    return run


def swap(value, axis, bit):
    count = lax.axis_size(axis)
    return lax.ppermute(value, axis, [(i, i ^ bit) for i in range(count)])


def bits_of(count):
    return [1 << i for i in range(count.bit_length() - 1)]


def rms_norm(values, gain):
    return values * lax.rsqrt(jnp.mean(values * values, axis=-1, keepdims=True) + epsilon) * gain


def norm_back(upstream, gain, values):
    scale = lax.rsqrt(jnp.mean(values * values, axis=-1, keepdims=True) + epsilon)
    scaled = upstream * gain
    inner = jnp.mean(scaled * values, axis=-1, keepdims=True)
    grad = scale * scaled - values * (scale * scale * scale * inner)
    return grad, jnp.sum(upstream * values * scale, axis=0, keepdims=True)


def bias_kernel(line_ref, grid_ref):
    rows = grid_ref.shape[1]
    spread = jnp.broadcast_to(line_ref[0], (rows, 2 * rows))
    grid_ref[0] = pltpu.roll(spread, 0, 1, stride=1, stride_axis=0)[:, :rows]


def bias_grid_of(line):
    heads, _, double = line.shape
    rows = double // 2
    return kernel_call(
        bias_kernel, 2,
        grid=(heads,),
        in_specs=[pl.BlockSpec((1, 1, double), lambda h: (h, 0, 0))],
        out_specs=pl.BlockSpec((1, rows, rows), lambda h: (h, 0, 0)),
        out_shape=in_hbm((heads, rows, rows), wide),
        name="bias_grid",
    )(line)


def diag_kernel(grid_ref, line_ref):
    packs, _, rows, _ = grid_ref.shape
    zero = jnp.zeros((8, rows), wide)
    held = None
    for slab in range(rows // 8):
        part = grid_ref[0, 0, 8 * slab : 8 * slab + 8, :].astype(wide)
        for pack in range(1, packs):
            part = part + grid_ref[pack, 0, 8 * slab : 8 * slab + 8, :].astype(wide)
        part = jnp.concatenate([part, zero], axis=1)
        if slab:
            part = pltpu.roll(part, 2 * rows - 8 * slab, 1)
        held = part if held is None else held + part
    total = held[0:1]
    for row in range(1, 8):
        total = total + pltpu.roll(held[row : row + 1], 2 * rows - row, 1)
    line_ref[0] = total


def diagonal_sums(grid):
    packs, heads, rows, _ = grid.shape
    return kernel_call(
        diag_kernel, 3,
        grid=(heads,),
        in_specs=[pl.BlockSpec((packs, 1, rows, rows), lambda h: (0, h, 0, 0))],
        out_specs=pl.BlockSpec((1, 1, 2 * rows), lambda h: (h, 0, 0)),
        out_shape=in_hbm((heads, 1, 2 * rows), wide),
        name="diagonal_sums",
    )(grid)


def shifted_text_kernel(tokens_ref, gain_ref, w_query_ref, w_key_ref, w_value_ref,
                        rows_ref, normed_ref, joined_ref, wide_ref):
    rows = rows_ref.shape[1]
    prompt_len = rows - tokens_ref.shape[1]
    width = w_query_ref.shape[0]
    wide_ref[:prompt_len, :] = jnp.zeros((prompt_len, wide_ref.shape[1]), wide)
    wide_ref[prompt_len:, :] = tokens_ref[0].astype(wide)
    values = wide_ref[...]
    rows_ref[0] = values.astype(low)
    normed = rms_norm(values, gain_ref[...]).astype(low)
    normed_ref[0] = normed
    for place, weight_ref in enumerate((w_query_ref, w_key_ref, w_value_ref)):
        joined_ref[0, :, place * width : (place + 1) * width] = nt(normed, weight_ref[...]).astype(low)


def text_projections(rows, tokens, gain, w_query, w_key, w_value):
    packs, text, model = tokens.shape
    width = w_query.shape[0]
    fixed = lambda p: (0, 0)
    moving = lambda p: (p, 0, 0)
    return kernel_call(
        shifted_text_kernel, 4.5,
        grid=(packs,),
        in_specs=[
            pl.BlockSpec((1, text, model), moving),
            pl.BlockSpec((1, model), fixed),
            pl.BlockSpec((width, model), fixed),
            pl.BlockSpec((width, model), fixed),
            pl.BlockSpec((width, model), fixed),
        ],
        out_specs=[
            pl.BlockSpec((1, rows, model), moving),
            pl.BlockSpec((1, rows, model), moving),
            pl.BlockSpec((1, rows, 3 * width), moving),
        ],
        out_shape=[
            in_hbm((packs, rows, model), low),
            in_hbm((packs, rows, model), low),
            in_hbm((packs, rows, 3 * width), low),
        ],
        scratch_shapes=[pltpu.VMEM((rows, model), wide)],
        name="text_projections",
    )(tokens, gain, w_query, w_key, w_value)


def prompt_kernel(place_ref, pieces_ref, gain_ref, w_query_ref, w_key_ref, w_value_ref,
                  rows_in, normed_in, joined_in, rows_out, normed_out, joined_out,
                  prompt_ref, rows_ref, normed_ref, joined_ref, load_sems, save_sems):
    count, part, _ = pieces_ref.shape
    packs = rows_ref.shape[0]
    top = count * part
    width = w_query_ref.shape[0]
    held = (rows_ref, normed_ref, joined_ref)
    loads = [
        pltpu.make_async_copy(source.at[:, pl.ds(0, top)], target, load_sems.at[i])
        for i, (source, target) in enumerate(zip((rows_in, normed_in, joined_in), held))
    ]
    for copy in loads:
        copy.start()
    for k in range(count):
        start = pl.multiple_of(jnp.bitwise_xor(place_ref[0], k) * part, part)
        prompt_ref[pl.ds(start, part), :] = pieces_ref[k]
    prompt = prompt_ref[...]
    normed = rms_norm(prompt.astype(wide), gain_ref[...]).astype(low)
    joined = jnp.concatenate(
        [nt(normed, ref[...]).astype(low) for ref in (w_query_ref, w_key_ref, w_value_ref)], axis=1
    )
    saves = []
    for i, (value, target) in enumerate(zip((prompt, normed, joined), (rows_out, normed_out, joined_out))):
        loads[i].wait()
        for pack in range(packs):
            held[i][pack] = held[i][pack] + value
        copy = pltpu.make_async_copy(held[i], target.at[:, pl.ds(0, top)], save_sems.at[i])
        copy.start()
        saves.append(copy)
    for copy in saves:
        copy.wait()


def add_prompt(place, pieces, gain, w_query, w_key, w_value, rows, normed, joined):
    packs, _, model = rows.shape
    width = w_query.shape[0]
    count, part, _ = pieces.shape
    top = count * part
    inside = pl.BlockSpec(memory_space=pltpu.VMEM)
    anywhere = pl.BlockSpec(memory_space=pl.ANY)
    return kernel_call(
        prompt_kernel, 2.5,
        in_specs=[pl.BlockSpec(memory_space=pltpu.SMEM)] + [inside] * 5 + [anywhere] * 3,
        out_specs=[anywhere] * 3,
        out_shape=[
            in_hbm(rows.shape, low),
            in_hbm(normed.shape, low),
            in_hbm(joined.shape, low),
        ],
        scratch_shapes=[
            pltpu.VMEM((top, model), low),
            pltpu.VMEM((packs, top, model), low),
            pltpu.VMEM((packs, top, model), low),
            pltpu.VMEM((packs, top, 3 * width), low),
            pltpu.SemaphoreType.DMA((3,)),
            pltpu.SemaphoreType.DMA((3,)),
        ],
        input_output_aliases={6: 0, 7: 1, 8: 2},
        name="add_prompt",
    )(place, pieces, gain, w_query, w_key, w_value, rows, normed, joined)


def look_up_kernel(ids_ref, table_any, placed_ref, out_ref, blocks_ref, sems):
    part = out_ref.shape[0]
    limit = table_any.shape[0]
    copies, inside = [], []
    for row in range(part):
        local = jnp.clip(ids_ref[row], 0, limit - 1)
        inside.append(local)
        start = pl.multiple_of(jnp.left_shift(jnp.right_shift(local, 4), 4), 16)
        copies.append(
            pltpu.make_async_copy(table_any.at[pl.ds(start, 16)], blocks_ref.at[row], sems.at[row])
        )
    for copy in copies:
        copy.start()
    for copy in copies:
        copy.wait()
    position = lax.broadcasted_iota(jnp.int32, blocks_ref.shape[1:], 0)
    for row in range(part):
        own = inside[row] == ids_ref[row]
        chosen = (position == jnp.bitwise_and(inside[row], 15)) & own
        found = jnp.sum(jnp.where(chosen, blocks_ref[row].astype(wide), 0.0), axis=0, keepdims=True)
        out_ref[row : row + 1, :] = placed_ref[row : row + 1, :] + found


def look_up_rows(ids, table, placed):
    part, model = placed.shape
    inside = pl.BlockSpec(memory_space=pltpu.VMEM)
    return kernel_call(
        look_up_kernel, 2.5,
        in_specs=[pl.BlockSpec(memory_space=pltpu.SMEM), pl.BlockSpec(memory_space=pl.ANY), inside],
        out_specs=inside,
        out_shape=jax.ShapeDtypeStruct((part, model), wide),
        scratch_shapes=[pltpu.VMEM((part, 16, model), low), pltpu.SemaphoreType.DMA((part,))],
        name="look_up",
    )(ids, table, placed)


def attention_step_kernel(
    prompt_len, heads, first, last, core_ref, joined_ref, bias_ref, seg_rows_ref, seg_cols_ref, w_out_ref, got_ref,
    *refs,
):
    if first == 0 and last == 1:
        send_ref, pair_ref, probs_ref, mixed_ref = refs[-4:]
    elif first == 0:
        send_ref, probs_ref, mixed_ref = refs[-3:]
    else:
        pair_ref, probs_ref, mixed_ref = refs[-3:]
    turn = pl.program_id(0) + first
    rows = joined_ref.shape[1]
    half = rows // 2
    width = w_out_ref.shape[0]
    size = width // heads
    mine = jnp.bitwise_xor(core_ref[0], 1 - turn)
    start = pl.multiple_of(mine * half, half)
    row_pos = start + lax.broadcasted_iota(jnp.int32, (half, rows), 0)
    col_pos = lax.broadcasted_iota(jnp.int32, (half, rows), 1)
    allowed = (
        (row_pos < prompt_len) | (col_pos < prompt_len) | (seg_rows_ref[0] == seg_cols_ref[0])
    )
    queries = joined_ref[0, pl.ds(start, half), :width]
    mixed = []
    for head in range(heads):
        keys = joined_ref[0, :, width + head * size : width + (head + 1) * size]
        values = joined_ref[0, :, 2 * width + head * size : 2 * width + (head + 1) * size]
        scores = nt(queries[:, head * size : (head + 1) * size], keys) + bias_ref[head]
        scores = jnp.where(allowed, scores, blocked)
        top = jnp.max(scores, axis=-1, keepdims=True)
        raised = jnp.exp(scores - top)
        total = jnp.sum(raised, axis=-1, keepdims=True)
        probs = (raised * (1.0 / total)).astype(low)
        probs_ref[0, head] = probs
        mixed.append(nn(probs, values).astype(low))
    mixed = jnp.concatenate(mixed, axis=1)
    mixed_ref[0] = mixed
    share = nn(mixed, w_out_ref[...])

    if first == 0:

        @pl.when(turn == 0)
        def _():
            send_ref[...] = share.astype(low)

    if last == 1:

        @pl.when(turn == 1)
        def _():
            pair_ref[...] = (share + got_ref[...].astype(wide)).astype(low)


def attention_step(step, packs, prompt_len, core, joined, bias, seg_rows, seg_cols, w_out, got, mixed_all):
    _, rows, triple = joined.shape
    heads = bias.shape[0]
    width, model = w_out.shape
    half = rows // 2
    first, last = (0 if step < packs else 1), (1 if step > 0 else 0)
    steps = last - first + 1
    if got is None:
        got = jnp.zeros((half, model), low)

    def pack(t):
        return step - (t + first)

    def block(t, core_ref):
        return jnp.bitwise_xor(core_ref[0], 1 - (t + first))

    out_specs = [pl.BlockSpec((half, model), lambda t, c: (0, 0))] * steps + [
        pl.BlockSpec((1, heads, half, rows), lambda t, c: (t, 0, 0, 0)),
        pl.BlockSpec((1, half, width), lambda t, c: (pack(t), block(t, c), 0)),
    ]
    out_shape = [jax.ShapeDtypeStruct((half, model), low)] * steps + [
        in_hbm((steps, heads, half, rows), low),
        in_hbm((packs, rows, width), low),
    ]
    in_specs = [
        pl.BlockSpec((1, rows, triple), lambda t, c: (pack(t), 0, 0)),
        pl.BlockSpec((heads, half, rows), lambda t, c: (0, block(t, c), 0)),
        pl.BlockSpec((1, half, 1), lambda t, c: (pack(t), block(t, c), 0)),
        pl.BlockSpec((1, 1, rows), lambda t, c: (pack(t), 0, 0)),
        pl.BlockSpec((width, model), lambda t, c: (0, 0)),
        pl.BlockSpec((half, model), lambda t, c: (0, 0)),
    ]
    args = [core, joined, bias, seg_rows, seg_cols, w_out, got]
    aliases = {}
    if mixed_all is not None:
        in_specs.append(pl.BlockSpec(memory_space=pl.ANY))
        args.append(mixed_all)
        aliases = {7: steps + 1}
    outs = kernel_call(
        functools.partial(attention_step_kernel, prompt_len, heads, first, last), 5,
        grid_spec=pltpu.PrefetchScalarGridSpec(
            num_scalar_prefetch=1, grid=(steps,), in_specs=in_specs, out_specs=out_specs
        ),
        out_shape=out_shape,
        input_output_aliases=aliases,
        name="attention_step",
    )(*args)
    send = outs[0] if first == 0 else None
    pair = outs[steps - 1] if last == 1 else None
    return send, pair, outs[-2], outs[-1]


def feed_step_kernel(first, last, step, place_ref, rows_any, cot_any, gain_ref, *refs):
    refs = list(refs)
    turns = list(range(first, last + 1))
    sums = [refs[2 * i : 2 * i + 2] for i in range(len(turns))]
    refs = refs[2 * len(turns) :]
    if last == 1:
        got_ref, refs = refs[0], refs[1:]
    w_in_any, w_out_any, in_a, in_b, out_a, out_b = refs[:6]
    (rows_ref, cot_ref, normed_ref, active_ref, hidden_ref, w_in_ref, w_out_ref,
     load_sems, save_sems) = refs[-9:]
    outs = refs[-9 - (3 + (1 if first == 0 else 0) + (4 if last == 1 else 0)) : -9]
    saved, rest = outs[:3], outs[3:]
    if first == 0:
        send_ref, rest = rest[0], rest[1:]
    if last == 1:
        result_ref, middle_ref, grad_ref, gain_grad_ref = rest
    half = rows_ref.shape[0] // len(turns)
    half_rows = in_a.shape[0]
    core, side, part = place_ref[0], place_ref[1], place_ref[2]
    near = pl.ds(pl.multiple_of(part * half_rows, half_rows), half_rows)
    away = pl.ds(pl.multiple_of((1 - part) * half_rows, half_rows), half_rows)

    def block(turn):
        mine = jnp.bitwise_xor(core, 1 - turn)
        return step - turn, pl.ds(pl.multiple_of(mine * half, half), half)

    def span(index):
        return pl.ds(index * half, half)

    row_loads = [
        pltpu.make_async_copy(rows_any.at[*block(turn)], rows_ref.at[span(i)], load_sems.at[i])
        for i, turn in enumerate(turns)
    ]
    cot_loads = [
        pltpu.make_async_copy(cot_any.at[*block(turn)], cot_ref.at[span(i)], load_sems.at[2 + i])
        for i, turn in enumerate(turns)
    ]
    in_loads = [
        pltpu.make_async_copy(w_in_any, w_in_ref.at[side], load_sems.at[4]),
        pltpu.make_async_copy(in_a, w_in_ref.at[1 - side, near], load_sems.at[5]),
        pltpu.make_async_copy(in_b, w_in_ref.at[1 - side, away], load_sems.at[6]),
    ]
    out_loads = [
        pltpu.make_async_copy(w_out_any, w_out_ref.at[side], load_sems.at[7]),
        pltpu.make_async_copy(out_a, w_out_ref.at[1 - side, near], load_sems.at[8]),
        pltpu.make_async_copy(out_b, w_out_ref.at[1 - side, away], load_sems.at[9]),
    ]
    for copy in row_loads + in_loads + cot_loads + out_loads:
        copy.start()
    for copy in row_loads:
        copy.wait()
    middles, scales = [], []
    for i, (pair_ref, far_ref) in enumerate(sums):
        middle = rows_ref[span(i), :].astype(wide) + (
            pair_ref[...].astype(wide) + far_ref[...].astype(wide)
        )
        scale = lax.rsqrt(jnp.mean(middle * middle, axis=-1, keepdims=True) + epsilon)
        normed_ref[span(i), :] = (middle * scale * gain_ref[...]).astype(low)
        middles.append(middle)
        scales.append(scale)
    for copy in in_loads + cot_loads + out_loads:
        copy.wait()
    saves = []

    def save(place, source, target):
        for i, turn in enumerate(turns):
            copy = pltpu.make_async_copy(
                source.at[span(i)], target.at[*block(turn)], save_sems.at[2 * place + i]
            )
            copy.start()
            saves.append(copy)

    save(0, normed_ref, saved[0])
    normed, cot = normed_ref[...], cot_ref[...]
    feed, back = None, None
    for quarter in range(2):
        inner = nn(normed, w_in_ref[quarter])
        share = 0.5 + 0.5 * lax.erf(inner * root_half)
        active = (inner * share).astype(low)
        slope = share + inner * (jnp.exp(-0.5 * inner * inner) * inv_root_tau)
        hidden = (nt(cot, w_out_ref[quarter]) * slope).astype(low)
        active_ref[quarter] = active
        hidden_ref[quarter] = hidden
        feed_share = nn(active, w_out_ref[quarter])
        back_share = nt(hidden, w_in_ref[quarter])
        feed = feed_share if feed is None else feed + feed_share
        back = back_share if back is None else back + back_share
    save(1, active_ref.at[side], saved[1])
    save(2, hidden_ref.at[side], saved[2])
    if first == 0:
        send_ref[:half, :] = feed[:half].astype(low)
        send_ref[half:, :] = back[:half].astype(low)
    if last == 1:
        middle, scale = middles[-1], scales[-1]
        result_ref[...] = (middle + (feed[-half:] + got_ref[:half, :].astype(wide))).astype(low)
        upstream = back[-half:] + got_ref[half:, :].astype(wide)
        scaled = upstream * gain_ref[...]
        inner = jnp.mean(scaled * middle, axis=-1, keepdims=True)
        grad = cot_ref[span(len(turns) - 1), :].astype(wide) + scale * scaled - middle * (
            scale * scale * scale * inner
        )
        middle_ref[...] = grad
        grad_ref[...] = grad.astype(low)
        share = jnp.sum(upstream * middle * scale, axis=0, keepdims=True)
        gain_grad_ref[...] = jnp.where(side == 0, share, 0.0)
    for copy in saves:
        copy.wait()


def feed_step(step, packs, place, rows, cot, gain, sums, far_sums, own_pair, own_far, got,
              w_in, w_out, in_halves, out_halves, kept):
    _, row_count, model = rows.shape
    hidden = w_in.shape[1]
    half = row_count // 2
    first, last = (0 if step < packs else 1), (1 if step > 0 else 0)
    steps = last - first + 1
    inside = pl.BlockSpec(memory_space=pltpu.VMEM)
    anywhere = pl.BlockSpec(memory_space=pl.ANY)
    args = [place, rows, cot, gain]
    in_specs = [pl.BlockSpec(memory_space=pltpu.SMEM), anywhere, anywhere, inside]
    flats = ([sums, far_sums] if first == 0 else []) + ([own_pair, own_far, got] if last == 1 else [])
    args += flats
    in_specs += [inside] * len(flats)
    args += [w_in, w_out, *in_halves, *out_halves]
    in_specs += [anywhere] * 6
    aliases = {}
    if kept is not None:
        in_specs += [anywhere] * 3
        aliases = {len(args) + i: i for i in range(3)}
        args += list(kept)
    out_specs = [anywhere] * 3
    out_shape = [
        in_hbm((packs, row_count, model), low),
        in_hbm((packs, row_count, hidden), low),
        in_hbm((packs, row_count, hidden), low),
    ]
    if first == 0:
        out_specs.append(inside)
        out_shape.append(jax.ShapeDtypeStruct((row_count, model), low))
    if last == 1:
        out_specs += [inside] * 4
        out_shape += [
            in_hbm((half, model), low),
            in_hbm((half, model), wide),
            jax.ShapeDtypeStruct((half, model), low),
            jax.ShapeDtypeStruct((1, model), wide),
        ]
    outs = kernel_call(
        functools.partial(feed_step_kernel, first, last, step), 4 + 4 * steps,
        in_specs=in_specs,
        out_specs=out_specs,
        scratch_shapes=[
            pltpu.VMEM((steps * half, model), low),
            pltpu.VMEM((steps * half, model), low),
            pltpu.VMEM((steps * half, model), low),
            pltpu.VMEM((2, steps * half, hidden), low),
            pltpu.VMEM((2, steps * half, hidden), low),
            pltpu.VMEM((2, model, hidden), low),
            pltpu.VMEM((2, hidden, model), low),
            pltpu.SemaphoreType.DMA((10,)),
            pltpu.SemaphoreType.DMA((6,)),
        ],
        out_shape=out_shape,
        input_output_aliases=aliases,
        name="feed_step",
    )(*args)
    sent = outs[3] if first == 0 else None
    own = outs[-4:] if last == 1 else (None,) * 4
    return outs[:3], sent, own


def attention_back_kernel(
    heads, has_back, has_prev, core_ref, *refs,
):
    refs = list(refs)
    if has_back:
        own_ref, far_ref, w_out_ref, probs_own_ref, probs_far_ref, joined_ref = refs[:6]
        refs = refs[6:]
    w_joined_ref = refs.pop(0)
    if has_prev:
        prev_ref, got_ref, values_ref, grad_ref, gain_ref, gain_in_ref, head_in_ref = refs[:7]
        refs = refs[7:]
    outs = refs[-((5 if has_back else 0) + (3 if has_prev else 0)):]
    if has_prev:
        pair_ref, gain_out_ref, head_out_ref = outs[:3]
        outs = outs[3:]
        pair = (nn(prev_ref[...], w_joined_ref[...]) + got_ref[...].astype(wide)).astype(low)
        pair_ref[...] = pair
        top = head_in_ref.shape[0]
        values, upstream = values_ref[0].astype(wide), pair.astype(wide)
        grad, share = norm_back(upstream, gain_ref[...], values)
        gain_out_ref[...] = gain_in_ref[...] + share
        grad = grad[:top] + jnp.where(core_ref[1] == 0, grad_ref[:top, :], 0.0)
        head_out_ref[...] = head_in_ref[...] + jnp.where(core_ref[0] == 0, grad, 0.0)
    if not has_back:
        return
    send_ref, own_grads_ref, grads_ref, scores_ref, whole_ref = outs
    rows = joined_ref.shape[1]
    half = rows // 2
    width = w_out_ref.shape[0]
    size = width // heads
    core = core_ref[0]
    starts = [pl.multiple_of(core * half, half), pl.multiple_of((1 - core) * half, half)]
    ups, asks, asked = [], [], [[], []]
    for side, ref in enumerate((own_ref, far_ref)):
        whole_ref[0, pl.ds(starts[side], half), :] = ref[...]
        ups.append(nt(ref[...], w_out_ref[...]).astype(low))
        asks.append(joined_ref[0, pl.ds(starts[side], half), :width])
    grad_keys, grad_values = [], []
    for head in range(heads):
        cols = slice(head * size, (head + 1) * size)
        keys = joined_ref[0, :, width + head * size : width + (head + 1) * size]
        values = joined_ref[0, :, 2 * width + head * size : 2 * width + (head + 1) * size]
        grad_key, grad_value = None, None
        for side, probs_ref in enumerate((probs_own_ref, probs_far_ref)):
            probs = probs_ref[0, head]
            upstream = ups[side][:, cols]
            grad_probs = nt(upstream, values)
            spread = probs.astype(wide)
            inner = jnp.sum(spread * grad_probs, axis=-1, keepdims=True)
            grad_scores = (spread * (grad_probs - inner)).astype(low)
            scores_ref[0, head, pl.ds(starts[side], half), :] = grad_scores
            value_share = tn(upstream, probs)
            key_share = tn(asks[side][:, cols], grad_scores)
            grad_value = value_share if grad_value is None else grad_value + value_share
            grad_key = key_share if grad_key is None else grad_key + key_share
            asked[side].append(nn(grad_scores, keys))
        grad_values.append(grad_value.T)
        grad_keys.append(grad_key.T)
    rest = jnp.concatenate(grad_keys + grad_values, axis=1).astype(low)
    grads_ref[0, :, width:] = rest
    for side in range(2):
        grads_ref[0, pl.ds(starts[side], half), :width] = jnp.concatenate(asked[side], axis=1).astype(low)
    own_grads_ref[...] = grads_ref[0, pl.ds(starts[0], half), :]
    send_ref[...] = nn(grads_ref[0, pl.ds(starts[1], half), :], w_joined_ref[...]).astype(low)


def attention_back_step(step, packs, heads, core, own, far, w_out, probs_own, probs_far, joined, w_joined,
                        prev, got, values, grad, gain, gain_sum, head_sum, kept):
    _, rows, triple = joined.shape
    width, model = w_out.shape
    half = rows // 2
    has_back, has_prev = step < packs, step > 0
    fixed = lambda t, c: (0, 0)
    flat = pl.BlockSpec((half, model), fixed)
    anywhere = pl.BlockSpec(memory_space=pl.ANY)
    in_specs, args, out_specs, out_shape, aliases = [], [core], [], [], {}
    if has_back:
        (own_place, probs_own), (far_place, probs_far) = probs_own, probs_far
        in_specs += [
            flat,
            flat,
            pl.BlockSpec((width, model), fixed),
            pl.BlockSpec((1, heads, half, rows), lambda t, c: (own_place, 0, 0, 0)),
            pl.BlockSpec((1, heads, half, rows), lambda t, c: (far_place, 0, 0, 0)),
            pl.BlockSpec((1, rows, triple), lambda t, c: (step, 0, 0)),
        ]
        args += [own, far, w_out, probs_own, probs_far, joined]
    in_specs.append(pl.BlockSpec((triple, model), fixed))
    args.append(w_joined)
    if has_prev:
        line = pl.BlockSpec((1, model), fixed)
        head = pl.BlockSpec(head_sum.shape, fixed)
        in_specs += [
            pl.BlockSpec((half, triple), fixed),
            flat,
            pl.BlockSpec((1, half, model), lambda t, c: (step - 1, c[0], 0)),
            flat,
            line,
            line,
            head,
        ]
        args += [prev, got, values, grad, gain, gain_sum, head_sum]
        out_specs += [flat, line, head]
        out_shape += [
            jax.ShapeDtypeStruct((half, model), low),
            jax.ShapeDtypeStruct((1, model), wide),
            jax.ShapeDtypeStruct(head_sum.shape, wide),
        ]
    if has_back:
        if kept is not None:
            in_specs += [anywhere] * 3
            aliases = {len(args) + i: len(out_shape) + 2 + i for i in range(3)}
            args += list(kept)
        out_specs += [
            flat,
            pl.BlockSpec((half, triple), fixed),
            pl.BlockSpec((1, rows, triple), lambda t, c: (step, 0, 0)),
            pl.BlockSpec((1, heads, rows, rows), lambda t, c: (step, 0, 0, 0)),
            pl.BlockSpec((1, rows, model), lambda t, c: (step, 0, 0)),
        ]
        out_shape += [
            jax.ShapeDtypeStruct((half, model), low),
            jax.ShapeDtypeStruct((half, triple), low),
            in_hbm((packs, rows, triple), low),
            in_hbm((packs, heads, rows, rows), low),
            in_hbm((packs, rows, model), low),
        ]
    outs = list(
        kernel_call(
            functools.partial(attention_back_kernel, heads, has_back, has_prev), 6,
            grid_spec=pltpu.PrefetchScalarGridSpec(
                num_scalar_prefetch=1, grid=(1,), in_specs=in_specs, out_specs=out_specs
            ),
            out_shape=out_shape,
            input_output_aliases=aliases,
                name="attention_back_step",
        )(*args)
    )
    done, outs = (outs[:3], outs[3:]) if has_prev else ((None,) * 3, outs)
    send, own_grads, *kept = outs if has_back else (None, None)
    return done, send, own_grads, kept


def finish_kernel(core_ref, rows_ref, pair_ref, far_ref, grad_ref, gain_ref, out_ref):
    upstream = pair_ref[...].astype(wide) + far_ref[...].astype(wide)
    grad, _ = norm_back(upstream, gain_ref[...], rows_ref[0].astype(wide))
    out_ref[...] = (grad_ref[...] + grad).astype(low)


def finish(pack, core, rows, pair, far, grad, gain):
    half, model = pair.shape
    fixed = lambda t, c: (0, 0)
    flat = pl.BlockSpec((half, model), fixed)
    return kernel_call(
        finish_kernel, 1.5,
        grid_spec=pltpu.PrefetchScalarGridSpec(
            num_scalar_prefetch=1,
            grid=(1,),
            in_specs=[
                pl.BlockSpec((1, half, model), lambda t, c: (pack, c[0], 0)),
                flat, flat, flat, pl.BlockSpec((1, model), fixed),
            ],
            out_specs=flat,
        ),
        out_shape=jax.ShapeDtypeStruct((half, model), low),
        name="finish",
    )(core, rows, pair, far, grad, gain)


def place_kernel(packs, core_ref, *refs):
    out_ref, sems = refs[-2:]
    half = out_ref.shape[1] // 2
    copies = []
    for pack in range(packs):
        for side in range(2):
            start = pl.multiple_of(jnp.bitwise_xor(core_ref[0], side) * half, half)
            copies.append(
                pltpu.make_async_copy(
                    refs[2 * pack + side], out_ref.at[pack, pl.ds(start, half)], sems.at[2 * pack + side]
                )
            )
    for copy in copies:
        copy.start()
    for copy in copies:
        copy.wait()


def place_halves(core, pairs):
    packs = len(pairs)
    half, model = pairs[0][0].shape
    anywhere = pl.BlockSpec(memory_space=pl.ANY)
    return kernel_call(
        functools.partial(place_kernel, packs), 2.5,
        in_specs=[pl.BlockSpec(memory_space=pltpu.SMEM)]
        + [pl.BlockSpec(memory_space=pltpu.VMEM)] * (2 * packs),
        out_specs=anywhere,
        out_shape=in_hbm((packs, 2 * half, model), low),
        scratch_shapes=[pltpu.SemaphoreType.DMA((2 * packs,))],
        name="place_halves",
    )(core, *[v for pair in pairs for v in pair])


def weave_kernel(packs, core_ref, *refs):
    out_ref, rows_ref, woven_ref = refs[-3:]
    half = rows_ref.shape[0] // 2
    text = out_ref.shape[0]
    for pack in range(packs):
        for side in range(2):
            start = pl.multiple_of(jnp.bitwise_xor(core_ref[0], side) * half, half)
            rows_ref[pl.ds(start, half), :] = refs[2 * pack + side][...].astype(wide)
        woven_ref[:, pack, :] = rows_ref[2 * half - text :, :]
    out_ref[...] = woven_ref[...].astype(low)


def weave_halves(core, pairs, text):
    packs = len(pairs)
    half, model = pairs[0][0].shape
    inside = pl.BlockSpec(memory_space=pltpu.VMEM)
    return kernel_call(
        functools.partial(weave_kernel, packs), 4,
        in_specs=[pl.BlockSpec(memory_space=pltpu.SMEM)] + [inside] * (2 * packs),
        out_specs=inside,
        out_shape=jax.ShapeDtypeStruct((text, packs, model), low),
        scratch_shapes=[pltpu.VMEM((2 * half, model), wide), pltpu.VMEM((text, packs, model), wide)],
        name="weave_halves",
    )(core, *[v for pair in pairs for v in pair])


def weight_kernel(pairs, where_ref, *refs):
    keep_ref, send_ref, total_ref = refs[-3:]
    column = 0
    for i in range(pairs):
        right = refs[2 * i + 1][...]
        total_ref[:, column : column + right.shape[1]] = tn(refs[2 * i][...], right)
        column += right.shape[1]
    count, block, _ = keep_ref.shape
    side = jnp.bitwise_and(where_ref[0], 1)
    for i in range(count):
        for ref, chosen in ((keep_ref, side), (send_ref, 1 - side)):
            start = pl.multiple_of((2 * i + chosen) * block, 8)
            ref[i] = total_ref[pl.ds(start, block), :].astype(low)


def weight_shares(where, count, pairs):
    rows, model = pairs[0][0].shape
    widths = [right.shape[1] for _, right in pairs]
    turns, width = 2, sum(widths)
    block = model // count
    in_specs = []
    for n in widths:
        in_specs += [
            pl.BlockSpec((rows, model // turns), lambda t, w: (0, t)),
            pl.BlockSpec((rows, n), lambda t, w: (0, 0)),
        ]
    out = pl.BlockSpec((count // 2 // turns, block, width), lambda t, w: (t, 0, 0))
    return kernel_call(
        functools.partial(weight_kernel, len(pairs)), 6,
        grid_spec=pltpu.PrefetchScalarGridSpec(
            num_scalar_prefetch=1,
            grid=(turns,),
            in_specs=in_specs,
            out_specs=[out, out],
            scratch_shapes=[pltpu.VMEM((model // turns, width), wide)],
        ),
        out_shape=[jax.ShapeDtypeStruct((count // 2, block, width), low)] * 2,
        name="weight_shares",
    )(where, *[value for pair in pairs for value in pair])


def tie(*values):
    return lax.optimization_barrier(values)


def stages_of(count):
    bits = bits_of(count)
    rest = bits[1:][::-1]
    return [bits[:1]] + [rest[i : i + 2] for i in range(0, len(rest), 2)]


class Scatter:
    def __init__(self, keep, send):
        count = lax.axis_size("dp")
        self.left = list(reversed(bits_of(count)))[:-1]
        self.stages = stages_of(count)[1:]
        self.shape = [2] * len(self.left) + list(keep.shape[1:])
        self.parts = [keep, swap(send, "dp", 1)]

    def send(self):
        where = lax.axis_index("dp")
        stage, self.stages = self.stages[0], self.stages[1:]
        axes = sorted(self.left.index(bit) for bit in stage)
        chosen = [self.left[axis] for axis in axes]
        self.left = [bit for bit in self.left if bit not in stage]

        def part(flip):
            value = self.share
            for axis, bit in reversed(list(zip(axes, chosen))):
                spot = (jnp.bitwise_xor(where, flip) // bit) % 2
                value = lax.dynamic_index_in_dim(value, spot, axis, keepdims=False)
            return value

        flips = [0]
        for bit in stage:
            flips += [flip | bit for flip in flips]
        self.parts = [part(0)] + [swap(part(flip), "dp", flip) for flip in flips[1:]]
        self.shape = self.parts[0].shape

    def take(self):
        total = self.parts[0].astype(wide)
        for value in self.parts[1:]:
            total = total + value.astype(wide)
        self.share = (total.astype(low) if self.left else total).reshape(self.shape)

    def step(self, *others):
        self.take()
        self.share, *others = tie(self.share, *others)
        self.parts = None
        if self.stages:
            self.send()
        return others

    def end(self):
        while self.parts:
            self.take()
            self.parts = None
            if self.stages:
                self.send()
        return self.share


def look_up(prompt_ids, table, prompt_delta):
    prompt_len = prompt_ids.shape[0]
    table_rows, model = table.shape
    groups = lax.axis_size("mp")
    part = -(-prompt_len // (16 * groups)) * 16
    dp_index, mp_index = lax.axis_index("dp"), lax.axis_index("mp")
    padded = jnp.pad(prompt_ids, (0, part * groups - prompt_len), constant_values=-1)
    ids = lax.dynamic_slice_in_dim(padded, mp_index * part, part)
    size, block = prompt_delta.shape[0], part * model
    line = jnp.pad(prompt_delta, (block, block))
    start = jnp.clip(block + mp_index * block - dp_index * size, 0, block + size)
    placed = lax.dynamic_slice_in_dim(line, start, block).reshape(part, model)
    local = jnp.where(ids < 0, -1, ids - dp_index * table_rows)
    if table_rows % 16 == 0:
        return look_up_rows(local, table, placed)
    selector = (local[:, None] == jnp.arange(table_rows, dtype=jnp.int32)[None, :]).astype(low)
    return jnp.dot(selector, table, preferred_element_type=wide) + placed


def own_half(weight):
    part = lax.axis_index("dp") % 2
    halves = weight.reshape(2, weight.shape[0] // 2, weight.shape[1])
    return lax.dynamic_index_in_dim(halves, part, 0, keepdims=False)


class Small:
    groups = 4

    def __init__(self, head, gain1, gain2, prompt_len):
        self.prompt_len, self.model = prompt_len, head.shape[1]
        self.mp_bits = bits_of(lax.axis_size("mp"))
        self.dp_bits = bits_of(lax.axis_size("dp"))[::-1]
        self.total = jnp.concatenate([head[:prompt_len], gain1, gain2], axis=0).astype(low)
        self.share = prompt_len // self.groups
        self.rows = -(-(self.share + 3) // 16) * 16
        self.rel = None

    def hop(self):
        if self.mp_bits:
            bit, self.mp_bits = self.mp_bits[0], self.mp_bits[1:]
            self.keep, self.got = self.total, swap(self.total, "mp", bit)
            return
        bit, place = self.dp_bits[0], lax.axis_size("dp").bit_length() - 1 - len(self.dp_bits)
        self.dp_bits = self.dp_bits[1:]
        self.keep, send = self.total, self.total
        if place < 2:
            side = (lax.axis_index("dp") // bit) % 2
            halves = self.total.reshape(2, self.total.shape[0] // 2, self.rows, self.model)
            send = lax.dynamic_index_in_dim(halves, 1 - side, 0, keepdims=False)
            self.keep = lax.dynamic_index_in_dim(halves, side, 0, keepdims=False)
        self.got = swap(send, "dp", bit)

    def land(self):
        total = self.keep.astype(wide) + self.got.astype(wide)
        self.total = total.astype(low) if self.dp_bits else total

    def add_rel(self, rel):
        self.rel = rel
        rel_row = jnp.pad(rel.reshape(1, -1), ((0, 0), (0, self.model - rel.size))).astype(low)
        rest = jnp.concatenate([self.total[self.prompt_len :], rel_row], axis=0)
        rest = jnp.broadcast_to(rest[None], (self.groups, 3, self.model))
        head = self.total[: self.prompt_len].reshape(self.groups, self.share, self.model)
        total = jnp.concatenate([head, rest], axis=1)
        self.total = jnp.pad(total, ((0, 0), (0, self.rows - self.share - 3), (0, 0)))

    def results(self):
        dp_count, dp_index = lax.axis_size("dp"), lax.axis_index("dp")
        total, share = self.total[0], self.share
        inside = dp_count // self.groups
        size = share * self.model // inside
        prompt_grad = lax.dynamic_slice_in_dim(total[:share].reshape(-1), (dp_index % inside) * size, size)
        width = self.model // dp_count
        gains = lax.dynamic_slice_in_dim(total[share : share + 2], dp_index * width, width, axis=1)
        piece = self.rel.size // dp_count
        rel_out = lax.dynamic_slice_in_dim(total[share + 2], dp_index * piece, piece)
        return prompt_grad, gains[0], gains[1], rel_out.reshape(-1, self.rel.shape[1])


def body(
    tokens, cotangent, segment_ids, prompt_ids, rel_buckets, table, prompt_delta, norm1_gain,
    w_query, w_key, w_value, w_output, rel_bias, norm2_gain, w_inner, w_outer,
):
    prompt_len = prompt_ids.shape[0]
    packs, rows, model = cotangent.shape
    bucket_count, heads = rel_bias.shape
    width = w_query.shape[1]
    groups = lax.axis_size("dp")
    mp_bits = bits_of(lax.axis_size("mp"))
    mp_index = lax.axis_index("mp").astype(jnp.int32)
    place = jnp.stack([mp_index % 2, (mp_index // 2) % 2, (lax.axis_index("dp") % 2).astype(jnp.int32)])
    gain1, gain2 = norm1_gain[None, :], norm2_gain[None, :]
    w_q, w_k, w_v = w_query.T, w_key.T, w_value.T

    in_near = swap(own_half(w_inner), "mp", 2)
    total = look_up(prompt_ids, table, prompt_delta)
    out_near = swap(own_half(w_outer), "mp", 2)

    w_joined = jnp.concatenate([w_q, w_k, w_v], axis=0)
    bucket_hot = (
        rel_buckets[:, None] == jnp.arange(bucket_count, dtype=jnp.int32)[None, :]
    ).astype(wide)
    bucket_hot = jnp.pad(bucket_hot, ((0, 1), (0, 0)))
    turned = jnp.roll(bucket_hot, -(rows - 1), axis=0)
    bias_line = jnp.dot(turned, rel_bias, precision=highest).T
    marks = jnp.pad(segment_ids, ((0, 0), (prompt_len, 0)), constant_values=-1)
    seg_rows, seg_cols = marks[:, :, None], marks[:, None, :]

    for hop, bit in enumerate(bits_of(groups)):
        got = swap(total, "dp", bit)
        if hop == 0:
            bias = bias_grid_of(bias_line[:, None, :])
            got, bias, seg_rows, seg_cols, w_joined = tie(got, bias, seg_rows, seg_cols, w_joined)
        if hop == 1:
            whole_rows, normed1, joined = text_projections(rows, tokens, gain1, w_q, w_k, w_v)
            got, whole_rows, normed1, joined, in_near = tie(got, whole_rows, normed1, joined, in_near)
        if hop == 2:
            got, in_near, out_near = tie(got, in_near, out_near)
            in_away = swap(in_near, "dp", 1)
        total = total + got
    pieces = total.astype(low)[None]
    for bit in mp_bits:
        pieces = jnp.concatenate([pieces, swap(pieces, "mp", bit)], axis=0)
    whole_rows, normed1, joined = add_prompt(
        mp_index.reshape(1), pieces, gain1, w_q, w_k, w_v, whole_rows, normed1, joined
    )

    pairs, fars, pairs_far, fars_far, probs_far, probs_own, mixed, got = [], [], [], [], [], [], None, None

    def attend(step):
        nonlocal mixed, got, place, in_away, out_near, out_away
        send, pair, probs, mixed = attention_step(
            step, packs, prompt_len, place, joined, bias, seg_rows, seg_cols, w_output, got, mixed
        )
        if step == 0:
            place, in_away, out_near, send = tie(place, in_away, out_near, send)
            out_away = swap(out_near, "dp", 1)
        else:
            place, pair = tie(place, pair)
        if send is not None:
            probs_far.append((0, probs))
            got = swap(send, "mp", 1)
        if pair is not None:
            probs_own.append((probs.shape[0] - 1, probs))
            pairs.append(pair)
            fars.append(swap(pair, "mp", 2))
            pairs_far.append(swap(pair, "mp", 1))
            fars_far.append(swap(fars[-1], "mp", 1))

    out_away = None

    def arrive(pack):
        nonlocal place
        place, fars[pack], pairs_far[pack], fars_far[pack] = tie(
            place, fars[pack], pairs_far[pack], fars_far[pack]
        )

    kept, sent, results, grads_wide, grads_low = None, None, [], [], []
    gain2_sum, none = 0.0, [None]
    back_kept, prev, got = None, None, None
    gain1_sum, head_sum = jnp.zeros((1, model), wide), jnp.zeros((128, model), wide)
    text_rows, pairs_back = [], []

    def feed(step):
        nonlocal kept, sent, gain2_sum, place
        kept, new_sent, done = feed_step(
            step, packs, place, whole_rows, cotangent, gain2,
            (pairs_far + none)[step], (fars_far + none)[step],
            (none + pairs)[step], (none + fars)[step], sent,
            w_inner, w_outer, (in_near, in_away), (out_near, out_away), kept,
        )
        if step < packs:
            place, new_sent = tie(place, new_sent)
            sent = swap(new_sent, "mp", 1)
        else:
            place, *done = tie(place, *done)
        if step > 0:
            results.append(done[0])
            grads_wide.append(done[1])
            grads_low.append((done[2], swap(done[2], "mp", 1)))
            gain2_sum = gain2_sum + done[3]

    def back(step):
        nonlocal back_kept, prev, got, gain1_sum, head_sum, place
        live = step < packs
        done, send, own_grads, back_new = attention_back_step(
            step, packs, heads, place, *(grads_low[step] if live else none * 2), w_output,
            probs_own[step] if live else None, probs_far[step] if live else None, joined, w_joined,
            prev, got, whole_rows, grads_wide[step - 1] if step else None, gain1, gain1_sum, head_sum,
            back_kept,
        )
        if live:
            place, send = tie(place, send)
            back_kept, prev, got = back_new, own_grads, swap(send, "mp", 1)
        if step > 0:
            pair, gain1_sum, head_sum = done
            pairs_back.append((pair, swap(pair, "mp", 2)))

    def end(pack):
        nonlocal place
        rows_low = finish(pack, place, whole_rows, *pairs_back[pack], grads_wide[pack], gain1)
        place, rows_low = tie(place, rows_low)
        text_rows.append((rows_low, swap(rows_low, "mp", 1)))

    def flat(value):
        return value.reshape(packs * rows, -1)

    for step in range(packs):
        attend(step)
    place, out_away = tie(place, out_away)
    arrive(0)
    feed(0)
    attend(packs)
    arrive(1)
    feed(1)
    for step in range(2, packs):
        arrive(step)
        feed(step)
        back(step - 2)
    feed(packs)
    normed2, active, hidden = kept
    where = lax.axis_index("dp").astype(jnp.int32).reshape(1)
    where, place = tie(where, place)
    inner_shares = weight_shares(where, groups, [(flat(normed2), flat(hidden))])
    place, *inner_shares = tie(place, *inner_shares)
    inner = Scatter(*inner_shares)
    back(packs - 2)
    where, place = tie(where, place)
    outer_shares = weight_shares(where, groups, [(flat(cotangent), flat(active))])
    place, *outer_shares = inner.step(place, *outer_shares)
    outer = Scatter(*outer_shares)
    end(0)
    back(packs - 1)
    inner_grad = inner.end()
    place, inner_grad = tie(place, inner_grad)
    end(1)
    grad_joined, scores, grad_rows = back_kept
    where, place = tie(where, place)
    tail_shares = weight_shares(
        where, groups, [(flat(normed1), flat(grad_joined)), (flat(grad_rows), flat(mixed))]
    )
    place, *tail_shares = outer.step(place, *tail_shares)
    tail = Scatter(*tail_shares)
    back(packs)
    place, head_sum, gain1_sum = tie(place, head_sum, gain1_sum)
    small = Small(head_sum, gain1_sum, gain2_sum, prompt_len)
    small.hop()
    place, scores = tie(place, scores)
    line = diagonal_sums(scores)[:, 0, :]
    rel_share = jnp.einsum("ht,tb->bh", line, turned, precision=highest)
    small.land()
    small.hop()
    place, rel_share = tie(place, rel_share)
    end(packs - 2)
    outer_grad = outer.end()
    place, outer_grad = tie(place, outer_grad)
    out = place_halves(place, [(v, swap(v, "mp", 1)) for v in results])
    place, out = tail.step(place, out)
    small.land()
    small.add_rel(rel_share)
    small.hop()
    end(packs - 1)
    small.land()
    place, small.total = tie(place, small.total)
    small.hop()
    grad_tokens = jnp.transpose(weave_halves(place, text_rows, rows - prompt_len), (1, 0, 2))
    while True:
        small.land()
        if not small.dp_bits:
            break
        small.hop()
    prompt_grad, gain1_grad, gain2_grad, rel_grad = small.results()
    tail, outer_grad = tail.end(), outer_grad.T
    return (
        out, grad_tokens, prompt_grad, gain1_grad,
        tail[:, :width], tail[:, width : 2 * width], tail[:, 2 * width : 3 * width],
        tail[:, 3 * width :].T, rel_grad, gain2_grad, inner_grad, outer_grad,
    )


def solution(mesh):
    in_specs = (
        P("dp", None, None),
        P("dp", None, None),
        P("dp", None),
        P(),
        P(),
        P("dp", None),
        P("dp"),
        P(),
        P(None, "mp"),
        P(None, "mp"),
        P(None, "mp"),
        P("mp", None),
        P(None, "mp"),
        P(),
        P(None, "mp"),
        P("mp", None),
    )
    out_specs = (
        P("dp", None, None),
        P("dp", None, None),
        P("dp"),
        P("dp"),
        P("dp", "mp"),
        P("dp", "mp"),
        P("dp", "mp"),
        P("mp", "dp"),
        P("dp", "mp"),
        P("dp"),
        P("dp", "mp"),
        P("mp", "dp"),
    )
    return jax.shard_map(body, mesh=mesh, in_specs=in_specs, out_specs=out_specs, check_vma=False)
```

```python
import functools

import jax
import jax.numpy as jnp
from jax import lax
from jax.experimental import pallas as pl
from jax.experimental.pallas import tpu as pltpu
from jax.sharding import PartitionSpec as P

epsilon = 1e-06
blocked = -1000000000.0
highest = lax.Precision.HIGHEST
low = jnp.bfloat16
wide = jnp.float32
root_half = 0.7071067811865476
inv_root_tau = 0.3989422804014327


def nn(left, right):
    return lax.dot_general(left, right, (((1,), (0,)), ((), ())), preferred_element_type=wide)


def nt(left, right):
    return lax.dot_general(left, right, (((1,), (1,)), ((), ())), preferred_element_type=wide)


def tn(left, right):
    return lax.dot_general(left, right, (((0,), (0,)), ((), ())), preferred_element_type=wide)


def params(mebibytes):
    return pltpu.CompilerParams(vmem_limit_bytes=mebibytes * 1024 * 1024)


def in_hbm(shape, dtype):
    return pltpu.HBM(shape, dtype)


def kernel_call(kernel, micros, vmem=16, near=(), least=400000, **rest):
    cost = pl.CostEstimate(flops=0, bytes_accessed=int(micros * 3.6e6), transcendentals=0)
    call = pl.pallas_call(kernel, cost_estimate=cost, compiler_params=params(vmem), **rest)

    def run(*args):
        return call(
            *[
                pltpu.with_memory_space_constraint(v, pltpu.HBM) if (v.size >= least or v.ndim == 4) and i not in near else v
                for i, v in enumerate(args)
            ]
        )

    return run


def swap(value, axis, bit):
    count = lax.axis_size(axis)
    return lax.ppermute(value, axis, [(i, i ^ bit) for i in range(count)])


def bits_of(count):
    return [1 << i for i in range(count.bit_length() - 1)]


def rms_norm(values, gain):
    return values * lax.rsqrt(jnp.mean(values * values, axis=-1, keepdims=True) + epsilon) * gain


def norm_back(upstream, gain, values):
    scale = lax.rsqrt(jnp.mean(values * values, axis=-1, keepdims=True) + epsilon)
    scaled = upstream * gain
    inner = jnp.mean(scaled * values, axis=-1, keepdims=True)
    grad = scale * scaled - values * (scale * scale * scale * inner)
    return grad, jnp.sum(upstream * values * scale, axis=0, keepdims=True)


def bias_kernel(line_ref, grid_ref):
    rows = grid_ref.shape[1]
    spread = jnp.broadcast_to(line_ref[0], (rows, 2 * rows))
    grid_ref[0] = pltpu.roll(spread, 0, 1, stride=1, stride_axis=0)[:, :rows]


def bias_grid_of(line):
    heads, _, double = line.shape
    rows = double // 2
    return kernel_call(
        bias_kernel, 2,
        grid=(heads,),
        in_specs=[pl.BlockSpec((1, 1, double), lambda h: (h, 0, 0))],
        out_specs=pl.BlockSpec((1, rows, rows), lambda h: (h, 0, 0)),
        out_shape=jax.ShapeDtypeStruct((heads, rows, rows), wide),
        name="bias_grid",
    )(line)


def diag_kernel(grid_ref, line_ref):
    packs, _, rows, _ = grid_ref.shape
    lanes = 128
    count = rows // lanes
    blocks = []
    for block in range(2 * count):
        total = jnp.zeros((lanes, lanes), wide)
        for band in range(count):
            column = (block + band) % (2 * count)
            if column < count:
                for pack in range(packs):
                    total = total + grid_ref[
                        pack, 0, band * lanes : (band + 1) * lanes, column * lanes : (column + 1) * lanes
                    ].astype(wide)
        blocks.append(total)
    held = jnp.concatenate(blocks, axis=1)
    total = held[:8]
    for slab in range(1, lanes // 8):
        total = total + pltpu.roll(held[8 * slab : 8 * slab + 8], 2 * rows - 8 * slab, 1)
    line = total[0:1]
    for row in range(1, 8):
        line = line + pltpu.roll(total[row : row + 1], 2 * rows - row, 1)
    line_ref[0] = line


def diagonal_sums(grid):
    packs, heads, rows, _ = grid.shape
    return kernel_call(
        diag_kernel, 3,
        grid=(heads,),
        in_specs=[pl.BlockSpec((packs, 1, rows, rows), lambda h: (0, h, 0, 0))],
        out_specs=pl.BlockSpec((1, 1, 2 * rows), lambda h: (h, 0, 0)),
        out_shape=in_hbm((heads, 1, 2 * rows), wide),
        name="diagonal_sums",
    )(grid)


def shifted_text_kernel(tokens_ref, gain_ref, weight_ref, *refs):
    rows_ref, normed_ref, joined_ref, wide_ref = refs[-4:]
    rows = rows_ref.shape[1]
    prompt_len = rows - tokens_ref.shape[1]
    wide_ref[:prompt_len, :] = jnp.zeros((prompt_len, wide_ref.shape[1]), wide)
    wide_ref[prompt_len:, :] = tokens_ref[0].astype(wide)
    values = wide_ref[...]
    rows_ref[0] = values.astype(low)
    normed = rms_norm(values, gain_ref[...]).astype(low)
    normed_ref[0] = normed
    joined_ref[0] = nt(normed, weight_ref[...]).astype(low)


def text_projections(first, count, rows, tokens, gain, weight, kept):
    packs, text, model = tokens.shape
    triple = weight.shape[0]
    fixed = lambda p: (0, 0)
    moving = lambda p: (first + p, 0, 0)
    return kernel_call(
        shifted_text_kernel, 1.2 * count,
        grid=(count,),
        in_specs=[
            pl.BlockSpec((1, text, model), moving),
            pl.BlockSpec((1, model), fixed),
            pl.BlockSpec((triple, model), fixed),
        ]
        + [pl.BlockSpec(memory_space=pl.ANY)] * len(kept),
        out_specs=[
            pl.BlockSpec((1, rows, model), moving),
            pl.BlockSpec((1, rows, model), moving),
            pl.BlockSpec((1, rows, triple), moving),
        ],
        out_shape=[
            in_hbm((packs, rows, model), low),
            in_hbm((packs, rows, model), low),
            in_hbm((packs, rows, triple), low),
        ],
        scratch_shapes=[pltpu.VMEM((rows, model), wide)],
        input_output_aliases={3 + i: i for i in range(len(kept))},
        name="text_projections",
    )(tokens, gain, weight, *kept)


def prompt_kernel(place_ref, pieces_ref, gain_ref, weight_ref, rows_in, normed_in, joined_in, rows_out, normed_out, joined_out,
                  prompt_ref, rows_ref, normed_ref, joined_ref, load_sems, save_sems):
    count, part, _ = pieces_ref.shape
    packs = rows_ref.shape[0]
    top = count * part
    held = (rows_ref, normed_ref, joined_ref)
    loads = [
        pltpu.make_async_copy(source.at[:, pl.ds(0, top)], target, load_sems.at[i])
        for i, (source, target) in enumerate(zip((rows_in, normed_in, joined_in), held))
    ]
    for copy in loads:
        copy.start()
    for k in range(count):
        start = pl.multiple_of(jnp.bitwise_xor(place_ref[0], k) * part, part)
        prompt_ref[pl.ds(start, part), :] = pieces_ref[k]
    prompt = prompt_ref[...]
    normed = rms_norm(prompt.astype(wide), gain_ref[...]).astype(low)
    joined = nt(normed, weight_ref[...]).astype(low)
    saves = []
    for i, (value, target) in enumerate(zip((prompt, normed, joined), (rows_out, normed_out, joined_out))):
        loads[i].wait()
        for pack in range(packs):
            held[i][pack] = held[i][pack] + value
        copy = pltpu.make_async_copy(held[i], target.at[:, pl.ds(0, top)], save_sems.at[i])
        copy.start()
        saves.append(copy)
    for copy in saves:
        copy.wait()


def add_prompt(place, pieces, gain, weight, rows, normed, joined):
    packs, _, model = rows.shape
    triple = weight.shape[0]
    count, part, _ = pieces.shape
    top = count * part
    inside = pl.BlockSpec(memory_space=pltpu.VMEM)
    anywhere = pl.BlockSpec(memory_space=pl.ANY)
    return kernel_call(
        prompt_kernel, 2.5,
        in_specs=[pl.BlockSpec(memory_space=pltpu.SMEM)] + [inside] * 3 + [anywhere] * 3,
        out_specs=[anywhere] * 3,
        out_shape=[
            in_hbm(rows.shape, low),
            in_hbm(normed.shape, low),
            in_hbm(joined.shape, low),
        ],
        scratch_shapes=[
            pltpu.VMEM((top, model), low),
            pltpu.VMEM((packs, top, model), low),
            pltpu.VMEM((packs, top, model), low),
            pltpu.VMEM((packs, top, triple), low),
            pltpu.SemaphoreType.DMA((3,)),
            pltpu.SemaphoreType.DMA((3,)),
        ],
        input_output_aliases={4: 0, 5: 1, 6: 2},
        name="add_prompt",
    )(place, pieces, gain, weight, rows, normed, joined)


def look_up_kernel(ids_ref, table_any, placed_ref, out_ref, blocks_ref, sems):
    part = out_ref.shape[0]
    limit = table_any.shape[0]
    copies, inside = [], []
    for row in range(part):
        local = jnp.clip(ids_ref[row], 0, limit - 1)
        inside.append(local)
        start = pl.multiple_of(jnp.left_shift(jnp.right_shift(local, 4), 4), 16)
        copies.append(
            pltpu.make_async_copy(table_any.at[pl.ds(start, 16)], blocks_ref.at[row], sems.at[row])
        )
    for copy in copies:
        copy.start()
    for copy in copies:
        copy.wait()
    position = lax.broadcasted_iota(jnp.int32, blocks_ref.shape[1:], 0)
    for row in range(part):
        own = inside[row] == ids_ref[row]
        chosen = (position == jnp.bitwise_and(inside[row], 15)) & own
        found = jnp.sum(jnp.where(chosen, blocks_ref[row].astype(wide), 0.0), axis=0, keepdims=True)
        out_ref[row : row + 1, :] = placed_ref[row : row + 1, :] + found


def look_up_rows(ids, table, placed):
    part, model = placed.shape
    inside = pl.BlockSpec(memory_space=pltpu.VMEM)
    return kernel_call(
        look_up_kernel, 2.5,
        in_specs=[pl.BlockSpec(memory_space=pltpu.SMEM), pl.BlockSpec(memory_space=pl.ANY), inside],
        out_specs=inside,
        out_shape=jax.ShapeDtypeStruct((part, model), wide),
        scratch_shapes=[pltpu.VMEM((part, 16, model), low), pltpu.SemaphoreType.DMA((part,))],
        name="look_up",
    )(ids, table, placed)


def attention_step_kernel(
    prompt_len, heads, first, last, core_ref, joined_ref, bias_ref, seg_rows_ref, seg_cols_ref, w_out_ref, got_ref,
    *refs,
):
    if first == 0 and last == 1:
        send_ref, pair_ref, probs_ref, mixed_ref = refs[-4:]
    elif first == 0:
        send_ref, probs_ref, mixed_ref = refs[-3:]
    else:
        pair_ref, probs_ref, mixed_ref = refs[-3:]
    turn = pl.program_id(0) + first
    rows = joined_ref.shape[1]
    half = rows // 2
    width = w_out_ref.shape[0]
    size = width // heads
    mine = jnp.bitwise_xor(core_ref[0], 1 - turn)
    start = pl.multiple_of(mine * half, half)
    row_pos = start + lax.broadcasted_iota(jnp.int32, (half, rows), 0)
    col_pos = lax.broadcasted_iota(jnp.int32, (half, rows), 1)
    allowed = (
        (row_pos < prompt_len) | (col_pos < prompt_len) | (seg_rows_ref[0] == seg_cols_ref[0])
    )
    queries = joined_ref[0, pl.ds(start, half), :width]
    mixed = []
    for head in range(heads):
        keys = joined_ref[0, :, width + head * size : width + (head + 1) * size]
        values = joined_ref[0, :, 2 * width + head * size : 2 * width + (head + 1) * size]
        scores = nt(queries[:, head * size : (head + 1) * size], keys) + bias_ref[head]
        scores = jnp.where(allowed, scores, blocked)
        top = jnp.max(scores, axis=-1, keepdims=True)
        raised = jnp.exp(scores - top)
        total = jnp.sum(raised, axis=-1, keepdims=True)
        probs = (raised * (1.0 / total)).astype(low)
        probs_ref[0, head] = probs
        mixed.append(nn(probs, values).astype(low))
    mixed = jnp.concatenate(mixed, axis=1)
    mixed_ref[0] = mixed
    share = nn(mixed, w_out_ref[...])

    if first == 0:

        @pl.when(turn == 0)
        def _():
            send_ref[...] = share.astype(low)

    if last == 1:

        @pl.when(turn == 1)
        def _():
            pair_ref[...] = (share + got_ref[...].astype(wide)).astype(low)


def attention_step(step, packs, prompt_len, core, joined, bias, seg_rows, seg_cols, w_out, got, mixed_all):
    _, rows, triple = joined.shape
    heads = bias.shape[0]
    width, model = w_out.shape
    half = rows // 2
    first, last = (0 if step < packs else 1), (1 if step > 0 else 0)
    steps = last - first + 1
    if got is None:
        got = jnp.zeros((half, model), low)

    def pack(t):
        return step - (t + first)

    def block(t, core_ref):
        return jnp.bitwise_xor(core_ref[0], 1 - (t + first))

    out_specs = [pl.BlockSpec((half, model), lambda t, c: (0, 0))] * steps + [
        pl.BlockSpec((1, heads, half, rows), lambda t, c: (t, 0, 0, 0)),
        pl.BlockSpec((1, half, width), lambda t, c: (pack(t), block(t, c), 0)),
    ]
    out_shape = [jax.ShapeDtypeStruct((half, model), low)] * steps + [
        in_hbm((steps, heads, half, rows), low),
        in_hbm((packs, rows, width), low),
    ]
    in_specs = [
        pl.BlockSpec((1, rows, triple), lambda t, c: (pack(t), 0, 0)),
        pl.BlockSpec((heads, half, rows), lambda t, c: (0, block(t, c), 0)),
        pl.BlockSpec((1, half, 1), lambda t, c: (pack(t), block(t, c), 0)),
        pl.BlockSpec((1, 1, rows), lambda t, c: (pack(t), 0, 0)),
        pl.BlockSpec((width, model), lambda t, c: (0, 0)),
        pl.BlockSpec((half, model), lambda t, c: (0, 0)),
    ]
    args = [core, joined, bias, seg_rows, seg_cols, w_out, got]
    aliases = {}
    if mixed_all is not None:
        in_specs.append(pl.BlockSpec(memory_space=pl.ANY))
        args.append(mixed_all)
        aliases = {7: steps + 1}
    outs = kernel_call(
        functools.partial(attention_step_kernel, prompt_len, heads, first, last), 5, near=(2,),
        grid_spec=pltpu.PrefetchScalarGridSpec(
            num_scalar_prefetch=1, grid=(steps,), in_specs=in_specs, out_specs=out_specs
        ),
        out_shape=out_shape,
        input_output_aliases=aliases,
        name="attention_step",
    )(*args)
    send = outs[0] if first == 0 else None
    pair = outs[steps - 1] if last == 1 else None
    return send, pair, outs[-2], outs[-1]


def feed_step_kernel(first, last, step, place_ref, rows_any, cot_any, gain_ref, *refs):
    refs = list(refs)
    turns = list(range(first, last + 1))
    sums = [refs[2 * i : 2 * i + 2] for i in range(len(turns))]
    refs = refs[2 * len(turns) :]
    if last == 1:
        got_ref, refs = refs[0], refs[1:]
    w_in_any, w_out_any, in_a, in_b, out_a, out_b = refs[:6]
    (rows_ref, cot_ref, normed_ref, active_ref, hidden_ref, result_ref, w_in_ref, w_out_ref,
     load_sems, save_sems) = refs[-10:]
    outs = refs[-10 - (3 + (1 if first == 0 else 0) + (4 if last == 1 else 0)) : -10]
    saved, rest = outs[:3], outs[3:]
    if first == 0:
        send_ref, rest = rest[0], rest[1:]
    if last == 1:
        middle_ref, grad_ref, gain_grad_ref, results_any = rest
    half = rows_ref.shape[0] // len(turns)
    half_rows = in_a.shape[0]
    core, side, part = place_ref[0], place_ref[1], place_ref[2]
    near = pl.ds(pl.multiple_of(part * half_rows, half_rows), half_rows)
    away = pl.ds(pl.multiple_of((1 - part) * half_rows, half_rows), half_rows)

    def block(turn):
        mine = jnp.bitwise_xor(core, 1 - turn)
        return step - turn, pl.ds(pl.multiple_of(mine * half, half), half)

    def span(index):
        return pl.ds(index * half, half)

    row_loads = [
        pltpu.make_async_copy(rows_any.at[*block(turn)], rows_ref.at[span(i)], load_sems.at[i])
        for i, turn in enumerate(turns)
    ]
    cot_loads = [
        pltpu.make_async_copy(cot_any.at[*block(turn)], cot_ref.at[span(i)], load_sems.at[2 + i])
        for i, turn in enumerate(turns)
    ]
    in_loads = [
        pltpu.make_async_copy(w_in_any, w_in_ref.at[side], load_sems.at[4]),
        pltpu.make_async_copy(in_a, w_in_ref.at[1 - side, near], load_sems.at[5]),
        pltpu.make_async_copy(in_b, w_in_ref.at[1 - side, away], load_sems.at[6]),
    ]
    out_loads = [
        pltpu.make_async_copy(w_out_any, w_out_ref.at[side], load_sems.at[7]),
        pltpu.make_async_copy(out_a, w_out_ref.at[1 - side, near], load_sems.at[8]),
        pltpu.make_async_copy(out_b, w_out_ref.at[1 - side, away], load_sems.at[9]),
    ]
    for copy in row_loads[::-1] + in_loads + cot_loads[::-1] + out_loads:
        copy.start()
    saves, kept = [], {}

    def save(index, place, source, target):
        copy = pltpu.make_async_copy(
            source, target.at[*block(turns[index])], save_sems.at[2 * place + index]
        )
        copy.start()
        saves.append(copy)

    def prepare(index):
        row_loads[index].wait()
        pair_ref, far_ref = sums[index]
        middle = rows_ref[span(index), :].astype(wide) + (
            pair_ref[...].astype(wide) + far_ref[...].astype(wide)
        )
        scale = lax.rsqrt(jnp.mean(middle * middle, axis=-1, keepdims=True) + epsilon)
        normed_ref[span(index), :] = (middle * scale * gain_ref[...]).astype(low)
        kept[index] = [middle, scale, None, None]
        save(index, 0, normed_ref.at[span(index)], saved[0])

    def expand(index, quarter):
        rows_at = span(index)
        inner = nn(normed_ref[rows_at, :], w_in_ref[quarter])
        share = 0.5 + 0.5 * lax.erf(inner * root_half)
        active = (inner * share).astype(low)
        slope = share + inner * (jnp.exp(-0.5 * inner * inner) * inv_root_tau)
        if quarter == 0 and index == len(turns) - 1:
            for copy in cot_loads + out_loads:
                copy.wait()
        hidden = (nt(cot_ref[rows_at, :], w_out_ref[quarter]) * slope).astype(low)
        active_ref[quarter, rows_at, :] = active
        hidden_ref[quarter, rows_at, :] = hidden
        feed_share = nn(active, w_out_ref[quarter])
        back_share = nt(hidden, w_in_ref[quarter])
        if quarter == 0:
            kept[index][2:] = [feed_share, back_share]
        else:
            kept[index][2] = kept[index][2] + feed_share
            kept[index][3] = kept[index][3] + back_share
            save(index, 1, active_ref.at[side, rows_at], saved[1])
            save(index, 2, hidden_ref.at[side, rows_at], saved[2])

    def finish_own(index):
        middle, scale, feed, back = kept[index]
        result_ref[...] = (middle + (feed + got_ref[:half, :].astype(wide))).astype(low)
        copy = pltpu.make_async_copy(result_ref, results_any.at[step - 1], save_sems.at[6])
        copy.start()
        saves.append(copy)
        upstream = back + got_ref[half:, :].astype(wide)
        scaled = upstream * gain_ref[...]
        inner = jnp.mean(scaled * middle, axis=-1, keepdims=True)
        grad = cot_ref[span(index), :].astype(wide) + scale * scaled - middle * (
            scale * scale * scale * inner
        )
        middle_ref[...] = grad
        grad_ref[...] = grad.astype(low)
        gain_grad_ref[...] = jnp.sum(upstream * middle * scale, axis=0, keepdims=True)

    def send_far(index):
        send_ref[:half, :] = kept[index][2].astype(low)
        send_ref[half:, :] = kept[index][3].astype(low)

    order = list(range(len(turns)))[::-1]
    prepare(order[0])
    for copy in in_loads:
        copy.wait()
    expand(order[0], 0)
    if len(order) == 2:
        prepare(order[1])
    expand(order[0], 1)
    if len(order) == 2:
        expand(order[1], 0)
    if last == 1:
        finish_own(order[0])
    if len(order) == 2:
        expand(order[1], 1)
    if first == 0:
        send_far(order[-1])
    for copy in saves:
        copy.wait()


def feed_step(step, packs, place, rows, cot, gain, sums, far_sums, own_pair, own_far, got,
              w_in, w_out, in_halves, out_halves, kept, results):
    _, row_count, model = rows.shape
    hidden = w_in.shape[1]
    half = row_count // 2
    first, last = (0 if step < packs else 1), (1 if step > 0 else 0)
    steps = last - first + 1
    inside = pl.BlockSpec(memory_space=pltpu.VMEM)
    anywhere = pl.BlockSpec(memory_space=pl.ANY)
    args = [place, rows, cot, gain]
    in_specs = [pl.BlockSpec(memory_space=pltpu.SMEM), anywhere, anywhere, inside]
    flats = ([sums, far_sums] if first == 0 else []) + ([own_pair, own_far, got] if last == 1 else [])
    args += flats
    in_specs += [inside] * len(flats)
    args += [w_in, w_out, *in_halves, *out_halves]
    in_specs += [anywhere] * 6
    aliases = {}
    if kept is not None:
        in_specs += [anywhere] * 3
        aliases = {len(args) + i: i for i in range(3)}
        args += list(kept)
    out_specs = [anywhere] * 3
    out_shape = [
        in_hbm((packs, row_count, model), low),
        in_hbm((packs, row_count, hidden), low),
        in_hbm((packs, row_count, hidden), low),
    ]
    if first == 0:
        out_specs.append(inside)
        out_shape.append(jax.ShapeDtypeStruct((row_count, model), low))
    if last == 1:
        if results is not None:
            in_specs.append(anywhere)
            aliases[len(args)] = len(out_shape) + 3
            args.append(results)
        out_specs += [inside] * 3 + [anywhere]
        out_shape += [
            in_hbm((half, model), wide),
            (jax.ShapeDtypeStruct if step < packs else in_hbm)((half, model), low),
            jax.ShapeDtypeStruct((1, model), wide),
            in_hbm((packs, half, model), low),
        ]
    outs = kernel_call(
        functools.partial(feed_step_kernel, first, last, step), 4 + 4 * steps, vmem=26,
        in_specs=in_specs,
        out_specs=out_specs,
        scratch_shapes=[
            pltpu.VMEM((steps * half, model), low),
            pltpu.VMEM((steps * half, model), low),
            pltpu.VMEM((steps * half, model), low),
            pltpu.VMEM((2, steps * half, hidden), low),
            pltpu.VMEM((2, steps * half, hidden), low),
            pltpu.VMEM((half, model), low),
            pltpu.VMEM((2, model, hidden), low),
            pltpu.VMEM((2, hidden, model), low),
            pltpu.SemaphoreType.DMA((10,)),
            pltpu.SemaphoreType.DMA((7,)),
        ],
        out_shape=out_shape,
        input_output_aliases=aliases,
        name="feed_step",
    )(*args)
    sent = outs[3] if first == 0 else None
    own = list(outs[-4:]) if last == 1 else [None] * 4
    return outs[:3], sent, own


def attention_back_kernel(
    heads, prompt_len, has_back, has_prev, core_ref, *refs,
):
    refs = list(refs)
    if has_back:
        own_ref, far_ref, w_out_ref, probs_own_ref, probs_far_ref, joined_ref = refs[:6]
        refs = refs[6:]
    w_joined_ref = refs.pop(0)
    if has_prev:
        prev_ref, got_ref, values_ref, grad_ref, gain_ref, gain_in_ref, head_in_ref = refs[:7]
        refs = refs[7:]
        if not has_back:
            other_gain_ref, refs = refs[0], refs[1:]
    outs = refs[-((5 if has_back else 0) + (3 if has_prev else 0)):]
    if has_prev:
        pair_ref, gain_out_ref, head_out_ref = outs[:3]
        outs = outs[3:]
        pair = (nn(prev_ref[...], w_joined_ref[...]) + got_ref[...].astype(wide)).astype(low)
        pair_ref[...] = pair
        top = head_in_ref.shape[0]
        values, upstream = values_ref[0].astype(wide), pair.astype(wide)
        grad, share = norm_back(upstream, gain_ref[...], values)
        gain_sum = gain_in_ref[...] + share
        gain_out_ref[...] = gain_sum
        grad = grad[:top] + jnp.where(core_ref[1] == 0, grad_ref[:top, :], 0.0)
        head_sum = head_in_ref[...] + jnp.where(core_ref[0] == 0, grad, 0.0)
        if has_back:
            head_out_ref[...] = head_sum
        else:
            groups, group_rows, _ = head_out_ref.shape
            rows = prompt_len // groups
            head_out_ref[...] = jnp.zeros(head_out_ref.shape, low)
            for group in range(groups):
                head_out_ref[group, :rows, :] = head_sum[group * rows : (group + 1) * rows].astype(low)
                head_out_ref[group, rows : rows + 1, :] = gain_sum.astype(low)
                head_out_ref[group, rows + 1 : rows + 2, :] = other_gain_ref[...].astype(low)
    if not has_back:
        return
    send_ref, own_grads_ref, grads_ref, scores_ref, whole_ref = outs
    rows = joined_ref.shape[1]
    half = rows // 2
    width = w_out_ref.shape[0]
    size = width // heads
    core = core_ref[0]
    starts = [pl.multiple_of(core * half, half), pl.multiple_of((1 - core) * half, half)]
    ups, asks, asked = [], [], [[], []]
    for side, ref in enumerate((own_ref, far_ref)):
        whole_ref[0, pl.ds(starts[side], half), :] = ref[...]
        ups.append(nt(ref[...], w_out_ref[...]).astype(low))
        asks.append(joined_ref[0, pl.ds(starts[side], half), :width])
    grad_keys, grad_values = [], []
    for head in range(heads):
        cols = slice(head * size, (head + 1) * size)
        keys = joined_ref[0, :, width + head * size : width + (head + 1) * size]
        values = joined_ref[0, :, 2 * width + head * size : 2 * width + (head + 1) * size]
        grad_key, grad_value = None, None
        for side, probs_ref in enumerate((probs_own_ref, probs_far_ref)):
            probs = probs_ref[0, head]
            upstream = ups[side][:, cols]
            grad_probs = nt(upstream, values)
            spread = probs.astype(wide)
            inner = jnp.sum(spread * grad_probs, axis=-1, keepdims=True)
            grad_scores = (spread * (grad_probs - inner)).astype(low)
            scores_ref[0, head, pl.ds(starts[side], half), :] = grad_scores
            value_share = tn(upstream, probs)
            key_share = tn(asks[side][:, cols], grad_scores)
            grad_value = value_share if grad_value is None else grad_value + value_share
            grad_key = key_share if grad_key is None else grad_key + key_share
            asked[side].append(nn(grad_scores, keys))
        grad_values.append(grad_value.T)
        grad_keys.append(grad_key.T)
    rest = jnp.concatenate(grad_keys + grad_values, axis=1).astype(low)
    grads_ref[0, :, width:] = rest
    for side in range(2):
        grads_ref[0, pl.ds(starts[side], half), :width] = jnp.concatenate(asked[side], axis=1).astype(low)
    own_grads_ref[...] = grads_ref[0, pl.ds(starts[0], half), :]
    send_ref[...] = nn(grads_ref[0, pl.ds(starts[1], half), :], w_joined_ref[...]).astype(low)


def attention_back_step(step, packs, heads, prompt_len, other_gain, core, own, far, w_out, probs_own, probs_far, joined, w_joined,
                        prev, got, values, grad, gain, gain_sum, head_sum, kept):
    _, rows, triple = joined.shape
    width, model = w_out.shape
    half = rows // 2
    has_back, has_prev = step < packs, step > 0
    fixed = lambda t, c: (0, 0)
    flat = pl.BlockSpec((half, model), fixed)
    anywhere = pl.BlockSpec(memory_space=pl.ANY)
    in_specs, args, out_specs, out_shape, aliases = [], [core], [], [], {}
    if has_back:
        (own_place, probs_own), (far_place, probs_far) = probs_own, probs_far
        in_specs += [
            flat,
            flat,
            pl.BlockSpec((width, model), fixed),
            pl.BlockSpec((1, heads, half, rows), lambda t, c: (own_place, 0, 0, 0)),
            pl.BlockSpec((1, heads, half, rows), lambda t, c: (far_place, 0, 0, 0)),
            pl.BlockSpec((1, rows, triple), lambda t, c: (step, 0, 0)),
        ]
        args += [own, far, w_out, probs_own, probs_far, joined]
    in_specs.append(pl.BlockSpec((triple, model), fixed))
    args.append(w_joined)
    if has_prev:
        line = pl.BlockSpec((1, model), fixed)
        head = pl.BlockSpec(head_sum.shape, fixed)
        in_specs += [
            pl.BlockSpec((half, triple), fixed),
            flat,
            pl.BlockSpec((1, half, model), lambda t, c: (step - 1, c[0], 0)),
            flat,
            line,
            line,
            head,
        ]
        args += [prev, got, values, grad, gain, gain_sum, head_sum]
        if has_back:
            head_out = in_hbm(head_sum.shape, wide)
        else:
            in_specs.append(line)
            args.append(other_gain)
            groups = Small.groups
            small = (groups, -(-(prompt_len // groups + 3) // 16) * 16, model)
            head, head_out = pl.BlockSpec(small, lambda t, c: (0, 0, 0)), jax.ShapeDtypeStruct(small, low)
        out_specs += [flat, line, head]
        out_shape += [
            jax.ShapeDtypeStruct((half, model), low),
            jax.ShapeDtypeStruct((1, model), wide),
            head_out,
        ]
    if has_back:
        if kept is not None:
            in_specs += [anywhere] * 3
            aliases = {len(args) + i: len(out_shape) + 2 + i for i in range(3)}
            args += list(kept)
        out_specs += [
            flat,
            pl.BlockSpec((half, triple), fixed),
            pl.BlockSpec((1, rows, triple), lambda t, c: (step, 0, 0)),
            pl.BlockSpec((1, heads, rows, rows), lambda t, c: (step, 0, 0, 0)),
            pl.BlockSpec((1, rows, model), lambda t, c: (step, 0, 0)),
        ]
        out_shape += [
            jax.ShapeDtypeStruct((half, model), low),
            in_hbm((half, triple), low),
            in_hbm((packs, rows, triple), low),
            in_hbm((packs, heads, rows, rows), low),
            in_hbm((packs, rows, model), low),
        ]
    outs = list(
        kernel_call(
            functools.partial(attention_back_kernel, heads, prompt_len, has_back, has_prev), 6,
            least=1000 if step == packs - 1 else 400000,
            grid_spec=pltpu.PrefetchScalarGridSpec(
                num_scalar_prefetch=1, grid=(1,), in_specs=in_specs, out_specs=out_specs
            ),
            out_shape=out_shape,
            input_output_aliases=aliases,
                name="attention_back_step",
        )(*args)
    )
    done, outs = (outs[:3], outs[3:]) if has_prev else ((None,) * 3, outs)
    send, own_grads, *kept = outs if has_back else (None, None)
    return done, send, own_grads, kept


def finish_kernel(packs, core_ref, rows_any, gain_ref, *refs):
    out_ref, rows_ref, sems = refs[-3:]
    half = rows_ref.shape[1]
    start = pl.multiple_of(core_ref[0] * half, half)
    copies = [
        pltpu.make_async_copy(rows_any.at[pack, pl.ds(start, half)], rows_ref.at[i], sems.at[i])
        for i, pack in enumerate(packs)
    ]
    for copy in copies:
        copy.start()
    for i, copy in enumerate(copies):
        copy.wait()
        pair_ref, far_ref, grad_ref = refs[3 * i : 3 * i + 3]
        upstream = pair_ref[...].astype(wide) + far_ref[...].astype(wide)
        grad, _ = norm_back(upstream, gain_ref[...], rows_ref[i].astype(wide))
        out_ref[i] = (grad_ref[...] + grad).astype(low)


def finish(packs, core, rows, gain, parts):
    half, model = parts[0][0].shape
    inside = pl.BlockSpec(memory_space=pltpu.VMEM)
    return kernel_call(
        functools.partial(finish_kernel, packs), 1.5 * len(packs), vmem=24,
        in_specs=[pl.BlockSpec(memory_space=pltpu.SMEM), pl.BlockSpec(memory_space=pl.ANY), inside]
        + [inside] * (3 * len(packs)),
        out_specs=inside,
        out_shape=jax.ShapeDtypeStruct((len(packs), half, model), low),
        scratch_shapes=[
            pltpu.VMEM((len(packs), half, model), low),
            pltpu.SemaphoreType.DMA((len(packs),)),
        ],
        name="finish",
    )(core, rows, gain, *[v for part in parts for v in part])


def place_kernel(core_ref, own_ref, far_ref, out_ref, sems):
    packs, half, _ = own_ref.shape
    copies = []
    for pack in range(packs):
        for side, ref in enumerate((own_ref, far_ref)):
            start = pl.multiple_of(jnp.bitwise_xor(core_ref[0], side) * half, half)
            copies.append(
                pltpu.make_async_copy(
                    ref.at[pack], out_ref.at[pack, pl.ds(start, half)], sems.at[2 * pack + side]
                )
            )
    for copy in copies:
        copy.start()
    for copy in copies:
        copy.wait()


def place_halves(core, own, far):
    packs, half, model = own.shape
    inside = pl.BlockSpec(memory_space=pltpu.VMEM)
    return kernel_call(
        place_kernel, 2.5, vmem=24, least=1000,
        in_specs=[pl.BlockSpec(memory_space=pltpu.SMEM), inside, inside],
        out_specs=pl.BlockSpec(memory_space=pl.ANY),
        out_shape=in_hbm((packs, 2 * half, model), low),
        scratch_shapes=[pltpu.SemaphoreType.DMA((2 * packs,))],
        name="place_halves",
    )(core, own, far)


def weave_kernel(core_ref, *refs):
    out_ref, rows_ref, woven_ref = refs[-3:]
    half = rows_ref.shape[0] // 2
    text = out_ref.shape[0]
    pack = 0
    for own_ref, far_ref in zip(refs[:-3:2], refs[1:-3:2]):
        for i in range(own_ref.shape[0]):
            for side, ref in enumerate((own_ref, far_ref)):
                start = pl.multiple_of(jnp.bitwise_xor(core_ref[0], side) * half, half)
                rows_ref[pl.ds(start, half), :] = ref[i].astype(wide)
            woven_ref[:, pack, :] = rows_ref[2 * half - text :, :]
            pack += 1
    out_ref[...] = woven_ref[...].astype(low)


def weave_halves(core, pairs, text):
    packs = sum(own.shape[0] for own, _ in pairs)
    _, half, model = pairs[0][0].shape
    inside = pl.BlockSpec(memory_space=pltpu.VMEM)
    return kernel_call(
        weave_kernel, 4, vmem=32, least=1000,
        in_specs=[pl.BlockSpec(memory_space=pltpu.SMEM)] + [inside] * (2 * len(pairs)),
        out_specs=inside,
        out_shape=jax.ShapeDtypeStruct((text, packs, model), low),
        scratch_shapes=[pltpu.VMEM((2 * half, model), wide), pltpu.VMEM((text, packs, model), wide)],
        name="weave_halves",
    )(core, *[v for pair in pairs for v in pair])


def weight_kernel(pairs, split, where_ref, *refs):
    if split:
        keep_ref, send_ref, total_ref = refs[-3:]
    else:
        whole_ref, total_ref = refs[-2:]
    column = 0
    for i in range(pairs):
        right = refs[2 * i + 1][...]
        total_ref[:, column : column + right.shape[1]] = tn(refs[2 * i][...], right)
        column += right.shape[1]
    if not split:
        whole_ref[...] = total_ref[...].astype(low)
        return
    count, block, _ = keep_ref.shape
    side = jnp.bitwise_and(where_ref[0], 1)
    for i in range(count):
        for ref, chosen in ((keep_ref, side), (send_ref, 1 - side)):
            start = pl.multiple_of((2 * i + chosen) * block, 8)
            ref[i] = total_ref[pl.ds(start, block), :].astype(low)


def weight_shares(where, count, pairs, split):
    rows, model = pairs[0][0].shape
    widths = [right.shape[1] for _, right in pairs]
    turns, width = 2, sum(widths)
    block = model // count
    in_specs = []
    for n in widths:
        in_specs += [
            pl.BlockSpec((rows, model // turns), lambda t, w: (0, t)),
            pl.BlockSpec((rows, n), lambda t, w: (0, 0)),
        ]
    if split:
        out_specs = [pl.BlockSpec((count // 2 // turns, block, width), lambda t, w: (t, 0, 0))] * 2
        out_shape = [jax.ShapeDtypeStruct((count // 2, block, width), low)] * 2
    else:
        out_specs = pl.BlockSpec((model // turns, width), lambda t, w: (t, 0))
        out_shape = in_hbm((model, width), low)
    return kernel_call(
        functools.partial(weight_kernel, len(pairs), split), 6, vmem=26,
        grid_spec=pltpu.PrefetchScalarGridSpec(
            num_scalar_prefetch=1,
            grid=(turns,),
            in_specs=in_specs,
            out_specs=out_specs,
            scratch_shapes=[pltpu.VMEM((model // turns, width), wide)],
        ),
        out_shape=out_shape,
        name="weight_shares",
    )(where, *[value for pair in pairs for value in pair])


def fold_kernel(count, where_ref, *refs):
    ins, outs = refs[:count], refs[count:]
    group = outs[0].shape[0]
    for flip, out_ref in enumerate(outs):
        for piece in range(group):
            spot = jnp.bitwise_xor(where_ref[0], flip)
            spot = spot * group + piece if len(outs) == 4 else piece * 2 + spot
            total = ins[0][spot].astype(wide)
            for ref in ins[1:]:
                total = total + ref[spot].astype(wide)
            out_ref[piece] = total.astype(out_ref.dtype)


def fold(where, parts, cuts):
    whole, block, width = parts[0].shape
    shape = (whole // cuts, block, width)
    inside = pl.BlockSpec(memory_space=pltpu.VMEM)
    return kernel_call(
        functools.partial(fold_kernel, len(parts)), 1.5, vmem=24,
        in_specs=[pl.BlockSpec(memory_space=pltpu.SMEM)] + [inside] * len(parts),
        out_specs=[inside] * cuts,
        out_shape=[jax.ShapeDtypeStruct(shape, low)] * cuts,
        name="fold",
    )(where, *parts)


def unfold_kernel(count, cuts, *refs):
    ins, outs = refs[:count], refs[count:]
    total = ins[0][0].astype(wide)
    for ref in ins[1:]:
        total = total + ref[0].astype(wide)
    for (start, width, turned), out_ref in zip(cuts, outs):
        piece = total[:, start : start + width]
        out_ref[...] = piece.T if turned else piece


def unfold(parts, cuts):
    block = parts[0].shape[1]
    inside = pl.BlockSpec(memory_space=pltpu.VMEM)
    return kernel_call(
        functools.partial(unfold_kernel, len(parts), cuts), 1.5,
        in_specs=[inside] * len(parts),
        out_specs=[inside] * len(cuts),
        out_shape=[
            jax.ShapeDtypeStruct((width, block) if turned else (block, width), wide)
            for _, width, turned in cuts
        ],
        name="unfold",
    )(*parts)


def small_fold_kernel(has_rel, side_ref, mine_ref, got_ref, *refs):
    keep_ref, send_ref, total_ref = refs[-3:]
    groups, rows, _ = mine_ref.shape
    half = groups // 2
    total_ref[...] = mine_ref[...].astype(wide) + got_ref[...].astype(wide)
    if has_rel:
        rel_ref, spot = refs[0], refs[1]
        for group in range(groups):
            total_ref[group, spot[0], :] = rel_ref[0, :]
    keep_ref[...] = total_ref[pl.ds(side_ref[0] * half, half)].astype(low)
    send_ref[...] = total_ref[pl.ds((1 - side_ref[0]) * half, half)].astype(low)


def small_fold(side, mine, got, rel=None, spot=None):
    groups, rows, model = mine.shape
    inside, scalar = pl.BlockSpec(memory_space=pltpu.VMEM), pl.BlockSpec(memory_space=pltpu.SMEM)
    more = [] if rel is None else [rel, jnp.full((1,), spot, jnp.int32)]
    return kernel_call(
        functools.partial(small_fold_kernel, rel is not None), 1,
        in_specs=[scalar, inside, inside] + ([inside, scalar] if more else []),
        out_specs=[inside] * 2,
        out_shape=[jax.ShapeDtypeStruct((groups // 2, rows, model), low)] * 2,
        scratch_shapes=[pltpu.VMEM((groups, rows, model), wide)],
        name="small_fold",
    )(side, mine, got, *more)


def tie(*values):
    return lax.optimization_barrier(values)


def stages_of(count):
    bits = bits_of(count)
    rest = bits[1:][::-1]
    return [bits[:1]] + [rest[i : i + 2] for i in range(0, len(rest), 2)]


class Scatter:
    def __init__(self, keep, send, cuts):
        self.bits, self.cuts = bits_of(lax.axis_size("dp"))[1:], cuts
        self.parts = [keep, swap(send, "dp", 1)]

    def step(self):
        if self.cuts == 4:
            bit, self.bits = self.bits[-2], self.bits[:-2]
        else:
            bit, self.bits = self.bits[0], self.bits[1:]
        where = ((lax.axis_index("dp") // bit) % self.cuts).astype(jnp.int32).reshape(1)
        own, *sends = fold(where, self.parts, self.cuts)
        self.parts = [own] + [swap(v, "dp", bit * (flip + 1)) for flip, v in enumerate(sends)]

    def end(self, pieces):
        while self.bits:
            self.step()
        return unfold(self.parts, pieces)


def look_up(prompt_ids, table, prompt_delta):
    prompt_len = prompt_ids.shape[0]
    table_rows, model = table.shape
    groups = lax.axis_size("mp")
    part = -(-prompt_len // (16 * groups)) * 16
    dp_index, mp_index = lax.axis_index("dp"), lax.axis_index("mp")
    padded = jnp.pad(prompt_ids, (0, part * groups - prompt_len), constant_values=-1)
    ids = lax.dynamic_slice_in_dim(padded, mp_index * part, part)
    size, block = prompt_delta.shape[0], part * model
    line = jnp.pad(prompt_delta, (block, block))
    start = jnp.clip(block + mp_index * block - dp_index * size, 0, block + size)
    placed = lax.dynamic_slice_in_dim(line, start, block).reshape(part, model)
    local = jnp.where(ids < 0, -1, ids - dp_index * table_rows)
    if table_rows % 16 == 0:
        return look_up_rows(local, table, placed)
    selector = (local[:, None] == jnp.arange(table_rows, dtype=jnp.int32)[None, :]).astype(low)
    return jnp.dot(selector, table, preferred_element_type=wide) + placed


def own_half(weight):
    part = lax.axis_index("dp") % 2
    halves = weight.reshape(2, weight.shape[0] // 2, weight.shape[1])
    return lax.dynamic_index_in_dim(halves, part, 0, keepdims=False)


class Small:
    groups = 4

    def __init__(self, total, prompt_len):
        self.total, self.share = total, prompt_len // self.groups
        self.mp_bits = bits_of(lax.axis_size("mp"))
        self.dp_bits = bits_of(lax.axis_size("dp"))[::-1]
        self.hops = 0
        self.hop_mp()

    def hop_mp(self):
        bit, self.mp_bits = self.mp_bits[0], self.mp_bits[1:]
        self.keep, self.got = self.total, swap(self.total, "mp", bit)

    def land(self):
        self.total = (self.keep.astype(wide) + self.got.astype(wide)).astype(low)

    def hop_dp(self, rel=None):
        bit, self.dp_bits = self.dp_bits[0], self.dp_bits[1:]
        if self.hops < 2:
            side = ((lax.axis_index("dp") // bit) % 2).astype(jnp.int32).reshape(1)
            if rel is not None:
                self.rel = rel
                rel = jnp.pad(rel.reshape(1, -1), ((0, 0), (0, self.keep.shape[2] - rel.size)))
            self.keep, send = small_fold(side, self.keep, self.got, rel, self.share + 2)
        else:
            self.land()
            self.keep = send = self.total
        self.hops += 1
        self.got = swap(send, "dp", bit)

    def results(self):
        while self.dp_bits:
            self.hop_dp()
        total = self.keep[0].astype(wide) + self.got[0].astype(wide)
        dp_count, dp_index = lax.axis_size("dp"), lax.axis_index("dp")
        share, model = self.share, total.shape[1]
        inside = dp_count // self.groups
        size = share * model // inside
        prompt_grad = lax.dynamic_slice_in_dim(total[:share].reshape(-1), (dp_index % inside) * size, size)
        width = model // dp_count
        gains = lax.dynamic_slice_in_dim(total[share : share + 2], dp_index * width, width, axis=1)
        piece = self.rel.size // dp_count
        rel_out = lax.dynamic_slice_in_dim(total[share + 2], dp_index * piece, piece)
        return prompt_grad, gains[0], gains[1], rel_out.reshape(-1, self.rel.shape[1])


def body(
    tokens, cotangent, segment_ids, prompt_ids, rel_buckets, table, prompt_delta, norm1_gain,
    w_query, w_key, w_value, w_output, rel_bias, norm2_gain, w_inner, w_outer,
):
    prompt_len = prompt_ids.shape[0]
    packs, rows, model = cotangent.shape
    bucket_count, heads = rel_bias.shape
    width = w_query.shape[1]
    groups = lax.axis_size("dp")
    mp_bits = bits_of(lax.axis_size("mp"))
    mp_index = lax.axis_index("mp").astype(jnp.int32)
    place = jnp.stack([mp_index % 2, (mp_index // 2) % 2, (lax.axis_index("dp") % 2).astype(jnp.int32)])
    gain1, gain2 = norm1_gain[None, :], norm2_gain[None, :]
    w_q, w_k, w_v = w_query.T, w_key.T, w_value.T

    in_near = swap(own_half(w_inner), "mp", 2)
    total = look_up(prompt_ids, table, prompt_delta)
    out_near = swap(own_half(w_outer), "mp", 2)

    w_joined = jnp.concatenate([w_q, w_k, w_v], axis=0)
    bucket_hot = (
        rel_buckets[:, None] == jnp.arange(bucket_count, dtype=jnp.int32)[None, :]
    ).astype(wide)
    bucket_hot = jnp.pad(bucket_hot, ((0, 1), (0, 0)))
    turned = jnp.roll(bucket_hot, -(rows - 1), axis=0)
    bias_line = jnp.dot(turned, rel_bias, precision=highest).T
    marks = jnp.pad(segment_ids, ((0, 0), (prompt_len, 0)), constant_values=-1)
    seg_rows, seg_cols = marks[:, :, None], marks[:, None, :]

    texts, half_packs = [], packs // 2
    for hop, bit in enumerate(bits_of(groups)):
        got = swap(total, "dp", bit)
        if hop == 0:
            bias = bias_grid_of(bias_line[:, None, :])
            got, bias, seg_rows, seg_cols = tie(got, bias, seg_rows, seg_cols)
        if hop == 1:
            texts = text_projections(0, half_packs, rows, tokens, gain1, w_joined, texts)
            got, *texts = tie(got, *texts)
        if hop == 2:
            texts = text_projections(half_packs, packs - half_packs, rows, tokens, gain1, w_joined, texts)
            got, *texts = tie(got, *texts)
            got, in_near, out_near = tie(got, in_near, out_near)
            in_away = swap(in_near, "dp", 1)
        total = total + got
    whole_rows, normed1, joined = texts
    pieces = total.astype(low)[None]
    for bit in mp_bits:
        pieces = jnp.concatenate([pieces, swap(pieces, "mp", bit)], axis=0)
    whole_rows, normed1, joined = add_prompt(
        mp_index.reshape(1), pieces, gain1, w_joined, whole_rows, normed1, joined
    )

    pairs, fars, pairs_far, fars_far, probs_far, probs_own, mixed, got = [], [], [], [], [], [], None, None

    def attend(step):
        nonlocal mixed, got, place, in_away, out_near, out_away
        send, pair, probs, mixed = attention_step(
            step, packs, prompt_len, place, joined, bias, seg_rows, seg_cols, w_output, got, mixed
        )
        if step == 0:
            place, in_away, out_near, send = tie(place, in_away, out_near, send)
            out_away = swap(out_near, "dp", 1)
        else:
            place, pair = tie(place, pair)
        if send is not None:
            probs_far.append((0, probs))
            got = swap(send, "mp", 1)
        if pair is not None:
            probs_own.append((probs.shape[0] - 1, probs))
            pairs.append(pair)
            fars.append(swap(pair, "mp", 2))
            pairs_far.append(swap(pair, "mp", 1))
            fars_far.append(swap(fars[-1], "mp", 1))

    out_away = None

    def arrive(pack):
        nonlocal place
        place, fars[pack], pairs_far[pack], fars_far[pack] = tie(
            place, fars[pack], pairs_far[pack], fars_far[pack]
        )

    kept, sent, results, grads_wide, grads_low = None, None, None, [], []
    gain2_sum, none = 0.0, [None]
    back_kept, prev, got = None, None, None
    gain1_sum, head_sum = jnp.zeros((1, model), wide), jnp.zeros((128, model), wide)
    text_rows, pairs_back = [], []

    def feed(step):
        nonlocal kept, sent, results, gain2_sum, place
        kept, new_sent, done = feed_step(
            step, packs, place, whole_rows, cotangent, gain2,
            (pairs_far + none)[step], (fars_far + none)[step],
            (none + pairs)[step], (none + fars)[step], sent,
            w_inner, w_outer, (in_near, in_away), (out_near, out_away), kept, results,
        )
        if step < packs:
            place, new_sent = tie(place, new_sent)
            sent = swap(new_sent, "mp", 1)
        else:
            place, done[1] = tie(place, done[1])
        if step > 0:
            grads_wide.append(done[0])
            grads_low.append((done[1], swap(done[1], "mp", 1)))
            gain2_sum, results = gain2_sum + done[2], done[3]

    def back(step):
        nonlocal back_kept, prev, got, gain1_sum, head_sum, place
        live = step < packs
        done, send, own_grads, back_new = attention_back_step(
            step, packs, heads, prompt_len, gain2_sum, place, *(grads_low[step] if live else none * 2), w_output,
            probs_own[step] if live else None, probs_far[step] if live else None, joined, w_joined,
            prev, got, whole_rows, grads_wide[step - 1] if step else None, gain1, gain1_sum, head_sum,
            back_kept,
        )
        if live:
            place, send = tie(place, send)
            back_kept, prev, got = back_new, own_grads, swap(send, "mp", 1)
        if step > 0:
            pair, gain1_sum, head_sum = done
            pairs_back.append([pair, swap(pair, "mp", 2)])

    def end(*ended):
        nonlocal place
        rows_low = finish(ended, place, whole_rows, gain1, [(*pairs_back[p], grads_wide[p]) for p in ended])
        place, rows_low = tie(place, rows_low)
        text_rows.append((rows_low, swap(rows_low, "mp", 1)))

    def flat(value):
        return value.reshape(packs * rows, -1)

    for step in range(packs):
        attend(step)
    place, out_away = tie(place, out_away)
    arrive(0)
    feed(0)
    attend(packs)
    arrive(1)
    feed(1)
    for step in range(2, packs):
        arrive(step)
        feed(step)
        back(step - 2)
    feed(packs)
    normed2, active, hidden = kept
    where = lax.axis_index("dp").astype(jnp.int32).reshape(1)
    where, place = tie(where, place)
    feed_shares = weight_shares(
        where, groups, [(flat(normed2), flat(hidden)), (flat(cotangent), flat(active))], True
    )
    place, *feed_shares = tie(place, *feed_shares)
    feed_sum = Scatter(*feed_shares, 2)
    back(packs - 2)
    far_results = swap(results, "mp", 1)
    place, far_results, *pairs_back[0] = tie(place, far_results, *pairs_back[0])
    back(packs - 1)
    place, *pairs_back[1] = tie(place, *pairs_back[1])
    place, *feed_sum.parts = tie(place, *feed_sum.parts)
    feed_sum.step()
    grad_joined, scores, grad_rows = back_kept
    where, place = tie(where, place)
    tail_shares = weight_shares(
        where, groups, [(flat(normed1), flat(grad_joined)), (flat(grad_rows), flat(mixed))], True
    )
    place, *tail_shares = tie(place, *tail_shares)
    place, *feed_sum.parts = tie(place, *feed_sum.parts)
    feed_sum.step()
    tail = Scatter(*tail_shares, 4)
    side_one = (mp_index // 2) % 2 == 1
    gain2_sum = jnp.where(side_one, 0.0, gain2_sum)
    back(packs)
    place, head_sum = tie(place, head_sum)
    small = Small(head_sum, prompt_len)
    place, scores = tie(place, scores)
    line = diagonal_sums(scores)[:, 0, :]
    rel_share = jnp.einsum("ht,tb->bh", line, turned, precision=highest)
    small.land()
    small.hop_mp()
    place, rel_share = tie(place, rel_share)
    end(*range(packs - 1))
    out = place_halves(place, results, far_results)
    place, out, *tail.parts = tie(place, out, *tail.parts)
    tail.step()
    place, tail.parts[0], *feed_sum.parts = tie(place, tail.parts[0], *feed_sum.parts)
    hidden_width = w_inner.shape[1]
    inner_grad, outer_grad = feed_sum.end(((0, hidden_width, False), (hidden_width, hidden_width, False)))
    place, small.got, inner_grad = tie(place, small.got, inner_grad)
    small.hop_dp(rel_share)
    end(packs - 1)
    place, small.got = tie(place, small.got)
    small.hop_dp()
    text_rows[-1] = tie(*text_rows[-1])
    place, *tail.parts = tie(place, *tail.parts)
    grad_tokens = weave_halves(place, text_rows, rows - prompt_len)
    grad_tokens = jnp.transpose(grad_tokens, (1, 0, 2))
    query_grad, key_grad, value_grad, output_grad = tail.end(
        tuple((i * width, width, i == 3) for i in range(4))
    )
    prompt_grad, gain1_grad, gain2_grad, rel_grad = small.results()
    return (
        out, grad_tokens, prompt_grad, gain1_grad, query_grad, key_grad, value_grad, output_grad,
        rel_grad, gain2_grad, inner_grad, outer_grad.T,
    )


def solution(mesh):
    in_specs = (
        P("dp", None, None),
        P("dp", None, None),
        P("dp", None),
        P(),
        P(),
        P("dp", None),
        P("dp"),
        P(),
        P(None, "mp"),
        P(None, "mp"),
        P(None, "mp"),
        P("mp", None),
        P(None, "mp"),
        P(),
        P(None, "mp"),
        P("mp", None),
    )
    out_specs = (
        P("dp", None, None),
        P("dp", None, None),
        P("dp"),
        P("dp"),
        P("dp", "mp"),
        P("dp", "mp"),
        P("dp", "mp"),
        P("mp", "dp"),
        P("dp", "mp"),
        P("dp"),
        P("dp", "mp"),
        P("mp", "dp"),
    )
    return jax.shard_map(body, mesh=mesh, in_specs=in_specs, out_specs=out_specs, check_vma=False)
```

```python
import functools

import jax
import jax.numpy as jnp
from jax import lax
from jax.experimental import pallas as pl
from jax.experimental.pallas import tpu as pltpu
from jax.sharding import PartitionSpec as P

epsilon = 1e-06
blocked = -1000000000.0
highest = lax.Precision.HIGHEST
low = jnp.bfloat16
wide = jnp.float32
root_half = 0.7071067811865476
inv_root_tau = 0.3989422804014327


def nn(left, right):
    return lax.dot_general(left, right, (((1,), (0,)), ((), ())), preferred_element_type=wide)


def nt(left, right):
    return lax.dot_general(left, right, (((1,), (1,)), ((), ())), preferred_element_type=wide)


def tn(left, right):
    return lax.dot_general(left, right, (((0,), (0,)), ((), ())), preferred_element_type=wide)


def params(mebibytes):
    return pltpu.CompilerParams(vmem_limit_bytes=mebibytes * 1024 * 1024)


def in_hbm(shape, dtype):
    return pltpu.HBM(shape, dtype)


def kernel_call(kernel, micros, vmem=16, near=(), least=400000, **rest):
    cost = pl.CostEstimate(flops=0, bytes_accessed=int(micros * 3.6e6), transcendentals=0)
    call = pl.pallas_call(kernel, cost_estimate=cost, compiler_params=params(vmem), **rest)

    def run(*args):
        return call(
            *[
                pltpu.with_memory_space_constraint(v, pltpu.HBM) if (v.size >= least or v.ndim == 4) and i not in near else v
                for i, v in enumerate(args)
            ]
        )

    return run


def swap(value, axis, bit):
    count = lax.axis_size(axis)
    return lax.ppermute(value, axis, [(i, i ^ bit) for i in range(count)])


def bits_of(count):
    return [1 << i for i in range(count.bit_length() - 1)]


def rms_norm(values, gain):
    return values * lax.rsqrt(jnp.mean(values * values, axis=-1, keepdims=True) + epsilon) * gain


def norm_back(upstream, gain, values):
    scale = lax.rsqrt(jnp.mean(values * values, axis=-1, keepdims=True) + epsilon)
    scaled = upstream * gain
    inner = jnp.mean(scaled * values, axis=-1, keepdims=True)
    grad = scale * scaled - values * (scale * scale * scale * inner)
    return grad, jnp.sum(upstream * values * scale, axis=0, keepdims=True)


def bias_kernel(line_ref, grid_ref):
    rows = grid_ref.shape[1]
    spread = jnp.broadcast_to(line_ref[0], (rows, 2 * rows))
    grid_ref[0] = pltpu.roll(spread, 0, 1, stride=1, stride_axis=0)[:, :rows]


def bias_grid_of(line):
    heads, _, double = line.shape
    rows = double // 2
    return kernel_call(
        bias_kernel, 2,
        grid=(heads,),
        in_specs=[pl.BlockSpec((1, 1, double), lambda h: (h, 0, 0))],
        out_specs=pl.BlockSpec((1, rows, rows), lambda h: (h, 0, 0)),
        out_shape=jax.ShapeDtypeStruct((heads, rows, rows), wide),
        name="bias_grid",
    )(line)


def diag_kernel(grid_ref, line_ref):
    packs, _, rows, _ = grid_ref.shape
    lanes = 128
    count = rows // lanes
    blocks = []
    for block in range(2 * count):
        total = jnp.zeros((lanes, lanes), wide)
        for band in range(count):
            column = (block + band) % (2 * count)
            if column < count:
                for pack in range(packs):
                    total = total + grid_ref[
                        pack, 0, band * lanes : (band + 1) * lanes, column * lanes : (column + 1) * lanes
                    ].astype(wide)
        blocks.append(total)
    held = jnp.concatenate(blocks, axis=1)
    total = held[:8]
    for slab in range(1, lanes // 8):
        total = total + pltpu.roll(held[8 * slab : 8 * slab + 8], 2 * rows - 8 * slab, 1)
    line = total[0:1]
    for row in range(1, 8):
        line = line + pltpu.roll(total[row : row + 1], 2 * rows - row, 1)
    line_ref[0] = line


def diagonal_sums(grid):
    packs, heads, rows, _ = grid.shape
    return kernel_call(
        diag_kernel, 3,
        grid=(heads,),
        in_specs=[pl.BlockSpec((packs, 1, rows, rows), lambda h: (0, h, 0, 0))],
        out_specs=pl.BlockSpec((1, 1, 2 * rows), lambda h: (h, 0, 0)),
        out_shape=in_hbm((heads, 1, 2 * rows), wide),
        name="diagonal_sums",
    )(grid)


def shifted_text_kernel(tokens_ref, gain_ref, weight_ref, *refs):
    rows_ref, normed_ref, joined_ref, wide_ref = refs[-4:]
    rows = rows_ref.shape[1]
    prompt_len = rows - tokens_ref.shape[1]
    wide_ref[:prompt_len, :] = jnp.zeros((prompt_len, wide_ref.shape[1]), wide)
    wide_ref[prompt_len:, :] = tokens_ref[0].astype(wide)
    values = wide_ref[...]
    rows_ref[0] = values.astype(low)
    normed = rms_norm(values, gain_ref[...]).astype(low)
    normed_ref[0] = normed
    joined_ref[0] = nt(normed, weight_ref[...]).astype(low)


def text_projections(first, count, rows, tokens, gain, weight, kept):
    packs, text, model = tokens.shape
    triple = weight.shape[0]
    fixed = lambda p: (0, 0)
    moving = lambda p: (first + p, 0, 0)
    return kernel_call(
        shifted_text_kernel, 1.2 * count,
        grid=(count,),
        in_specs=[
            pl.BlockSpec((1, text, model), moving),
            pl.BlockSpec((1, model), fixed),
            pl.BlockSpec((triple, model), fixed),
        ]
        + [pl.BlockSpec(memory_space=pl.ANY)] * len(kept),
        out_specs=[
            pl.BlockSpec((1, rows, model), moving),
            pl.BlockSpec((1, rows, model), moving),
            pl.BlockSpec((1, rows, triple), moving),
        ],
        out_shape=[
            in_hbm((packs, rows, model), low),
            in_hbm((packs, rows, model), low),
            in_hbm((packs, rows, triple), low),
        ],
        scratch_shapes=[pltpu.VMEM((rows, model), wide)],
        input_output_aliases={3 + i: i for i in range(len(kept))},
        name="text_projections",
    )(tokens, gain, weight, *kept)


def prompt_kernel(place_ref, pieces_ref, gain_ref, weight_ref, rows_in, normed_in, joined_in, rows_out, normed_out, joined_out,
                  prompt_ref, rows_ref, normed_ref, joined_ref, load_sems, save_sems):
    count, part, _ = pieces_ref.shape
    packs = rows_ref.shape[0]
    top = count * part
    held = (rows_ref, normed_ref, joined_ref)
    loads = [
        pltpu.make_async_copy(source.at[:, pl.ds(0, top)], target, load_sems.at[i])
        for i, (source, target) in enumerate(zip((rows_in, normed_in, joined_in), held))
    ]
    for copy in loads:
        copy.start()
    for k in range(count):
        start = pl.multiple_of(jnp.bitwise_xor(place_ref[0], k) * part, part)
        prompt_ref[pl.ds(start, part), :] = pieces_ref[k]
    prompt = prompt_ref[...]
    normed = rms_norm(prompt.astype(wide), gain_ref[...]).astype(low)
    joined = nt(normed, weight_ref[...]).astype(low)
    saves = []
    for i, (value, target) in enumerate(zip((prompt, normed, joined), (rows_out, normed_out, joined_out))):
        loads[i].wait()
        for pack in range(packs):
            held[i][pack] = held[i][pack] + value
        copy = pltpu.make_async_copy(held[i], target.at[:, pl.ds(0, top)], save_sems.at[i])
        copy.start()
        saves.append(copy)
    for copy in saves:
        copy.wait()


def add_prompt(place, pieces, gain, weight, rows, normed, joined):
    packs, _, model = rows.shape
    triple = weight.shape[0]
    count, part, _ = pieces.shape
    top = count * part
    inside = pl.BlockSpec(memory_space=pltpu.VMEM)
    anywhere = pl.BlockSpec(memory_space=pl.ANY)
    return kernel_call(
        prompt_kernel, 2.5,
        in_specs=[pl.BlockSpec(memory_space=pltpu.SMEM)] + [inside] * 3 + [anywhere] * 3,
        out_specs=[anywhere] * 3,
        out_shape=[
            in_hbm(rows.shape, low),
            in_hbm(normed.shape, low),
            in_hbm(joined.shape, low),
        ],
        scratch_shapes=[
            pltpu.VMEM((top, model), low),
            pltpu.VMEM((packs, top, model), low),
            pltpu.VMEM((packs, top, model), low),
            pltpu.VMEM((packs, top, triple), low),
            pltpu.SemaphoreType.DMA((3,)),
            pltpu.SemaphoreType.DMA((3,)),
        ],
        input_output_aliases={4: 0, 5: 1, 6: 2},
        name="add_prompt",
    )(place, pieces, gain, weight, rows, normed, joined)


def look_up_kernel(ids_ref, table_any, placed_ref, out_ref, blocks_ref, total_ref, sems):
    part = out_ref.shape[0]
    limit = table_any.shape[0]
    copies, inside = [], []
    for row in range(part):
        local = jnp.clip(ids_ref[row], 0, limit - 1)
        inside.append(local)
        start = pl.multiple_of(jnp.left_shift(jnp.right_shift(local, 4), 4), 16)
        copies.append(
            pltpu.make_async_copy(table_any.at[pl.ds(start, 16)], blocks_ref.at[row], sems.at[row])
        )
    for copy in copies:
        copy.start()
    for copy in copies:
        copy.wait()
    position = lax.broadcasted_iota(jnp.int32, blocks_ref.shape[1:], 0)
    for row in range(part):
        own = inside[row] == ids_ref[row]
        chosen = (position == jnp.bitwise_and(inside[row], 15)) & own
        found = jnp.sum(jnp.where(chosen, blocks_ref[row].astype(wide), 0.0), axis=0, keepdims=True)
        total_ref[row : row + 1, :] = placed_ref[row : row + 1, :] + found
    out_ref[...] = total_ref[...].astype(low)


def look_up_rows(ids, table, placed):
    part, model = placed.shape
    inside = pl.BlockSpec(memory_space=pltpu.VMEM)
    return kernel_call(
        look_up_kernel, 2.5,
        in_specs=[pl.BlockSpec(memory_space=pltpu.SMEM), pl.BlockSpec(memory_space=pl.ANY), inside],
        out_specs=inside,
        out_shape=jax.ShapeDtypeStruct((part, model), low),
        scratch_shapes=[
            pltpu.VMEM((part, 16, model), low),
            pltpu.VMEM((part, model), wide),
            pltpu.SemaphoreType.DMA((part,)),
        ],
        name="look_up",
    )(ids, table, placed)


def attention_step_kernel(
    prompt_len, heads, first, last, step, core_ref, joined_any, bias_ref, seg_rows_ref, seg_cols_ref, w_out_ref, *refs,
):
    turns = list(range(first, last + 1))
    refs = list(refs)
    if last == 1:
        got_ref, refs = refs[0], refs[1:]
    joined_ref, probs_ref, mixed_ref, load_sems, save_sems = refs[-5:]
    outs = refs[-5 - 2 * len(turns) - 1 : -5]
    flat_refs, probs_outs, mixed_any = outs[: len(turns)], outs[len(turns) : -1], outs[-1]
    rows = joined_ref.shape[1]
    half = rows // 2
    width = w_out_ref.shape[0]
    size = width // heads
    loads = [
        pltpu.make_async_copy(joined_any.at[step - turn], joined_ref.at[i], load_sems.at[i])
        for i, turn in enumerate(turns)
    ]
    for copy in loads:
        copy.start()
    saves = []
    col_pos = lax.broadcasted_iota(jnp.int32, (half, rows), 1)
    for i, turn in enumerate(turns):
        pack = step - turn
        mine = jnp.bitwise_xor(core_ref[0], 1 - turn)
        start = pl.multiple_of(mine * half, half)
        here = pl.ds(start, half)
        row_pos = start + lax.broadcasted_iota(jnp.int32, (half, rows), 0)
        allowed = (
            (row_pos < prompt_len)
            | (col_pos < prompt_len)
            | (seg_rows_ref[here, pack : pack + 1] == seg_cols_ref[pack : pack + 1, :])
        )
        loads[i].wait()
        queries = joined_ref[i, here, :width]
        mixed = []
        for head in range(heads):
            keys = joined_ref[i, :, width + head * size : width + (head + 1) * size]
            values = joined_ref[i, :, 2 * width + head * size : 2 * width + (head + 1) * size]
            scores = nt(queries[:, head * size : (head + 1) * size], keys) + bias_ref[head, here, :]
            scores = jnp.where(allowed, scores, blocked)
            top = jnp.max(scores, axis=-1, keepdims=True)
            raised = jnp.exp(scores - top)
            total = jnp.sum(raised, axis=-1, keepdims=True)
            probs = (raised * (1.0 / total)).astype(low)
            probs_ref[i, head] = probs
            copy = pltpu.make_async_copy(
                probs_ref.at[i, head], probs_outs[i].at[0, head], save_sems.at[i * (heads + 1) + head]
            )
            copy.start()
            saves.append(copy)
            mixed.append(nn(probs, values).astype(low))
        mixed = jnp.concatenate(mixed, axis=1)
        mixed_ref[i] = mixed
        copy = pltpu.make_async_copy(
            mixed_ref.at[i], mixed_any.at[pack, here], save_sems.at[i * (heads + 1) + heads]
        )
        copy.start()
        saves.append(copy)
        share = nn(mixed, w_out_ref[...])
        if turn == 1:
            share = share + got_ref[...].astype(wide)
        flat_refs[i][...] = share.astype(low)
    for copy in saves:
        copy.wait()


def attention_step(step, packs, prompt_len, core, joined, bias, seg_rows, seg_cols, w_out, got, mixed_all):
    _, rows, triple = joined.shape
    heads = bias.shape[0]
    width, model = w_out.shape
    half = rows // 2
    first, last = (0 if step < packs else 1), (1 if step > 0 else 0)
    steps = last - first + 1
    inside = pl.BlockSpec(memory_space=pltpu.VMEM)
    anywhere = pl.BlockSpec(memory_space=pl.ANY)
    in_specs = [pl.BlockSpec(memory_space=pltpu.SMEM), anywhere] + [inside] * 4
    args = [core, joined, bias, seg_rows, seg_cols, w_out]
    if last == 1:
        in_specs.append(inside)
        args.append(got)
    aliases = {}
    if mixed_all is not None:
        aliases = {len(args): 2 * steps}
        in_specs.append(anywhere)
        args.append(mixed_all)
    outs = kernel_call(
        functools.partial(attention_step_kernel, prompt_len, heads, first, last, step), 5, near=(2,), vmem=24,
        in_specs=in_specs,
        out_specs=[inside] * steps + [anywhere] * (steps + 1),
        out_shape=[jax.ShapeDtypeStruct((half, model), low)] * steps
        + [in_hbm((1, heads, half, rows), low)] * steps
        + [in_hbm((packs, rows, width), low)],
        scratch_shapes=[
            pltpu.VMEM((steps, rows, triple), low),
            pltpu.VMEM((steps, heads, half, rows), low),
            pltpu.VMEM((steps, half, width), low),
            pltpu.SemaphoreType.DMA((steps,)),
            pltpu.SemaphoreType.DMA((steps * (heads + 1),)),
        ],
        input_output_aliases=aliases,
        name="attention_step",
    )(*args)
    send, probs_send = (outs[0], outs[steps]) if first == 0 else (None, None)
    pair, probs_own = (outs[steps - 1], outs[2 * steps - 1]) if last == 1 else (None, None)
    return send, pair, probs_send, probs_own, outs[-1]


def feed_step_kernel(first, last, step, place_ref, rows_any, cot_any, gain_ref, *refs):
    refs = list(refs)
    turns = list(range(first, last + 1))
    sums = [refs[2 * i : 2 * i + 2] for i in range(len(turns))]
    refs = refs[2 * len(turns) :]
    if last == 1:
        got_ref, refs = refs[0], refs[1:]
    w_in_any, w_out_any, in_a, in_b, out_a, out_b = refs[:6]
    (rows_ref, cot_ref, normed_ref, active_ref, hidden_ref, result_ref, w_in_ref, w_out_ref,
     load_sems, save_sems) = refs[-10:]
    outs = refs[-10 - (3 + (1 if first == 0 else 0) + (4 if last == 1 else 0)) : -10]
    saved, rest = outs[:3], outs[3:]
    if first == 0:
        send_ref, rest = rest[0], rest[1:]
    if last == 1:
        middle_ref, grad_ref, gain_grad_ref, results_any = rest
    half = rows_ref.shape[0] // len(turns)
    half_rows = in_a.shape[0]
    core, side, part = place_ref[0], place_ref[1], place_ref[2]
    near = pl.ds(pl.multiple_of(part * half_rows, half_rows), half_rows)
    away = pl.ds(pl.multiple_of((1 - part) * half_rows, half_rows), half_rows)

    def block(turn):
        mine = jnp.bitwise_xor(core, 1 - turn)
        return step - turn, pl.ds(pl.multiple_of(mine * half, half), half)

    def span(index):
        return pl.ds(index * half, half)

    row_loads = [
        pltpu.make_async_copy(rows_any.at[*block(turn)], rows_ref.at[span(i)], load_sems.at[i])
        for i, turn in enumerate(turns)
    ]
    cot_loads = [
        pltpu.make_async_copy(cot_any.at[*block(turn)], cot_ref.at[span(i)], load_sems.at[2 + i])
        for i, turn in enumerate(turns)
    ]
    in_loads = [
        pltpu.make_async_copy(w_in_any, w_in_ref.at[side], load_sems.at[4]),
        pltpu.make_async_copy(in_a, w_in_ref.at[1 - side, near], load_sems.at[5]),
        pltpu.make_async_copy(in_b, w_in_ref.at[1 - side, away], load_sems.at[6]),
    ]
    out_loads = [
        pltpu.make_async_copy(w_out_any, w_out_ref.at[side], load_sems.at[7]),
        pltpu.make_async_copy(out_a, w_out_ref.at[1 - side, near], load_sems.at[8]),
        pltpu.make_async_copy(out_b, w_out_ref.at[1 - side, away], load_sems.at[9]),
    ]
    for copy in row_loads[::-1] + in_loads + cot_loads[::-1] + out_loads:
        copy.start()
    saves, kept = [], {}

    def save(index, place, source, target):
        copy = pltpu.make_async_copy(
            source, target.at[*block(turns[index])], save_sems.at[2 * place + index]
        )
        copy.start()
        saves.append(copy)

    def prepare(index):
        row_loads[index].wait()
        pair_ref, far_ref = sums[index]
        middle = rows_ref[span(index), :].astype(wide) + (
            pair_ref[...].astype(wide) + far_ref[...].astype(wide)
        )
        scale = lax.rsqrt(jnp.mean(middle * middle, axis=-1, keepdims=True) + epsilon)
        normed_ref[span(index), :] = (middle * scale * gain_ref[...]).astype(low)
        kept[index] = [middle, scale, None, None]
        save(index, 0, normed_ref.at[span(index)], saved[0])

    def expand(index, quarter):
        rows_at = span(index)
        inner = nn(normed_ref[rows_at, :], w_in_ref[quarter])
        share = 0.5 + 0.5 * lax.erf(inner * root_half)
        active = (inner * share).astype(low)
        slope = share + inner * (jnp.exp(-0.5 * inner * inner) * inv_root_tau)
        if quarter == 0 and index == len(turns) - 1:
            for copy in cot_loads + out_loads:
                copy.wait()
        hidden = (nt(cot_ref[rows_at, :], w_out_ref[quarter]) * slope).astype(low)
        active_ref[quarter, rows_at, :] = active
        hidden_ref[quarter, rows_at, :] = hidden
        feed_share = nn(active, w_out_ref[quarter])
        back_share = nt(hidden, w_in_ref[quarter])
        if quarter == 0:
            kept[index][2:] = [feed_share, back_share]
        else:
            kept[index][2] = kept[index][2] + feed_share
            kept[index][3] = kept[index][3] + back_share
            save(index, 1, active_ref.at[side, rows_at], saved[1])
            save(index, 2, hidden_ref.at[side, rows_at], saved[2])

    def finish_own(index):
        middle, scale, feed, back = kept[index]
        result_ref[...] = (middle + (feed + got_ref[:half, :].astype(wide))).astype(low)
        copy = pltpu.make_async_copy(result_ref, results_any.at[step - 1], save_sems.at[6])
        copy.start()
        saves.append(copy)
        upstream = back + got_ref[half:, :].astype(wide)
        scaled = upstream * gain_ref[...]
        inner = jnp.mean(scaled * middle, axis=-1, keepdims=True)
        grad = cot_ref[span(index), :].astype(wide) + scale * scaled - middle * (
            scale * scale * scale * inner
        )
        middle_ref[...] = grad
        grad_ref[...] = grad.astype(low)
        gain_grad_ref[...] = jnp.sum(upstream * middle * scale, axis=0, keepdims=True)

    def send_far(index):
        send_ref[:half, :] = kept[index][2].astype(low)
        send_ref[half:, :] = kept[index][3].astype(low)

    order = list(range(len(turns)))[::-1]
    prepare(order[0])
    for copy in in_loads:
        copy.wait()
    expand(order[0], 0)
    if len(order) == 2:
        prepare(order[1])
    expand(order[0], 1)
    if len(order) == 2:
        expand(order[1], 0)
    if last == 1:
        finish_own(order[0])
    if len(order) == 2:
        expand(order[1], 1)
    if first == 0:
        send_far(order[-1])
    for copy in saves:
        copy.wait()


def feed_step(step, packs, place, rows, cot, gain, sums, far_sums, own_pair, own_far, got,
              w_in, w_out, in_halves, out_halves, kept, results):
    _, row_count, model = rows.shape
    hidden = w_in.shape[1]
    half = row_count // 2
    first, last = (0 if step < packs else 1), (1 if step > 0 else 0)
    steps = last - first + 1
    inside = pl.BlockSpec(memory_space=pltpu.VMEM)
    anywhere = pl.BlockSpec(memory_space=pl.ANY)
    args = [place, rows, cot, gain]
    in_specs = [pl.BlockSpec(memory_space=pltpu.SMEM), anywhere, anywhere, inside]
    flats = ([sums, far_sums] if first == 0 else []) + ([own_pair, own_far, got] if last == 1 else [])
    args += flats
    in_specs += [inside] * len(flats)
    args += [w_in, w_out, *in_halves, *out_halves]
    in_specs += [anywhere] * 6
    aliases = {}
    if kept is not None:
        in_specs += [anywhere] * 3
        aliases = {len(args) + i: i for i in range(3)}
        args += list(kept)
    out_specs = [anywhere] * 3
    out_shape = [
        in_hbm((packs, row_count, model), low),
        in_hbm((packs, row_count, hidden), low),
        in_hbm((packs, row_count, hidden), low),
    ]
    if first == 0:
        out_specs.append(inside)
        out_shape.append(jax.ShapeDtypeStruct((row_count, model), low))
    if last == 1:
        if results is not None:
            in_specs.append(anywhere)
            aliases[len(args)] = len(out_shape) + 3
            args.append(results)
        out_specs += [inside] * 3 + [anywhere]
        out_shape += [
            in_hbm((half, model), wide),
            (jax.ShapeDtypeStruct if step < packs else in_hbm)((half, model), low),
            jax.ShapeDtypeStruct((1, model), wide),
            in_hbm((packs, half, model), low),
        ]
    outs = kernel_call(
        functools.partial(feed_step_kernel, first, last, step), 4 + 4 * steps, vmem=26,
        in_specs=in_specs,
        out_specs=out_specs,
        scratch_shapes=[
            pltpu.VMEM((steps * half, model), low),
            pltpu.VMEM((steps * half, model), low),
            pltpu.VMEM((steps * half, model), low),
            pltpu.VMEM((2, steps * half, hidden), low),
            pltpu.VMEM((2, steps * half, hidden), low),
            pltpu.VMEM((half, model), low),
            pltpu.VMEM((2, model, hidden), low),
            pltpu.VMEM((2, hidden, model), low),
            pltpu.SemaphoreType.DMA((10,)),
            pltpu.SemaphoreType.DMA((7,)),
        ],
        out_shape=out_shape,
        input_output_aliases=aliases,
        name="feed_step",
    )(*args)
    sent = outs[3] if first == 0 else None
    own = list(outs[-4:]) if last == 1 else [None] * 4
    return outs[:3], sent, own


def attention_back_kernel(
    heads, prompt_len, has_back, has_prev, core_ref, *refs,
):
    refs = list(refs)
    if has_back:
        own_ref, far_ref, w_out_ref, probs_own_ref, probs_far_ref, joined_ref = refs[:6]
        refs = refs[6:]
    w_joined_ref = refs.pop(0)
    if has_prev:
        prev_ref, got_ref, values_ref, grad_ref, gain_ref, gain_in_ref, head_in_ref = refs[:7]
        refs = refs[7:]
        if not has_back:
            other_gain_ref, refs = refs[0], refs[1:]
    outs = refs[-((5 if has_back else 0) + (3 if has_prev else 0)):]
    if has_prev:
        pair_ref, gain_out_ref, head_out_ref = outs[:3]
        outs = outs[3:]
        pair = (nn(prev_ref[...], w_joined_ref[...]) + got_ref[...].astype(wide)).astype(low)
        pair_ref[...] = pair
        top = head_in_ref.shape[0]
        values, upstream = values_ref[0].astype(wide), pair.astype(wide)
        grad, share = norm_back(upstream, gain_ref[...], values)
        gain_sum = gain_in_ref[...] + share
        gain_out_ref[...] = gain_sum
        grad = grad[:top] + jnp.where(core_ref[1] == 0, grad_ref[...], 0.0)
        head_sum = head_in_ref[...] + jnp.where(core_ref[0] == 0, grad, 0.0)
        if has_back:
            head_out_ref[...] = head_sum
        else:
            groups, group_rows, _ = head_out_ref.shape
            rows = prompt_len // groups
            head_out_ref[...] = jnp.zeros(head_out_ref.shape, low)
            for group in range(groups):
                head_out_ref[group, :rows, :] = head_sum[group * rows : (group + 1) * rows].astype(low)
                head_out_ref[group, rows : rows + 1, :] = gain_sum.astype(low)
                head_out_ref[group, rows + 1 : rows + 2, :] = other_gain_ref[...].astype(low)
    if not has_back:
        return
    send_ref, own_grads_ref, grads_ref, scores_ref, whole_ref = outs
    rows = joined_ref.shape[1]
    half = rows // 2
    width = w_out_ref.shape[0]
    size = width // heads
    core = core_ref[0]
    starts = [pl.multiple_of(core * half, half), pl.multiple_of((1 - core) * half, half)]
    ups, asks, asked = [], [], [[], []]
    for side, ref in enumerate((own_ref, far_ref)):
        whole_ref[0, pl.ds(starts[side], half), :] = ref[...]
        ups.append(nt(ref[...], w_out_ref[...]).astype(low))
        asks.append(joined_ref[0, pl.ds(starts[side], half), :width])
    grad_keys, grad_values = [], []
    for head in range(heads):
        cols = slice(head * size, (head + 1) * size)
        keys = joined_ref[0, :, width + head * size : width + (head + 1) * size]
        values = joined_ref[0, :, 2 * width + head * size : 2 * width + (head + 1) * size]
        grad_key, grad_value = None, None
        for side, probs_ref in enumerate((probs_own_ref, probs_far_ref)):
            probs = probs_ref[0, head]
            upstream = ups[side][:, cols]
            grad_probs = nt(upstream, values)
            spread = probs.astype(wide)
            inner = jnp.sum(spread * grad_probs, axis=-1, keepdims=True)
            grad_scores = (spread * (grad_probs - inner)).astype(low)
            scores_ref[0, head, pl.ds(starts[side], half), :] = grad_scores
            value_share = tn(upstream, probs)
            key_share = tn(asks[side][:, cols], grad_scores)
            grad_value = value_share if grad_value is None else grad_value + value_share
            grad_key = key_share if grad_key is None else grad_key + key_share
            asked[side].append(nn(grad_scores, keys))
        grad_values.append(grad_value.T)
        grad_keys.append(grad_key.T)
    rest = jnp.concatenate(grad_keys + grad_values, axis=1).astype(low)
    grads_ref[0, :, width:] = rest
    for side in range(2):
        grads_ref[0, pl.ds(starts[side], half), :width] = jnp.concatenate(asked[side], axis=1).astype(low)
    own_grads_ref[...] = grads_ref[0, pl.ds(starts[0], half), :]
    send_ref[...] = nn(grads_ref[0, pl.ds(starts[1], half), :], w_joined_ref[...]).astype(low)


def attention_back_step(step, packs, heads, prompt_len, other_gain, core, own, far, w_out, probs_own, probs_far, joined, w_joined,
                        prev, got, values, grad, gain, gain_sum, head_sum, kept):
    _, rows, triple = joined.shape
    width, model = w_out.shape
    half = rows // 2
    has_back, has_prev = step < packs, step > 0
    fixed = lambda t, c: (0, 0)
    flat = pl.BlockSpec((half, model), fixed)
    anywhere = pl.BlockSpec(memory_space=pl.ANY)
    in_specs, args, out_specs, out_shape, aliases = [], [core], [], [], {}
    if has_back:
        in_specs += [
            flat,
            flat,
            pl.BlockSpec((width, model), fixed),
            pl.BlockSpec((1, heads, half, rows), lambda t, c: (0, 0, 0, 0)),
            pl.BlockSpec((1, heads, half, rows), lambda t, c: (0, 0, 0, 0)),
            pl.BlockSpec((1, rows, triple), lambda t, c: (step, 0, 0)),
        ]
        args += [own, far, w_out, probs_own, probs_far, joined]
    in_specs.append(pl.BlockSpec((triple, model), fixed))
    args.append(w_joined)
    if has_prev:
        line = pl.BlockSpec((1, model), fixed)
        head = pl.BlockSpec(head_sum.shape, fixed)
        in_specs += [
            pl.BlockSpec((half, triple), fixed),
            flat,
            pl.BlockSpec((1, half, model), lambda t, c: (step - 1, c[0], 0)),
            head,
            line,
            line,
            head,
        ]
        args += [prev, got, values, grad, gain, gain_sum, head_sum]
        if has_back:
            head_out = in_hbm(head_sum.shape, wide)
        else:
            in_specs.append(line)
            args.append(other_gain)
            groups = Small.groups
            small = (groups, -(-(prompt_len // groups + 3) // 16) * 16, model)
            head, head_out = pl.BlockSpec(small, lambda t, c: (0, 0, 0)), jax.ShapeDtypeStruct(small, low)
        out_specs += [flat, line, head]
        out_shape += [
            jax.ShapeDtypeStruct((half, model), low),
            jax.ShapeDtypeStruct((1, model), wide),
            head_out,
        ]
    if has_back:
        if kept is not None:
            in_specs += [anywhere] * 3
            aliases = {len(args) + i: len(out_shape) + 2 + i for i in range(3)}
            args += list(kept)
        out_specs += [
            flat,
            pl.BlockSpec((half, triple), fixed),
            pl.BlockSpec((1, rows, triple), lambda t, c: (step, 0, 0)),
            pl.BlockSpec((1, heads, rows, rows), lambda t, c: (step, 0, 0, 0)),
            pl.BlockSpec((1, rows, model), lambda t, c: (step, 0, 0)),
        ]
        out_shape += [
            jax.ShapeDtypeStruct((half, model), low),
            in_hbm((half, triple), low),
            in_hbm((packs, rows, triple), low),
            in_hbm((packs, heads, rows, rows), low),
            in_hbm((packs, rows, model), low),
        ]
    outs = list(
        kernel_call(
            functools.partial(attention_back_kernel, heads, prompt_len, has_back, has_prev), 6,
            least=1000 if step == packs - 1 else 400000,
            grid_spec=pltpu.PrefetchScalarGridSpec(
                num_scalar_prefetch=1, grid=(1,), in_specs=in_specs, out_specs=out_specs
            ),
            out_shape=out_shape,
            input_output_aliases=aliases,
                name="attention_back_step",
        )(*args)
    )
    done, outs = (outs[:3], outs[3:]) if has_prev else ((None,) * 3, outs)
    send, own_grads, *kept = outs if has_back else (None, None)
    return done, send, own_grads, kept


def finish_kernel(packs, core_ref, rows_any, gain_ref, *refs):
    out_ref, rows_ref, sems = refs[-3:]
    half = rows_ref.shape[1]
    start = pl.multiple_of(core_ref[0] * half, half)
    copies = [
        pltpu.make_async_copy(rows_any.at[pack, pl.ds(start, half)], rows_ref.at[i], sems.at[i])
        for i, pack in enumerate(packs)
    ]
    for copy in copies:
        copy.start()
    for i, copy in enumerate(copies):
        copy.wait()
        pair_ref, far_ref, grad_ref = refs[3 * i : 3 * i + 3]
        upstream = pair_ref[...].astype(wide) + far_ref[...].astype(wide)
        grad, _ = norm_back(upstream, gain_ref[...], rows_ref[i].astype(wide))
        out_ref[i] = (grad_ref[...] + grad).astype(low)


def finish(packs, core, rows, gain, parts):
    half, model = parts[0][0].shape
    inside = pl.BlockSpec(memory_space=pltpu.VMEM)
    return kernel_call(
        functools.partial(finish_kernel, packs), 1.5 * len(packs), vmem=24,
        in_specs=[pl.BlockSpec(memory_space=pltpu.SMEM), pl.BlockSpec(memory_space=pl.ANY), inside]
        + [inside] * (3 * len(packs)),
        out_specs=inside,
        out_shape=jax.ShapeDtypeStruct((len(packs), half, model), low),
        scratch_shapes=[
            pltpu.VMEM((len(packs), half, model), low),
            pltpu.SemaphoreType.DMA((len(packs),)),
        ],
        name="finish",
    )(core, rows, gain, *[v for part in parts for v in part])


def place_kernel(core_ref, own_ref, far_ref, out_ref, sems):
    packs, half, _ = own_ref.shape
    copies = []
    for pack in range(packs):
        for side, ref in enumerate((own_ref, far_ref)):
            start = pl.multiple_of(jnp.bitwise_xor(core_ref[0], side) * half, half)
            copies.append(
                pltpu.make_async_copy(
                    ref.at[pack], out_ref.at[pack, pl.ds(start, half)], sems.at[2 * pack + side]
                )
            )
    for copy in copies:
        copy.start()
    for copy in copies:
        copy.wait()


def place_halves(core, own, far):
    packs, half, model = own.shape
    inside = pl.BlockSpec(memory_space=pltpu.VMEM)
    return kernel_call(
        place_kernel, 2.5, vmem=24, least=1000,
        in_specs=[pl.BlockSpec(memory_space=pltpu.SMEM), inside, inside],
        out_specs=pl.BlockSpec(memory_space=pl.ANY),
        out_shape=in_hbm((packs, 2 * half, model), low),
        scratch_shapes=[pltpu.SemaphoreType.DMA((2 * packs,))],
        name="place_halves",
    )(core, own, far)


def weave_kernel(core_ref, *refs):
    out_ref, rows_ref, woven_ref = refs[-3:]
    half = rows_ref.shape[0] // 2
    text = out_ref.shape[0]
    pack = 0
    for own_ref, far_ref in zip(refs[:-3:2], refs[1:-3:2]):
        for i in range(own_ref.shape[0]):
            for side, ref in enumerate((own_ref, far_ref)):
                start = pl.multiple_of(jnp.bitwise_xor(core_ref[0], side) * half, half)
                rows_ref[pl.ds(start, half), :] = ref[i].astype(wide)
            woven_ref[:, pack, :] = rows_ref[2 * half - text :, :]
            pack += 1
    out_ref[...] = woven_ref[...].astype(low)


def weave_halves(core, pairs, text):
    packs = sum(own.shape[0] for own, _ in pairs)
    _, half, model = pairs[0][0].shape
    inside = pl.BlockSpec(memory_space=pltpu.VMEM)
    return kernel_call(
        weave_kernel, 4, vmem=32, least=1000,
        in_specs=[pl.BlockSpec(memory_space=pltpu.SMEM)] + [inside] * (2 * len(pairs)),
        out_specs=inside,
        out_shape=jax.ShapeDtypeStruct((text, packs, model), low),
        scratch_shapes=[pltpu.VMEM((2 * half, model), wide), pltpu.VMEM((text, packs, model), wide)],
        name="weave_halves",
    )(core, *[v for pair in pairs for v in pair])


def weight_kernel(pairs, split, where_ref, *refs):
    if split:
        keep_ref, send_ref, total_ref = refs[-3:]
    else:
        whole_ref, total_ref = refs[-2:]
    column = 0
    for i in range(pairs):
        right = refs[2 * i + 1][...]
        total_ref[:, column : column + right.shape[1]] = tn(refs[2 * i][...], right)
        column += right.shape[1]
    if not split:
        whole_ref[...] = total_ref[...].astype(low)
        return
    count, block, _ = keep_ref.shape
    side = jnp.bitwise_and(where_ref[0], 1)
    for i in range(count):
        for ref, chosen in ((keep_ref, side), (send_ref, 1 - side)):
            start = pl.multiple_of((2 * i + chosen) * block, 8)
            ref[i] = total_ref[pl.ds(start, block), :].astype(low)


def weight_shares(where, count, pairs, split):
    rows, model = pairs[0][0].shape
    widths = [right.shape[1] for _, right in pairs]
    turns, width = 2, sum(widths)
    block = model // count
    in_specs = []
    for n in widths:
        in_specs += [
            pl.BlockSpec((rows, model // turns), lambda t, w: (0, t)),
            pl.BlockSpec((rows, n), lambda t, w: (0, 0)),
        ]
    if split:
        out_specs = [pl.BlockSpec((count // 2 // turns, block, width), lambda t, w: (t, 0, 0))] * 2
        out_shape = [jax.ShapeDtypeStruct((count // 2, block, width), low)] * 2
    else:
        out_specs = pl.BlockSpec((model // turns, width), lambda t, w: (t, 0))
        out_shape = in_hbm((model, width), low)
    return kernel_call(
        functools.partial(weight_kernel, len(pairs), split), 6, vmem=26,
        grid_spec=pltpu.PrefetchScalarGridSpec(
            num_scalar_prefetch=1,
            grid=(turns,),
            in_specs=in_specs,
            out_specs=out_specs,
            scratch_shapes=[pltpu.VMEM((model // turns, width), wide)],
        ),
        out_shape=out_shape,
        name="weight_shares",
    )(where, *[value for pair in pairs for value in pair])


def fold_kernel(count, where_ref, *refs):
    ins, outs = refs[:count], refs[count:]
    group = outs[0].shape[0]
    for flip, out_ref in enumerate(outs):
        for piece in range(group):
            spot = jnp.bitwise_xor(where_ref[0], flip)
            spot = spot * group + piece if len(outs) == 4 else piece * 2 + spot
            total = ins[0][spot].astype(wide)
            for ref in ins[1:]:
                total = total + ref[spot].astype(wide)
            out_ref[piece] = total.astype(out_ref.dtype)


def fold(where, parts, cuts):
    whole, block, width = parts[0].shape
    shape = (whole // cuts, block, width)
    inside = pl.BlockSpec(memory_space=pltpu.VMEM)
    return kernel_call(
        functools.partial(fold_kernel, len(parts)), 1.5, vmem=24,
        in_specs=[pl.BlockSpec(memory_space=pltpu.SMEM)] + [inside] * len(parts),
        out_specs=[inside] * cuts,
        out_shape=[jax.ShapeDtypeStruct(shape, low)] * cuts,
        name="fold",
    )(where, *parts)


def unfold_kernel(count, cuts, *refs):
    ins, outs = refs[:count], refs[count:]
    total = ins[0][0].astype(wide)
    for ref in ins[1:]:
        total = total + ref[0].astype(wide)
    for (start, width, turned), out_ref in zip(cuts, outs):
        piece = total[:, start : start + width]
        out_ref[...] = piece.T if turned else piece


def unfold(parts, cuts):
    block = parts[0].shape[1]
    inside = pl.BlockSpec(memory_space=pltpu.VMEM)
    return kernel_call(
        functools.partial(unfold_kernel, len(parts), cuts), 1.5,
        in_specs=[inside] * len(parts),
        out_specs=[inside] * len(cuts),
        out_shape=[
            jax.ShapeDtypeStruct((width, block) if turned else (block, width), wide)
            for _, width, turned in cuts
        ],
        name="unfold",
    )(*parts)


def small_fold_kernel(has_rel, side_ref, mine_ref, got_ref, *refs):
    keep_ref, send_ref, total_ref = refs[-3:]
    groups, rows, _ = mine_ref.shape
    half = groups // 2
    total_ref[...] = mine_ref[...].astype(wide) + got_ref[...].astype(wide)
    if has_rel:
        rel_ref, spot = refs[0], refs[1]
        for group in range(groups):
            total_ref[group, spot[0], :] = rel_ref[0, :]
    keep_ref[...] = total_ref[pl.ds(side_ref[0] * half, half)].astype(low)
    send_ref[...] = total_ref[pl.ds((1 - side_ref[0]) * half, half)].astype(low)


def small_fold(side, mine, got, rel=None, spot=None):
    groups, rows, model = mine.shape
    inside, scalar = pl.BlockSpec(memory_space=pltpu.VMEM), pl.BlockSpec(memory_space=pltpu.SMEM)
    more = [] if rel is None else [rel, jnp.full((1,), spot, jnp.int32)]
    return kernel_call(
        functools.partial(small_fold_kernel, rel is not None), 1,
        in_specs=[scalar, inside, inside] + ([inside, scalar] if more else []),
        out_specs=[inside] * 2,
        out_shape=[jax.ShapeDtypeStruct((groups // 2, rows, model), low)] * 2,
        scratch_shapes=[pltpu.VMEM((groups, rows, model), wide)],
        name="small_fold",
    )(side, mine, got, *more)


def tie(*values):
    return lax.optimization_barrier(values)


def stages_of(count):
    bits = bits_of(count)
    rest = bits[1:][::-1]
    return [bits[:1]] + [rest[i : i + 2] for i in range(0, len(rest), 2)]


class Scatter:
    def __init__(self, keep, send, cuts):
        self.bits, self.cuts = bits_of(lax.axis_size("dp"))[1:], cuts
        self.parts = [keep, swap(send, "dp", 1)]

    def step(self):
        if self.cuts == 4:
            bit, self.bits = self.bits[-2], self.bits[:-2]
        else:
            bit, self.bits = self.bits[0], self.bits[1:]
        where = ((lax.axis_index("dp") // bit) % self.cuts).astype(jnp.int32).reshape(1)
        own, *sends = fold(where, self.parts, self.cuts)
        self.parts = [own] + [swap(v, "dp", bit * (flip + 1)) for flip, v in enumerate(sends)]

    def end(self, pieces):
        while self.bits:
            self.step()
        return unfold(self.parts, pieces)


def look_up(prompt_ids, table, prompt_delta):
    prompt_len = prompt_ids.shape[0]
    table_rows, model = table.shape
    groups = 2
    part = -(-prompt_len // (16 * groups)) * 16
    dp_index, mp_index = lax.axis_index("dp"), lax.axis_index("mp") % groups
    padded = jnp.pad(prompt_ids, (0, part * groups - prompt_len), constant_values=-1)
    ids = lax.dynamic_slice_in_dim(padded, mp_index * part, part)
    size, block = prompt_delta.shape[0], part * model
    line = jnp.pad(prompt_delta, (block, block))
    start = jnp.clip(block + mp_index * block - dp_index * size, 0, block + size)
    placed = lax.dynamic_slice_in_dim(line, start, block).reshape(part, model)
    local = jnp.where(ids < 0, -1, ids - dp_index * table_rows)
    if table_rows % 16 == 0:
        return look_up_rows(local, table, placed)
    selector = (local[:, None] == jnp.arange(table_rows, dtype=jnp.int32)[None, :]).astype(low)
    return (jnp.dot(selector, table, preferred_element_type=wide) + placed).astype(low)


def own_half(weight):
    part = lax.axis_index("dp") % 2
    halves = weight.reshape(2, weight.shape[0] // 2, weight.shape[1])
    return lax.dynamic_index_in_dim(halves, part, 0, keepdims=False)


class Small:
    groups = 4

    def __init__(self, total, prompt_len):
        self.total, self.share = total, prompt_len // self.groups
        self.mp_bits = bits_of(lax.axis_size("mp"))
        self.dp_bits = bits_of(lax.axis_size("dp"))[::-1]
        self.hops = 0
        self.hop_mp()

    def hop_mp(self):
        bit, self.mp_bits = self.mp_bits[0], self.mp_bits[1:]
        self.keep, self.got = self.total, swap(self.total, "mp", bit)

    def land(self):
        self.total = (self.keep.astype(wide) + self.got.astype(wide)).astype(low)

    def hop_dp(self, rel=None):
        bit, self.dp_bits = self.dp_bits[0], self.dp_bits[1:]
        if self.hops < 2:
            side = ((lax.axis_index("dp") // bit) % 2).astype(jnp.int32).reshape(1)
            if rel is not None:
                self.rel = rel
                rel = jnp.pad(rel.reshape(1, -1), ((0, 0), (0, self.keep.shape[2] - rel.size)))
            self.keep, send = small_fold(side, self.keep, self.got, rel, self.share + 2)
        else:
            self.land()
            self.keep = send = self.total
        self.hops += 1
        self.got = swap(send, "dp", bit)

    def results(self):
        while self.dp_bits:
            self.hop_dp()
        total = self.keep[0].astype(wide) + self.got[0].astype(wide)
        dp_count, dp_index = lax.axis_size("dp"), lax.axis_index("dp")
        share, model = self.share, total.shape[1]
        inside = dp_count // self.groups
        size = share * model // inside
        prompt_grad = lax.dynamic_slice_in_dim(total[:share].reshape(-1), (dp_index % inside) * size, size)
        width = model // dp_count
        gains = lax.dynamic_slice_in_dim(total[share : share + 2], dp_index * width, width, axis=1)
        piece = self.rel.size // dp_count
        rel_out = lax.dynamic_slice_in_dim(total[share + 2], dp_index * piece, piece)
        return prompt_grad, gains[0], gains[1], rel_out.reshape(-1, self.rel.shape[1])


def body(
    tokens, cotangent, segment_ids, prompt_ids, rel_buckets, table, prompt_delta, norm1_gain,
    w_query, w_key, w_value, w_output, rel_bias, norm2_gain, w_inner, w_outer,
):
    prompt_len = prompt_ids.shape[0]
    packs, rows, model = cotangent.shape
    bucket_count, heads = rel_bias.shape
    width = w_query.shape[1]
    groups = lax.axis_size("dp")
    mp_bits = bits_of(lax.axis_size("mp"))
    mp_index = lax.axis_index("mp").astype(jnp.int32)
    place = jnp.stack([mp_index % 2, (mp_index // 2) % 2, (lax.axis_index("dp") % 2).astype(jnp.int32)])
    gain1, gain2 = norm1_gain[None, :], norm2_gain[None, :]
    w_q, w_k, w_v = w_query.T, w_key.T, w_value.T

    in_near = swap(own_half(w_inner), "mp", 2)
    total = look_up(prompt_ids, table, prompt_delta)

    w_joined = jnp.concatenate([w_q, w_k, w_v], axis=0)
    bucket_hot = (
        rel_buckets[:, None] == jnp.arange(bucket_count, dtype=jnp.int32)[None, :]
    ).astype(wide)
    bucket_hot = jnp.pad(bucket_hot, ((0, 1), (0, 0)))
    turned = jnp.roll(bucket_hot, -(rows - 1), axis=0)
    bias_line = jnp.dot(turned, rel_bias, precision=highest).T
    marks = jnp.pad(segment_ids, ((0, 0), (prompt_len, 0)), constant_values=-1)
    seg_rows, seg_cols = marks.T, marks

    texts, half_packs = [], packs // 2
    for hop, bit in enumerate(bits_of(groups)):
        got = swap(total, "dp", bit)
        if hop == 0:
            bias = bias_grid_of(bias_line[:, None, :])
            got, bias, seg_rows, seg_cols = tie(got, bias, seg_rows, seg_cols)
        if hop == 1:
            texts = text_projections(0, half_packs, rows, tokens, gain1, w_joined, texts)
            got, *texts = tie(got, *texts)
        if hop == 2:
            texts = text_projections(half_packs, packs - half_packs, rows, tokens, gain1, w_joined, texts)
            got, *texts = tie(got, *texts)
            got, in_near = tie(got, in_near)
            in_away = swap(in_near, "dp", 1)
            out_near = swap(own_half(w_outer), "mp", 2)
        total = (total.astype(wide) + got.astype(wide)).astype(low)
    whole_rows, normed1, joined = texts
    pieces = jnp.stack([total, swap(total, "mp", 1)])
    whole_rows, normed1, joined = add_prompt(
        place[:1], pieces, gain1, w_joined, whole_rows, normed1, joined
    )

    pairs, fars, pairs_far, fars_far, probs_far, probs_own, mixed, got = [], [], [], [], [], [], None, None

    def attend(step):
        nonlocal mixed, got, place, in_away, out_near, out_away
        send, pair, probs_send, probs_pair, mixed = attention_step(
            step, packs, prompt_len, place, joined, bias, seg_rows, seg_cols, w_output, got, mixed
        )
        if step == 0:
            place, out_near, send = tie(place, out_near, send)
            out_away = swap(out_near, "dp", 1)
        else:
            place, pair = tie(place, pair)
        if step == 1:
            place, in_away = tie(place, in_away)
        if send is not None:
            probs_far.append(probs_send)
            got = swap(send, "mp", 1)
        if pair is not None:
            probs_own.append(probs_pair)
            pairs.append(pair)
            fars.append(swap(pair, "mp", 2))
            pairs_far.append(swap(pair, "mp", 1))
            fars_far.append(swap(fars[-1], "mp", 1))

    out_away = None

    def arrive(pack):
        nonlocal place
        place, fars[pack], pairs_far[pack], fars_far[pack] = tie(
            place, fars[pack], pairs_far[pack], fars_far[pack]
        )

    kept, sent, results, grads_wide, grads_low = None, None, None, [], []
    gain2_sum, none = 0.0, [None]
    back_kept, prev, got = None, None, None
    gain1_sum, head_sum = jnp.zeros((1, model), wide), jnp.zeros((128, model), wide)
    text_rows, pairs_back = [], []

    def feed(step):
        nonlocal kept, sent, results, gain2_sum, place
        kept, new_sent, done = feed_step(
            step, packs, place, whole_rows, cotangent, gain2,
            (pairs_far + none)[step], (fars_far + none)[step],
            (none + pairs)[step], (none + fars)[step], sent,
            w_inner, w_outer, (in_near, in_away), (out_near, out_away), kept, results,
        )
        if step < packs:
            place, new_sent = tie(place, new_sent)
            sent = swap(new_sent, "mp", 1)
        else:
            place, done[1] = tie(place, done[1])
        if step > 0:
            grads_wide.append(done[0])
            grads_low.append((done[1], swap(done[1], "mp", 1)))
            gain2_sum, results = gain2_sum + done[2], done[3]

    def back(step):
        nonlocal back_kept, prev, got, gain1_sum, head_sum, place
        live = step < packs
        done, send, own_grads, back_new = attention_back_step(
            step, packs, heads, prompt_len, gain2_sum, place, *(grads_low[step] if live else none * 2), w_output,
            probs_own[step] if live else None, probs_far[step] if live else None, joined, w_joined,
            prev, got, whole_rows, grads_wide[step - 1] if step else None, gain1, gain1_sum, head_sum,
            back_kept,
        )
        if live:
            place, send = tie(place, send)
            back_kept, prev, got = back_new, own_grads, swap(send, "mp", 1)
        if step > 0:
            pair, gain1_sum, head_sum = done
            pairs_back.append([pair, swap(pair, "mp", 2)])

    def end(*ended):
        nonlocal place
        rows_low = finish(ended, place, whole_rows, gain1, [(*pairs_back[p], grads_wide[p]) for p in ended])
        place, rows_low = tie(place, rows_low)
        text_rows.append((rows_low, swap(rows_low, "mp", 1)))

    def flat(value):
        return value.reshape(packs * rows, -1)

    for step in range(packs):
        attend(step)
    place, out_away = tie(place, out_away)
    arrive(0)
    feed(0)
    attend(packs)
    arrive(1)
    feed(1)
    for step in range(2, packs):
        arrive(step)
        feed(step)
        back(step - 2)
    feed(packs)
    normed2, active, hidden = kept
    where = lax.axis_index("dp").astype(jnp.int32).reshape(1)
    where, place = tie(where, place)
    feed_shares = weight_shares(
        where, groups, [(flat(normed2), flat(hidden)), (flat(cotangent), flat(active))], True
    )
    place, *feed_shares = tie(place, *feed_shares)
    feed_sum = Scatter(*feed_shares, 2)
    back(packs - 2)
    far_results = swap(results, "mp", 1)
    place, far_results, *pairs_back[0] = tie(place, far_results, *pairs_back[0])
    back(packs - 1)
    place, *pairs_back[1] = tie(place, *pairs_back[1])
    place, *feed_sum.parts = tie(place, *feed_sum.parts)
    feed_sum.step()
    grad_joined, scores, grad_rows = back_kept
    where, place = tie(where, place)
    tail_shares = weight_shares(
        where, groups, [(flat(normed1), flat(grad_joined)), (flat(grad_rows), flat(mixed))], True
    )
    place, *tail_shares = tie(place, *tail_shares)
    place, *feed_sum.parts = tie(place, *feed_sum.parts)
    feed_sum.step()
    tail = Scatter(*tail_shares, 4)
    side_one = (mp_index // 2) % 2 == 1
    gain2_sum = jnp.where(side_one, 0.0, gain2_sum)
    back(packs)
    place, head_sum = tie(place, head_sum)
    small = Small(head_sum, prompt_len)
    place, scores = tie(place, scores)
    line = diagonal_sums(scores)[:, 0, :]
    rel_share = jnp.einsum("ht,tb->bh", line, turned, precision=highest)
    small.land()
    small.hop_mp()
    place, rel_share = tie(place, rel_share)
    end(*range(packs - 1))
    out = place_halves(place, results, far_results)
    place, out, *tail.parts = tie(place, out, *tail.parts)
    tail.step()
    place, tail.parts[0], *feed_sum.parts = tie(place, tail.parts[0], *feed_sum.parts)
    hidden_width = w_inner.shape[1]
    inner_grad, outer_grad = feed_sum.end(((0, hidden_width, False), (hidden_width, hidden_width, False)))
    place, small.got, inner_grad = tie(place, small.got, inner_grad)
    small.hop_dp(rel_share)
    end(packs - 1)
    place, small.got = tie(place, small.got)
    small.hop_dp()
    text_rows[-1] = tie(*text_rows[-1])
    place, *tail.parts = tie(place, *tail.parts)
    grad_tokens = weave_halves(place, text_rows, rows - prompt_len)
    grad_tokens = jnp.transpose(grad_tokens, (1, 0, 2))
    query_grad, key_grad, value_grad, output_grad = tail.end(
        tuple((i * width, width, i == 3) for i in range(4))
    )
    prompt_grad, gain1_grad, gain2_grad, rel_grad = small.results()
    return (
        out, grad_tokens, prompt_grad, gain1_grad, query_grad, key_grad, value_grad, output_grad,
        rel_grad, gain2_grad, inner_grad, outer_grad.T,
    )


def solution(mesh):
    in_specs = (
        P("dp", None, None),
        P("dp", None, None),
        P("dp", None),
        P(),
        P(),
        P("dp", None),
        P("dp"),
        P(),
        P(None, "mp"),
        P(None, "mp"),
        P(None, "mp"),
        P("mp", None),
        P(None, "mp"),
        P(),
        P(None, "mp"),
        P("mp", None),
    )
    out_specs = (
        P("dp", None, None),
        P("dp", None, None),
        P("dp"),
        P("dp"),
        P("dp", "mp"),
        P("dp", "mp"),
        P("dp", "mp"),
        P("mp", "dp"),
        P("dp", "mp"),
        P("dp"),
        P("dp", "mp"),
        P("mp", "dp"),
    )
    return jax.shard_map(body, mesh=mesh, in_specs=in_specs, out_specs=out_specs, check_vma=False)
```

```python
import functools

import jax
import jax.numpy as jnp
from jax import lax
from jax.experimental import pallas as pl
from jax.experimental.pallas import tpu as pltpu
from jax.sharding import PartitionSpec as P

epsilon = 1e-06
blocked = -1000000000.0
highest = lax.Precision.HIGHEST
low = jnp.bfloat16
wide = jnp.float32
root_half = 0.7071067811865476
inv_root_tau = 0.3989422804014327


def nn(left, right):
    return lax.dot_general(left, right, (((1,), (0,)), ((), ())), preferred_element_type=wide)


def nt(left, right):
    return lax.dot_general(left, right, (((1,), (1,)), ((), ())), preferred_element_type=wide)


def tn(left, right):
    return lax.dot_general(left, right, (((0,), (0,)), ((), ())), preferred_element_type=wide)


def params(mebibytes):
    return pltpu.CompilerParams(vmem_limit_bytes=mebibytes * 1024 * 1024)


def in_hbm(shape, dtype):
    return pltpu.HBM(shape, dtype)


def kernel_call(kernel, micros, vmem=16, near=(), least=400000, **rest):
    cost = pl.CostEstimate(flops=0, bytes_accessed=int(micros * 3.6e6), transcendentals=0)
    call = pl.pallas_call(kernel, cost_estimate=cost, compiler_params=params(vmem), **rest)

    def run(*args):
        return call(
            *[
                pltpu.with_memory_space_constraint(v, pltpu.HBM) if (v.size >= least or v.ndim == 4) and i not in near else v
                for i, v in enumerate(args)
            ]
        )

    return run


def swap(value, axis, bit):
    count = lax.axis_size(axis)
    return lax.ppermute(value, axis, [(i, i ^ bit) for i in range(count)])


def bits_of(count):
    return [1 << i for i in range(count.bit_length() - 1)]


def rms_norm(values, gain):
    return values * lax.rsqrt(jnp.mean(values * values, axis=-1, keepdims=True) + epsilon) * gain


def norm_back(upstream, gain, values):
    scale = lax.rsqrt(jnp.mean(values * values, axis=-1, keepdims=True) + epsilon)
    scaled = upstream * gain
    inner = jnp.mean(scaled * values, axis=-1, keepdims=True)
    grad = scale * scaled - values * (scale * scale * scale * inner)
    return grad, jnp.sum(upstream * values * scale, axis=0, keepdims=True)


def bias_kernel(line_ref, grid_ref):
    rows = grid_ref.shape[1]
    spread = jnp.broadcast_to(line_ref[0], (rows, 2 * rows))
    grid_ref[0] = pltpu.roll(spread, 0, 1, stride=1, stride_axis=0)[:, :rows]


def bias_grid_of(line):
    heads, _, double = line.shape
    rows = double // 2
    return kernel_call(
        bias_kernel, 2,
        grid=(heads,),
        in_specs=[pl.BlockSpec((1, 1, double), lambda h: (h, 0, 0))],
        out_specs=pl.BlockSpec((1, rows, rows), lambda h: (h, 0, 0)),
        out_shape=jax.ShapeDtypeStruct((heads, rows, rows), wide),
        name="bias_grid",
    )(line)


def diagonal_line(grid_ref):
    packs, rows, _ = grid_ref.shape
    lanes = 128
    count = rows // lanes
    blocks = []
    for block in range(2 * count):
        total = jnp.zeros((lanes, lanes), wide)
        for band in range(count):
            column = (block + band) % (2 * count)
            if column < count:
                for pack in range(packs):
                    total = total + grid_ref[
                        pack, band * lanes : (band + 1) * lanes, column * lanes : (column + 1) * lanes
                    ].astype(wide)
        blocks.append(total)
    held = jnp.concatenate(blocks, axis=1)
    total = held[:8]
    for slab in range(1, lanes // 8):
        total = total + pltpu.roll(held[8 * slab : 8 * slab + 8], 2 * rows - 8 * slab, 1)
    line = total[0:1]
    for row in range(1, 8):
        line = line + pltpu.roll(total[row : row + 1], 2 * rows - row, 1)
    return line


def shifted_text_kernel(tokens_ref, gain_ref, weight_ref, *refs):
    rows_ref, normed_ref, joined_ref, wide_ref = refs[-4:]
    rows = rows_ref.shape[1]
    prompt_len = rows - tokens_ref.shape[1]
    wide_ref[:prompt_len, :] = jnp.zeros((prompt_len, wide_ref.shape[1]), wide)
    wide_ref[prompt_len:, :] = tokens_ref[0].astype(wide)
    values = wide_ref[...]
    rows_ref[0] = values.astype(low)
    normed = rms_norm(values, gain_ref[...]).astype(low)
    normed_ref[0] = normed
    joined_ref[0] = nt(normed, weight_ref[...]).astype(low)


def text_projections(first, count, rows, tokens, gain, weight, kept):
    packs, text, model = tokens.shape
    triple = weight.shape[0]
    fixed = lambda p: (0, 0)
    moving = lambda p: (first + p, 0, 0)
    return kernel_call(
        shifted_text_kernel, 1.2 * count,
        grid=(count,),
        in_specs=[
            pl.BlockSpec((1, text, model), moving),
            pl.BlockSpec((1, model), fixed),
            pl.BlockSpec((triple, model), fixed),
        ]
        + [pl.BlockSpec(memory_space=pl.ANY)] * len(kept),
        out_specs=[
            pl.BlockSpec((1, rows, model), moving),
            pl.BlockSpec((1, rows, model), moving),
            pl.BlockSpec((1, rows, triple), moving),
        ],
        out_shape=[
            in_hbm((packs, rows, model), low),
            in_hbm((packs, rows, model), low),
            in_hbm((packs, rows, triple), low),
        ],
        scratch_shapes=[pltpu.VMEM((rows, model), wide)],
        input_output_aliases={3 + i: i for i in range(len(kept))},
        name="text_projections",
    )(tokens, gain, weight, *kept)


def prompt_kernel(place_ref, pieces_ref, gain_ref, weight_ref, rows_in, normed_in, joined_in, rows_out, normed_out, joined_out,
                  prompt_ref, rows_ref, normed_ref, joined_ref, load_sems, save_sems):
    count, part, _ = pieces_ref.shape
    packs = rows_ref.shape[0]
    top = count * part
    held = (rows_ref, normed_ref, joined_ref)
    loads = [
        pltpu.make_async_copy(source.at[:, pl.ds(0, top)], target, load_sems.at[i])
        for i, (source, target) in enumerate(zip((rows_in, normed_in, joined_in), held))
    ]
    for copy in loads:
        copy.start()
    for k in range(count):
        start = pl.multiple_of(jnp.bitwise_xor(place_ref[0], k) * part, part)
        prompt_ref[pl.ds(start, part), :] = pieces_ref[k]
    prompt = prompt_ref[...]
    normed = rms_norm(prompt.astype(wide), gain_ref[...]).astype(low)
    joined = nt(normed, weight_ref[...]).astype(low)
    saves = []
    for i, (value, target) in enumerate(zip((prompt, normed, joined), (rows_out, normed_out, joined_out))):
        loads[i].wait()
        for pack in range(packs):
            held[i][pack] = held[i][pack] + value
        copy = pltpu.make_async_copy(held[i], target.at[:, pl.ds(0, top)], save_sems.at[i])
        copy.start()
        saves.append(copy)
    for copy in saves:
        copy.wait()


def add_prompt(place, pieces, gain, weight, rows, normed, joined):
    packs, _, model = rows.shape
    triple = weight.shape[0]
    count, part, _ = pieces.shape
    top = count * part
    inside = pl.BlockSpec(memory_space=pltpu.VMEM)
    anywhere = pl.BlockSpec(memory_space=pl.ANY)
    return kernel_call(
        prompt_kernel, 2.5,
        in_specs=[pl.BlockSpec(memory_space=pltpu.SMEM)] + [inside] * 3 + [anywhere] * 3,
        out_specs=[anywhere] * 3,
        out_shape=[
            in_hbm(rows.shape, low),
            in_hbm(normed.shape, low),
            in_hbm(joined.shape, low),
        ],
        scratch_shapes=[
            pltpu.VMEM((top, model), low),
            pltpu.VMEM((packs, top, model), low),
            pltpu.VMEM((packs, top, model), low),
            pltpu.VMEM((packs, top, triple), low),
            pltpu.SemaphoreType.DMA((3,)),
            pltpu.SemaphoreType.DMA((3,)),
        ],
        input_output_aliases={4: 0, 5: 1, 6: 2},
        name="add_prompt",
    )(place, pieces, gain, weight, rows, normed, joined)


def look_up_kernel(ids_ref, table_any, placed_ref, out_ref, blocks_ref, total_ref, sems):
    part = out_ref.shape[0]
    limit = table_any.shape[0]
    copies, inside = [], []
    for row in range(part):
        local = jnp.clip(ids_ref[row], 0, limit - 1)
        inside.append(local)
        start = pl.multiple_of(jnp.left_shift(jnp.right_shift(local, 4), 4), 16)
        copies.append(
            pltpu.make_async_copy(table_any.at[pl.ds(start, 16)], blocks_ref.at[row], sems.at[row])
        )
    for copy in copies:
        copy.start()
    for copy in copies:
        copy.wait()
    position = lax.broadcasted_iota(jnp.int32, blocks_ref.shape[1:], 0)
    for row in range(part):
        own = inside[row] == ids_ref[row]
        chosen = (position == jnp.bitwise_and(inside[row], 15)) & own
        found = jnp.sum(jnp.where(chosen, blocks_ref[row].astype(wide), 0.0), axis=0, keepdims=True)
        total_ref[row : row + 1, :] = placed_ref[row : row + 1, :] + found
    out_ref[...] = total_ref[...].astype(low)


def look_up_rows(ids, table, placed):
    part, model = placed.shape
    inside = pl.BlockSpec(memory_space=pltpu.VMEM)
    return kernel_call(
        look_up_kernel, 2.5,
        in_specs=[pl.BlockSpec(memory_space=pltpu.SMEM), pl.BlockSpec(memory_space=pl.ANY), inside],
        out_specs=inside,
        out_shape=jax.ShapeDtypeStruct((part, model), low),
        scratch_shapes=[
            pltpu.VMEM((part, 16, model), low),
            pltpu.VMEM((part, model), wide),
            pltpu.SemaphoreType.DMA((part,)),
        ],
        name="look_up",
    )(ids, table, placed)


def attention_step_kernel(
    prompt_len, heads, first, last, step, core_ref, joined_any, bias_ref, seg_rows_ref, seg_cols_ref, w_out_ref, *refs,
):
    turns = list(range(first, last + 1))
    refs = list(refs)
    if last == 1:
        got_ref, refs = refs[0], refs[1:]
    joined_ref, probs_ref, mixed_ref, load_sems, save_sems = refs[-5:]
    outs = refs[-5 - 2 * len(turns) - 1 : -5]
    flat_refs, probs_outs, mixed_any = outs[: len(turns)], outs[len(turns) : -1], outs[-1]
    rows = joined_ref.shape[1]
    half = rows // 2
    width = w_out_ref.shape[0]
    size = width // heads
    loads = [
        pltpu.make_async_copy(joined_any.at[step - turn], joined_ref.at[i], load_sems.at[i])
        for i, turn in enumerate(turns)
    ]
    for copy in loads:
        copy.start()
    saves = []
    col_pos = lax.broadcasted_iota(jnp.int32, (half, rows), 1)
    for i, turn in enumerate(turns):
        pack = step - turn
        mine = jnp.bitwise_xor(core_ref[0], 1 - turn)
        start = pl.multiple_of(mine * half, half)
        here = pl.ds(start, half)
        row_pos = start + lax.broadcasted_iota(jnp.int32, (half, rows), 0)
        allowed = (
            (row_pos < prompt_len)
            | (col_pos < prompt_len)
            | (seg_rows_ref[here, pack : pack + 1] == seg_cols_ref[pack : pack + 1, :])
        )
        loads[i].wait()
        queries = joined_ref[i, here, :width]
        mixed = []
        for head in range(heads):
            keys = joined_ref[i, :, width + head * size : width + (head + 1) * size]
            values = joined_ref[i, :, 2 * width + head * size : 2 * width + (head + 1) * size]
            scores = nt(queries[:, head * size : (head + 1) * size], keys) + bias_ref[head, here, :]
            scores = jnp.where(allowed, scores, blocked)
            top = jnp.max(scores, axis=-1, keepdims=True)
            raised = jnp.exp(scores - top)
            total = jnp.sum(raised, axis=-1, keepdims=True)
            probs = (raised * (1.0 / total)).astype(low)
            probs_ref[i, head] = probs
            copy = pltpu.make_async_copy(
                probs_ref.at[i, head], probs_outs[i].at[0, head], save_sems.at[i * (heads + 1) + head]
            )
            copy.start()
            saves.append(copy)
            mixed.append(nn(probs, values).astype(low))
        mixed = jnp.concatenate(mixed, axis=1)
        mixed_ref[i] = mixed
        copy = pltpu.make_async_copy(
            mixed_ref.at[i], mixed_any.at[pack, here], save_sems.at[i * (heads + 1) + heads]
        )
        copy.start()
        saves.append(copy)
        share = nn(mixed, w_out_ref[...])
        if turn == 1:
            share = share + got_ref[...].astype(wide)
        flat_refs[i][...] = share.astype(low)
    for copy in saves:
        copy.wait()


def attention_step(step, packs, prompt_len, core, joined, bias, seg_rows, seg_cols, w_out, got, mixed_all):
    _, rows, triple = joined.shape
    heads = bias.shape[0]
    width, model = w_out.shape
    half = rows // 2
    first, last = (0 if step < packs else 1), (1 if step > 0 else 0)
    steps = last - first + 1
    inside = pl.BlockSpec(memory_space=pltpu.VMEM)
    anywhere = pl.BlockSpec(memory_space=pl.ANY)
    in_specs = [pl.BlockSpec(memory_space=pltpu.SMEM), anywhere] + [inside] * 4
    args = [core, joined, bias, seg_rows, seg_cols, w_out]
    if last == 1:
        in_specs.append(inside)
        args.append(got)
    aliases = {}
    if mixed_all is not None:
        aliases = {len(args): 2 * steps}
        in_specs.append(anywhere)
        args.append(mixed_all)
    outs = kernel_call(
        functools.partial(attention_step_kernel, prompt_len, heads, first, last, step), 5, near=(2,), vmem=24,
        in_specs=in_specs,
        out_specs=[inside] * steps + [anywhere] * (steps + 1),
        out_shape=[jax.ShapeDtypeStruct((half, model), low)] * steps
        + [in_hbm((1, heads, half, rows), low)] * steps
        + [in_hbm((packs, rows, width), low)],
        scratch_shapes=[
            pltpu.VMEM((steps, rows, triple), low),
            pltpu.VMEM((steps, heads, half, rows), low),
            pltpu.VMEM((steps, half, width), low),
            pltpu.SemaphoreType.DMA((steps,)),
            pltpu.SemaphoreType.DMA((steps * (heads + 1),)),
        ],
        input_output_aliases=aliases,
        name="attention_step",
    )(*args)
    send, probs_send = (outs[0], outs[steps]) if first == 0 else (None, None)
    pair, probs_own = (outs[steps - 1], outs[2 * steps - 1]) if last == 1 else (None, None)
    return send, pair, probs_send, probs_own, outs[-1]


def feed_step_kernel(first, last, step, place_ref, rows_any, cot_any, gain_ref, *refs):
    refs = list(refs)
    turns = list(range(first, last + 1))
    sums = [refs[2 * i : 2 * i + 2] for i in range(len(turns))]
    refs = refs[2 * len(turns) :]
    if last == 1:
        got_ref, refs = refs[0], refs[1:]
    w_in_any, w_out_any, in_a, in_b, out_a, out_b = refs[:6]
    (rows_ref, cot_ref, normed_ref, active_ref, hidden_ref, result_ref, w_in_ref, w_out_ref,
     load_sems, save_sems) = refs[-10:]
    outs = refs[-10 - (3 + (1 if first == 0 else 0) + (4 if last == 1 else 0)) : -10]
    saved, rest = outs[:3], outs[3:]
    if first == 0:
        send_ref, rest = rest[0], rest[1:]
    if last == 1:
        middle_ref, grad_ref, gain_grad_ref, results_any = rest
    half = rows_ref.shape[0] // len(turns)
    half_rows = in_a.shape[0]
    core, side, part = place_ref[0], place_ref[1], place_ref[2]
    near = pl.ds(pl.multiple_of(part * half_rows, half_rows), half_rows)
    away = pl.ds(pl.multiple_of((1 - part) * half_rows, half_rows), half_rows)

    def block(turn):
        mine = jnp.bitwise_xor(core, 1 - turn)
        return step - turn, pl.ds(pl.multiple_of(mine * half, half), half)

    def span(index):
        return pl.ds(index * half, half)

    row_loads = [
        pltpu.make_async_copy(rows_any.at[*block(turn)], rows_ref.at[span(i)], load_sems.at[i])
        for i, turn in enumerate(turns)
    ]
    cot_loads = [
        pltpu.make_async_copy(cot_any.at[*block(turn)], cot_ref.at[span(i)], load_sems.at[2 + i])
        for i, turn in enumerate(turns)
    ]
    in_loads = [
        pltpu.make_async_copy(w_in_any, w_in_ref.at[side], load_sems.at[4]),
        pltpu.make_async_copy(in_a, w_in_ref.at[1 - side, near], load_sems.at[5]),
        pltpu.make_async_copy(in_b, w_in_ref.at[1 - side, away], load_sems.at[6]),
    ]
    out_loads = [
        pltpu.make_async_copy(w_out_any, w_out_ref.at[side], load_sems.at[7]),
        pltpu.make_async_copy(out_a, w_out_ref.at[1 - side, near], load_sems.at[8]),
        pltpu.make_async_copy(out_b, w_out_ref.at[1 - side, away], load_sems.at[9]),
    ]
    for copy in row_loads[::-1] + in_loads + cot_loads[::-1] + out_loads:
        copy.start()
    saves, kept = [], {}

    def save(index, place, source, target):
        copy = pltpu.make_async_copy(
            source, target.at[*block(turns[index])], save_sems.at[2 * place + index]
        )
        copy.start()
        saves.append(copy)

    def prepare(index):
        row_loads[index].wait()
        pair_ref, far_ref = sums[index]
        middle = rows_ref[span(index), :].astype(wide) + (
            pair_ref[...].astype(wide) + far_ref[...].astype(wide)
        )
        scale = lax.rsqrt(jnp.mean(middle * middle, axis=-1, keepdims=True) + epsilon)
        normed_ref[span(index), :] = (middle * scale * gain_ref[...]).astype(low)
        kept[index] = [middle, scale, None, None]
        save(index, 0, normed_ref.at[span(index)], saved[0])

    def expand(index, quarter):
        rows_at = span(index)
        inner = nn(normed_ref[rows_at, :], w_in_ref[quarter])
        share = 0.5 + 0.5 * lax.erf(inner * root_half)
        active = (inner * share).astype(low)
        slope = share + inner * (jnp.exp(-0.5 * inner * inner) * inv_root_tau)
        if quarter == 0 and index == len(turns) - 1:
            for copy in cot_loads + out_loads:
                copy.wait()
        hidden = (nt(cot_ref[rows_at, :], w_out_ref[quarter]) * slope).astype(low)
        active_ref[quarter, rows_at, :] = active
        hidden_ref[quarter, rows_at, :] = hidden
        feed_share = nn(active, w_out_ref[quarter])
        back_share = nt(hidden, w_in_ref[quarter])
        if quarter == 0:
            kept[index][2:] = [feed_share, back_share]
        else:
            kept[index][2] = kept[index][2] + feed_share
            kept[index][3] = kept[index][3] + back_share
            save(index, 1, active_ref.at[side, rows_at], saved[1])
            save(index, 2, hidden_ref.at[side, rows_at], saved[2])

    def finish_own(index):
        middle, scale, feed, back = kept[index]
        result_ref[...] = (middle + (feed + got_ref[:half, :].astype(wide))).astype(low)
        copy = pltpu.make_async_copy(result_ref, results_any.at[step - 1], save_sems.at[6])
        copy.start()
        saves.append(copy)
        upstream = back + got_ref[half:, :].astype(wide)
        scaled = upstream * gain_ref[...]
        inner = jnp.mean(scaled * middle, axis=-1, keepdims=True)
        grad = cot_ref[span(index), :].astype(wide) + scale * scaled - middle * (
            scale * scale * scale * inner
        )
        middle_ref[...] = grad
        grad_ref[...] = grad.astype(low)
        gain_grad_ref[...] = jnp.sum(upstream * middle * scale, axis=0, keepdims=True)

    def send_far(index):
        send_ref[:half, :] = kept[index][2].astype(low)
        send_ref[half:, :] = kept[index][3].astype(low)

    order = list(range(len(turns)))[::-1]
    prepare(order[0])
    for copy in in_loads:
        copy.wait()
    expand(order[0], 0)
    if len(order) == 2:
        prepare(order[1])
    expand(order[0], 1)
    if len(order) == 2:
        expand(order[1], 0)
    if last == 1:
        finish_own(order[0])
    if len(order) == 2:
        expand(order[1], 1)
    if first == 0:
        send_far(order[-1])
    for copy in saves:
        copy.wait()


def feed_step(step, packs, place, rows, cot, gain, sums, far_sums, own_pair, own_far, got,
              w_in, w_out, in_halves, out_halves, kept, results):
    _, row_count, model = rows.shape
    hidden = w_in.shape[1]
    half = row_count // 2
    first, last = (0 if step < packs else 1), (1 if step > 0 else 0)
    steps = last - first + 1
    inside = pl.BlockSpec(memory_space=pltpu.VMEM)
    anywhere = pl.BlockSpec(memory_space=pl.ANY)
    args = [place, rows, cot, gain]
    in_specs = [pl.BlockSpec(memory_space=pltpu.SMEM), anywhere, anywhere, inside]
    flats = ([sums, far_sums] if first == 0 else []) + ([own_pair, own_far, got] if last == 1 else [])
    args += flats
    in_specs += [inside] * len(flats)
    args += [w_in, w_out, *in_halves, *out_halves]
    in_specs += [anywhere] * 6
    aliases = {}
    if kept is not None:
        in_specs += [anywhere] * 3
        aliases = {len(args) + i: i for i in range(3)}
        args += list(kept)
    out_specs = [anywhere] * 3
    out_shape = [
        in_hbm((packs, row_count, model), low),
        in_hbm((packs, row_count, hidden), low),
        in_hbm((packs, row_count, hidden), low),
    ]
    if first == 0:
        out_specs.append(inside)
        out_shape.append(jax.ShapeDtypeStruct((row_count, model), low))
    if last == 1:
        if results is not None:
            in_specs.append(anywhere)
            aliases[len(args)] = len(out_shape) + 3
            args.append(results)
        out_specs += [inside] * 3 + [anywhere]
        out_shape += [
            in_hbm((half, model), wide),
            (jax.ShapeDtypeStruct if step < packs else in_hbm)((half, model), low),
            jax.ShapeDtypeStruct((1, model), wide),
            in_hbm((packs, half, model), low),
        ]
    outs = kernel_call(
        functools.partial(feed_step_kernel, first, last, step), 4 + 4 * steps, vmem=26,
        in_specs=in_specs,
        out_specs=out_specs,
        scratch_shapes=[
            pltpu.VMEM((steps * half, model), low),
            pltpu.VMEM((steps * half, model), low),
            pltpu.VMEM((steps * half, model), low),
            pltpu.VMEM((2, steps * half, hidden), low),
            pltpu.VMEM((2, steps * half, hidden), low),
            pltpu.VMEM((half, model), low),
            pltpu.VMEM((2, model, hidden), low),
            pltpu.VMEM((2, hidden, model), low),
            pltpu.SemaphoreType.DMA((10,)),
            pltpu.SemaphoreType.DMA((7,)),
        ],
        out_shape=out_shape,
        input_output_aliases=aliases,
        name="feed_step",
    )(*args)
    sent = outs[3] if first == 0 else None
    own = list(outs[-4:]) if last == 1 else [None] * 4
    return outs[:3], sent, own


def attention_back_kernel(
    heads, prompt_len, has_back, has_prev, core_ref, *refs,
):
    refs = list(refs)
    if has_back:
        own_ref, far_ref, w_out_ref, probs_own_ref, probs_far_ref, joined_ref = refs[:6]
        refs = refs[6:]
    w_joined_ref = refs.pop(0)
    if has_prev:
        prev_ref, got_ref, values_ref, grad_ref, gain_ref, gain_in_ref, head_in_ref = refs[:7]
        refs = refs[7:]
        if not has_back:
            other_gain_ref, refs = refs[0], refs[1:]
    outs = refs[-((5 if has_back else 0) + (3 if has_prev else 0)):]
    if has_prev:
        pair_ref, gain_out_ref, head_out_ref = outs[:3]
        outs = outs[3:]
        pair = (nn(prev_ref[...], w_joined_ref[...]) + got_ref[...].astype(wide)).astype(low)
        pair_ref[...] = pair
        top = head_in_ref.shape[0]
        values, upstream = values_ref[0].astype(wide), pair.astype(wide)
        grad, share = norm_back(upstream, gain_ref[...], values)
        gain_sum = gain_in_ref[...] + share
        gain_out_ref[...] = gain_sum
        grad = grad[:top] + jnp.where(core_ref[1] == 0, grad_ref[...], 0.0)
        head_sum = head_in_ref[...] + jnp.where(core_ref[0] == 0, grad, 0.0)
        if has_back:
            head_out_ref[...] = head_sum
        else:
            groups, group_rows, _ = head_out_ref.shape
            rows = prompt_len // groups
            head_out_ref[...] = jnp.zeros(head_out_ref.shape, low)
            for group in range(groups):
                head_out_ref[group, :rows, :] = head_sum[group * rows : (group + 1) * rows].astype(low)
                head_out_ref[group, rows : rows + 1, :] = gain_sum.astype(low)
                head_out_ref[group, rows + 1 : rows + 2, :] = other_gain_ref[...].astype(low)
    if not has_back:
        return
    send_ref, own_grads_ref, grads_ref, scores_ref, whole_ref = outs
    rows = joined_ref.shape[1]
    half = rows // 2
    width = w_out_ref.shape[0]
    size = width // heads
    core = core_ref[0]
    starts = [pl.multiple_of(core * half, half), pl.multiple_of((1 - core) * half, half)]
    ups, asks, asked = [], [], [[], []]
    for side, ref in enumerate((own_ref, far_ref)):
        whole_ref[0, pl.ds(starts[side], half), :] = ref[...]
        ups.append(nt(ref[...], w_out_ref[...]).astype(low))
        asks.append(joined_ref[0, pl.ds(starts[side], half), :width])
    grad_keys, grad_values = [], []
    for head in range(heads):
        cols = slice(head * size, (head + 1) * size)
        keys = joined_ref[0, :, width + head * size : width + (head + 1) * size]
        values = joined_ref[0, :, 2 * width + head * size : 2 * width + (head + 1) * size]
        grad_key, grad_value = None, None
        for side, probs_ref in enumerate((probs_own_ref, probs_far_ref)):
            probs = probs_ref[0, head]
            upstream = ups[side][:, cols]
            grad_probs = nt(upstream, values)
            spread = probs.astype(wide)
            inner = jnp.sum(spread * grad_probs, axis=-1, keepdims=True)
            grad_scores = (spread * (grad_probs - inner)).astype(low)
            scores_ref[0, head, pl.ds(starts[side], half), :] = grad_scores
            value_share = tn(upstream, probs)
            key_share = tn(asks[side][:, cols], grad_scores)
            grad_value = value_share if grad_value is None else grad_value + value_share
            grad_key = key_share if grad_key is None else grad_key + key_share
            asked[side].append(nn(grad_scores, keys))
        grad_values.append(grad_value.T)
        grad_keys.append(grad_key.T)
    rest = jnp.concatenate(grad_keys + grad_values, axis=1).astype(low)
    grads_ref[0, :, width:] = rest
    for side in range(2):
        grads_ref[0, pl.ds(starts[side], half), :width] = jnp.concatenate(asked[side], axis=1).astype(low)
    own_grads_ref[...] = grads_ref[0, pl.ds(starts[0], half), :]
    send_ref[...] = nn(grads_ref[0, pl.ds(starts[1], half), :], w_joined_ref[...]).astype(low)


def attention_back_step(step, packs, heads, prompt_len, other_gain, core, own, far, w_out, probs_own, probs_far, joined, w_joined,
                        prev, got, values, grad, gain, gain_sum, head_sum, kept):
    _, rows, triple = joined.shape
    width, model = w_out.shape
    half = rows // 2
    has_back, has_prev = step < packs, step > 0
    fixed = lambda t, c: (0, 0)
    flat = pl.BlockSpec((half, model), fixed)
    anywhere = pl.BlockSpec(memory_space=pl.ANY)
    in_specs, args, out_specs, out_shape, aliases = [], [core], [], [], {}
    if has_back:
        in_specs += [
            flat,
            flat,
            pl.BlockSpec((width, model), fixed),
            pl.BlockSpec((1, heads, half, rows), lambda t, c: (0, 0, 0, 0)),
            pl.BlockSpec((1, heads, half, rows), lambda t, c: (0, 0, 0, 0)),
            pl.BlockSpec((1, rows, triple), lambda t, c: (step, 0, 0)),
        ]
        args += [own, far, w_out, probs_own, probs_far, joined]
    in_specs.append(pl.BlockSpec((triple, model), fixed))
    args.append(w_joined)
    if has_prev:
        line = pl.BlockSpec((1, model), fixed)
        head = pl.BlockSpec(head_sum.shape, fixed)
        in_specs += [
            pl.BlockSpec((half, triple), fixed),
            flat,
            pl.BlockSpec((1, half, model), lambda t, c: (step - 1, c[0], 0)),
            head,
            line,
            line,
            head,
        ]
        args += [prev, got, values, grad, gain, gain_sum, head_sum]
        if has_back:
            head_out = in_hbm(head_sum.shape, wide)
        else:
            in_specs.append(line)
            args.append(other_gain)
            groups = Small.groups
            small = (groups, -(-(prompt_len // groups + 3) // 16) * 16, model)
            head, head_out = pl.BlockSpec(small, lambda t, c: (0, 0, 0)), jax.ShapeDtypeStruct(small, low)
        out_specs += [flat, line, head]
        out_shape += [
            jax.ShapeDtypeStruct((half, model), low),
            jax.ShapeDtypeStruct((1, model), wide),
            head_out,
        ]
    if has_back:
        if kept is not None:
            in_specs += [anywhere] * 3
            aliases = {len(args) + i: len(out_shape) + 2 + i for i in range(3)}
            args += list(kept)
        out_specs += [
            flat,
            pl.BlockSpec((half, triple), fixed),
            pl.BlockSpec((1, rows, triple), lambda t, c: (step, 0, 0)),
            pl.BlockSpec((1, heads, rows, rows), lambda t, c: (step, 0, 0, 0)),
            pl.BlockSpec((1, rows, model), lambda t, c: (step, 0, 0)),
        ]
        out_shape += [
            jax.ShapeDtypeStruct((half, model), low),
            in_hbm((half, triple), low),
            in_hbm((packs, rows, triple), low),
            in_hbm((packs, heads, rows, rows), low),
            in_hbm((packs, rows, model), low),
        ]
    outs = list(
        kernel_call(
            functools.partial(attention_back_kernel, heads, prompt_len, has_back, has_prev), 6,
            least=1000 if step == packs - 1 else 400000,
            grid_spec=pltpu.PrefetchScalarGridSpec(
                num_scalar_prefetch=1, grid=(1,), in_specs=in_specs, out_specs=out_specs
            ),
            out_shape=out_shape,
            input_output_aliases=aliases,
                name="attention_back_step",
        )(*args)
    )
    done, outs = (outs[:3], outs[3:]) if has_prev else ((None,) * 3, outs)
    send, own_grads, *kept = outs if has_back else (None, None)
    return done, send, own_grads, kept


def finish_kernel(packs, core_ref, rows_any, gain_ref, *refs):
    out_ref, rows_ref, sems = refs[-3:]
    half = rows_ref.shape[1]
    start = pl.multiple_of(core_ref[0] * half, half)
    copies = [
        pltpu.make_async_copy(rows_any.at[pack, pl.ds(start, half)], rows_ref.at[i], sems.at[i])
        for i, pack in enumerate(packs)
    ]
    for copy in copies:
        copy.start()
    for i, copy in enumerate(copies):
        copy.wait()
        pair_ref, far_ref, grad_ref = refs[3 * i : 3 * i + 3]
        upstream = pair_ref[...].astype(wide) + far_ref[...].astype(wide)
        grad, _ = norm_back(upstream, gain_ref[...], rows_ref[i].astype(wide))
        out_ref[i] = (grad_ref[...] + grad).astype(low)


def finish(packs, core, rows, gain, parts):
    half, model = parts[0][0].shape
    inside = pl.BlockSpec(memory_space=pltpu.VMEM)
    return kernel_call(
        functools.partial(finish_kernel, packs), 1.5 * len(packs), vmem=24,
        in_specs=[pl.BlockSpec(memory_space=pltpu.SMEM), pl.BlockSpec(memory_space=pl.ANY), inside]
        + [inside] * (3 * len(packs)),
        out_specs=inside,
        out_shape=jax.ShapeDtypeStruct((len(packs), half, model), low),
        scratch_shapes=[
            pltpu.VMEM((len(packs), half, model), low),
            pltpu.SemaphoreType.DMA((len(packs),)),
        ],
        name="finish",
    )(core, rows, gain, *[v for part in parts for v in part])


def middle_kernel(packs, place_ref, scores_any, rows_any, gain_ref, own_ref, far_ref, *refs):
    refs, (line_ref, ended_ref, out_any, scores_ref, values_ref, load_sems, save_sems) = refs[:-7], refs[-7:]
    heads = scores_ref.shape[0]
    half = values_ref.shape[1]
    core = place_ref[0]
    start = pl.multiple_of(core * half, half)
    value_loads = [
        pltpu.make_async_copy(rows_any.at[pack, pl.ds(start, half)], values_ref.at[i], load_sems.at[i])
        for i, pack in enumerate(packs)
    ]
    score_loads = [
        pltpu.make_async_copy(scores_any.at[:, head], scores_ref.at[head], load_sems.at[len(packs) + head])
        for head in range(heads)
    ]
    for copy in value_loads + score_loads:
        copy.start()
    saves = []
    for pack in range(own_ref.shape[0]):
        for side, ref in enumerate((own_ref, far_ref)):
            there = pl.ds(pl.multiple_of(jnp.bitwise_xor(core, side) * half, half), half)
            copy = pltpu.make_async_copy(ref.at[pack], out_any.at[pack, there], save_sems.at[2 * pack + side])
            copy.start()
            saves.append(copy)
    for i, copy in enumerate(value_loads):
        copy.wait()
        pair_ref, far_pair_ref, grad_ref = refs[3 * i : 3 * i + 3]
        upstream = pair_ref[...].astype(wide) + far_pair_ref[...].astype(wide)
        grad, _ = norm_back(upstream, gain_ref[...], values_ref[i].astype(wide))
        ended_ref[i] = (grad_ref[...] + grad).astype(low)
    for head, copy in enumerate(score_loads):
        copy.wait()
        line_ref[head] = diagonal_line(scores_ref.at[head])
    for copy in saves:
        copy.wait()


def middle_work(packs, place, scores, rows, gain, own, far, parts):
    count, heads, row_count, _ = scores.shape
    _, half, model = own.shape
    inside, anywhere = pl.BlockSpec(memory_space=pltpu.VMEM), pl.BlockSpec(memory_space=pl.ANY)
    return kernel_call(
        functools.partial(middle_kernel, packs), 12, vmem=40, least=1000,
        in_specs=[pl.BlockSpec(memory_space=pltpu.SMEM), anywhere, anywhere] + [inside] * (3 + 3 * len(packs)),
        out_specs=[inside, inside, anywhere],
        out_shape=[
            jax.ShapeDtypeStruct((heads, 1, 2 * row_count), wide),
            jax.ShapeDtypeStruct((len(packs), half, model), low),
            in_hbm((count, row_count, model), low),
        ],
        scratch_shapes=[
            pltpu.VMEM((heads, count, row_count, row_count), low),
            pltpu.VMEM((len(packs), half, model), low),
            pltpu.SemaphoreType.DMA((len(packs) + heads,)),
            pltpu.SemaphoreType.DMA((2 * count,)),
        ],
        name="middle_work",
    )(place, scores, rows, gain, own, far, *[v for part in parts for v in part])


def weave_kernel(core_ref, *refs):
    out_ref, rows_ref, woven_ref = refs[-3:]
    half = rows_ref.shape[0] // 2
    text = out_ref.shape[0]
    pack = 0
    for own_ref, far_ref in zip(refs[:-3:2], refs[1:-3:2]):
        for i in range(own_ref.shape[0]):
            for side, ref in enumerate((own_ref, far_ref)):
                start = pl.multiple_of(jnp.bitwise_xor(core_ref[0], side) * half, half)
                rows_ref[pl.ds(start, half), :] = ref[i].astype(wide)
            woven_ref[:, pack, :] = rows_ref[2 * half - text :, :]
            pack += 1
    out_ref[...] = woven_ref[...].astype(low)


def weave_halves(core, pairs, text):
    packs = sum(own.shape[0] for own, _ in pairs)
    _, half, model = pairs[0][0].shape
    inside = pl.BlockSpec(memory_space=pltpu.VMEM)
    return kernel_call(
        weave_kernel, 4, vmem=32, least=1000,
        in_specs=[pl.BlockSpec(memory_space=pltpu.SMEM)] + [inside] * (2 * len(pairs)),
        out_specs=inside,
        out_shape=jax.ShapeDtypeStruct((text, packs, model), low),
        scratch_shapes=[pltpu.VMEM((2 * half, model), wide), pltpu.VMEM((text, packs, model), wide)],
        name="weave_halves",
    )(core, *[v for pair in pairs for v in pair])


def weight_kernel(pairs, split, where_ref, *refs):
    if split:
        keep_ref, send_ref, total_ref = refs[-3:]
    else:
        whole_ref, total_ref = refs[-2:]
    column = 0
    for i in range(pairs):
        right = refs[2 * i + 1][...]
        total_ref[:, column : column + right.shape[1]] = tn(refs[2 * i][...], right)
        column += right.shape[1]
    if not split:
        whole_ref[...] = total_ref[...].astype(low)
        return
    count, block, _ = keep_ref.shape
    side = jnp.bitwise_and(where_ref[0], 1)
    for i in range(count):
        for ref, chosen in ((keep_ref, side), (send_ref, 1 - side)):
            start = pl.multiple_of((2 * i + chosen) * block, 8)
            ref[i] = total_ref[pl.ds(start, block), :].astype(low)


def weight_shares(where, count, pairs, split):
    rows, model = pairs[0][0].shape
    widths = [right.shape[1] for _, right in pairs]
    turns, width = 2, sum(widths)
    block = model // count
    in_specs = []
    for n in widths:
        in_specs += [
            pl.BlockSpec((rows, model // turns), lambda t, w: (0, t)),
            pl.BlockSpec((rows, n), lambda t, w: (0, 0)),
        ]
    if split:
        out_specs = [pl.BlockSpec((count // 2 // turns, block, width), lambda t, w: (t, 0, 0))] * 2
        out_shape = [jax.ShapeDtypeStruct((count // 2, block, width), low)] * 2
    else:
        out_specs = pl.BlockSpec((model // turns, width), lambda t, w: (t, 0))
        out_shape = in_hbm((model, width), low)
    return kernel_call(
        functools.partial(weight_kernel, len(pairs), split), 6, vmem=26,
        grid_spec=pltpu.PrefetchScalarGridSpec(
            num_scalar_prefetch=1,
            grid=(turns,),
            in_specs=in_specs,
            out_specs=out_specs,
            scratch_shapes=[pltpu.VMEM((model // turns, width), wide)],
        ),
        out_shape=out_shape,
        name="weight_shares",
    )(where, *[value for pair in pairs for value in pair])


def fold_kernel(count, where_ref, *refs):
    ins, outs = refs[:count], refs[count:]
    group = outs[0].shape[0]
    for flip, out_ref in enumerate(outs):
        for piece in range(group):
            spot = jnp.bitwise_xor(where_ref[0], flip)
            spot = spot * group + piece if len(outs) == 4 else piece * 2 + spot
            total = ins[0][spot].astype(wide)
            for ref in ins[1:]:
                total = total + ref[spot].astype(wide)
            out_ref[piece] = total.astype(out_ref.dtype)


def fold(where, parts, cuts):
    whole, block, width = parts[0].shape
    shape = (whole // cuts, block, width)
    inside = pl.BlockSpec(memory_space=pltpu.VMEM)
    return kernel_call(
        functools.partial(fold_kernel, len(parts)), 1.5, vmem=24,
        in_specs=[pl.BlockSpec(memory_space=pltpu.SMEM)] + [inside] * len(parts),
        out_specs=[inside] * cuts,
        out_shape=[jax.ShapeDtypeStruct(shape, low)] * cuts,
        name="fold",
    )(where, *parts)


def unfold_kernel(count, cuts, *refs):
    ins, outs = refs[:count], refs[count:]
    total = ins[0][0].astype(wide)
    for ref in ins[1:]:
        total = total + ref[0].astype(wide)
    for (start, width, turned), out_ref in zip(cuts, outs):
        piece = total[:, start : start + width]
        out_ref[...] = piece.T if turned else piece


def unfold(parts, cuts):
    block = parts[0].shape[1]
    inside = pl.BlockSpec(memory_space=pltpu.VMEM)
    return kernel_call(
        functools.partial(unfold_kernel, len(parts), cuts), 1.5,
        in_specs=[inside] * len(parts),
        out_specs=[inside] * len(cuts),
        out_shape=[
            jax.ShapeDtypeStruct((width, block) if turned else (block, width), wide)
            for _, width, turned in cuts
        ],
        name="unfold",
    )(*parts)


def joint_fold_kernel(spot, where_ref, keep_ref, got_ref, mine_ref, near_ref, rel_ref, *refs):
    outs, total_ref = refs[:4], refs[4]
    block = keep_ref.shape[1]
    group = keep_ref.shape[0] // 4
    for flip, out_ref in enumerate(outs):
        chosen = jnp.bitwise_xor(where_ref[0], flip)
        for piece in range(group):
            total = keep_ref[chosen * group + piece].astype(wide) + got_ref[chosen * group + piece].astype(wide)
            out_ref[piece * block : (piece + 1) * block, :] = total.astype(low)
        total_ref[...] = mine_ref[chosen].astype(wide) + near_ref[chosen].astype(wide)
        total_ref[spot : spot + 1, :] = rel_ref[...]
        out_ref[group * block :, :] = total_ref[...].astype(low)


def joint_fold(where, parts, smalls, rel, spot):
    whole, block, width = parts[0].shape
    rows = smalls[0].shape[1]
    shape = (whole // 4 * block + rows, width)
    inside = pl.BlockSpec(memory_space=pltpu.VMEM)
    return kernel_call(
        functools.partial(joint_fold_kernel, spot), 2,
        in_specs=[pl.BlockSpec(memory_space=pltpu.SMEM)] + [inside] * 5,
        out_specs=[inside] * 4,
        out_shape=[jax.ShapeDtypeStruct(shape, low)] * 4,
        scratch_shapes=[pltpu.VMEM((rows, width), wide)],
        name="joint_fold",
    )(where, *parts, *smalls, rel)


def joint_unfold_kernel(cuts, *refs):
    ins, outs = refs[:4], refs[4:]
    total = ins[0][...].astype(wide)
    for ref in ins[1:]:
        total = total + ref[...].astype(wide)
    small = outs[-1].shape[0]
    outs[-1][...] = total[-small:].astype(low)
    for (start, width, turned), out_ref in zip(cuts, outs):
        piece = total[:-small, start : start + width]
        out_ref[...] = piece.T if turned else piece


def joint_unfold(parts, cuts, rows):
    block = parts[0].shape[0] - rows
    inside = pl.BlockSpec(memory_space=pltpu.VMEM)
    return kernel_call(
        functools.partial(joint_unfold_kernel, cuts), 1.5,
        in_specs=[inside] * 4,
        out_specs=[inside] * (len(cuts) + 1),
        out_shape=[
            jax.ShapeDtypeStruct((width, block) if turned else (block, width), wide)
            for _, width, turned in cuts
        ]
        + [jax.ShapeDtypeStruct((rows, parts[0].shape[1]), low)],
        name="joint_unfold",
    )(*parts)


def tie(*values):
    return lax.optimization_barrier(values)


def stages_of(count):
    bits = bits_of(count)
    rest = bits[1:][::-1]
    return [bits[:1]] + [rest[i : i + 2] for i in range(0, len(rest), 2)]


class Scatter:
    def __init__(self, keep, send, cuts):
        self.bits, self.cuts = bits_of(lax.axis_size("dp"))[1:], cuts
        self.parts = [keep, swap(send, "dp", 1)]

    def step(self):
        if self.cuts == 4:
            bit, self.bits = self.bits[-2], self.bits[:-2]
        else:
            bit, self.bits = self.bits[0], self.bits[1:]
        where = ((lax.axis_index("dp") // bit) % self.cuts).astype(jnp.int32).reshape(1)
        own, *sends = fold(where, self.parts, self.cuts)
        self.parts = [own] + [swap(v, "dp", bit * (flip + 1)) for flip, v in enumerate(sends)]

    def end(self, pieces):
        while self.bits:
            self.step()
        return unfold(self.parts, pieces)


def look_up(prompt_ids, table, prompt_delta):
    prompt_len = prompt_ids.shape[0]
    table_rows, model = table.shape
    groups = 2
    part = -(-prompt_len // (16 * groups)) * 16
    dp_index, mp_index = lax.axis_index("dp"), lax.axis_index("mp") % groups
    padded = jnp.pad(prompt_ids, (0, part * groups - prompt_len), constant_values=-1)
    ids = lax.dynamic_slice_in_dim(padded, mp_index * part, part)
    size, block = prompt_delta.shape[0], part * model
    line = jnp.pad(prompt_delta, (block, block))
    start = jnp.clip(block + mp_index * block - dp_index * size, 0, block + size)
    placed = lax.dynamic_slice_in_dim(line, start, block).reshape(part, model)
    local = jnp.where(ids < 0, -1, ids - dp_index * table_rows)
    if table_rows % 16 == 0:
        return look_up_rows(local, table, placed)
    selector = (local[:, None] == jnp.arange(table_rows, dtype=jnp.int32)[None, :]).astype(low)
    return (jnp.dot(selector, table, preferred_element_type=wide) + placed).astype(low)


def own_half(weight):
    part = lax.axis_index("dp") % 2
    halves = weight.reshape(2, weight.shape[0] // 2, weight.shape[1])
    return lax.dynamic_index_in_dim(halves, part, 0, keepdims=False)


class Small:
    groups = 4

    def __init__(self, total, prompt_len):
        self.total, self.share = total, prompt_len // self.groups
        self.mp_bits = bits_of(lax.axis_size("mp"))
        self.hop_mp()

    def hop_mp(self):
        bit, self.mp_bits = self.mp_bits[0], self.mp_bits[1:]
        self.keep, self.got = self.total, swap(self.total, "mp", bit)

    def land(self):
        self.total = (self.keep.astype(wide) + self.got.astype(wide)).astype(low)

    def join(self, tail, rel):
        self.rel = rel
        row = jnp.pad(rel.reshape(1, -1), ((0, 0), (0, self.keep.shape[2] - rel.size)))
        high, tail.bits = tail.bits[-2], tail.bits[:-2]
        where = ((lax.axis_index("dp") // high) % 4).astype(jnp.int32).reshape(1)
        self.block = tail.parts[0].shape[1]
        own, *sends = joint_fold(where, tail.parts, (self.keep, self.got), row, self.share + 2)
        self.parts = [own] + [swap(v, "dp", high * (flip + 1)) for flip, v in enumerate(sends)]

    def split(self, tail, cuts):
        rows = self.keep.shape[1]
        if not tail.bits:
            *results, self.total = joint_unfold(self.parts, cuts, rows)
            return results
        tail.parts = [v[:-rows].reshape(-1, self.block, v.shape[1]) for v in self.parts]
        self.total = sum(v[-rows:].astype(wide) for v in self.parts).astype(low)
        return tail.end(cuts)

    def results(self):
        dp_count, dp_index = lax.axis_size("dp"), lax.axis_index("dp")
        total = self.total
        for bit in bits_of(dp_count)[:-2]:
            total = total.astype(low)
            total = total.astype(wide) + swap(total, "dp", bit).astype(wide)
        share, model = self.share, total.shape[1]
        inside = dp_count // self.groups
        size = share * model // inside
        prompt_grad = lax.dynamic_slice_in_dim(total[:share].reshape(-1), (dp_index % inside) * size, size)
        width = model // dp_count
        gains = lax.dynamic_slice_in_dim(total[share : share + 2], dp_index * width, width, axis=1)
        piece = self.rel.size // dp_count
        rel_out = lax.dynamic_slice_in_dim(total[share + 2], dp_index * piece, piece)
        return prompt_grad, gains[0], gains[1], rel_out.reshape(-1, self.rel.shape[1])


def body(
    tokens, cotangent, segment_ids, prompt_ids, rel_buckets, table, prompt_delta, norm1_gain,
    w_query, w_key, w_value, w_output, rel_bias, norm2_gain, w_inner, w_outer,
):
    prompt_len = prompt_ids.shape[0]
    packs, rows, model = cotangent.shape
    bucket_count, heads = rel_bias.shape
    width = w_query.shape[1]
    groups = lax.axis_size("dp")
    mp_bits = bits_of(lax.axis_size("mp"))
    mp_index = lax.axis_index("mp").astype(jnp.int32)
    place = jnp.stack([mp_index % 2, (mp_index // 2) % 2, (lax.axis_index("dp") % 2).astype(jnp.int32)])
    gain1, gain2 = norm1_gain[None, :], norm2_gain[None, :]
    w_q, w_k, w_v = w_query.T, w_key.T, w_value.T

    in_near = swap(own_half(w_inner), "mp", 2)
    total = look_up(prompt_ids, table, prompt_delta)

    w_joined = jnp.concatenate([w_q, w_k, w_v], axis=0)
    bucket_hot = (
        rel_buckets[:, None] == jnp.arange(bucket_count, dtype=jnp.int32)[None, :]
    ).astype(wide)
    bucket_hot = jnp.pad(bucket_hot, ((0, 1), (0, 0)))
    turned = jnp.roll(bucket_hot, -(rows - 1), axis=0)
    bias_line = jnp.dot(turned, rel_bias, precision=highest).T
    marks = jnp.pad(segment_ids, ((0, 0), (prompt_len, 0)), constant_values=-1)
    seg_rows, seg_cols = marks.T, marks

    texts, half_packs = [], packs // 2
    for hop, bit in enumerate(bits_of(groups)):
        got = swap(total, "dp", bit)
        if hop == 0:
            bias = bias_grid_of(bias_line[:, None, :])
            got, bias, seg_rows, seg_cols = tie(got, bias, seg_rows, seg_cols)
        if hop == 1:
            texts = text_projections(0, half_packs, rows, tokens, gain1, w_joined, texts)
            got, *texts = tie(got, *texts)
        if hop == 2:
            texts = text_projections(half_packs, packs - half_packs, rows, tokens, gain1, w_joined, texts)
            got, *texts = tie(got, *texts)
            got, in_near = tie(got, in_near)
            in_away = swap(in_near, "dp", 1)
            out_near = swap(own_half(w_outer), "mp", 2)
        total = (total.astype(wide) + got.astype(wide)).astype(low)
    whole_rows, normed1, joined = texts
    pieces = jnp.stack([total, swap(total, "mp", 1)])
    whole_rows, normed1, joined = add_prompt(
        place[:1], pieces, gain1, w_joined, whole_rows, normed1, joined
    )

    pairs, fars, pairs_far, fars_far, probs_far, probs_own, mixed, got = [], [], [], [], [], [], None, None

    def attend(step):
        nonlocal mixed, got, place, in_away, out_near, out_away
        send, pair, probs_send, probs_pair, mixed = attention_step(
            step, packs, prompt_len, place, joined, bias, seg_rows, seg_cols, w_output, got, mixed
        )
        if step == 0:
            place, out_near, send = tie(place, out_near, send)
            out_away = swap(out_near, "dp", 1)
        else:
            place, pair = tie(place, pair)
        if step == 1:
            place, in_away = tie(place, in_away)
        if send is not None:
            probs_far.append(probs_send)
            got = swap(send, "mp", 1)
        if pair is not None:
            probs_own.append(probs_pair)
            pairs.append(pair)
            fars.append(swap(pair, "mp", 2))
            pairs_far.append(swap(pair, "mp", 1))
            fars_far.append(swap(fars[-1], "mp", 1))

    out_away = None

    def arrive(pack):
        nonlocal place
        place, fars[pack], pairs_far[pack], fars_far[pack] = tie(
            place, fars[pack], pairs_far[pack], fars_far[pack]
        )

    kept, sent, results, grads_wide, grads_low = None, None, None, [], []
    gain2_sum, none = 0.0, [None]
    back_kept, prev, got = None, None, None
    gain1_sum, head_sum = jnp.zeros((1, model), wide), jnp.zeros((128, model), wide)
    text_rows, pairs_back = [], []

    def feed(step):
        nonlocal kept, sent, results, gain2_sum, place
        kept, new_sent, done = feed_step(
            step, packs, place, whole_rows, cotangent, gain2,
            (pairs_far + none)[step], (fars_far + none)[step],
            (none + pairs)[step], (none + fars)[step], sent,
            w_inner, w_outer, (in_near, in_away), (out_near, out_away), kept, results,
        )
        if step < packs:
            place, new_sent = tie(place, new_sent)
            sent = swap(new_sent, "mp", 1)
        else:
            place, done[1] = tie(place, done[1])
        if step > 0:
            grads_wide.append(done[0])
            grads_low.append((done[1], swap(done[1], "mp", 1)))
            gain2_sum, results = gain2_sum + done[2], done[3]

    def back(step):
        nonlocal back_kept, prev, got, gain1_sum, head_sum, place
        live = step < packs
        done, send, own_grads, back_new = attention_back_step(
            step, packs, heads, prompt_len, gain2_sum, place, *(grads_low[step] if live else none * 2), w_output,
            probs_own[step] if live else None, probs_far[step] if live else None, joined, w_joined,
            prev, got, whole_rows, grads_wide[step - 1] if step else None, gain1, gain1_sum, head_sum,
            back_kept,
        )
        if live:
            place, send = tie(place, send)
            back_kept, prev, got = back_new, own_grads, swap(send, "mp", 1)
        if step > 0:
            pair, gain1_sum, head_sum = done
            pairs_back.append([pair, swap(pair, "mp", 2)])

    def near(pack):
        nonlocal place
        place, pairs_far[pack] = tie(place, pairs_far[pack])

    def meet(pack):
        nonlocal place
        place, grads_low[pack] = tie(place, grads_low[pack])

    def end(*ended):
        nonlocal place
        rows_low = finish(ended, place, whole_rows, gain1, [(*pairs_back[p], grads_wide[p]) for p in ended])
        place, rows_low = tie(place, rows_low)
        text_rows.append((rows_low, swap(rows_low, "mp", 1)))

    def flat(value):
        return value.reshape(packs * rows, -1)

    for step in range(packs):
        attend(step)
    place, out_away = tie(place, out_away)
    arrive(0)
    feed(0)
    attend(packs)
    arrive(1)
    near(2)
    feed(1)
    for step in range(2, packs):
        arrive(step)
        meet(step - 2)
        if step + 1 < packs:
            near(step + 1)
        feed(step)
        back(step - 2)
    meet(packs - 2)
    feed(packs)
    normed2, active, hidden = kept
    where = lax.axis_index("dp").astype(jnp.int32).reshape(1)
    where, place = tie(where, place)
    inner_shares = weight_shares(where, groups, [(flat(normed2), flat(hidden))], True)
    place, inner_shares = tie(place, inner_shares)
    inner = Scatter(*inner_shares, 2)
    where, place = tie(where, place)
    outer_shares = weight_shares(where, groups, [(flat(cotangent), flat(active))], True)
    place, outer_shares = tie(place, outer_shares)
    outer = Scatter(*outer_shares, 2)
    meet(packs - 1)
    back(packs - 2)
    far_results = swap(results, "mp", 1)
    place, far_results, pairs_back[0], inner.parts = tie(place, far_results, pairs_back[0], inner.parts)
    inner.step()
    back(packs - 1)
    place, pairs_back[1], inner.parts, outer.parts = tie(place, pairs_back[1], inner.parts, outer.parts)
    inner.step()
    outer.step()
    place, inner.parts[0], outer.parts[0] = tie(place, inner.parts[0], outer.parts[0])
    grad_joined, scores, grad_rows = back_kept
    where, place = tie(where, place)
    tail_shares = weight_shares(
        where, groups, [(flat(normed1), flat(grad_joined)), (flat(grad_rows), flat(mixed))], True
    )
    place, *tail_shares = tie(place, *tail_shares)
    tail = Scatter(*tail_shares, 4)
    side_one = (mp_index // 2) % 2 == 1
    gain2_sum = jnp.where(side_one, 0.0, gain2_sum)
    back(packs)
    place, head_sum = tie(place, head_sum)
    small = Small(head_sum, prompt_len)
    place, outer.parts = tie(place, outer.parts)
    outer.step()
    place, outer.parts[0] = tie(place, outer.parts[0])
    small.land()
    small.hop_mp()
    early = list(range(packs - 1))
    line, rows_low, out = middle_work(
        early, place, scores, whole_rows, gain1, results, far_results,
        [(*pairs_back[p], grads_wide[p]) for p in early],
    )
    place, line, rows_low = tie(place, line, rows_low)
    text_rows.append((rows_low, swap(rows_low, "mp", 1)))
    rel_share = jnp.einsum("ht,tb->bh", line[:, 0, :], turned, precision=highest)
    place, rel_share, tail.parts, small.got = tie(place, rel_share, tail.parts, small.got)
    small.join(tail, rel_share)
    place, small.parts[0], inner.parts, outer.parts = tie(place, small.parts[0], inner.parts, outer.parts)
    whole_width = ((0, w_inner.shape[1], False),)
    (inner_grad,), (outer_grad,) = inner.end(whole_width), outer.end(whole_width)
    place, inner_grad, outer_grad = tie(place, inner_grad, outer_grad)
    end(packs - 1)
    place, text_rows[-1] = tie(place, text_rows[-1])
    grad_tokens = weave_halves(place, text_rows, rows - prompt_len)
    grad_tokens, small.parts = tie(grad_tokens, small.parts)
    grad_tokens = jnp.transpose(grad_tokens, (1, 0, 2))
    query_grad, key_grad, value_grad, output_grad = small.split(
        tail, tuple((i * width, width, i == 3) for i in range(4))
    )
    prompt_grad, gain1_grad, gain2_grad, rel_grad = small.results()
    return (
        out, grad_tokens, prompt_grad, gain1_grad, query_grad, key_grad, value_grad, output_grad,
        rel_grad, gain2_grad, inner_grad, outer_grad.T,
    )


def solution(mesh):
    in_specs = (
        P("dp", None, None),
        P("dp", None, None),
        P("dp", None),
        P(),
        P(),
        P("dp", None),
        P("dp"),
        P(),
        P(None, "mp"),
        P(None, "mp"),
        P(None, "mp"),
        P("mp", None),
        P(None, "mp"),
        P(),
        P(None, "mp"),
        P("mp", None),
    )
    out_specs = (
        P("dp", None, None),
        P("dp", None, None),
        P("dp"),
        P("dp"),
        P("dp", "mp"),
        P("dp", "mp"),
        P("dp", "mp"),
        P("mp", "dp"),
        P("dp", "mp"),
        P("dp"),
        P("dp", "mp"),
        P("mp", "dp"),
    )
    return jax.shard_map(body, mesh=mesh, in_specs=in_specs, out_specs=out_specs, check_vma=False)
```

```python
import functools

import jax
import jax.numpy as jnp
from jax import lax
from jax.experimental import pallas as pl
from jax.experimental.pallas import tpu as pltpu
from jax.sharding import PartitionSpec as P

epsilon = 1e-06
blocked = -1000000000.0
highest = lax.Precision.HIGHEST
low = jnp.bfloat16
wide = jnp.float32
root_half = 0.7071067811865476
inv_root_tau = 0.3989422804014327


def nn(left, right):
    return lax.dot_general(left, right, (((1,), (0,)), ((), ())), preferred_element_type=wide)


def nt(left, right):
    return lax.dot_general(left, right, (((1,), (1,)), ((), ())), preferred_element_type=wide)


def tn(left, right):
    return lax.dot_general(left, right, (((0,), (0,)), ((), ())), preferred_element_type=wide)


def params(mebibytes):
    return pltpu.CompilerParams(vmem_limit_bytes=mebibytes * 1024 * 1024)


def in_hbm(shape, dtype):
    return pltpu.HBM(shape, dtype)


def kernel_call(kernel, micros, vmem=16, near=(), least=400000, **rest):
    cost = pl.CostEstimate(flops=0, bytes_accessed=int(micros * 3.6e6), transcendentals=0)
    call = pl.pallas_call(kernel, cost_estimate=cost, compiler_params=params(vmem), **rest)

    def run(*args):
        return call(
            *[
                pltpu.with_memory_space_constraint(v, pltpu.HBM) if (v.size >= least or v.ndim == 4) and i not in near else v
                for i, v in enumerate(args)
            ]
        )

    return run


def swap(value, axis, bit):
    count = lax.axis_size(axis)
    return lax.ppermute(value, axis, [(i, i ^ bit) for i in range(count)])


def bits_of(count):
    return [1 << i for i in range(count.bit_length() - 1)]


def rms_norm(values, gain):
    return values * lax.rsqrt(jnp.mean(values * values, axis=-1, keepdims=True) + epsilon) * gain


def norm_back(upstream, gain, values):
    scale = lax.rsqrt(jnp.mean(values * values, axis=-1, keepdims=True) + epsilon)
    scaled = upstream * gain
    inner = jnp.mean(scaled * values, axis=-1, keepdims=True)
    grad = scale * scaled - values * (scale * scale * scale * inner)
    return grad, jnp.sum(upstream * values * scale, axis=0, keepdims=True)


def bias_kernel(line_ref, grid_ref):
    rows = grid_ref.shape[1]
    spread = jnp.broadcast_to(line_ref[0], (rows, 2 * rows))
    grid_ref[0] = pltpu.roll(spread, 0, 1, stride=1, stride_axis=0)[:, :rows]


def bias_grid_of(line):
    heads, _, double = line.shape
    rows = double // 2
    return kernel_call(
        bias_kernel, 2,
        grid=(heads,),
        in_specs=[pl.BlockSpec((1, 1, double), lambda h: (h, 0, 0))],
        out_specs=pl.BlockSpec((1, rows, rows), lambda h: (h, 0, 0)),
        out_shape=jax.ShapeDtypeStruct((heads, rows, rows), wide),
        name="bias_grid",
    )(line)


def diagonal_line(grid_ref):
    packs, rows, _ = grid_ref.shape
    lanes = 128
    count = rows // lanes
    blocks = []
    for block in range(2 * count):
        total = jnp.zeros((lanes, lanes), wide)
        for band in range(count):
            column = (block + band) % (2 * count)
            if column < count:
                for pack in range(packs):
                    total = total + grid_ref[
                        pack, band * lanes : (band + 1) * lanes, column * lanes : (column + 1) * lanes
                    ].astype(wide)
        blocks.append(total)
    held = jnp.concatenate(blocks, axis=1)
    total = held[:8]
    for slab in range(1, lanes // 8):
        total = total + pltpu.roll(held[8 * slab : 8 * slab + 8], 2 * rows - 8 * slab, 1)
    line = total[0:1]
    for row in range(1, 8):
        line = line + pltpu.roll(total[row : row + 1], 2 * rows - row, 1)
    return line


def shifted_text_kernel(tokens_ref, gain_ref, weight_ref, *refs):
    rows_ref, normed_ref, joined_ref, wide_ref = refs[-4:]
    rows = rows_ref.shape[1]
    prompt_len = rows - tokens_ref.shape[1]
    wide_ref[:prompt_len, :] = jnp.zeros((prompt_len, wide_ref.shape[1]), wide)
    wide_ref[prompt_len:, :] = tokens_ref[0].astype(wide)
    values = wide_ref[...]
    rows_ref[0] = values.astype(low)
    normed = rms_norm(values, gain_ref[...]).astype(low)
    normed_ref[0] = normed
    joined_ref[0] = nt(normed, weight_ref[...]).astype(low)


def text_projections(first, count, rows, tokens, gain, weight, kept):
    packs, text, model = tokens.shape
    triple = weight.shape[0]
    fixed = lambda p: (0, 0)
    moving = lambda p: (first + p, 0, 0)
    return kernel_call(
        shifted_text_kernel, 1.2 * count,
        grid=(count,),
        in_specs=[
            pl.BlockSpec((1, text, model), moving),
            pl.BlockSpec((1, model), fixed),
            pl.BlockSpec((triple, model), fixed),
        ]
        + [pl.BlockSpec(memory_space=pl.ANY)] * len(kept),
        out_specs=[
            pl.BlockSpec((1, rows, model), moving),
            pl.BlockSpec((1, rows, model), moving),
            pl.BlockSpec((1, rows, triple), moving),
        ],
        out_shape=[
            in_hbm((packs, rows, model), low),
            in_hbm((packs, rows, model), low),
            in_hbm((packs, rows, triple), low),
        ],
        scratch_shapes=[pltpu.VMEM((rows, model), wide)],
        input_output_aliases={3 + i: i for i in range(len(kept))},
        name="text_projections",
    )(tokens, gain, weight, *kept)


def prompt_kernel(place_ref, pieces_ref, gain_ref, weight_ref, rows_in, normed_in, joined_in, rows_out, normed_out, joined_out,
                  prompt_ref, rows_ref, normed_ref, joined_ref, load_sems, save_sems):
    count, part, _ = pieces_ref.shape
    packs = rows_ref.shape[0]
    top = count * part
    held = (rows_ref, normed_ref, joined_ref)
    loads = [
        pltpu.make_async_copy(source.at[:, pl.ds(0, top)], target, load_sems.at[i])
        for i, (source, target) in enumerate(zip((rows_in, normed_in, joined_in), held))
    ]
    for copy in loads:
        copy.start()
    for k in range(count):
        start = pl.multiple_of(jnp.bitwise_xor(place_ref[0], k) * part, part)
        prompt_ref[pl.ds(start, part), :] = pieces_ref[k]
    prompt = prompt_ref[...]
    normed = rms_norm(prompt.astype(wide), gain_ref[...]).astype(low)
    joined = nt(normed, weight_ref[...]).astype(low)
    saves = []
    for i, (value, target) in enumerate(zip((prompt, normed, joined), (rows_out, normed_out, joined_out))):
        loads[i].wait()
        for pack in range(packs):
            held[i][pack] = held[i][pack] + value
        copy = pltpu.make_async_copy(held[i], target.at[:, pl.ds(0, top)], save_sems.at[i])
        copy.start()
        saves.append(copy)
    for copy in saves:
        copy.wait()


def add_prompt(place, pieces, gain, weight, rows, normed, joined):
    packs, _, model = rows.shape
    triple = weight.shape[0]
    count, part, _ = pieces.shape
    top = count * part
    inside = pl.BlockSpec(memory_space=pltpu.VMEM)
    anywhere = pl.BlockSpec(memory_space=pl.ANY)
    return kernel_call(
        prompt_kernel, 2.5,
        in_specs=[pl.BlockSpec(memory_space=pltpu.SMEM)] + [inside] * 3 + [anywhere] * 3,
        out_specs=[anywhere] * 3,
        out_shape=[
            in_hbm(rows.shape, low),
            in_hbm(normed.shape, low),
            in_hbm(joined.shape, low),
        ],
        scratch_shapes=[
            pltpu.VMEM((top, model), low),
            pltpu.VMEM((packs, top, model), low),
            pltpu.VMEM((packs, top, model), low),
            pltpu.VMEM((packs, top, triple), low),
            pltpu.SemaphoreType.DMA((3,)),
            pltpu.SemaphoreType.DMA((3,)),
        ],
        input_output_aliases={4: 0, 5: 1, 6: 2},
        name="add_prompt",
    )(place, pieces, gain, weight, rows, normed, joined)


def look_up_kernel(ids_ref, table_any, target_ref, placed_ref, out_ref, blocks_ref, sems):
    part = out_ref.shape[0]
    limit = table_any.shape[0]

    def each(act):
        for row in range(part):
            local = ids_ref[row]

            @pl.when((local >= 0) & (local < limit))
            def _():
                start = pl.multiple_of(jnp.left_shift(jnp.right_shift(local, 4), 4), 16)
                act(
                    pltpu.make_async_copy(
                        table_any.at[pl.ds(start, 16)], blocks_ref.at[pl.ds(16 * row, 16)], sems.at[row]
                    )
                )

    blocks_ref[...] = jnp.zeros(blocks_ref.shape, low)
    each(lambda copy: copy.start())
    position = lax.broadcasted_iota(jnp.int32, (part, 16 * part), 1)
    chosen = jnp.where(position == target_ref[...], 1.0, 0.0).astype(low)
    each(lambda copy: copy.wait())
    out_ref[...] = (nn(chosen, blocks_ref[...]) + placed_ref[...]).astype(low)


def look_up_rows(ids, table, placed):
    part, model = placed.shape
    inside = pl.BlockSpec(memory_space=pltpu.VMEM)
    own = (ids >= 0) & (ids < table.shape[0])
    target = jnp.where(own, 16 * jnp.arange(part, dtype=jnp.int32) + ids % 16, -1)[:, None]
    return kernel_call(
        look_up_kernel, 2.5,
        in_specs=[pl.BlockSpec(memory_space=pltpu.SMEM), pl.BlockSpec(memory_space=pl.ANY), inside, inside],
        out_specs=inside,
        out_shape=jax.ShapeDtypeStruct((part, model), low),
        scratch_shapes=[pltpu.VMEM((16 * part, model), low), pltpu.SemaphoreType.DMA((part,))],
        name="look_up",
    )(ids, table, target, placed)


def attention_step_kernel(
    prompt_len, heads, first, last, step, core_ref, joined_any, bias_ref, seg_rows_ref, seg_cols_ref, w_out_ref, *refs,
):
    turns = list(range(first, last + 1))
    refs = list(refs)
    if last == 1:
        got_ref, refs = refs[0], refs[1:]
    joined_ref, probs_ref, mixed_ref, load_sems, save_sems = refs[-5:]
    outs = refs[-5 - 2 * len(turns) - 1 : -5]
    flat_refs, probs_outs, mixed_any = outs[: len(turns)], outs[len(turns) : -1], outs[-1]
    rows = joined_ref.shape[1]
    half = rows // 2
    width = w_out_ref.shape[0]
    size = width // heads
    loads = [
        pltpu.make_async_copy(joined_any.at[step - turn], joined_ref.at[i], load_sems.at[i])
        for i, turn in enumerate(turns)
    ]
    for copy in loads:
        copy.start()
    saves = []
    col_pos = lax.broadcasted_iota(jnp.int32, (half, rows), 1)
    for i, turn in enumerate(turns):
        pack = step - turn
        mine = jnp.bitwise_xor(core_ref[0], 1 - turn)
        start = pl.multiple_of(mine * half, half)
        here = pl.ds(start, half)
        row_pos = start + lax.broadcasted_iota(jnp.int32, (half, rows), 0)
        allowed = (
            (row_pos < prompt_len)
            | (col_pos < prompt_len)
            | (seg_rows_ref[here, pack : pack + 1] == seg_cols_ref[pack : pack + 1, :])
        )
        loads[i].wait()
        queries = joined_ref[i, here, :width]
        mixed = []
        for head in range(heads):
            keys = joined_ref[i, :, width + head * size : width + (head + 1) * size]
            values = joined_ref[i, :, 2 * width + head * size : 2 * width + (head + 1) * size]
            scores = nt(queries[:, head * size : (head + 1) * size], keys) + bias_ref[head, here, :]
            scores = jnp.where(allowed, scores, blocked)
            top = jnp.max(scores, axis=-1, keepdims=True)
            raised = jnp.exp(scores - top)
            total = jnp.sum(raised, axis=-1, keepdims=True)
            probs = (raised * (1.0 / total)).astype(low)
            probs_ref[i, head] = probs
            copy = pltpu.make_async_copy(
                probs_ref.at[i, head], probs_outs[i].at[0, head], save_sems.at[i * (heads + 1) + head]
            )
            copy.start()
            saves.append(copy)
            mixed.append(nn(probs, values).astype(low))
        mixed = jnp.concatenate(mixed, axis=1)
        mixed_ref[i] = mixed
        copy = pltpu.make_async_copy(
            mixed_ref.at[i], mixed_any.at[pack, here], save_sems.at[i * (heads + 1) + heads]
        )
        copy.start()
        saves.append(copy)
        share = nn(mixed, w_out_ref[...])
        if turn == 1:
            share = share + got_ref[...].astype(wide)
        flat_refs[i][...] = share.astype(low)
    for copy in saves:
        copy.wait()


def attention_step(step, packs, prompt_len, core, joined, bias, seg_rows, seg_cols, w_out, got, mixed_all):
    _, rows, triple = joined.shape
    heads = bias.shape[0]
    width, model = w_out.shape
    half = rows // 2
    first, last = (0 if step < packs else 1), (1 if step > 0 else 0)
    steps = last - first + 1
    inside = pl.BlockSpec(memory_space=pltpu.VMEM)
    anywhere = pl.BlockSpec(memory_space=pl.ANY)
    in_specs = [pl.BlockSpec(memory_space=pltpu.SMEM), anywhere] + [inside] * 4
    args = [core, joined, bias, seg_rows, seg_cols, w_out]
    if last == 1:
        in_specs.append(inside)
        args.append(got)
    aliases = {}
    if mixed_all is not None:
        aliases = {len(args): 2 * steps}
        in_specs.append(anywhere)
        args.append(mixed_all)
    outs = kernel_call(
        functools.partial(attention_step_kernel, prompt_len, heads, first, last, step), 5, near=(2,), vmem=24,
        in_specs=in_specs,
        out_specs=[inside] * steps + [anywhere] * (steps + 1),
        out_shape=[jax.ShapeDtypeStruct((half, model), low)] * steps
        + [in_hbm((1, heads, half, rows), low)] * steps
        + [in_hbm((packs, rows, width), low)],
        scratch_shapes=[
            pltpu.VMEM((steps, rows, triple), low),
            pltpu.VMEM((steps, heads, half, rows), low),
            pltpu.VMEM((steps, half, width), low),
            pltpu.SemaphoreType.DMA((steps,)),
            pltpu.SemaphoreType.DMA((steps * (heads + 1),)),
        ],
        input_output_aliases=aliases,
        name="attention_step",
    )(*args)
    send, probs_send = (outs[0], outs[steps]) if first == 0 else (None, None)
    pair, probs_own = (outs[steps - 1], outs[2 * steps - 1]) if last == 1 else (None, None)
    return send, pair, probs_send, probs_own, outs[-1]


def feed_step_kernel(first, last, step, place_ref, rows_any, cot_any, gain_ref, *refs):
    refs = list(refs)
    turns = list(range(first, last + 1))
    sums = [refs[2 * i : 2 * i + 2] for i in range(len(turns))]
    refs = refs[2 * len(turns) :]
    if last == 1:
        got_ref, refs = refs[0], refs[1:]
    w_in_any, w_out_any, in_a, in_b, out_a, out_b = refs[:6]
    (rows_ref, cot_ref, normed_ref, active_ref, hidden_ref, result_ref, w_in_ref, w_out_ref,
     load_sems, save_sems) = refs[-10:]
    outs = refs[-10 - (3 + (1 if first == 0 else 0) + (4 if last == 1 else 0)) : -10]
    saved, rest = outs[:3], outs[3:]
    if first == 0:
        send_ref, rest = rest[0], rest[1:]
    if last == 1:
        middle_ref, grad_ref, gain_grad_ref, results_any = rest
    half = rows_ref.shape[0] // len(turns)
    half_rows = in_a.shape[0]
    core, side, part = place_ref[0], place_ref[1], place_ref[2]
    near = pl.ds(pl.multiple_of(part * half_rows, half_rows), half_rows)
    away = pl.ds(pl.multiple_of((1 - part) * half_rows, half_rows), half_rows)

    def block(turn):
        mine = jnp.bitwise_xor(core, 1 - turn)
        return step - turn, pl.ds(pl.multiple_of(mine * half, half), half)

    def span(index):
        return pl.ds(index * half, half)

    row_loads = [
        pltpu.make_async_copy(rows_any.at[*block(turn)], rows_ref.at[span(i)], load_sems.at[i])
        for i, turn in enumerate(turns)
    ]
    cot_loads = [
        pltpu.make_async_copy(cot_any.at[*block(turn)], cot_ref.at[span(i)], load_sems.at[2 + i])
        for i, turn in enumerate(turns)
    ]
    in_loads = [
        pltpu.make_async_copy(w_in_any, w_in_ref.at[side], load_sems.at[4]),
        pltpu.make_async_copy(in_a, w_in_ref.at[1 - side, near], load_sems.at[5]),
        pltpu.make_async_copy(in_b, w_in_ref.at[1 - side, away], load_sems.at[6]),
    ]
    out_loads = [
        pltpu.make_async_copy(w_out_any, w_out_ref.at[side], load_sems.at[7]),
        pltpu.make_async_copy(out_a, w_out_ref.at[1 - side, near], load_sems.at[8]),
        pltpu.make_async_copy(out_b, w_out_ref.at[1 - side, away], load_sems.at[9]),
    ]
    for copy in row_loads[::-1] + in_loads + cot_loads[::-1] + out_loads:
        copy.start()
    saves, kept = [], {}

    def save(index, place, source, target):
        copy = pltpu.make_async_copy(
            source, target.at[*block(turns[index])], save_sems.at[2 * place + index]
        )
        copy.start()
        saves.append(copy)

    def prepare(index):
        row_loads[index].wait()
        pair_ref, far_ref = sums[index]
        middle = rows_ref[span(index), :].astype(wide) + (
            pair_ref[...].astype(wide) + far_ref[...].astype(wide)
        )
        scale = lax.rsqrt(jnp.mean(middle * middle, axis=-1, keepdims=True) + epsilon)
        normed_ref[span(index), :] = (middle * scale * gain_ref[...]).astype(low)
        kept[index] = [middle, scale, None, None]
        save(index, 0, normed_ref.at[span(index)], saved[0])

    def expand(index, quarter):
        rows_at = span(index)
        inner = nn(normed_ref[rows_at, :], w_in_ref[quarter])
        share = 0.5 + 0.5 * lax.erf(inner * root_half)
        active = (inner * share).astype(low)
        slope = share + inner * (jnp.exp(-0.5 * inner * inner) * inv_root_tau)
        if quarter == 0 and index == len(turns) - 1:
            for copy in cot_loads + out_loads:
                copy.wait()
        hidden = (nt(cot_ref[rows_at, :], w_out_ref[quarter]) * slope).astype(low)
        active_ref[quarter, rows_at, :] = active
        hidden_ref[quarter, rows_at, :] = hidden
        feed_share = nn(active, w_out_ref[quarter])
        back_share = nt(hidden, w_in_ref[quarter])
        if quarter == 0:
            kept[index][2:] = [feed_share, back_share]
        else:
            kept[index][2] = kept[index][2] + feed_share
            kept[index][3] = kept[index][3] + back_share
            save(index, 1, active_ref.at[side, rows_at], saved[1])
            save(index, 2, hidden_ref.at[side, rows_at], saved[2])

    def finish_own(index):
        middle, scale, feed, back = kept[index]
        result_ref[...] = (middle + (feed + got_ref[:half, :].astype(wide))).astype(low)
        copy = pltpu.make_async_copy(result_ref, results_any.at[step - 1], save_sems.at[6])
        copy.start()
        saves.append(copy)
        upstream = back + got_ref[half:, :].astype(wide)
        scaled = upstream * gain_ref[...]
        inner = jnp.mean(scaled * middle, axis=-1, keepdims=True)
        grad = cot_ref[span(index), :].astype(wide) + scale * scaled - middle * (
            scale * scale * scale * inner
        )
        middle_ref[...] = grad
        grad_ref[...] = grad.astype(low)
        gain_grad_ref[...] = jnp.sum(upstream * middle * scale, axis=0, keepdims=True)

    def send_far(index):
        send_ref[:half, :] = kept[index][2].astype(low)
        send_ref[half:, :] = kept[index][3].astype(low)

    order = list(range(len(turns)))[::-1]
    prepare(order[0])
    for copy in in_loads:
        copy.wait()
    expand(order[0], 0)
    if len(order) == 2:
        prepare(order[1])
    expand(order[0], 1)
    if len(order) == 2:
        expand(order[1], 0)
    if last == 1:
        finish_own(order[0])
    if len(order) == 2:
        expand(order[1], 1)
    if first == 0:
        send_far(order[-1])
    for copy in saves:
        copy.wait()


def feed_step(step, packs, place, rows, cot, gain, sums, far_sums, own_pair, own_far, got,
              w_in, w_out, in_halves, out_halves, kept, results):
    _, row_count, model = rows.shape
    hidden = w_in.shape[1]
    half = row_count // 2
    first, last = (0 if step < packs else 1), (1 if step > 0 else 0)
    steps = last - first + 1
    inside = pl.BlockSpec(memory_space=pltpu.VMEM)
    anywhere = pl.BlockSpec(memory_space=pl.ANY)
    args = [place, rows, cot, gain]
    in_specs = [pl.BlockSpec(memory_space=pltpu.SMEM), anywhere, anywhere, inside]
    flats = ([sums, far_sums] if first == 0 else []) + ([own_pair, own_far, got] if last == 1 else [])
    args += flats
    in_specs += [inside] * len(flats)
    args += [w_in, w_out, *in_halves, *out_halves]
    in_specs += [anywhere] * 6
    aliases = {}
    if kept is not None:
        in_specs += [anywhere] * 3
        aliases = {len(args) + i: i for i in range(3)}
        args += list(kept)
    out_specs = [anywhere] * 3
    out_shape = [
        in_hbm((packs, row_count, model), low),
        in_hbm((packs, row_count, hidden), low),
        in_hbm((packs, row_count, hidden), low),
    ]
    if first == 0:
        out_specs.append(inside)
        out_shape.append(jax.ShapeDtypeStruct((row_count, model), low))
    if last == 1:
        if results is not None:
            in_specs.append(anywhere)
            aliases[len(args)] = len(out_shape) + 3
            args.append(results)
        out_specs += [inside] * 3 + [anywhere]
        out_shape += [
            in_hbm((half, model), wide),
            (jax.ShapeDtypeStruct if step < packs else in_hbm)((half, model), low),
            jax.ShapeDtypeStruct((1, model), wide),
            in_hbm((packs, half, model), low),
        ]
    outs = kernel_call(
        functools.partial(feed_step_kernel, first, last, step), 4 + 4 * steps, vmem=26,
        in_specs=in_specs,
        out_specs=out_specs,
        scratch_shapes=[
            pltpu.VMEM((steps * half, model), low),
            pltpu.VMEM((steps * half, model), low),
            pltpu.VMEM((steps * half, model), low),
            pltpu.VMEM((2, steps * half, hidden), low),
            pltpu.VMEM((2, steps * half, hidden), low),
            pltpu.VMEM((half, model), low),
            pltpu.VMEM((2, model, hidden), low),
            pltpu.VMEM((2, hidden, model), low),
            pltpu.SemaphoreType.DMA((10,)),
            pltpu.SemaphoreType.DMA((7,)),
        ],
        out_shape=out_shape,
        input_output_aliases=aliases,
        name="feed_step",
    )(*args)
    sent = outs[3] if first == 0 else None
    own = list(outs[-4:]) if last == 1 else [None] * 4
    return outs[:3], sent, own


def attention_back_kernel(
    heads, prompt_len, has_back, has_prev, core_ref, *refs,
):
    refs = list(refs)
    if has_back:
        own_ref, far_ref, w_out_ref, probs_own_ref, probs_far_ref, joined_ref = refs[:6]
        refs = refs[6:]
    w_joined_ref = refs.pop(0)
    if has_prev:
        prev_ref, got_ref, values_ref, grad_ref, gain_ref, gain_in_ref, head_in_ref = refs[:7]
        refs = refs[7:]
        if not has_back:
            other_gain_ref, refs = refs[0], refs[1:]
    outs = refs[-((5 if has_back else 0) + (3 if has_prev else 0)):]
    if has_prev:
        pair_ref, gain_out_ref, head_out_ref = outs[:3]
        outs = outs[3:]
        pair = (nn(prev_ref[...], w_joined_ref[...]) + got_ref[...].astype(wide)).astype(low)
        pair_ref[...] = pair
        top = head_in_ref.shape[0]
        values, upstream = values_ref[0].astype(wide), pair.astype(wide)
        grad, share = norm_back(upstream, gain_ref[...], values)
        gain_sum = gain_in_ref[...] + share
        gain_out_ref[...] = gain_sum
        grad = grad[:top] + jnp.where(core_ref[1] == 0, grad_ref[...], 0.0)
        head_sum = head_in_ref[...] + jnp.where(core_ref[0] == 0, grad, 0.0)
        if has_back:
            head_out_ref[...] = head_sum
        else:
            groups, group_rows, _ = head_out_ref.shape
            rows = prompt_len // groups
            head_out_ref[...] = jnp.zeros(head_out_ref.shape, low)
            for group in range(groups):
                head_out_ref[group, :rows, :] = head_sum[group * rows : (group + 1) * rows].astype(low)
                head_out_ref[group, rows : rows + 1, :] = gain_sum.astype(low)
                head_out_ref[group, rows + 1 : rows + 2, :] = other_gain_ref[...].astype(low)
    if not has_back:
        return
    send_ref, own_grads_ref, grads_ref, scores_ref, whole_ref = outs
    rows = joined_ref.shape[1]
    half = rows // 2
    width = w_out_ref.shape[0]
    size = width // heads
    core = core_ref[0]
    starts = [pl.multiple_of(core * half, half), pl.multiple_of((1 - core) * half, half)]
    ups, asks, asked = [], [], [[], []]
    for side, ref in enumerate((own_ref, far_ref)):
        whole_ref[0, pl.ds(starts[side], half), :] = ref[...]
        ups.append(nt(ref[...], w_out_ref[...]).astype(low))
        asks.append(joined_ref[0, pl.ds(starts[side], half), :width])
    grad_keys, grad_values = [], []
    for head in range(heads):
        cols = slice(head * size, (head + 1) * size)
        keys = joined_ref[0, :, width + head * size : width + (head + 1) * size]
        values = joined_ref[0, :, 2 * width + head * size : 2 * width + (head + 1) * size]
        grad_key, grad_value = None, None
        for side, probs_ref in enumerate((probs_own_ref, probs_far_ref)):
            probs = probs_ref[0, head]
            upstream = ups[side][:, cols]
            grad_probs = nt(upstream, values)
            spread = probs.astype(wide)
            inner = jnp.sum(spread * grad_probs, axis=-1, keepdims=True)
            grad_scores = (spread * (grad_probs - inner)).astype(low)
            scores_ref[0, head, pl.ds(starts[side], half), :] = grad_scores
            value_share = tn(upstream, probs)
            key_share = tn(asks[side][:, cols], grad_scores)
            grad_value = value_share if grad_value is None else grad_value + value_share
            grad_key = key_share if grad_key is None else grad_key + key_share
            asked[side].append(nn(grad_scores, keys))
        grad_values.append(grad_value.T)
        grad_keys.append(grad_key.T)
    rest = jnp.concatenate(grad_keys + grad_values, axis=1).astype(low)
    grads_ref[0, :, width:] = rest
    for side in range(2):
        grads_ref[0, pl.ds(starts[side], half), :width] = jnp.concatenate(asked[side], axis=1).astype(low)
    own_grads_ref[...] = grads_ref[0, pl.ds(starts[0], half), :]
    send_ref[...] = nn(grads_ref[0, pl.ds(starts[1], half), :], w_joined_ref[...]).astype(low)


def attention_back_step(step, packs, heads, prompt_len, other_gain, core, own, far, w_out, probs_own, probs_far, joined, w_joined,
                        prev, got, values, grad, gain, gain_sum, head_sum, kept):
    _, rows, triple = joined.shape
    width, model = w_out.shape
    half = rows // 2
    has_back, has_prev = step < packs, step > 0
    fixed = lambda t, c: (0, 0)
    flat = pl.BlockSpec((half, model), fixed)
    anywhere = pl.BlockSpec(memory_space=pl.ANY)
    in_specs, args, out_specs, out_shape, aliases = [], [core], [], [], {}
    if has_back:
        in_specs += [
            flat,
            flat,
            pl.BlockSpec((width, model), fixed),
            pl.BlockSpec((1, heads, half, rows), lambda t, c: (0, 0, 0, 0)),
            pl.BlockSpec((1, heads, half, rows), lambda t, c: (0, 0, 0, 0)),
            pl.BlockSpec((1, rows, triple), lambda t, c: (step, 0, 0)),
        ]
        args += [own, far, w_out, probs_own, probs_far, joined]
    in_specs.append(pl.BlockSpec((triple, model), fixed))
    args.append(w_joined)
    if has_prev:
        line = pl.BlockSpec((1, model), fixed)
        head = pl.BlockSpec(head_sum.shape, fixed)
        in_specs += [
            pl.BlockSpec((half, triple), fixed),
            flat,
            pl.BlockSpec((1, half, model), lambda t, c: (step - 1, c[0], 0)),
            head,
            line,
            line,
            head,
        ]
        args += [prev, got, values, grad, gain, gain_sum, head_sum]
        if has_back:
            head_out = in_hbm(head_sum.shape, wide)
        else:
            in_specs.append(line)
            args.append(other_gain)
            groups = Small.groups
            small = (groups, -(-(prompt_len // groups + 3) // 16) * 16, model)
            head, head_out = pl.BlockSpec(small, lambda t, c: (0, 0, 0)), jax.ShapeDtypeStruct(small, low)
        out_specs += [flat, line, head]
        out_shape += [
            jax.ShapeDtypeStruct((half, model), low),
            jax.ShapeDtypeStruct((1, model), wide),
            head_out,
        ]
    if has_back:
        if kept is not None:
            in_specs += [anywhere] * 3
            aliases = {len(args) + i: len(out_shape) + 2 + i for i in range(3)}
            args += list(kept)
        out_specs += [
            flat,
            pl.BlockSpec((half, triple), fixed),
            pl.BlockSpec((1, rows, triple), lambda t, c: (step, 0, 0)),
            pl.BlockSpec((1, heads, rows, rows), lambda t, c: (step, 0, 0, 0)),
            pl.BlockSpec((1, rows, model), lambda t, c: (step, 0, 0)),
        ]
        out_shape += [
            jax.ShapeDtypeStruct((half, model), low),
            in_hbm((half, triple), low),
            in_hbm((packs, rows, triple), low),
            in_hbm((packs, heads, rows, rows), low),
            in_hbm((packs, rows, model), low),
        ]
    outs = list(
        kernel_call(
            functools.partial(attention_back_kernel, heads, prompt_len, has_back, has_prev), 6,
            least=1000 if step == packs - 1 else 400000,
            grid_spec=pltpu.PrefetchScalarGridSpec(
                num_scalar_prefetch=1, grid=(1,), in_specs=in_specs, out_specs=out_specs
            ),
            out_shape=out_shape,
            input_output_aliases=aliases,
                name="attention_back_step",
        )(*args)
    )
    done, outs = (outs[:3], outs[3:]) if has_prev else ((None,) * 3, outs)
    send, own_grads, *kept = outs if has_back else (None, None)
    return done, send, own_grads, kept


def finish_kernel(packs, core_ref, rows_any, gain_ref, *refs):
    out_ref, rows_ref, sems = refs[-3:]
    half = rows_ref.shape[1]
    start = pl.multiple_of(core_ref[0] * half, half)
    copies = [
        pltpu.make_async_copy(rows_any.at[pack, pl.ds(start, half)], rows_ref.at[i], sems.at[i])
        for i, pack in enumerate(packs)
    ]
    for copy in copies:
        copy.start()
    for i, copy in enumerate(copies):
        copy.wait()
        pair_ref, far_ref, grad_ref = refs[3 * i : 3 * i + 3]
        upstream = pair_ref[...].astype(wide) + far_ref[...].astype(wide)
        grad, _ = norm_back(upstream, gain_ref[...], rows_ref[i].astype(wide))
        out_ref[i] = (grad_ref[...] + grad).astype(low)


def finish(packs, core, rows, gain, parts):
    half, model = parts[0][0].shape
    inside = pl.BlockSpec(memory_space=pltpu.VMEM)
    return kernel_call(
        functools.partial(finish_kernel, packs), 1.5 * len(packs), vmem=24,
        in_specs=[pl.BlockSpec(memory_space=pltpu.SMEM), pl.BlockSpec(memory_space=pl.ANY), inside]
        + [inside] * (3 * len(packs)),
        out_specs=inside,
        out_shape=jax.ShapeDtypeStruct((len(packs), half, model), low),
        scratch_shapes=[
            pltpu.VMEM((len(packs), half, model), low),
            pltpu.SemaphoreType.DMA((len(packs),)),
        ],
        name="finish",
    )(core, rows, gain, *[v for part in parts for v in part])


def middle_kernel(packs, place_ref, scores_any, rows_any, gain_ref, own_ref, far_ref, *refs):
    refs, (line_ref, ended_ref, out_any, scores_ref, values_ref, load_sems, save_sems) = refs[:-7], refs[-7:]
    heads = scores_ref.shape[0]
    half = values_ref.shape[1]
    core = place_ref[0]
    start = pl.multiple_of(core * half, half)
    value_loads = [
        pltpu.make_async_copy(rows_any.at[pack, pl.ds(start, half)], values_ref.at[i], load_sems.at[i])
        for i, pack in enumerate(packs)
    ]
    score_loads = [
        pltpu.make_async_copy(scores_any.at[:, head], scores_ref.at[head], load_sems.at[len(packs) + head])
        for head in range(heads)
    ]
    for copy in value_loads + score_loads:
        copy.start()
    saves = []
    for pack in range(own_ref.shape[0]):
        for side, ref in enumerate((own_ref, far_ref)):
            there = pl.ds(pl.multiple_of(jnp.bitwise_xor(core, side) * half, half), half)
            copy = pltpu.make_async_copy(ref.at[pack], out_any.at[pack, there], save_sems.at[2 * pack + side])
            copy.start()
            saves.append(copy)
    for i, copy in enumerate(value_loads):
        copy.wait()
        pair_ref, far_pair_ref, grad_ref = refs[3 * i : 3 * i + 3]
        upstream = pair_ref[...].astype(wide) + far_pair_ref[...].astype(wide)
        grad, _ = norm_back(upstream, gain_ref[...], values_ref[i].astype(wide))
        ended_ref[i] = (grad_ref[...] + grad).astype(low)
    for head, copy in enumerate(score_loads):
        copy.wait()
        line_ref[head] = diagonal_line(scores_ref.at[head])
    for copy in saves:
        copy.wait()


def middle_work(packs, place, scores, rows, gain, own, far, parts):
    count, heads, row_count, _ = scores.shape
    _, half, model = own.shape
    inside, anywhere = pl.BlockSpec(memory_space=pltpu.VMEM), pl.BlockSpec(memory_space=pl.ANY)
    return kernel_call(
        functools.partial(middle_kernel, packs), 12, vmem=40, least=1000,
        in_specs=[pl.BlockSpec(memory_space=pltpu.SMEM), anywhere, anywhere] + [inside] * (3 + 3 * len(packs)),
        out_specs=[inside, inside, anywhere],
        out_shape=[
            jax.ShapeDtypeStruct((heads, 1, 2 * row_count), wide),
            jax.ShapeDtypeStruct((len(packs), half, model), low),
            in_hbm((count, row_count, model), low),
        ],
        scratch_shapes=[
            pltpu.VMEM((heads, count, row_count, row_count), low),
            pltpu.VMEM((len(packs), half, model), low),
            pltpu.SemaphoreType.DMA((len(packs) + heads,)),
            pltpu.SemaphoreType.DMA((2 * count,)),
        ],
        name="middle_work",
    )(place, scores, rows, gain, own, far, *[v for part in parts for v in part])


def weave_kernel(core_ref, *refs):
    out_ref, rows_ref, woven_ref = refs[-3:]
    half = rows_ref.shape[0] // 2
    text = out_ref.shape[0]
    pack = 0
    for own_ref, far_ref in zip(refs[:-3:2], refs[1:-3:2]):
        for i in range(own_ref.shape[0]):
            for side, ref in enumerate((own_ref, far_ref)):
                start = pl.multiple_of(jnp.bitwise_xor(core_ref[0], side) * half, half)
                rows_ref[pl.ds(start, half), :] = ref[i].astype(wide)
            woven_ref[:, pack, :] = rows_ref[2 * half - text :, :]
            pack += 1
    out_ref[...] = woven_ref[...].astype(low)


def weave_halves(core, pairs, text):
    packs = sum(own.shape[0] for own, _ in pairs)
    _, half, model = pairs[0][0].shape
    inside = pl.BlockSpec(memory_space=pltpu.VMEM)
    return kernel_call(
        weave_kernel, 4, vmem=32, least=1000,
        in_specs=[pl.BlockSpec(memory_space=pltpu.SMEM)] + [inside] * (2 * len(pairs)),
        out_specs=inside,
        out_shape=jax.ShapeDtypeStruct((text, packs, model), low),
        scratch_shapes=[pltpu.VMEM((2 * half, model), wide), pltpu.VMEM((text, packs, model), wide)],
        name="weave_halves",
    )(core, *[v for pair in pairs for v in pair])


def weight_kernel(pairs, split, where_ref, *refs):
    if split:
        keep_ref, send_ref, total_ref = refs[-3:]
    else:
        whole_ref, total_ref = refs[-2:]
    column = 0
    for i in range(pairs):
        right = refs[2 * i + 1][...]
        total_ref[:, column : column + right.shape[1]] = tn(refs[2 * i][...], right)
        column += right.shape[1]
    if not split:
        whole_ref[...] = total_ref[...].astype(low)
        return
    count, block, _ = keep_ref.shape
    side = jnp.bitwise_and(where_ref[0], 1)
    for i in range(count):
        for ref, chosen in ((keep_ref, side), (send_ref, 1 - side)):
            start = pl.multiple_of((2 * i + chosen) * block, 8)
            ref[i] = total_ref[pl.ds(start, block), :].astype(low)


def weight_shares(where, count, pairs, split):
    rows, model = pairs[0][0].shape
    widths = [right.shape[1] for _, right in pairs]
    turns, width = 2, sum(widths)
    block = model // count
    in_specs = []
    for n in widths:
        in_specs += [
            pl.BlockSpec((rows, model // turns), lambda t, w: (0, t)),
            pl.BlockSpec((rows, n), lambda t, w: (0, 0)),
        ]
    if split:
        out_specs = [pl.BlockSpec((count // 2 // turns, block, width), lambda t, w: (t, 0, 0))] * 2
        out_shape = [jax.ShapeDtypeStruct((count // 2, block, width), low)] * 2
    else:
        out_specs = pl.BlockSpec((model // turns, width), lambda t, w: (t, 0))
        out_shape = in_hbm((model, width), low)
    return kernel_call(
        functools.partial(weight_kernel, len(pairs), split), 6, vmem=26,
        grid_spec=pltpu.PrefetchScalarGridSpec(
            num_scalar_prefetch=1,
            grid=(turns,),
            in_specs=in_specs,
            out_specs=out_specs,
            scratch_shapes=[pltpu.VMEM((model // turns, width), wide)],
        ),
        out_shape=out_shape,
        name="weight_shares",
    )(where, *[value for pair in pairs for value in pair])


def fold_kernel(count, where_ref, *refs):
    ins, outs = refs[:count], refs[count:]
    group = outs[0].shape[0]
    for flip, out_ref in enumerate(outs):
        for piece in range(group):
            spot = jnp.bitwise_xor(where_ref[0], flip)
            spot = spot * group + piece if len(outs) == 4 else piece * 2 + spot
            total = ins[0][spot].astype(wide)
            for ref in ins[1:]:
                total = total + ref[spot].astype(wide)
            out_ref[piece] = total.astype(out_ref.dtype)


def fold(where, parts, cuts):
    whole, block, width = parts[0].shape
    shape = (whole // cuts, block, width)
    inside = pl.BlockSpec(memory_space=pltpu.VMEM)
    return kernel_call(
        functools.partial(fold_kernel, len(parts)), 1.5, vmem=24,
        in_specs=[pl.BlockSpec(memory_space=pltpu.SMEM)] + [inside] * len(parts),
        out_specs=[inside] * cuts,
        out_shape=[jax.ShapeDtypeStruct(shape, low)] * cuts,
        name="fold",
    )(where, *parts)


def unfold_kernel(count, cuts, *refs):
    ins, outs = refs[:count], refs[count:]
    total = ins[0][0].astype(wide)
    for ref in ins[1:]:
        total = total + ref[0].astype(wide)
    for (start, width, turned), out_ref in zip(cuts, outs):
        piece = total[:, start : start + width]
        out_ref[...] = piece.T if turned else piece


def unfold(parts, cuts):
    block = parts[0].shape[1]
    inside = pl.BlockSpec(memory_space=pltpu.VMEM)
    return kernel_call(
        functools.partial(unfold_kernel, len(parts), cuts), 1.5,
        in_specs=[inside] * len(parts),
        out_specs=[inside] * len(cuts),
        out_shape=[
            jax.ShapeDtypeStruct((width, block) if turned else (block, width), wide)
            for _, width, turned in cuts
        ],
        name="unfold",
    )(*parts)


def joint_fold_kernel(spot, where_ref, keep_ref, got_ref, mine_ref, near_ref, rel_ref, *refs):
    outs, total_ref = refs[:4], refs[4]
    block = keep_ref.shape[1]
    group = keep_ref.shape[0] // 4
    for flip, out_ref in enumerate(outs):
        chosen = jnp.bitwise_xor(where_ref[0], flip)
        for piece in range(group):
            total = keep_ref[chosen * group + piece].astype(wide) + got_ref[chosen * group + piece].astype(wide)
            out_ref[piece * block : (piece + 1) * block, :] = total.astype(low)
        total_ref[...] = mine_ref[chosen].astype(wide) + near_ref[chosen].astype(wide)
        total_ref[spot : spot + 1, :] = rel_ref[...]
        out_ref[group * block :, :] = total_ref[...].astype(low)


def joint_fold(where, parts, smalls, rel, spot):
    whole, block, width = parts[0].shape
    rows = smalls[0].shape[1]
    shape = (whole // 4 * block + rows, width)
    inside = pl.BlockSpec(memory_space=pltpu.VMEM)
    return kernel_call(
        functools.partial(joint_fold_kernel, spot), 2,
        in_specs=[pl.BlockSpec(memory_space=pltpu.SMEM)] + [inside] * 5,
        out_specs=[inside] * 4,
        out_shape=[jax.ShapeDtypeStruct(shape, low)] * 4,
        scratch_shapes=[pltpu.VMEM((rows, width), wide)],
        name="joint_fold",
    )(where, *parts, *smalls, rel)


def joint_unfold_kernel(cuts, *refs):
    ins, outs = refs[:4], refs[4:]
    total = ins[0][...].astype(wide)
    for ref in ins[1:]:
        total = total + ref[...].astype(wide)
    small = outs[-1].shape[0]
    outs[-1][...] = total[-small:].astype(low)
    for (start, width, turned), out_ref in zip(cuts, outs):
        piece = total[:-small, start : start + width]
        out_ref[...] = piece.T if turned else piece


def joint_unfold(parts, cuts, rows):
    block = parts[0].shape[0] - rows
    inside = pl.BlockSpec(memory_space=pltpu.VMEM)
    return kernel_call(
        functools.partial(joint_unfold_kernel, cuts), 1.5,
        in_specs=[inside] * 4,
        out_specs=[inside] * (len(cuts) + 1),
        out_shape=[
            jax.ShapeDtypeStruct((width, block) if turned else (block, width), wide)
            for _, width, turned in cuts
        ]
        + [jax.ShapeDtypeStruct((rows, parts[0].shape[1]), low)],
        name="joint_unfold",
    )(*parts)


def tie(*values):
    return lax.optimization_barrier(values)


def stages_of(count):
    bits = bits_of(count)
    rest = bits[1:][::-1]
    return [bits[:1]] + [rest[i : i + 2] for i in range(0, len(rest), 2)]


class Scatter:
    def __init__(self, keep, send, cuts):
        self.bits, self.cuts = bits_of(lax.axis_size("dp"))[1:], cuts
        self.parts = [keep, swap(send, "dp", 1)]

    def step(self):
        if self.cuts == 4:
            bit, self.bits = self.bits[-2], self.bits[:-2]
        else:
            bit, self.bits = self.bits[0], self.bits[1:]
        where = ((lax.axis_index("dp") // bit) % self.cuts).astype(jnp.int32).reshape(1)
        own, *sends = fold(where, self.parts, self.cuts)
        self.parts = [own] + [swap(v, "dp", bit * (flip + 1)) for flip, v in enumerate(sends)]

    def end(self, pieces):
        while self.bits:
            self.step()
        return unfold(self.parts, pieces)


def look_up(prompt_ids, table, prompt_delta):
    prompt_len = prompt_ids.shape[0]
    table_rows, model = table.shape
    groups = 2
    part = -(-prompt_len // (16 * groups)) * 16
    dp_index, mp_index = lax.axis_index("dp"), lax.axis_index("mp") % groups
    padded = jnp.pad(prompt_ids, (0, part * groups - prompt_len), constant_values=-1)
    ids = lax.dynamic_slice_in_dim(padded, mp_index * part, part)
    size, block = prompt_delta.shape[0], part * model
    line = jnp.pad(prompt_delta, (block, block))
    start = jnp.clip(block + mp_index * block - dp_index * size, 0, block + size)
    placed = lax.dynamic_slice_in_dim(line, start, block).reshape(part, model)
    local = jnp.where(ids < 0, -1, ids - dp_index * table_rows)
    if table_rows % 16 == 0:
        return look_up_rows(local, table, placed)
    selector = (local[:, None] == jnp.arange(table_rows, dtype=jnp.int32)[None, :]).astype(low)
    return (jnp.dot(selector, table, preferred_element_type=wide) + placed).astype(low)


def own_half(weight):
    part = lax.axis_index("dp") % 2
    halves = weight.reshape(2, weight.shape[0] // 2, weight.shape[1])
    return lax.dynamic_index_in_dim(halves, part, 0, keepdims=False)


class Small:
    groups = 4

    def __init__(self, total, prompt_len):
        self.total, self.share = total, prompt_len // self.groups
        self.mp_bits = bits_of(lax.axis_size("mp"))
        self.hop_mp()

    def hop_mp(self):
        bit, self.mp_bits = self.mp_bits[0], self.mp_bits[1:]
        self.keep, self.got = self.total, swap(self.total, "mp", bit)

    def land(self):
        self.total = (self.keep.astype(wide) + self.got.astype(wide)).astype(low)

    def join(self, tail, rel):
        self.rel = rel
        row = jnp.pad(rel.reshape(1, -1), ((0, 0), (0, self.keep.shape[2] - rel.size)))
        high, tail.bits = tail.bits[-2], tail.bits[:-2]
        where = ((lax.axis_index("dp") // high) % 4).astype(jnp.int32).reshape(1)
        self.block = tail.parts[0].shape[1]
        own, *sends = joint_fold(where, tail.parts, (self.keep, self.got), row, self.share + 2)
        self.parts = [own] + [swap(v, "dp", high * (flip + 1)) for flip, v in enumerate(sends)]

    def split(self, tail, cuts):
        rows = self.keep.shape[1]
        if not tail.bits:
            *results, self.total = joint_unfold(self.parts, cuts, rows)
            return results
        tail.parts = [v[:-rows].reshape(-1, self.block, v.shape[1]) for v in self.parts]
        self.total = sum(v[-rows:].astype(wide) for v in self.parts).astype(low)
        return tail.end(cuts)

    def results(self):
        dp_count, dp_index = lax.axis_size("dp"), lax.axis_index("dp")
        total = self.total
        for bit in bits_of(dp_count)[:-2]:
            total = total.astype(low)
            total = total.astype(wide) + swap(total, "dp", bit).astype(wide)
        share, model = self.share, total.shape[1]
        inside = dp_count // self.groups
        size = share * model // inside
        prompt_grad = lax.dynamic_slice_in_dim(total[:share].reshape(-1), (dp_index % inside) * size, size)
        width = model // dp_count
        gains = lax.dynamic_slice_in_dim(total[share : share + 2], dp_index * width, width, axis=1)
        piece = self.rel.size // dp_count
        rel_out = lax.dynamic_slice_in_dim(total[share + 2], dp_index * piece, piece)
        return prompt_grad, gains[0], gains[1], rel_out.reshape(-1, self.rel.shape[1])


def body(
    tokens, cotangent, segment_ids, prompt_ids, rel_buckets, table, prompt_delta, norm1_gain,
    w_query, w_key, w_value, w_output, rel_bias, norm2_gain, w_inner, w_outer,
):
    prompt_len = prompt_ids.shape[0]
    packs, rows, model = cotangent.shape
    bucket_count, heads = rel_bias.shape
    width = w_query.shape[1]
    groups = lax.axis_size("dp")
    mp_bits = bits_of(lax.axis_size("mp"))
    mp_index = lax.axis_index("mp").astype(jnp.int32)
    place = jnp.stack([mp_index % 2, (mp_index // 2) % 2, (lax.axis_index("dp") % 2).astype(jnp.int32)])
    gain1, gain2 = norm1_gain[None, :], norm2_gain[None, :]
    w_q, w_k, w_v = w_query.T, w_key.T, w_value.T

    in_near = swap(own_half(w_inner), "mp", 2)
    total = look_up(prompt_ids, table, prompt_delta)

    w_joined = jnp.concatenate([w_q, w_k, w_v], axis=0)
    bucket_hot = (
        rel_buckets[:, None] == jnp.arange(bucket_count, dtype=jnp.int32)[None, :]
    ).astype(wide)
    bucket_hot = jnp.pad(bucket_hot, ((0, 1), (0, 0)))
    turned = jnp.roll(bucket_hot, -(rows - 1), axis=0)
    bias_line = jnp.dot(turned, rel_bias, precision=highest).T
    marks = jnp.pad(segment_ids, ((0, 0), (prompt_len, 0)), constant_values=-1)
    seg_rows, seg_cols = marks.T, marks

    texts, half_packs = [], packs // 2
    for hop, bit in enumerate(bits_of(groups)):
        got = swap(total, "dp", bit)
        if hop == 0:
            bias = bias_grid_of(bias_line[:, None, :])
            got, bias, seg_rows, seg_cols = tie(got, bias, seg_rows, seg_cols)
        if hop == 1:
            texts = text_projections(0, half_packs, rows, tokens, gain1, w_joined, texts)
            got, *texts = tie(got, *texts)
        if hop == 2:
            texts = text_projections(half_packs, packs - half_packs, rows, tokens, gain1, w_joined, texts)
            got, *texts = tie(got, *texts)
            got, in_near = tie(got, in_near)
            in_away = swap(in_near, "dp", 1)
            out_near = swap(own_half(w_outer), "mp", 2)
        total = (total.astype(wide) + got.astype(wide)).astype(low)
    whole_rows, normed1, joined = texts
    pieces = jnp.stack([total, swap(total, "mp", 1)])
    whole_rows, normed1, joined = add_prompt(
        place[:1], pieces, gain1, w_joined, whole_rows, normed1, joined
    )

    pairs, fars, pairs_far, fars_far, probs_far, probs_own, mixed, got = [], [], [], [], [], [], None, None

    def attend(step):
        nonlocal mixed, got, place, in_away, out_near, out_away
        send, pair, probs_send, probs_pair, mixed = attention_step(
            step, packs, prompt_len, place, joined, bias, seg_rows, seg_cols, w_output, got, mixed
        )
        if step == 0:
            place, out_near, send = tie(place, out_near, send)
            out_away = swap(out_near, "dp", 1)
        else:
            place, pair = tie(place, pair)
        if step == 1:
            place, in_away = tie(place, in_away)
        if send is not None:
            probs_far.append(probs_send)
            got = swap(send, "mp", 1)
        if pair is not None:
            probs_own.append(probs_pair)
            pairs.append(pair)
            fars.append(swap(pair, "mp", 2))
            pairs_far.append(swap(pair, "mp", 1))
            fars_far.append(swap(fars[-1], "mp", 1))

    out_away = None

    def arrive(pack):
        nonlocal place
        place, fars[pack], pairs_far[pack], fars_far[pack] = tie(
            place, fars[pack], pairs_far[pack], fars_far[pack]
        )

    kept, sent, results, grads_wide, grads_low = None, None, None, [], []
    gain2_sum, none = 0.0, [None]
    back_kept, prev, got = None, None, None
    gain1_sum, head_sum = jnp.zeros((1, model), wide), jnp.zeros((128, model), wide)
    text_rows, pairs_back = [], []

    def feed(step):
        nonlocal kept, sent, results, gain2_sum, place
        kept, new_sent, done = feed_step(
            step, packs, place, whole_rows, cotangent, gain2,
            (pairs_far + none)[step], (fars_far + none)[step],
            (none + pairs)[step], (none + fars)[step], sent,
            w_inner, w_outer, (in_near, in_away), (out_near, out_away), kept, results,
        )
        if step < packs:
            place, new_sent = tie(place, new_sent)
            sent = swap(new_sent, "mp", 1)
        else:
            place, done[1] = tie(place, done[1])
        if step > 0:
            grads_wide.append(done[0])
            grads_low.append((done[1], swap(done[1], "mp", 1)))
            gain2_sum, results = gain2_sum + done[2], done[3]

    def back(step):
        nonlocal back_kept, prev, got, gain1_sum, head_sum, place
        live = step < packs
        done, send, own_grads, back_new = attention_back_step(
            step, packs, heads, prompt_len, gain2_sum, place, *(grads_low[step] if live else none * 2), w_output,
            probs_own[step] if live else None, probs_far[step] if live else None, joined, w_joined,
            prev, got, whole_rows, grads_wide[step - 1] if step else None, gain1, gain1_sum, head_sum,
            back_kept,
        )
        if live:
            place, send = tie(place, send)
            back_kept, prev, got = back_new, own_grads, swap(send, "mp", 1)
        if step > 0:
            pair, gain1_sum, head_sum = done
            pairs_back.append([pair, swap(pair, "mp", 2)])

    def near(pack):
        nonlocal place
        place, pairs_far[pack] = tie(place, pairs_far[pack])

    def meet(pack):
        nonlocal place
        place, grads_low[pack] = tie(place, grads_low[pack])

    def end(*ended):
        nonlocal place
        rows_low = finish(ended, place, whole_rows, gain1, [(*pairs_back[p], grads_wide[p]) for p in ended])
        place, rows_low = tie(place, rows_low)
        text_rows.append((rows_low, swap(rows_low, "mp", 1)))

    def flat(value):
        return value.reshape(packs * rows, -1)

    for step in range(packs):
        attend(step)
    place, out_away = tie(place, out_away)
    arrive(0)
    feed(0)
    attend(packs)
    arrive(1)
    near(2)
    feed(1)
    for step in range(2, packs):
        arrive(step)
        meet(step - 2)
        if step + 1 < packs:
            near(step + 1)
        feed(step)
        back(step - 2)
    meet(packs - 2)
    feed(packs)
    normed2, active, hidden = kept
    where = lax.axis_index("dp").astype(jnp.int32).reshape(1)
    where, place = tie(where, place)
    inner_shares = weight_shares(where, groups, [(flat(normed2), flat(hidden))], True)
    place, inner_shares = tie(place, inner_shares)
    inner = Scatter(*inner_shares, 2)
    where, place = tie(where, place)
    outer_shares = weight_shares(where, groups, [(flat(cotangent), flat(active))], True)
    place, outer_shares = tie(place, outer_shares)
    outer = Scatter(*outer_shares, 2)
    meet(packs - 1)
    back(packs - 2)
    far_results = swap(results, "mp", 1)
    place, far_results, pairs_back[0], inner.parts = tie(place, far_results, pairs_back[0], inner.parts)
    inner.step()
    back(packs - 1)
    place, pairs_back[1], inner.parts, outer.parts = tie(place, pairs_back[1], inner.parts, outer.parts)
    inner.step()
    outer.step()
    place, inner.parts[0], outer.parts[0] = tie(place, inner.parts[0], outer.parts[0])
    grad_joined, scores, grad_rows = back_kept
    where, place = tie(where, place)
    tail_shares = weight_shares(
        where, groups, [(flat(normed1), flat(grad_joined)), (flat(grad_rows), flat(mixed))], True
    )
    place, *tail_shares = tie(place, *tail_shares)
    tail = Scatter(*tail_shares, 4)
    side_one = (mp_index // 2) % 2 == 1
    gain2_sum = jnp.where(side_one, 0.0, gain2_sum)
    back(packs)
    place, head_sum = tie(place, head_sum)
    small = Small(head_sum, prompt_len)
    place, outer.parts = tie(place, outer.parts)
    outer.step()
    place, outer.parts[0] = tie(place, outer.parts[0])
    small.land()
    small.hop_mp()
    early = list(range(packs - 1))
    line, rows_low, out = middle_work(
        early, place, scores, whole_rows, gain1, results, far_results,
        [(*pairs_back[p], grads_wide[p]) for p in early],
    )
    place, line, rows_low = tie(place, line, rows_low)
    text_rows.append((rows_low, swap(rows_low, "mp", 1)))
    rel_share = jnp.einsum("ht,tb->bh", line[:, 0, :], turned, precision=highest)
    place, rel_share, tail.parts, small.got = tie(place, rel_share, tail.parts, small.got)
    small.join(tail, rel_share)
    place, inner.parts, outer.parts = tie(place, inner.parts, outer.parts)
    whole_width = ((0, w_inner.shape[1], False),)
    (inner_grad,), (outer_grad,) = inner.end(whole_width), outer.end(whole_width)
    place, inner_grad, outer_grad = tie(place, inner_grad, outer_grad)
    end(packs - 1)
    place, text_rows[-1] = tie(place, text_rows[-1])
    grad_tokens = weave_halves(place, text_rows, rows - prompt_len)
    grad_tokens, small.parts = tie(grad_tokens, small.parts)
    grad_tokens = jnp.transpose(grad_tokens, (1, 0, 2))
    query_grad, key_grad, value_grad, output_grad = small.split(
        tail, tuple((i * width, width, i == 3) for i in range(4))
    )
    prompt_grad, gain1_grad, gain2_grad, rel_grad = small.results()
    return (
        out, grad_tokens, prompt_grad, gain1_grad, query_grad, key_grad, value_grad, output_grad,
        rel_grad, gain2_grad, inner_grad, outer_grad.T,
    )


def solution(mesh):
    in_specs = (
        P("dp", None, None),
        P("dp", None, None),
        P("dp", None),
        P(),
        P(),
        P("dp", None),
        P("dp"),
        P(),
        P(None, "mp"),
        P(None, "mp"),
        P(None, "mp"),
        P("mp", None),
        P(None, "mp"),
        P(),
        P(None, "mp"),
        P("mp", None),
    )
    out_specs = (
        P("dp", None, None),
        P("dp", None, None),
        P("dp"),
        P("dp"),
        P("dp", "mp"),
        P("dp", "mp"),
        P("dp", "mp"),
        P("mp", "dp"),
        P("dp", "mp"),
        P("dp"),
        P("dp", "mp"),
        P("mp", "dp"),
    )
    return jax.shard_map(body, mesh=mesh, in_specs=in_specs, out_specs=out_specs, check_vma=False)
```

```python
import functools

import jax
import jax.numpy as jnp
from jax import lax
from jax.experimental import pallas as pl
from jax.experimental.pallas import tpu as pltpu
from jax.sharding import PartitionSpec as P

epsilon = 1e-06
blocked = -1000000000.0
highest = lax.Precision.HIGHEST
low = jnp.bfloat16
wide = jnp.float32
root_half = 0.7071067811865476
inv_root_tau = 0.3989422804014327


def nn(left, right):
    return lax.dot_general(left, right, (((1,), (0,)), ((), ())), preferred_element_type=wide)


def nt(left, right):
    return lax.dot_general(left, right, (((1,), (1,)), ((), ())), preferred_element_type=wide)


def tn(left, right):
    return lax.dot_general(left, right, (((0,), (0,)), ((), ())), preferred_element_type=wide)


def params(mebibytes):
    return pltpu.CompilerParams(vmem_limit_bytes=mebibytes * 1024 * 1024)


def in_hbm(shape, dtype):
    return pltpu.HBM(shape, dtype)


def kernel_call(kernel, micros, vmem=16, near=(), least=400000, **rest):
    cost = pl.CostEstimate(flops=0, bytes_accessed=int(micros * 3.6e6), transcendentals=0)
    call = pl.pallas_call(kernel, cost_estimate=cost, compiler_params=params(vmem), **rest)

    def run(*args):
        return call(
            *[
                pltpu.with_memory_space_constraint(v, pltpu.HBM) if (v.size >= least or v.ndim == 4) and i not in near else v
                for i, v in enumerate(args)
            ]
        )

    return run


def swap(value, axis, bit):
    count = lax.axis_size(axis)
    return lax.ppermute(value, axis, [(i, i ^ bit) for i in range(count)])


def bits_of(count):
    return [1 << i for i in range(count.bit_length() - 1)]


def rms_norm(values, gain):
    return values * lax.rsqrt(jnp.mean(values * values, axis=-1, keepdims=True) + epsilon) * gain


def norm_back(upstream, gain, values):
    scale = lax.rsqrt(jnp.mean(values * values, axis=-1, keepdims=True) + epsilon)
    scaled = upstream * gain
    inner = jnp.mean(scaled * values, axis=-1, keepdims=True)
    grad = scale * scaled - values * (scale * scale * scale * inner)
    return grad, jnp.sum(upstream * values * scale, axis=0, keepdims=True)


def bias_kernel(line_ref, grid_ref):
    rows = grid_ref.shape[1]
    spread = jnp.broadcast_to(line_ref[0], (rows, 2 * rows))
    grid_ref[0] = pltpu.roll(spread, 0, 1, stride=1, stride_axis=0)[:, :rows]


def bias_grid_of(line):
    heads, _, double = line.shape
    rows = double // 2
    return kernel_call(
        bias_kernel, 2,
        grid=(heads,),
        in_specs=[pl.BlockSpec((1, 1, double), lambda h: (h, 0, 0))],
        out_specs=pl.BlockSpec((1, rows, rows), lambda h: (h, 0, 0)),
        out_shape=jax.ShapeDtypeStruct((heads, rows, rows), wide),
        name="bias_grid",
    )(line)


def diagonal_line(grid_ref):
    packs, rows, _ = grid_ref.shape
    lanes = 128
    count = rows // lanes
    blocks = []
    for block in range(2 * count):
        total = jnp.zeros((lanes, lanes), wide)
        for band in range(count):
            column = (block + band) % (2 * count)
            if column < count:
                for pack in range(packs):
                    total = total + grid_ref[
                        pack, band * lanes : (band + 1) * lanes, column * lanes : (column + 1) * lanes
                    ].astype(wide)
        blocks.append(total)
    held = jnp.concatenate(blocks, axis=1)
    total = held[:8]
    for slab in range(1, lanes // 8):
        total = total + pltpu.roll(held[8 * slab : 8 * slab + 8], 2 * rows - 8 * slab, 1)
    line = total[0:1]
    for row in range(1, 8):
        line = line + pltpu.roll(total[row : row + 1], 2 * rows - row, 1)
    return line


def shifted_text_kernel(tokens_ref, gain_ref, weight_ref, *refs):
    rows_ref, normed_ref, joined_ref, wide_ref = refs[-4:]
    rows = rows_ref.shape[1]
    prompt_len = rows - tokens_ref.shape[1]
    wide_ref[:prompt_len, :] = jnp.zeros((prompt_len, wide_ref.shape[1]), wide)
    wide_ref[prompt_len:, :] = tokens_ref[0].astype(wide)
    values = wide_ref[...]
    rows_ref[0] = values.astype(low)
    normed = rms_norm(values, gain_ref[...]).astype(low)
    normed_ref[0] = normed
    joined_ref[0] = nt(normed, weight_ref[...]).astype(low)


def text_projections(first, count, rows, tokens, gain, weight, kept):
    packs, text, model = tokens.shape
    triple = weight.shape[0]
    fixed = lambda p: (0, 0)
    moving = lambda p: (first + p, 0, 0)
    return kernel_call(
        shifted_text_kernel, 1.2 * count,
        grid=(count,),
        in_specs=[
            pl.BlockSpec((1, text, model), moving),
            pl.BlockSpec((1, model), fixed),
            pl.BlockSpec((triple, model), fixed),
        ]
        + [pl.BlockSpec(memory_space=pl.ANY)] * len(kept),
        out_specs=[
            pl.BlockSpec((1, rows, model), moving),
            pl.BlockSpec((1, rows, model), moving),
            pl.BlockSpec((1, rows, triple), moving),
        ],
        out_shape=[
            in_hbm((packs, rows, model), low),
            in_hbm((packs, rows, model), low),
            in_hbm((packs, rows, triple), low),
        ],
        scratch_shapes=[pltpu.VMEM((rows, model), wide)],
        input_output_aliases={3 + i: i for i in range(len(kept))},
        name="text_projections",
    )(tokens, gain, weight, *kept)


def prompt_kernel(place_ref, pieces_ref, gain_ref, weight_ref, rows_in, normed_in, joined_in, rows_out, normed_out, joined_out,
                  prompt_ref, rows_ref, normed_ref, joined_ref, load_sems, save_sems):
    count, part, _ = pieces_ref.shape
    packs = rows_ref.shape[0]
    top = count * part
    held = (rows_ref, normed_ref, joined_ref)
    loads = [
        pltpu.make_async_copy(source.at[:, pl.ds(0, top)], target, load_sems.at[i])
        for i, (source, target) in enumerate(zip((rows_in, normed_in, joined_in), held))
    ]
    for copy in loads:
        copy.start()
    for k in range(count):
        start = pl.multiple_of(jnp.bitwise_xor(place_ref[0], k) * part, part)
        prompt_ref[pl.ds(start, part), :] = pieces_ref[k]
    prompt = prompt_ref[...]
    normed = rms_norm(prompt.astype(wide), gain_ref[...]).astype(low)
    joined = nt(normed, weight_ref[...]).astype(low)
    saves = []
    for i, (value, target) in enumerate(zip((prompt, normed, joined), (rows_out, normed_out, joined_out))):
        loads[i].wait()
        for pack in range(packs):
            held[i][pack] = held[i][pack] + value
        copy = pltpu.make_async_copy(held[i], target.at[:, pl.ds(0, top)], save_sems.at[i])
        copy.start()
        saves.append(copy)
    for copy in saves:
        copy.wait()


def add_prompt(place, pieces, gain, weight, rows, normed, joined):
    packs, _, model = rows.shape
    triple = weight.shape[0]
    count, part, _ = pieces.shape
    top = count * part
    inside = pl.BlockSpec(memory_space=pltpu.VMEM)
    anywhere = pl.BlockSpec(memory_space=pl.ANY)
    return kernel_call(
        prompt_kernel, 2.5,
        in_specs=[pl.BlockSpec(memory_space=pltpu.SMEM)] + [inside] * 3 + [anywhere] * 3,
        out_specs=[anywhere] * 3,
        out_shape=[
            in_hbm(rows.shape, low),
            in_hbm(normed.shape, low),
            in_hbm(joined.shape, low),
        ],
        scratch_shapes=[
            pltpu.VMEM((top, model), low),
            pltpu.VMEM((packs, top, model), low),
            pltpu.VMEM((packs, top, model), low),
            pltpu.VMEM((packs, top, triple), low),
            pltpu.SemaphoreType.DMA((3,)),
            pltpu.SemaphoreType.DMA((3,)),
        ],
        input_output_aliases={4: 0, 5: 1, 6: 2},
        name="add_prompt",
    )(place, pieces, gain, weight, rows, normed, joined)


def look_up_kernel(ids_ref, table_any, target_ref, placed_ref, out_ref, blocks_ref, sems):
    part = out_ref.shape[0]
    limit = table_any.shape[0]

    def each(act):
        for row in range(part):
            local = ids_ref[row]

            @pl.when((local >= 0) & (local < limit))
            def _():
                start = pl.multiple_of(jnp.left_shift(jnp.right_shift(local, 4), 4), 16)
                act(
                    pltpu.make_async_copy(
                        table_any.at[pl.ds(start, 16)], blocks_ref.at[pl.ds(16 * row, 16)], sems.at[row]
                    )
                )

    blocks_ref[...] = jnp.zeros(blocks_ref.shape, low)
    each(lambda copy: copy.start())
    position = lax.broadcasted_iota(jnp.int32, (part, 16 * part), 1)
    chosen = jnp.where(position == target_ref[...], 1.0, 0.0).astype(low)
    each(lambda copy: copy.wait())
    out_ref[...] = (nn(chosen, blocks_ref[...]) + placed_ref[...]).astype(low)


def look_up_rows(ids, table, placed):
    part, model = placed.shape
    inside = pl.BlockSpec(memory_space=pltpu.VMEM)
    own = (ids >= 0) & (ids < table.shape[0])
    target = jnp.where(own, 16 * jnp.arange(part, dtype=jnp.int32) + ids % 16, -1)[:, None]
    return kernel_call(
        look_up_kernel, 2.5,
        in_specs=[pl.BlockSpec(memory_space=pltpu.SMEM), pl.BlockSpec(memory_space=pl.ANY), inside, inside],
        out_specs=inside,
        out_shape=jax.ShapeDtypeStruct((part, model), low),
        scratch_shapes=[pltpu.VMEM((16 * part, model), low), pltpu.SemaphoreType.DMA((part,))],
        name="look_up",
    )(ids, table, target, placed)


def attention_step_kernel(
    prompt_len, heads, first, last, step, core_ref, joined_any, bias_ref, seg_rows_ref, seg_cols_ref, w_out_ref, *refs,
):
    turns = list(range(first, last + 1))
    refs = list(refs)
    if last == 1:
        got_ref, refs = refs[0], refs[1:]
    joined_ref, probs_ref, mixed_ref, load_sems, save_sems = refs[-5:]
    outs = refs[-5 - 2 * len(turns) - 1 : -5]
    flat_refs, probs_outs, mixed_any = outs[: len(turns)], outs[len(turns) : -1], outs[-1]
    rows = joined_ref.shape[1]
    half = rows // 2
    width = w_out_ref.shape[0]
    size = width // heads
    loads = [
        pltpu.make_async_copy(joined_any.at[step - turn], joined_ref.at[i], load_sems.at[i])
        for i, turn in enumerate(turns)
    ]
    for copy in loads:
        copy.start()
    saves = []
    col_pos = lax.broadcasted_iota(jnp.int32, (half, rows), 1)
    for i, turn in enumerate(turns):
        pack = step - turn
        mine = jnp.bitwise_xor(core_ref[0], 1 - turn)
        start = pl.multiple_of(mine * half, half)
        here = pl.ds(start, half)
        row_pos = start + lax.broadcasted_iota(jnp.int32, (half, rows), 0)
        allowed = (
            (row_pos < prompt_len)
            | (col_pos < prompt_len)
            | (seg_rows_ref[here, pack : pack + 1] == seg_cols_ref[pack : pack + 1, :])
        )
        loads[i].wait()
        queries = joined_ref[i, here, :width]
        mixed = []
        for head in range(heads):
            keys = joined_ref[i, :, width + head * size : width + (head + 1) * size]
            values = joined_ref[i, :, 2 * width + head * size : 2 * width + (head + 1) * size]
            scores = nt(queries[:, head * size : (head + 1) * size], keys) + bias_ref[head, here, :]
            scores = jnp.where(allowed, scores, blocked)
            top = jnp.max(scores, axis=-1, keepdims=True)
            raised = jnp.exp(scores - top)
            total = jnp.sum(raised, axis=-1, keepdims=True)
            probs = (raised * (1.0 / total)).astype(low)
            probs_ref[i, head] = probs
            copy = pltpu.make_async_copy(
                probs_ref.at[i, head], probs_outs[i].at[0, head], save_sems.at[i * (heads + 1) + head]
            )
            copy.start()
            saves.append(copy)
            mixed.append(nn(probs, values).astype(low))
        mixed = jnp.concatenate(mixed, axis=1)
        mixed_ref[i] = mixed
        copy = pltpu.make_async_copy(
            mixed_ref.at[i], mixed_any.at[pack, here], save_sems.at[i * (heads + 1) + heads]
        )
        copy.start()
        saves.append(copy)
        share = nn(mixed, w_out_ref[...])
        if turn == 1:
            share = share + got_ref[...].astype(wide)
        flat_refs[i][...] = share.astype(low)
    for copy in saves:
        copy.wait()


def attention_step(step, packs, prompt_len, core, joined, bias, seg_rows, seg_cols, w_out, got, mixed_all):
    _, rows, triple = joined.shape
    heads = bias.shape[0]
    width, model = w_out.shape
    half = rows // 2
    first, last = (0 if step < packs else 1), (1 if step > 0 else 0)
    steps = last - first + 1
    inside = pl.BlockSpec(memory_space=pltpu.VMEM)
    anywhere = pl.BlockSpec(memory_space=pl.ANY)
    in_specs = [pl.BlockSpec(memory_space=pltpu.SMEM), anywhere] + [inside] * 4
    args = [core, joined, bias, seg_rows, seg_cols, w_out]
    if last == 1:
        in_specs.append(inside)
        args.append(got)
    aliases = {}
    if mixed_all is not None:
        aliases = {len(args): 2 * steps}
        in_specs.append(anywhere)
        args.append(mixed_all)
    outs = kernel_call(
        functools.partial(attention_step_kernel, prompt_len, heads, first, last, step), 5, near=(2,), vmem=24,
        in_specs=in_specs,
        out_specs=[inside] * steps + [anywhere] * (steps + 1),
        out_shape=[jax.ShapeDtypeStruct((half, model), low)] * steps
        + [in_hbm((1, heads, half, rows), low)] * steps
        + [in_hbm((packs, rows, width), low)],
        scratch_shapes=[
            pltpu.VMEM((steps, rows, triple), low),
            pltpu.VMEM((steps, heads, half, rows), low),
            pltpu.VMEM((steps, half, width), low),
            pltpu.SemaphoreType.DMA((steps,)),
            pltpu.SemaphoreType.DMA((steps * (heads + 1),)),
        ],
        input_output_aliases=aliases,
        name="attention_step",
    )(*args)
    send, probs_send = (outs[0], outs[steps]) if first == 0 else (None, None)
    pair, probs_own = (outs[steps - 1], outs[2 * steps - 1]) if last == 1 else (None, None)
    return send, pair, probs_send, probs_own, outs[-1]


def feed_step_kernel(first, last, step, place_ref, rows_any, cot_any, gain_ref, *refs):
    refs = list(refs)
    turns = list(range(first, last + 1))
    sums = [refs[2 * i : 2 * i + 2] for i in range(len(turns))]
    refs = refs[2 * len(turns) :]
    if last == 1:
        got_ref, refs = refs[0], refs[1:]
    w_in_any, w_out_any, in_a, in_b, out_a, out_b = refs[:6]
    (rows_ref, cot_ref, normed_ref, active_ref, hidden_ref, result_ref, w_in_ref, w_out_ref,
     load_sems, save_sems) = refs[-10:]
    outs = refs[-10 - (3 + (1 if first == 0 else 0) + (4 if last == 1 else 0)) : -10]
    saved, rest = outs[:3], outs[3:]
    if first == 0:
        send_ref, rest = rest[0], rest[1:]
    if last == 1:
        middle_ref, grad_ref, gain_grad_ref, results_any = rest
    half = rows_ref.shape[0] // len(turns)
    half_rows = in_a.shape[0]
    core, side, part = place_ref[0], place_ref[1], place_ref[2]
    near = pl.ds(pl.multiple_of(part * half_rows, half_rows), half_rows)
    away = pl.ds(pl.multiple_of((1 - part) * half_rows, half_rows), half_rows)

    def block(turn):
        mine = jnp.bitwise_xor(core, 1 - turn)
        return step - turn, pl.ds(pl.multiple_of(mine * half, half), half)

    def span(index):
        return pl.ds(index * half, half)

    row_loads = [
        pltpu.make_async_copy(rows_any.at[*block(turn)], rows_ref.at[span(i)], load_sems.at[i])
        for i, turn in enumerate(turns)
    ]
    cot_loads = [
        pltpu.make_async_copy(cot_any.at[*block(turn)], cot_ref.at[span(i)], load_sems.at[2 + i])
        for i, turn in enumerate(turns)
    ]
    in_loads = [
        pltpu.make_async_copy(w_in_any, w_in_ref.at[side], load_sems.at[4]),
        pltpu.make_async_copy(in_a, w_in_ref.at[1 - side, near], load_sems.at[5]),
        pltpu.make_async_copy(in_b, w_in_ref.at[1 - side, away], load_sems.at[6]),
    ]
    out_loads = [
        pltpu.make_async_copy(w_out_any, w_out_ref.at[side], load_sems.at[7]),
        pltpu.make_async_copy(out_a, w_out_ref.at[1 - side, near], load_sems.at[8]),
        pltpu.make_async_copy(out_b, w_out_ref.at[1 - side, away], load_sems.at[9]),
    ]
    for copy in row_loads[::-1] + in_loads + cot_loads[::-1] + out_loads:
        copy.start()
    saves, kept = [], {}

    def save(index, place, source, target):
        copy = pltpu.make_async_copy(
            source, target.at[*block(turns[index])], save_sems.at[2 * place + index]
        )
        copy.start()
        saves.append(copy)

    def prepare(index):
        row_loads[index].wait()
        pair_ref, far_ref = sums[index]
        middle = rows_ref[span(index), :].astype(wide) + (
            pair_ref[...].astype(wide) + far_ref[...].astype(wide)
        )
        scale = lax.rsqrt(jnp.mean(middle * middle, axis=-1, keepdims=True) + epsilon)
        normed_ref[span(index), :] = (middle * scale * gain_ref[...]).astype(low)
        kept[index] = [middle, scale, None, None]
        save(index, 0, normed_ref.at[span(index)], saved[0])

    def expand(index, quarter):
        rows_at = span(index)
        inner = nn(normed_ref[rows_at, :], w_in_ref[quarter])
        share = 0.5 + 0.5 * lax.erf(inner * root_half)
        active = (inner * share).astype(low)
        slope = share + inner * (jnp.exp(-0.5 * inner * inner) * inv_root_tau)
        if quarter == 0 and index == len(turns) - 1:
            for copy in cot_loads + out_loads:
                copy.wait()
        hidden = (nt(cot_ref[rows_at, :], w_out_ref[quarter]) * slope).astype(low)
        active_ref[quarter, rows_at, :] = active
        hidden_ref[quarter, rows_at, :] = hidden
        feed_share = nn(active, w_out_ref[quarter])
        back_share = nt(hidden, w_in_ref[quarter])
        if quarter == 0:
            kept[index][2:] = [feed_share, back_share]
        else:
            kept[index][2] = kept[index][2] + feed_share
            kept[index][3] = kept[index][3] + back_share
            save(index, 1, active_ref.at[side, rows_at], saved[1])
            save(index, 2, hidden_ref.at[side, rows_at], saved[2])

    def finish_own(index):
        middle, scale, feed, back = kept[index]
        result_ref[...] = (middle + (feed + got_ref[:half, :].astype(wide))).astype(low)
        copy = pltpu.make_async_copy(result_ref, results_any.at[step - 1], save_sems.at[6])
        copy.start()
        saves.append(copy)
        upstream = back + got_ref[half:, :].astype(wide)
        scaled = upstream * gain_ref[...]
        inner = jnp.mean(scaled * middle, axis=-1, keepdims=True)
        grad = cot_ref[span(index), :].astype(wide) + scale * scaled - middle * (
            scale * scale * scale * inner
        )
        middle_ref[...] = grad
        grad_ref[...] = grad.astype(low)
        gain_grad_ref[...] = jnp.sum(upstream * middle * scale, axis=0, keepdims=True)

    def send_far(index):
        send_ref[:half, :] = kept[index][2].astype(low)
        send_ref[half:, :] = kept[index][3].astype(low)

    order = list(range(len(turns)))[::-1]
    prepare(order[0])
    for copy in in_loads:
        copy.wait()
    expand(order[0], 0)
    if len(order) == 2:
        prepare(order[1])
    expand(order[0], 1)
    if len(order) == 2:
        expand(order[1], 0)
    if last == 1:
        finish_own(order[0])
    if len(order) == 2:
        expand(order[1], 1)
    if first == 0:
        send_far(order[-1])
    for copy in saves:
        copy.wait()


def feed_step(step, packs, place, rows, cot, gain, sums, far_sums, own_pair, own_far, got,
              w_in, w_out, in_halves, out_halves, kept, results):
    _, row_count, model = rows.shape
    hidden = w_in.shape[1]
    half = row_count // 2
    first, last = (0 if step < packs else 1), (1 if step > 0 else 0)
    steps = last - first + 1
    inside = pl.BlockSpec(memory_space=pltpu.VMEM)
    anywhere = pl.BlockSpec(memory_space=pl.ANY)
    args = [place, rows, cot, gain]
    in_specs = [pl.BlockSpec(memory_space=pltpu.SMEM), anywhere, anywhere, inside]
    flats = ([sums, far_sums] if first == 0 else []) + ([own_pair, own_far, got] if last == 1 else [])
    args += flats
    in_specs += [inside] * len(flats)
    args += [w_in, w_out, *in_halves, *out_halves]
    in_specs += [anywhere] * 6
    aliases = {}
    if kept is not None:
        in_specs += [anywhere] * 3
        aliases = {len(args) + i: i for i in range(3)}
        args += list(kept)
    out_specs = [anywhere] * 3
    out_shape = [
        in_hbm((packs, row_count, model), low),
        in_hbm((packs, row_count, hidden), low),
        in_hbm((packs, row_count, hidden), low),
    ]
    if first == 0:
        out_specs.append(inside)
        out_shape.append(jax.ShapeDtypeStruct((row_count, model), low))
    if last == 1:
        if results is not None:
            in_specs.append(anywhere)
            aliases[len(args)] = len(out_shape) + 3
            args.append(results)
        out_specs += [inside] * 3 + [anywhere]
        out_shape += [
            in_hbm((half, model), wide),
            (jax.ShapeDtypeStruct if step < packs else in_hbm)((half, model), low),
            jax.ShapeDtypeStruct((1, model), wide),
            in_hbm((packs, half, model), low),
        ]
    outs = kernel_call(
        functools.partial(feed_step_kernel, first, last, step), 4 + 4 * steps, vmem=26,
        in_specs=in_specs,
        out_specs=out_specs,
        scratch_shapes=[
            pltpu.VMEM((steps * half, model), low),
            pltpu.VMEM((steps * half, model), low),
            pltpu.VMEM((steps * half, model), low),
            pltpu.VMEM((2, steps * half, hidden), low),
            pltpu.VMEM((2, steps * half, hidden), low),
            pltpu.VMEM((half, model), low),
            pltpu.VMEM((2, model, hidden), low),
            pltpu.VMEM((2, hidden, model), low),
            pltpu.SemaphoreType.DMA((10,)),
            pltpu.SemaphoreType.DMA((7,)),
        ],
        out_shape=out_shape,
        input_output_aliases=aliases,
        name="feed_step",
    )(*args)
    sent = outs[3] if first == 0 else None
    own = list(outs[-4:]) if last == 1 else [None] * 4
    return outs[:3], sent, own


def attention_back_kernel(
    heads, prompt_len, has_back, has_prev, core_ref, *refs,
):
    refs = list(refs)
    if has_back:
        own_ref, far_ref, w_out_ref, probs_own_ref, probs_far_ref, joined_ref = refs[:6]
        refs = refs[6:]
    w_joined_ref = refs.pop(0)
    if has_prev:
        prev_ref, got_ref, values_ref, grad_ref, gain_ref, gain_in_ref, head_in_ref = refs[:7]
        refs = refs[7:]
        if not has_back:
            other_gain_ref, refs = refs[0], refs[1:]
    outs = refs[-((5 if has_back else 0) + (3 if has_prev else 0)):]
    if has_prev:
        pair_ref, gain_out_ref, head_out_ref = outs[:3]
        outs = outs[3:]
        pair = (nn(prev_ref[...], w_joined_ref[...]) + got_ref[...].astype(wide)).astype(low)
        pair_ref[...] = pair
        top = head_in_ref.shape[0]
        values, upstream = values_ref[0].astype(wide), pair.astype(wide)
        grad, share = norm_back(upstream, gain_ref[...], values)
        gain_sum = gain_in_ref[...] + share
        gain_out_ref[...] = gain_sum
        grad = grad[:top] + jnp.where(core_ref[1] == 0, grad_ref[...], 0.0)
        head_sum = head_in_ref[...] + jnp.where(core_ref[0] == 0, grad, 0.0)
        if has_back:
            head_out_ref[...] = head_sum
        else:
            groups, group_rows, _ = head_out_ref.shape
            rows = prompt_len // groups
            head_out_ref[...] = jnp.zeros(head_out_ref.shape, low)
            for group in range(groups):
                head_out_ref[group, :rows, :] = head_sum[group * rows : (group + 1) * rows].astype(low)
                head_out_ref[group, rows : rows + 1, :] = gain_sum.astype(low)
                head_out_ref[group, rows + 1 : rows + 2, :] = other_gain_ref[...].astype(low)
    if not has_back:
        return
    send_ref, own_grads_ref, grads_ref, scores_ref, whole_ref = outs
    rows = joined_ref.shape[1]
    half = rows // 2
    width = w_out_ref.shape[0]
    size = width // heads
    core = core_ref[0]
    starts = [pl.multiple_of(core * half, half), pl.multiple_of((1 - core) * half, half)]
    ups, asks, asked = [], [], [[], []]
    for side, ref in enumerate((own_ref, far_ref)):
        whole_ref[0, pl.ds(starts[side], half), :] = ref[...]
        ups.append(nt(ref[...], w_out_ref[...]).astype(low))
        asks.append(joined_ref[0, pl.ds(starts[side], half), :width])
    grad_keys, grad_values = [], []
    for head in range(heads):
        cols = slice(head * size, (head + 1) * size)
        keys = joined_ref[0, :, width + head * size : width + (head + 1) * size]
        values = joined_ref[0, :, 2 * width + head * size : 2 * width + (head + 1) * size]
        grad_key, grad_value = None, None
        for side, probs_ref in enumerate((probs_own_ref, probs_far_ref)):
            probs = probs_ref[0, head]
            upstream = ups[side][:, cols]
            grad_probs = nt(upstream, values)
            spread = probs.astype(wide)
            inner = jnp.sum(spread * grad_probs, axis=-1, keepdims=True)
            grad_scores = (spread * (grad_probs - inner)).astype(low)
            scores_ref[0, head, pl.ds(starts[side], half), :] = grad_scores
            value_share = tn(upstream, probs)
            key_share = tn(asks[side][:, cols], grad_scores)
            grad_value = value_share if grad_value is None else grad_value + value_share
            grad_key = key_share if grad_key is None else grad_key + key_share
            asked[side].append(nn(grad_scores, keys))
        grad_values.append(grad_value.T)
        grad_keys.append(grad_key.T)
    rest = jnp.concatenate(grad_keys + grad_values, axis=1).astype(low)
    grads_ref[0, :, width:] = rest
    for side in range(2):
        grads_ref[0, pl.ds(starts[side], half), :width] = jnp.concatenate(asked[side], axis=1).astype(low)
    own_grads_ref[...] = grads_ref[0, pl.ds(starts[0], half), :]
    send_ref[...] = nn(grads_ref[0, pl.ds(starts[1], half), :], w_joined_ref[...]).astype(low)


def attention_back_step(step, packs, heads, prompt_len, other_gain, core, own, far, w_out, probs_own, probs_far, joined, w_joined,
                        prev, got, values, grad, gain, gain_sum, head_sum, kept):
    _, rows, triple = joined.shape
    width, model = w_out.shape
    half = rows // 2
    has_back, has_prev = step < packs, step > 0
    fixed = lambda t, c: (0, 0)
    flat = pl.BlockSpec((half, model), fixed)
    anywhere = pl.BlockSpec(memory_space=pl.ANY)
    in_specs, args, out_specs, out_shape, aliases = [], [core], [], [], {}
    if has_back:
        in_specs += [
            flat,
            flat,
            pl.BlockSpec((width, model), fixed),
            pl.BlockSpec((1, heads, half, rows), lambda t, c: (0, 0, 0, 0)),
            pl.BlockSpec((1, heads, half, rows), lambda t, c: (0, 0, 0, 0)),
            pl.BlockSpec((1, rows, triple), lambda t, c: (step, 0, 0)),
        ]
        args += [own, far, w_out, probs_own, probs_far, joined]
    in_specs.append(pl.BlockSpec((triple, model), fixed))
    args.append(w_joined)
    if has_prev:
        line = pl.BlockSpec((1, model), fixed)
        head = pl.BlockSpec(head_sum.shape, fixed)
        in_specs += [
            pl.BlockSpec((half, triple), fixed),
            flat,
            pl.BlockSpec((1, half, model), lambda t, c: (step - 1, c[0], 0)),
            head,
            line,
            line,
            head,
        ]
        args += [prev, got, values, grad, gain, gain_sum, head_sum]
        if has_back:
            head_out = in_hbm(head_sum.shape, wide)
        else:
            in_specs.append(line)
            args.append(other_gain)
            groups = Small.groups
            small = (groups, -(-(prompt_len // groups + 3) // 16) * 16, model)
            head, head_out = pl.BlockSpec(small, lambda t, c: (0, 0, 0)), jax.ShapeDtypeStruct(small, low)
        out_specs += [flat, line, head]
        out_shape += [
            jax.ShapeDtypeStruct((half, model), low),
            jax.ShapeDtypeStruct((1, model), wide),
            head_out,
        ]
    if has_back:
        if kept is not None:
            in_specs += [anywhere] * 3
            aliases = {len(args) + i: len(out_shape) + 2 + i for i in range(3)}
            args += list(kept)
        out_specs += [
            flat,
            pl.BlockSpec((half, triple), fixed),
            pl.BlockSpec((1, rows, triple), lambda t, c: (step, 0, 0)),
            pl.BlockSpec((1, heads, rows, rows), lambda t, c: (step, 0, 0, 0)),
            pl.BlockSpec((1, rows, model), lambda t, c: (step, 0, 0)),
        ]
        out_shape += [
            jax.ShapeDtypeStruct((half, model), low),
            in_hbm((half, triple), low),
            in_hbm((packs, rows, triple), low),
            in_hbm((packs, heads, rows, rows), low),
            in_hbm((packs, rows, model), low),
        ]
    outs = list(
        kernel_call(
            functools.partial(attention_back_kernel, heads, prompt_len, has_back, has_prev), 6,
            least=1000 if step == packs - 1 else 400000,
            grid_spec=pltpu.PrefetchScalarGridSpec(
                num_scalar_prefetch=1, grid=(1,), in_specs=in_specs, out_specs=out_specs
            ),
            out_shape=out_shape,
            input_output_aliases=aliases,
                name="attention_back_step",
        )(*args)
    )
    done, outs = (outs[:3], outs[3:]) if has_prev else ((None,) * 3, outs)
    send, own_grads, *kept = outs if has_back else (None, None)
    return done, send, own_grads, kept


def finish_kernel(packs, core_ref, rows_any, gain_ref, *refs):
    out_ref, rows_ref, sems = refs[-3:]
    half = rows_ref.shape[1]
    start = pl.multiple_of(core_ref[0] * half, half)
    copies = [
        pltpu.make_async_copy(rows_any.at[pack, pl.ds(start, half)], rows_ref.at[i], sems.at[i])
        for i, pack in enumerate(packs)
    ]
    for copy in copies:
        copy.start()
    for i, copy in enumerate(copies):
        copy.wait()
        pair_ref, far_ref, grad_ref = refs[3 * i : 3 * i + 3]
        upstream = pair_ref[...].astype(wide) + far_ref[...].astype(wide)
        grad, _ = norm_back(upstream, gain_ref[...], rows_ref[i].astype(wide))
        out_ref[i] = (grad_ref[...] + grad).astype(low)


def finish(packs, core, rows, gain, parts):
    half, model = parts[0][0].shape
    inside = pl.BlockSpec(memory_space=pltpu.VMEM)
    return kernel_call(
        functools.partial(finish_kernel, packs), 1.5 * len(packs), vmem=24,
        in_specs=[pl.BlockSpec(memory_space=pltpu.SMEM), pl.BlockSpec(memory_space=pl.ANY), inside]
        + [inside] * (3 * len(packs)),
        out_specs=inside,
        out_shape=jax.ShapeDtypeStruct((len(packs), half, model), low),
        scratch_shapes=[
            pltpu.VMEM((len(packs), half, model), low),
            pltpu.SemaphoreType.DMA((len(packs),)),
        ],
        name="finish",
    )(core, rows, gain, *[v for part in parts for v in part])


def middle_kernel(packs, place_ref, scores_any, rows_any, gain_ref, own_ref, far_ref, *refs):
    refs, (line_ref, ended_ref, out_any, scores_ref, values_ref, load_sems, save_sems) = refs[:-7], refs[-7:]
    heads = scores_ref.shape[0]
    half = values_ref.shape[1]
    core = place_ref[0]
    start = pl.multiple_of(core * half, half)
    value_loads = [
        pltpu.make_async_copy(rows_any.at[pack, pl.ds(start, half)], values_ref.at[i], load_sems.at[i])
        for i, pack in enumerate(packs)
    ]
    score_loads = [
        pltpu.make_async_copy(scores_any.at[:, head], scores_ref.at[head], load_sems.at[len(packs) + head])
        for head in range(heads)
    ]
    for copy in value_loads + score_loads:
        copy.start()
    saves = []
    for pack in range(own_ref.shape[0]):
        for side, ref in enumerate((own_ref, far_ref)):
            there = pl.ds(pl.multiple_of(jnp.bitwise_xor(core, side) * half, half), half)
            copy = pltpu.make_async_copy(ref.at[pack], out_any.at[pack, there], save_sems.at[2 * pack + side])
            copy.start()
            saves.append(copy)
    for i, copy in enumerate(value_loads):
        copy.wait()
        pair_ref, far_pair_ref, grad_ref = refs[3 * i : 3 * i + 3]
        upstream = pair_ref[...].astype(wide) + far_pair_ref[...].astype(wide)
        grad, _ = norm_back(upstream, gain_ref[...], values_ref[i].astype(wide))
        ended_ref[i] = (grad_ref[...] + grad).astype(low)
    for head, copy in enumerate(score_loads):
        copy.wait()
        line_ref[head] = diagonal_line(scores_ref.at[head])
    for copy in saves:
        copy.wait()


def middle_work(packs, place, scores, rows, gain, own, far, parts):
    count, heads, row_count, _ = scores.shape
    _, half, model = own.shape
    inside, anywhere = pl.BlockSpec(memory_space=pltpu.VMEM), pl.BlockSpec(memory_space=pl.ANY)
    return kernel_call(
        functools.partial(middle_kernel, packs), 12, vmem=40, least=1000,
        in_specs=[pl.BlockSpec(memory_space=pltpu.SMEM), anywhere, anywhere] + [inside] * (3 + 3 * len(packs)),
        out_specs=[inside, inside, anywhere],
        out_shape=[
            jax.ShapeDtypeStruct((heads, 1, 2 * row_count), wide),
            jax.ShapeDtypeStruct((len(packs), half, model), low),
            in_hbm((count, row_count, model), low),
        ],
        scratch_shapes=[
            pltpu.VMEM((heads, count, row_count, row_count), low),
            pltpu.VMEM((len(packs), half, model), low),
            pltpu.SemaphoreType.DMA((len(packs) + heads,)),
            pltpu.SemaphoreType.DMA((2 * count,)),
        ],
        name="middle_work",
    )(place, scores, rows, gain, own, far, *[v for part in parts for v in part])


def weave_kernel(core_ref, *refs):
    out_ref, rows_ref, woven_ref = refs[-3:]
    half = rows_ref.shape[0] // 2
    text = out_ref.shape[0]
    pack = 0
    for own_ref, far_ref in zip(refs[:-3:2], refs[1:-3:2]):
        for i in range(own_ref.shape[0]):
            for side, ref in enumerate((own_ref, far_ref)):
                start = pl.multiple_of(jnp.bitwise_xor(core_ref[0], side) * half, half)
                rows_ref[pl.ds(start, half), :] = ref[i].astype(wide)
            woven_ref[:, pack, :] = rows_ref[2 * half - text :, :]
            pack += 1
    out_ref[...] = woven_ref[...].astype(low)


def weave_halves(core, pairs, text):
    packs = sum(own.shape[0] for own, _ in pairs)
    _, half, model = pairs[0][0].shape
    inside = pl.BlockSpec(memory_space=pltpu.VMEM)
    return kernel_call(
        weave_kernel, 4, vmem=32, least=1000,
        in_specs=[pl.BlockSpec(memory_space=pltpu.SMEM)] + [inside] * (2 * len(pairs)),
        out_specs=inside,
        out_shape=jax.ShapeDtypeStruct((text, packs, model), low),
        scratch_shapes=[pltpu.VMEM((2 * half, model), wide), pltpu.VMEM((text, packs, model), wide)],
        name="weave_halves",
    )(core, *[v for pair in pairs for v in pair])


def weight_kernel(pairs, split, where_ref, *refs):
    if split:
        keep_ref, send_ref, total_ref = refs[-3:]
    else:
        whole_ref, total_ref = refs[-2:]
    column = 0
    for i in range(pairs):
        right = refs[2 * i + 1][...]
        total_ref[:, column : column + right.shape[1]] = tn(refs[2 * i][...], right)
        column += right.shape[1]
    if not split:
        whole_ref[...] = total_ref[...].astype(low)
        return
    count, block, _ = keep_ref.shape
    side = jnp.bitwise_and(where_ref[0], 1)
    for i in range(count):
        for ref, chosen in ((keep_ref, side), (send_ref, 1 - side)):
            start = pl.multiple_of((2 * i + chosen) * block, 8)
            ref[i] = total_ref[pl.ds(start, block), :].astype(low)


def weight_shares(where, count, pairs, split):
    rows, model = pairs[0][0].shape
    widths = [right.shape[1] for _, right in pairs]
    turns, width = 2, sum(widths)
    block = model // count
    in_specs = []
    for n in widths:
        in_specs += [
            pl.BlockSpec((rows, model // turns), lambda t, w: (0, t)),
            pl.BlockSpec((rows, n), lambda t, w: (0, 0)),
        ]
    if split:
        out_specs = [pl.BlockSpec((count // 2 // turns, block, width), lambda t, w: (t, 0, 0))] * 2
        out_shape = [jax.ShapeDtypeStruct((count // 2, block, width), low)] * 2
    else:
        out_specs = pl.BlockSpec((model // turns, width), lambda t, w: (t, 0))
        out_shape = in_hbm((model, width), low)
    return kernel_call(
        functools.partial(weight_kernel, len(pairs), split), 6, vmem=26,
        grid_spec=pltpu.PrefetchScalarGridSpec(
            num_scalar_prefetch=1,
            grid=(turns,),
            in_specs=in_specs,
            out_specs=out_specs,
            scratch_shapes=[pltpu.VMEM((model // turns, width), wide)],
        ),
        out_shape=out_shape,
        name="weight_shares",
    )(where, *[value for pair in pairs for value in pair])


def fold_kernel(count, where_ref, *refs):
    ins, outs = refs[:count], refs[count:]
    group = outs[0].shape[0]
    for flip, out_ref in enumerate(outs):
        for piece in range(group):
            spot = jnp.bitwise_xor(where_ref[0], flip)
            spot = spot * group + piece if len(outs) == 4 else piece * 2 + spot
            total = ins[0][spot].astype(wide)
            for ref in ins[1:]:
                total = total + ref[spot].astype(wide)
            out_ref[piece] = total.astype(out_ref.dtype)


def fold(where, parts, cuts):
    whole, block, width = parts[0].shape
    shape = (whole // cuts, block, width)
    inside = pl.BlockSpec(memory_space=pltpu.VMEM)
    return kernel_call(
        functools.partial(fold_kernel, len(parts)), 1.5, vmem=24,
        in_specs=[pl.BlockSpec(memory_space=pltpu.SMEM)] + [inside] * len(parts),
        out_specs=[inside] * cuts,
        out_shape=[jax.ShapeDtypeStruct(shape, low)] * cuts,
        name="fold",
    )(where, *parts)


def unfold_kernel(count, cuts, *refs):
    ins, outs = refs[:count], refs[count:]
    total = ins[0][0].astype(wide)
    for ref in ins[1:]:
        total = total + ref[0].astype(wide)
    for (start, width, turned), out_ref in zip(cuts, outs):
        piece = total[:, start : start + width]
        out_ref[...] = piece.T if turned else piece


def unfold_both_kernel(*refs):
    count = (len(refs) - 2) // 2
    for i in range(2):
        ins = refs[i * count : (i + 1) * count]
        total = ins[0][0].astype(wide)
        for ref in ins[1:]:
            total = total + ref[0].astype(wide)
        refs[2 * count + i][...] = total


def unfold_both(first, second):
    inside = pl.BlockSpec(memory_space=pltpu.VMEM)
    return kernel_call(
        unfold_both_kernel, 1.5,
        in_specs=[inside] * (2 * len(first)),
        out_specs=[inside] * 2,
        out_shape=[jax.ShapeDtypeStruct(parts[0].shape[1:], wide) for parts in (first, second)],
        name="unfold_both",
    )(*first, *second)


def unfold(parts, cuts):
    block = parts[0].shape[1]
    inside = pl.BlockSpec(memory_space=pltpu.VMEM)
    return kernel_call(
        functools.partial(unfold_kernel, len(parts), cuts), 1.5,
        in_specs=[inside] * len(parts),
        out_specs=[inside] * len(cuts),
        out_shape=[
            jax.ShapeDtypeStruct((width, block) if turned else (block, width), wide)
            for _, width, turned in cuts
        ],
        name="unfold",
    )(*parts)


def joint_fold_kernel(spot, where_ref, keep_ref, got_ref, mine_ref, near_ref, rel_ref, *refs):
    outs, total_ref = refs[:4], refs[4]
    block = keep_ref.shape[1]
    group = keep_ref.shape[0] // 4
    for flip, out_ref in enumerate(outs):
        chosen = jnp.bitwise_xor(where_ref[0], flip)
        for piece in range(group):
            total = keep_ref[chosen * group + piece].astype(wide) + got_ref[chosen * group + piece].astype(wide)
            out_ref[piece * block : (piece + 1) * block, :] = total.astype(low)
        total_ref[...] = mine_ref[chosen].astype(wide) + near_ref[chosen].astype(wide)
        total_ref[spot : spot + 1, :] = rel_ref[...]
        out_ref[group * block :, :] = total_ref[...].astype(low)


def joint_fold(where, parts, smalls, rel, spot):
    whole, block, width = parts[0].shape
    rows = smalls[0].shape[1]
    shape = (whole // 4 * block + rows, width)
    inside = pl.BlockSpec(memory_space=pltpu.VMEM)
    return kernel_call(
        functools.partial(joint_fold_kernel, spot), 2,
        in_specs=[pl.BlockSpec(memory_space=pltpu.SMEM)] + [inside] * 5,
        out_specs=[inside] * 4,
        out_shape=[jax.ShapeDtypeStruct(shape, low)] * 4,
        scratch_shapes=[pltpu.VMEM((rows, width), wide)],
        name="joint_fold",
    )(where, *parts, *smalls, rel)


def joint_unfold_kernel(cuts, *refs):
    ins, outs = refs[:4], refs[4:]
    total = ins[0][...].astype(wide)
    for ref in ins[1:]:
        total = total + ref[...].astype(wide)
    small = outs[-1].shape[0]
    outs[-1][...] = total[-small:].astype(low)
    for (start, width, turned), out_ref in zip(cuts, outs):
        piece = total[:-small, start : start + width]
        out_ref[...] = piece.T if turned else piece


def joint_unfold(parts, cuts, rows):
    block = parts[0].shape[0] - rows
    inside = pl.BlockSpec(memory_space=pltpu.VMEM)
    return kernel_call(
        functools.partial(joint_unfold_kernel, cuts), 1.5,
        in_specs=[inside] * 4,
        out_specs=[inside] * (len(cuts) + 1),
        out_shape=[
            jax.ShapeDtypeStruct((width, block) if turned else (block, width), wide)
            for _, width, turned in cuts
        ]
        + [jax.ShapeDtypeStruct((rows, parts[0].shape[1]), low)],
        name="joint_unfold",
    )(*parts)


def tie(*values):
    return lax.optimization_barrier(values)


def stages_of(count):
    bits = bits_of(count)
    rest = bits[1:][::-1]
    return [bits[:1]] + [rest[i : i + 2] for i in range(0, len(rest), 2)]


class Scatter:
    def __init__(self, keep, send, cuts):
        self.bits, self.cuts = bits_of(lax.axis_size("dp"))[1:], cuts
        self.parts = [keep, swap(send, "dp", 1)]

    def step(self):
        if self.cuts == 4:
            bit, self.bits = self.bits[-2], self.bits[:-2]
        else:
            bit, self.bits = self.bits[0], self.bits[1:]
        where = ((lax.axis_index("dp") // bit) % self.cuts).astype(jnp.int32).reshape(1)
        own, *sends = fold(where, self.parts, self.cuts)
        self.parts = [own] + [swap(v, "dp", bit * (flip + 1)) for flip, v in enumerate(sends)]

    def end(self, pieces):
        while self.bits:
            self.step()
        return unfold(self.parts, pieces)


def look_up(prompt_ids, table, prompt_delta):
    prompt_len = prompt_ids.shape[0]
    table_rows, model = table.shape
    groups = 2
    part = -(-prompt_len // (16 * groups)) * 16
    dp_index, mp_index = lax.axis_index("dp"), lax.axis_index("mp") % groups
    padded = jnp.pad(prompt_ids, (0, part * groups - prompt_len), constant_values=-1)
    ids = lax.dynamic_slice_in_dim(padded, mp_index * part, part)
    size, block = prompt_delta.shape[0], part * model
    line = jnp.pad(prompt_delta, (block, block))
    start = jnp.clip(block + mp_index * block - dp_index * size, 0, block + size)
    placed = lax.dynamic_slice_in_dim(line, start, block).reshape(part, model)
    local = jnp.where(ids < 0, -1, ids - dp_index * table_rows)
    if table_rows % 16 == 0:
        return look_up_rows(local, table, placed)
    selector = (local[:, None] == jnp.arange(table_rows, dtype=jnp.int32)[None, :]).astype(low)
    return (jnp.dot(selector, table, preferred_element_type=wide) + placed).astype(low)


def own_half(weight):
    part = lax.axis_index("dp") % 2
    halves = weight.reshape(2, weight.shape[0] // 2, weight.shape[1])
    return lax.dynamic_index_in_dim(halves, part, 0, keepdims=False)


class Small:
    groups = 4

    def __init__(self, total, prompt_len):
        self.total, self.share = total, prompt_len // self.groups
        self.mp_bits = bits_of(lax.axis_size("mp"))
        self.hop_mp()

    def hop_mp(self):
        bit, self.mp_bits = self.mp_bits[0], self.mp_bits[1:]
        self.keep, self.got = self.total, swap(self.total, "mp", bit)

    def land(self):
        self.total = (self.keep.astype(wide) + self.got.astype(wide)).astype(low)

    def join(self, tail, rel):
        self.rel = rel
        row = jnp.pad(rel.reshape(1, -1), ((0, 0), (0, self.keep.shape[2] - rel.size)))
        high, tail.bits = tail.bits[-2], tail.bits[:-2]
        where = ((lax.axis_index("dp") // high) % 4).astype(jnp.int32).reshape(1)
        self.block = tail.parts[0].shape[1]
        own, *sends = joint_fold(where, tail.parts, (self.keep, self.got), row, self.share + 2)
        self.parts = [own] + [swap(v, "dp", high * (flip + 1)) for flip, v in enumerate(sends)]

    def split(self, tail, cuts):
        rows = self.keep.shape[1]
        if not tail.bits:
            *results, self.total = joint_unfold(self.parts, cuts, rows)
            return results
        tail.parts = [v[:-rows].reshape(-1, self.block, v.shape[1]) for v in self.parts]
        self.total = sum(v[-rows:].astype(wide) for v in self.parts).astype(low)
        return tail.end(cuts)

    def results(self):
        dp_count, dp_index = lax.axis_size("dp"), lax.axis_index("dp")
        total = self.total
        for bit in bits_of(dp_count)[:-2]:
            total = total.astype(low)
            total = total.astype(wide) + swap(total, "dp", bit).astype(wide)
        share, model = self.share, total.shape[1]
        inside = dp_count // self.groups
        size = share * model // inside
        prompt_grad = lax.dynamic_slice_in_dim(total[:share].reshape(-1), (dp_index % inside) * size, size)
        width = model // dp_count
        gains = lax.dynamic_slice_in_dim(total[share : share + 2], dp_index * width, width, axis=1)
        piece = self.rel.size // dp_count
        rel_out = lax.dynamic_slice_in_dim(total[share + 2], dp_index * piece, piece)
        return prompt_grad, gains[0], gains[1], rel_out.reshape(-1, self.rel.shape[1])


def body(
    tokens, cotangent, segment_ids, prompt_ids, rel_buckets, table, prompt_delta, norm1_gain,
    w_query, w_key, w_value, w_output, rel_bias, norm2_gain, w_inner, w_outer,
):
    prompt_len = prompt_ids.shape[0]
    packs, rows, model = cotangent.shape
    bucket_count, heads = rel_bias.shape
    width = w_query.shape[1]
    groups = lax.axis_size("dp")
    mp_bits = bits_of(lax.axis_size("mp"))
    mp_index = lax.axis_index("mp").astype(jnp.int32)
    place = jnp.stack([mp_index % 2, (mp_index // 2) % 2, (lax.axis_index("dp") % 2).astype(jnp.int32)])
    gain1, gain2 = norm1_gain[None, :], norm2_gain[None, :]
    w_q, w_k, w_v = w_query.T, w_key.T, w_value.T

    in_near = swap(own_half(w_inner), "mp", 2)
    total = look_up(prompt_ids, table, prompt_delta)

    w_joined = jnp.concatenate([w_q, w_k, w_v], axis=0)
    bucket_hot = (
        rel_buckets[:, None] == jnp.arange(bucket_count, dtype=jnp.int32)[None, :]
    ).astype(wide)
    bucket_hot = jnp.pad(bucket_hot, ((0, 1), (0, 0)))
    turned = jnp.roll(bucket_hot, -(rows - 1), axis=0)
    bias_line = jnp.dot(turned, rel_bias, precision=highest).T
    marks = jnp.pad(segment_ids, ((0, 0), (prompt_len, 0)), constant_values=-1)
    seg_rows, seg_cols = marks.T, marks

    texts, half_packs = [], packs // 2
    for hop, bit in enumerate(bits_of(groups)):
        got = swap(total, "dp", bit)
        if hop == 0:
            bias = bias_grid_of(bias_line[:, None, :])
            got, bias, seg_rows, seg_cols = tie(got, bias, seg_rows, seg_cols)
        if hop == 1:
            texts = text_projections(0, half_packs, rows, tokens, gain1, w_joined, texts)
            got, *texts = tie(got, *texts)
        if hop == 2:
            texts = text_projections(half_packs, packs - half_packs, rows, tokens, gain1, w_joined, texts)
            got, *texts = tie(got, *texts)
            got, in_near = tie(got, in_near)
            in_away = swap(in_near, "dp", 1)
            out_near = swap(own_half(w_outer), "mp", 2)
        total = (total.astype(wide) + got.astype(wide)).astype(low)
    whole_rows, normed1, joined = texts
    pieces = jnp.stack([total, swap(total, "mp", 1)])
    whole_rows, normed1, joined = add_prompt(
        place[:1], pieces, gain1, w_joined, whole_rows, normed1, joined
    )

    pairs, fars, pairs_far, fars_far, probs_far, probs_own, mixed, got = [], [], [], [], [], [], None, None

    def attend(step):
        nonlocal mixed, got, place, in_away, out_near, out_away
        send, pair, probs_send, probs_pair, mixed = attention_step(
            step, packs, prompt_len, place, joined, bias, seg_rows, seg_cols, w_output, got, mixed
        )
        if step == 0:
            place, out_near, send = tie(place, out_near, send)
            out_away = swap(out_near, "dp", 1)
        else:
            place, pair = tie(place, pair)
        if step == 1:
            place, in_away = tie(place, in_away)
        if send is not None:
            probs_far.append(probs_send)
            got = swap(send, "mp", 1)
        if pair is not None:
            probs_own.append(probs_pair)
            pairs.append(pair)
            fars.append(swap(pair, "mp", 2))
            pairs_far.append(swap(pair, "mp", 1))
            fars_far.append(swap(fars[-1], "mp", 1))

    out_away = None

    def arrive(pack):
        nonlocal place
        place, fars[pack], pairs_far[pack], fars_far[pack] = tie(
            place, fars[pack], pairs_far[pack], fars_far[pack]
        )

    kept, sent, results, grads_wide, grads_low = None, None, None, [], []
    gain2_sum, none = 0.0, [None]
    back_kept, prev, got = None, None, None
    gain1_sum, head_sum = jnp.zeros((1, model), wide), jnp.zeros((128, model), wide)
    text_rows, pairs_back = [], []

    def feed(step):
        nonlocal kept, sent, results, gain2_sum, place
        kept, new_sent, done = feed_step(
            step, packs, place, whole_rows, cotangent, gain2,
            (pairs_far + none)[step], (fars_far + none)[step],
            (none + pairs)[step], (none + fars)[step], sent,
            w_inner, w_outer, (in_near, in_away), (out_near, out_away), kept, results,
        )
        if step < packs:
            place, new_sent = tie(place, new_sent)
            sent = swap(new_sent, "mp", 1)
        else:
            place, done[1] = tie(place, done[1])
        if step > 0:
            grads_wide.append(done[0])
            grads_low.append((done[1], swap(done[1], "mp", 1)))
            gain2_sum, results = gain2_sum + done[2], done[3]

    def back(step):
        nonlocal back_kept, prev, got, gain1_sum, head_sum, place
        live = step < packs
        done, send, own_grads, back_new = attention_back_step(
            step, packs, heads, prompt_len, gain2_sum, place, *(grads_low[step] if live else none * 2), w_output,
            probs_own[step] if live else None, probs_far[step] if live else None, joined, w_joined,
            prev, got, whole_rows, grads_wide[step - 1] if step else None, gain1, gain1_sum, head_sum,
            back_kept,
        )
        if live:
            place, send = tie(place, send)
            back_kept, prev, got = back_new, own_grads, swap(send, "mp", 1)
        if step > 0:
            pair, gain1_sum, head_sum = done
            pairs_back.append([pair, swap(pair, "mp", 2)])

    def meet(pack):
        nonlocal place
        place, grads_low[pack] = tie(place, grads_low[pack])

    def end(*ended):
        nonlocal place
        rows_low = finish(ended, place, whole_rows, gain1, [(*pairs_back[p], grads_wide[p]) for p in ended])
        place, rows_low = tie(place, rows_low)
        text_rows.append((rows_low, swap(rows_low, "mp", 1)))

    def flat(value):
        return value.reshape(packs * rows, -1)

    for step in range(packs):
        attend(step)
    place, out_away = tie(place, out_away)
    arrive(0)
    feed(0)
    attend(packs)
    arrive(1)
    feed(1)
    for step in range(2, packs):
        arrive(step)
        meet(step - 2)
        feed(step)
        back(step - 2)
    meet(packs - 2)
    feed(packs)
    normed2, active, hidden = kept
    where = lax.axis_index("dp").astype(jnp.int32).reshape(1)
    where, place = tie(where, place)
    inner_shares = weight_shares(where, groups, [(flat(normed2), flat(hidden))], True)
    place, inner_shares = tie(place, inner_shares)
    inner = Scatter(*inner_shares, 2)
    where, place = tie(where, place)
    outer_shares = weight_shares(where, groups, [(flat(cotangent), flat(active))], True)
    place, outer_shares = tie(place, outer_shares)
    outer = Scatter(*outer_shares, 2)
    meet(packs - 1)
    back(packs - 2)
    far_results = swap(results, "mp", 1)
    place, far_results, pairs_back[0], inner.parts = tie(place, far_results, pairs_back[0], inner.parts)
    inner.step()
    back(packs - 1)
    place, pairs_back[1], inner.parts, outer.parts = tie(place, pairs_back[1], inner.parts, outer.parts)
    inner.step()
    outer.step()
    place, inner.parts[0], outer.parts[0] = tie(place, inner.parts[0], outer.parts[0])
    grad_joined, scores, grad_rows = back_kept
    where, place = tie(where, place)
    tail_shares = weight_shares(
        where, groups, [(flat(normed1), flat(grad_joined)), (flat(grad_rows), flat(mixed))], True
    )
    place, *tail_shares = tie(place, *tail_shares)
    tail = Scatter(*tail_shares, 4)
    side_one = (mp_index // 2) % 2 == 1
    gain2_sum = jnp.where(side_one, 0.0, gain2_sum)
    back(packs)
    place, head_sum = tie(place, head_sum)
    small = Small(head_sum, prompt_len)
    place, outer.parts = tie(place, outer.parts)
    outer.step()
    place, outer.parts[0] = tie(place, outer.parts[0])
    small.land()
    small.hop_mp()
    early = list(range(packs - 1))
    line, rows_low, out = middle_work(
        early, place, scores, whole_rows, gain1, results, far_results,
        [(*pairs_back[p], grads_wide[p]) for p in early],
    )
    place, line, rows_low = tie(place, line, rows_low)
    text_rows.append((rows_low, swap(rows_low, "mp", 1)))
    rel_share = jnp.einsum("ht,tb->bh", line[:, 0, :], turned, precision=highest)
    place, rel_share, tail.parts, small.got = tie(place, rel_share, tail.parts, small.got)
    small.join(tail, rel_share)
    place, inner.parts, outer.parts = tie(place, inner.parts, outer.parts)
    while inner.bits:
        inner.step()
    while outer.bits:
        outer.step()
    inner_grad, outer_grad = unfold_both(inner.parts, outer.parts)
    end(packs - 1)
    place, text_rows[-1] = tie(place, text_rows[-1])
    grad_tokens = weave_halves(place, text_rows, rows - prompt_len)
    grad_tokens, small.parts = tie(grad_tokens, small.parts)
    grad_tokens = jnp.transpose(grad_tokens, (1, 0, 2))
    query_grad, key_grad, value_grad, output_grad = small.split(
        tail, tuple((i * width, width, i == 3) for i in range(4))
    )
    prompt_grad, gain1_grad, gain2_grad, rel_grad = small.results()
    return (
        out, grad_tokens, prompt_grad, gain1_grad, query_grad, key_grad, value_grad, output_grad,
        rel_grad, gain2_grad, inner_grad, outer_grad.T,
    )


def solution(mesh):
    in_specs = (
        P("dp", None, None),
        P("dp", None, None),
        P("dp", None),
        P(),
        P(),
        P("dp", None),
        P("dp"),
        P(),
        P(None, "mp"),
        P(None, "mp"),
        P(None, "mp"),
        P("mp", None),
        P(None, "mp"),
        P(),
        P(None, "mp"),
        P("mp", None),
    )
    out_specs = (
        P("dp", None, None),
        P("dp", None, None),
        P("dp"),
        P("dp"),
        P("dp", "mp"),
        P("dp", "mp"),
        P("dp", "mp"),
        P("mp", "dp"),
        P("dp", "mp"),
        P("dp"),
        P("dp", "mp"),
        P("mp", "dp"),
    )
    return jax.shard_map(body, mesh=mesh, in_specs=in_specs, out_specs=out_specs, check_vma=False)
```
